32 devices in a mesh: batch: 8 (over y, x, core), slab: 4 (over z).
Axes of the slice: x: 2, y: 2, z: 4, core: 2. Of those that a mesh axis runs over, the one named last changes fastest.
Arguments:
- points: bfloat16 [7, 35, 16384], P(None, None, ('batch', 'slab')), may hold values from -6 to 6
- point_counts: int32 [16384], P(('batch', 'slab')), may hold values from 1 to 35, as said below
- voxel_cells: int32 [16384], P(('batch', 'slab')), may hold values from 0 to 4095, as said below
- pos_anchors: int32 [8, 40], P('batch'), may hold values from 0 to 1023, as said below
- pos_counts: int32 [8], P('batch'), may hold values from 0 to 40, as said below
- reg_targets: float32 [8, 14, 16, 32], P('batch'), may hold values from -6 to 6
- params: float32 [2537584], P('slab')
- moment1: float32 [2537584], P('slab'), may hold values from -1.9073486e-06 to 1.9073486e-06
- moment2: float32 [2537584], P('slab'), may hold values from 1.5763025e-15 to 6.30521e-15
Outputs:
- head_maps: float32 [8, 16, 16, 32], P('batch', None, 'slab')
- points_grad: float32 [7, 35, 16384], P(None, None, ('batch', 'slab'))
- new_moment1: float32 [2537584], P('slab')
- new_moment2: float32 [2537584], P('slab')
- new_params: float32 [2537584], P('slab')
- grad_norm: float32 [], replicated
The draws below stay inside these ranges and needn't reach their ends.
Inputs may be any that keep to these rules, and one draw needn't show every extreme that they name: `point_counts`: at least one point; every block of 512 voxels has a voxel with 35. `voxel_cells`: distinct within each block of 512 voxels (one scene, one slab). `pos_anchors`: distinct within a scene. `pos_counts`: some scene has 40, some has none.
All inputs are finite; a program needn't handle non-finite values.
Results may differ from the reference program's by a relative error of at most 0.017.
Values may be sent and summed in bfloat16 or wider, within the bound.
No kernel may reach another device: no remote copies, remote signals or barrier semaphores. Data moves between devices by JAX's collectives and lax.ppermute only.
A program may use at most 192 MiB of HBM per device.

```python
import math
import jax
import jax.numpy as jnp
from jax import lax

VF1 = 16
VF2 = 64
FC = 128
C3 = 64
R1 = 128
R3 = 256
UP = 256
PTS = 35
POSMAX = 40
STEP = 10
VOX_DEV = 512
GY = 32
GX = 64
HY = 16
HX = 32
ANCH = 1024
SCENES = 8
VOXELS = 16384
NPARAM = 2537584
N_SLAB = 4


def draw_params(key, part):
    key = jax.random.fold_in(key, 11)
    layer_list = [((VF1, 7), 7), ((VF2, 2 * VF1), 2 * VF1), ((FC, 2 * VF2), 2 * VF2), ((3, 3, 3, FC, C3), 27 * FC), ((3, 3, 3, C3, C3), 27 * C3), ((3, 3, 3, C3, C3), 27 * C3), ((3, 3, 2 * C3, R1), 18 * C3), ((3, 3, R1, R1), 9 * R1), ((3, 3, R1, R3), 9 * R1), ((3, 3, R1, UP), 9 * R1), ((2, 2, R1, UP), R1), ((4, 4, R3, UP), R3), ((3 * UP, 16), 3 * UP)]
    pieces = []
    for number, layer_item in enumerate(layer_list):
        entries = math.prod(layer_item[0])
        normal_part = jax.random.normal(jax.random.fold_in(key, number), (entries,), jnp.float32)
        pieces.append(normal_part * float(layer_item[1]) ** (-0.5))
    return jnp.concatenate(pieces)


def draw_point_counts(key, part):
    key = jax.random.fold_in(key, 12)
    counts = jax.random.randint(key, (VOXELS,), 1, PTS + 1, jnp.int32)
    return counts.at[::VOX_DEV].set(PTS)


def draw_voxel_cells(key, part):
    key = jax.random.fold_in(key, 13)
    block_keys = jax.random.split(key, VOXELS // VOX_DEV)

    def one_block(block_key):
        return jax.random.permutation(block_key, 2 * GY * GX)[:VOX_DEV]
    return jax.vmap(one_block)(block_keys).reshape(VOXELS).astype(jnp.int32)


def draw_pos_anchors(key, part):
    key = jax.random.fold_in(key, 14)
    scene_keys = jax.random.split(key, SCENES)

    def one_scene(scene_key):
        return jax.random.permutation(scene_key, ANCH)[:POSMAX]
    return jax.vmap(one_scene)(scene_keys).astype(jnp.int32)


def draw_pos_counts(key, part):
    key = jax.random.fold_in(key, 15)
    counts = jax.random.randint(key, (SCENES,), 0, POSMAX + 1, jnp.int32)
    return counts.at[0].set(POSMAX).at[SCENES - 1].set(0)


def shard_levels(own_key, dims, cuts, least, largest):
    factor_of = 1.0
    for dim, blocks in cuts:
        steps = jax.random.uniform(jax.random.fold_in(jax.random.fold_in(own_key, 6), dim), (blocks,), jnp.float32, least / len(cuts), largest / len(cuts))
        factor_of = factor_of * jnp.repeat(jnp.exp(steps), dims[dim] // blocks).reshape((-1,) + (1,) * (len(dims) - 1 - dim))
    return factor_of


def gaussian(key, dims, deviation, reach, cuts=(), held_as=jnp.bfloat16):
    result = deviation * jax.random.normal(key, dims, jnp.float32)
    if cuts:
        result = result * shard_levels(key, dims, cuts, -0.22, 0.18)
    return jnp.clip(result, -reach, reach).astype(held_as)


def setup_inputs(seed: int = 0) -> dict:
    streams_of = jax.random.split(jax.random.key(seed), 10)
    points = gaussian(streams_of[0], (7, PTS, VOXELS), 1.0, 6.0, ((2, 32),))
    point_counts = draw_point_counts(jax.random.fold_in(streams_of[9], 71), 0)
    voxel_cells = draw_voxel_cells(jax.random.fold_in(streams_of[9], 71), 0)
    pos_anchors = draw_pos_anchors(jax.random.fold_in(streams_of[9], 71), 0)
    pos_counts = draw_pos_counts(jax.random.fold_in(streams_of[9], 71), 0)
    reg_targets = gaussian(streams_of[5], (SCENES, 14, HY, HX), 1.0, 6.0, ((0, 8),), jnp.float32)
    params = draw_params(jax.random.fold_in(streams_of[9], 71), 0)
    moment1 = gaussian(streams_of[7], (NPARAM,), (0.111 * 0.002 * NPARAM ** -0.5), 1.9073486328125e-06, ((0, 4),), jnp.float32)
    moment2 = jnp.clip(jnp.exp(math.log(6.305209921341447e-15) - 1.3862944 * jax.random.uniform(streams_of[8], (NPARAM,), jnp.float32) ** shard_levels(streams_of[8], (NPARAM,), ((0, 4),), -0.2, 0.2)), 1.5763024803353617e-15, 6.305209921341447e-15)
    return {"points": points, "point_counts": point_counts, "voxel_cells": voxel_cells, "pos_anchors": pos_anchors, "pos_counts": pos_counts, "reg_targets": reg_targets, "params": params, "moment1": moment1, "moment2": moment2}


@jax.custom_vjp
def low(v):
    return lax.optimization_barrier(v.astype(jnp.bfloat16)).astype(jnp.float32)

@jax.custom_vjp
def low_back(v):
    return v

def low_keep(v):
    return (low(v), None)

def low_pass(kept, grad):
    return (grad,)

def back_keep(v):
    return (v, None)

def back_low(kept, grad):
    return (low(grad),)
low.defvjp(low_keep, low_pass)
low_back.defvjp(back_keep, back_low)
highest = lax.Precision.HIGHEST
beta_one = 0.9
beta_two = 0.999
adam_eps = 1e-08
learn_rate = 0.02
weight_decay = 0.01
clip_level = 0.002

def layer_shapes():
    return [(VF1, 7), (VF2, 2 * VF1), (FC, 2 * VF2), (3, 3, 3, FC, C3), (3, 3, 3, C3, C3), (3, 3, 3, C3, C3), (3, 3, 2 * C3, R1), (3, 3, R1, R1), (3, 3, R1, R3), (3, 3, R1, UP), (2, 2, R1, UP), (4, 4, R3, UP), (3 * UP, 16)]

def unpack(flat_values):
    pieces = []
    offset = 0
    for layer_shape in layer_shapes():
        entries = math.prod(layer_shape)
        pieces.append(flat_values[offset:offset + entries].reshape(layer_shape))
        offset += entries
    return pieces

def rounded(values):
    return low_back(low(values))

def vfe_forward(vfe_one, vfe_two, vfe_three, cloud_points, counts):
    slots = jnp.arange(cloud_points.shape[1], dtype=jnp.int32)
    valid = (slots[:, None] < counts[None, :]).astype(jnp.float32)
    inverse = 1.0 / counts.astype(jnp.float32)
    first_part = jax.nn.silu(jnp.einsum('oc,cpv->opv', vfe_one, cloud_points, precision=highest))
    first_mean = lax.optimization_barrier(jnp.sum(first_part * valid, axis=1)) * inverse
    joined_one = rounded(jnp.concatenate([first_part, jnp.broadcast_to(first_mean[:, None, :], first_part.shape)], 0))
    second_part = jax.nn.silu(jnp.einsum('oc,cpv->opv', vfe_two, joined_one, precision=highest))
    second_mean = lax.optimization_barrier(jnp.sum(second_part * valid, axis=1)) * inverse
    joined_two = rounded(jnp.concatenate([second_part, jnp.broadcast_to(second_mean[:, None, :], second_part.shape)], 0))
    third_part = jax.nn.silu(jnp.einsum('oc,cpv->opv', vfe_three, joined_two, precision=highest))
    return lax.optimization_barrier(jnp.sum(third_part * valid, axis=1)) * inverse

def conv_volume(volume, kernel, stride, pad_depth):
    return lax.conv_general_dilated(volume, kernel, (stride, 1, 1), ((pad_depth, pad_depth), (1, 1), (1, 1)), dimension_numbers=('NDHWC', 'DHWIO', 'NDHWC'), precision=highest)

def plane_conv(image, kernel, stride):
    return lax.conv_general_dilated(image, kernel, (stride, stride), ((1, 1), (1, 1)), dimension_numbers=('NHWC', 'HWIO', 'NHWC'), precision=highest)

def upsample(image, kernel):
    factor = kernel.shape[0]
    spread = jnp.einsum('nijc,abco->niajbo', image, kernel, precision=highest)
    return spread.reshape(image.shape[0], image.shape[1] * factor, image.shape[2] * factor, kernel.shape[3])

def region_forward(region_kernels, bird_view, anchors, anchor_counts, targets):
    conv_a, conv_b, conv_c, up_a, up_b, up_c, head_kernel = region_kernels
    level_one = rounded(jax.nn.silu(plane_conv(bird_view, conv_a, 2)))
    level_two = rounded(jax.nn.silu(plane_conv(level_one, conv_b, 2)))
    level_three = rounded(jax.nn.silu(plane_conv(level_two, conv_c, 2)))
    joined = rounded(jnp.concatenate([jax.nn.silu(plane_conv(level_one, up_a, 1)), jax.nn.silu(upsample(level_two, up_b)), jax.nn.silu(upsample(level_three, up_c))], -1))
    scene_count, map_rows, map_cols = (joined.shape[0], joined.shape[1], joined.shape[2])
    cells = map_rows * map_cols
    head_maps = jnp.einsum('nijc,ck->nkij', joined, head_kernel, precision=highest)
    flat_maps = head_maps.reshape(scene_count, 16, cells)
    logits = flat_maps[:, 0:2].reshape(scene_count, 2 * cells)
    places = jnp.arange(2 * cells, dtype=jnp.int32)
    live = (jnp.arange(anchors.shape[1], dtype=jnp.int32)[None, :] < anchor_counts[:, None]).astype(jnp.float32)
    positive = lax.optimization_barrier(jnp.sum((anchors[:, :, None] == places[None, None, :]).astype(jnp.float32) * live[:, :, None], axis=1))
    class_loss = jnp.sum(jax.nn.softplus(logits) - positive * logits) / (2.0 * cells)
    boxes = flat_maps[:, 2:16].reshape(scene_count, 2, 7, cells)
    goals = targets.reshape(scene_count, 2, 7, cells)
    differ = boxes - goals
    magnitude = jnp.abs(differ)
    huber = jnp.where(magnitude < 1.0, 0.5 * differ * differ, magnitude - 0.5)
    weight_pos = positive.reshape(scene_count, 2, 1, cells)
    per_scene = lax.optimization_barrier(jnp.sum(huber * weight_pos, axis=(1, 2, 3))) / jnp.maximum(anchor_counts.astype(jnp.float32), 1.0)
    return (class_loss + jnp.sum(per_scene), head_maps)

def reference(points, point_counts, voxel_cells, pos_anchors, pos_counts, reg_targets, params, moment1, moment2):
    voxel_ids = jnp.arange(VOXELS, dtype=jnp.int32)
    scene_index = voxel_ids // (N_SLAB * VOX_DEV)
    depth_index = 2 * (voxel_ids // VOX_DEV % N_SLAB) + voxel_cells // (GY * GX)
    row_index = voxel_cells // GX % GY
    column_index = voxel_cells % GX

    def forward(flat_values, point_cloud):
        kernels = unpack(low(flat_values))
        features = vfe_forward(kernels[0], kernels[1], kernels[2], point_cloud, point_counts)
        grid_cells = jnp.zeros((SCENES, 2 * N_SLAB, GY, GX, FC), jnp.float32)
        grid_cells = rounded(grid_cells.at[scene_index, depth_index, row_index, column_index].set(features.T))
        first_volume = rounded(jax.nn.silu(conv_volume(grid_cells, kernels[3], 2, 1)))
        second_volume = rounded(jax.nn.silu(conv_volume(first_volume, kernels[4], 1, 1)))
        third_volume = rounded(jax.nn.silu(conv_volume(second_volume, kernels[5], 2, 1)))
        bird_view = jnp.transpose(third_volume, (0, 2, 3, 1, 4)).reshape(SCENES, GY, GX, 2 * C3)
        return region_forward(kernels[6:], bird_view, pos_anchors, pos_counts, reg_targets)
    point_cloud = points.astype(jnp.float32)
    loss_value, backward, head_maps = jax.vjp(forward, params, point_cloud, has_aux=True)
    grads, points_grad = backward(jnp.ones_like(loss_value))
    grad_norm = jnp.sqrt(jnp.sum(grads * grads))
    clipped = grads * (clip_level / jnp.maximum(grad_norm, clip_level))
    new_moment1 = beta_one * moment1 + (1.0 - beta_one) * clipped
    new_moment2 = beta_two * moment2 + (1.0 - beta_two) * clipped * clipped
    direction = new_moment1 / (1.0 - beta_one ** STEP) / (jnp.sqrt(new_moment2 / (1.0 - beta_two ** STEP)) + adam_eps)
    new_params = params - learn_rate * (direction + weight_decay * params)
    return (head_maps, points_grad, new_moment1, new_moment2, new_params, grad_norm)
```

```python
import functools
import math

import jax
import jax.numpy as jnp
from jax import lax
from jax.experimental import pallas as pl
from jax.experimental.pallas import tpu as pltpu
from jax.sharding import PartitionSpec as P

VF1 = 16
VF2 = 64
FC = 128
C3 = 64
STEP = 10
GY = 32
GX = 64
PTS = 35
VOX = 512
SLABS = 4
ROWS = GY // SLABS
LANES = 128
NPARAM = 2537584
SHARD = NPARAM // SLABS

TILE = 16
STRIDE_T = 310
SHARD_T = 312
PAD_T = 320
FLAT_R = 4960
CONV_R0 = 144
CONV_R = 3456
PLANE_T0 = 225
PLANE_T = 1014
GRAD_T = 3 * STRIDE_T + SHARD_T
WIDE_T = (369, 1233)
CONV_T = 256

beta_one = 0.9
beta_two = 0.999
adam_eps = 1e-08
learn_rate = 0.02
weight_decay = 0.01
clip_level = 0.002

f32 = jnp.float32
bf16 = jnp.bfloat16
VMEM_LIMIT = 56 * 1024 * 1024


def call(kernel, out_shape, in_specs, out_specs, scratch=()):
    return pl.pallas_call(
        kernel,
        out_shape=out_shape,
        in_specs=in_specs,
        out_specs=out_specs,
        scratch_shapes=list(scratch),
        compiler_params=pltpu.CompilerParams(vmem_limit_bytes=VMEM_LIMIT),
    )


def vmem():
    return pl.BlockSpec(memory_space=pltpu.VMEM)


def smem():
    return pl.BlockSpec(memory_space=pltpu.SMEM)


def anywhere():
    return pl.BlockSpec(memory_space=pl.ANY)


def shape(dims, dtype=f32):
    return jax.ShapeDtypeStruct(dims, dtype)


def mm(a, b):
    return lax.dot_general(a, b, (((1,), (0,)), ((), ())), preferred_element_type=f32)


def mm_nt(a, b):
    return lax.dot_general(a, b, (((1,), (1,)), ((), ())), preferred_element_type=f32)


def mm_tn(a, b):
    return lax.dot_general(a, b, (((0,), (0,)), ((), ())), preferred_element_type=f32)


def sigmoid(z):
    return 0.5 * jnp.tanh(0.5 * z) + 0.5


def silu(z):
    return z * sigmoid(z)


def silu_slope(z):
    s = sigmoid(z)
    return s * (1.0 + z * (1.0 - s))


def lane_of(dims):
    return lax.broadcasted_iota(jnp.int32, dims, len(dims) - 1)


def row_of(dims):
    return lax.broadcasted_iota(jnp.int32, dims, 0)


def lane_roll(x, shift):
    shift = shift % x.shape[-1]
    return x if shift == 0 else pltpu.roll(x, shift, x.ndim - 1)


def shift_in(v, d, width):
    if d == 0:
        return v
    place = row_of(v.shape) % width
    keep = place > 0 if d > 0 else place < width - 1
    return jnp.where(keep, pltpu.roll(v, d % v.shape[0], 0), 0.0)


def shift_out(v, d, width):
    if d == 0:
        return v
    edge = jnp.zeros((width,) + v.shape[1:], v.dtype)
    if d > 0:
        return jnp.concatenate([edge, v[:-width]], 0)
    return jnp.concatenate([v[width:], edge], 0)


def spread_kernel(slab_ref, flat_ref, out_ref, nat):
    nat[...] = jnp.zeros_like(nat)
    span = 480
    for s in range(SLABS):

        @pl.when(slab_ref[0] == s)
        def _(s=s):
            lanes, first = 16 + 28 * s, 15 - 4 * s
            lane = lane_of((span, LANES))
            count = FLAT_R // span + (FLAT_R % span > 0)
            for i in range(count):
                r0 = i * span
                n = min(span, FLAT_R - r0)
                rolled = lane_roll(flat_ref[r0 : r0 + n, :], lanes)
                nat[first + r0 : first + r0 + n, :] += jnp.where(lane[:n] >= lanes, rolled, 0.0)
                nat[first + r0 + 1 : first + r0 + 1 + n, :] += jnp.where(
                    lane[:n] < lanes, rolled, 0.0
                )
            low = max(0, min(SHARD_T // 2, (WIDE_T[0] - STRIDE_T * s + 1) // 2))
            high = max(low, min(SHARD_T // 2, (WIDE_T[1] - STRIDE_T * s + 1) // 2))
            for a, b, wide in ((0, low, False), (low, high, True), (high, SHARD_T // 2, False)):

                def block(i, carry, wide=wide):
                    base = pl.multiple_of(32 * i, 32)
                    if wide:
                        even = nat[pl.ds(base, 16, stride=2), :]
                        odd = nat[pl.ds(base + 1, 16, stride=2), :]
                    else:
                        even = nat[pl.ds(base, 16), :]
                        odd = nat[pl.ds(base + 16, 16), :]
                    out_ref[2 * i] = even.astype(bf16)
                    out_ref[2 * i + 1] = odd.astype(bf16)
                    return carry

                if b > a:
                    lax.fori_loop(a, b, block, 0, unroll=4)

    for t in range(SHARD_T, PAD_T):
        out_ref[t] = jnp.zeros((TILE, LANES), bf16)


def spread_shard(slab, flat_rows):
    return call(
        spread_kernel,
        shape((PAD_T, TILE, LANES), bf16),
        [smem(), vmem()],
        vmem(),
        [pltpu.VMEM((5120, LANES), f32)],
    )(slab, flat_rows)


def gather_kernel(slab_ref, quarter_ref, early_ref, out_ref, squares_ref, nat):
    span = 480
    for s in range(SLABS):

        @pl.when(slab_ref[0] == s)
        def _(s=s):
            lanes, first = 16 + 28 * s, 15 - 4 * s
            low = max(0, min(SHARD_T // 2, (WIDE_T[0] - STRIDE_T * s + 1) // 2))
            high = max(low, min(SHARD_T // 2, (WIDE_T[1] - STRIDE_T * s + 1) // 2))
            for a, b, wide in ((0, low, False), (low, high, True), (high, SHARD_T // 2, False)):

                def block(i, carry, wide=wide):
                    base = pl.multiple_of(32 * i, 32)
                    even, odd = quarter_ref[2 * i], quarter_ref[2 * i + 1]
                    if wide:
                        nat[pl.ds(base, 16, stride=2), :] = even
                        nat[pl.ds(base + 1, 16, stride=2), :] = odd
                    else:
                        nat[pl.ds(base, 16), :] = even
                        nat[pl.ds(base + 16, 16), :] = odd
                    return carry

                if b > a:
                    lax.fori_loop(a, b, block, 0, unroll=4)
            if s == 0:
                rows = CONV_R + CONV_R0 + TILE
                nat[0:rows, :] = early_ref[0:rows, :].astype(f32)
            lane = lane_of((span, LANES))
            total = jnp.zeros((8, LANES), f32)
            count = FLAT_R // span + (FLAT_R % span > 0)
            for i in range(count):
                r0 = i * span
                n = min(span, FLAT_R - r0)
                here = lane_roll(nat[first + r0 : first + r0 + n, :], -lanes)
                after = lane_roll(nat[first + r0 + 1 : first + r0 + 1 + n, :], -lanes)
                value = jnp.where(lane[:n] < LANES - lanes, here, after)
                if r0 + n > SHARD // LANES:
                    place = (row_of((n, LANES)) + r0) * LANES + lane[:n]
                    value = jnp.where(place < SHARD, value, 0.0)
                out_ref[r0 : r0 + n, :] = value
                total += jnp.sum((value * value).reshape(n // 8, 8, LANES), axis=0)
            squares_ref[...] = total


def gather_shard(slab, quarter, early):
    return call(
        gather_kernel,
        (shape((FLAT_R, LANES)), shape((8, LANES))),
        [smem(), vmem(), vmem()],
        (vmem(), vmem()),
        [pltpu.VMEM((5120, LANES), f32)],
    )(slab, quarter, early)


PART = 5
VFE_SCRATCH = [
    pltpu.VMEM((VOX // LANES, PTS * 16, LANES), f32),
    pltpu.VMEM((16, LANES), f32),
    pltpu.VMEM((64, LANES), f32),
    pltpu.VMEM((PTS * 16, VOX), bf16),
    pltpu.VMEM((PTS * 64, VOX), bf16),
]


def spread_points(points_ref, x_scr):
    x_scr[...] = jnp.zeros_like(x_scr)
    for c in range(7):
        plane = points_ref[c].astype(f32)
        for b in range(VOX // LANES):
            x_scr[b, pl.ds(c, PTS, stride=16), :] = plane[:, b * LANES : (b + 1) * LANES]


def vfe_weights(rows_ref, w1_scr, w2_scr):
    line = rows_ref[0].astype(f32)
    lane = lane_of((16, LANES))
    for o in range(VF1):
        w1_scr[o : o + 1, :] = jnp.where(lane < 7, lane_roll(line, -(16 + 7 * o)), 0.0)[15:16]
    two = rows_ref[1].astype(f32)
    for k in range(4):
        w2_scr[pl.ds(k, 16, stride=4), :] = jnp.where(lane < 32, lane_roll(two, -32 * k), 0.0)
    w1 = w1_scr[...].astype(bf16)[:, 0:16]
    w2 = w2_scr[...]
    w2a = w2.astype(bf16)[:, 0:16]
    w2b = lane_roll(w2, -16).astype(bf16)[:, 0:16]
    w3 = rows_ref[2:10].reshape(FC, LANES)
    w3a = w3[:, 0:64]
    w3b = lane_roll(w3.astype(f32), -64).astype(bf16)[:, 0:64]
    return w1, w2a, w2b, w3a, w3b


def part_of(ref, i, height):
    return jnp.concatenate(
        [
            ref[pl.ds(pl.multiple_of((PART * i + k) * height, height), height), :]
            for k in range(PART)
        ],
        1,
    )


def points_part(ref, i):
    return jnp.concatenate(
        [
            ref[b, pl.ds(pl.multiple_of((PART * i + k) * 16, 16), 16), :]
            for k in range(PART)
            for b in range(VOX // LANES)
        ],
        1,
    )


def set_points_part(ref, i, value):
    for k in range(PART):
        for b in range(VOX // LANES):
            at = k * VOX + b * LANES
            ref[b, pl.ds(pl.multiple_of((PART * i + k) * 16, 16), 16), :] = value[:, at : at + LANES]


def set_part(ref, i, height, value):
    for k in range(PART):
        ref[pl.ds(pl.multiple_of((PART * i + k) * height, height), height), :] = value[
            :, k * VOX : (k + 1) * VOX
        ].astype(ref.dtype)


def part_sum(value):
    total = value[:, 0:VOX]
    for k in range(1, PART):
        total = total + value[:, k * VOX : (k + 1) * VOX]
    return total


def valid_part(i, counts):
    return jnp.concatenate([(PART * i + k < counts).astype(f32) for k in range(PART)], 1)


def widen(value):
    return jnp.concatenate([value] * PART, 1)


def vfe_front(weights, counts, inverse, x_scr, j1_scr, j2_scr, z1_scr=None, z2_scr=None):
    w1, w2a, w2b, w3a, w3b = weights

    def layer_one(i, total):
        z = mm(w1, points_part(x_scr, i).astype(bf16))
        value = silu(z)
        set_part(j1_scr, i, 16, value)
        if z1_scr is not None:
            set_part(z1_scr, i, 16, z)
        return total + part_sum(value * valid_part(i, counts))

    total = lax.fori_loop(0, PTS // PART, layer_one, jnp.zeros((VF1, VOX), f32))
    mean_one = (total * inverse).astype(bf16)
    shared_two = widen(mm(w2b, mean_one))

    def layer_two(i, total):
        z = mm(w2a, part_of(j1_scr, i, 16)) + shared_two
        value = silu(z)
        set_part(j2_scr, i, 64, value)
        if z2_scr is not None:
            set_part(z2_scr, i, 64, z)
        return total + part_sum(value * valid_part(i, counts))

    total = lax.fori_loop(0, PTS // PART, layer_two, jnp.zeros((VF2, VOX), f32))
    mean_two = (total * inverse).astype(bf16)
    shared_three = widen(mm(w3b, mean_two))
    return mean_one, mean_two, shared_three


def encode_kernel(points_ref, counts_ref, cells_ref, rows_ref, out_ref, x_scr, w1_scr, w2_scr, j1_scr, j2_scr):
    spread_points(points_ref, x_scr)
    weights = vfe_weights(rows_ref, w1_scr, w2_scr)
    counts = counts_ref[...]
    inverse = 1.0 / counts.astype(f32)
    _, _, shared_three = vfe_front(weights, counts, inverse, x_scr, j1_scr, j2_scr)
    w3a = weights[3]

    def layer_three(i, total):
        value = silu(mm(w3a, part_of(j2_scr, i, 64)) + shared_three)
        return total + part_sum(value * valid_part(i, counts))

    total = lax.fori_loop(0, PTS // PART, layer_three, jnp.zeros((FC, VOX), f32))
    out_ref[0:FC, :] = (total * inverse).astype(bf16)
    cells = cells_ref[...]
    row = row_of((16, VOX))
    high, low = cells // GX, cells % GX
    out_ref[FC : FC + 16, :] = jnp.where(row == 0, high, low).astype(f32).astype(bf16)


def encode(points, counts, cells, rows):
    return call(
        encode_kernel,
        shape((FC + 16, VOX), bf16),
        [vmem()] * 4,
        vmem(),
        VFE_SCRATCH,
    )(points, counts, cells, rows)


def encode_back_kernel(
    points_ref, counts_ref, rows_ref, grad_ref, out_ref, weight_ref,
    x_scr, w1_scr, w2_scr, j1_scr, j2_scr, z1_scr, z2_scr, d1_scr, d2_scr,
):
    spread_points(points_ref, x_scr)
    weights = vfe_weights(rows_ref, w1_scr, w2_scr)
    w1, w2a, w2b, w3a, w3b = weights
    counts = counts_ref[...]
    inverse = 1.0 / counts.astype(f32)
    mean_one, mean_two, shared_three = vfe_front(
        weights, counts, inverse, x_scr, j1_scr, j2_scr, z1_scr, z2_scr
    )
    grad = grad_ref[0].astype(f32)
    for t in range(1, SLABS):
        grad = grad + grad_ref[t].astype(f32)
    grad_three = widen(grad * inverse)
    parts = PTS // PART

    def back_three(i, carry):
        total, weight = carry
        j2 = part_of(j2_scr, i, 64)
        z = mm(w3a, j2) + shared_three
        dz = grad_three * valid_part(i, counts) * silu_slope(z)
        low = dz.astype(bf16)
        set_part(d2_scr, i, 64, mm_tn(w3a, low))
        return total + part_sum(dz), weight + mm_nt(low, j2)

    total, grad_w3a = lax.fori_loop(
        0, parts, back_three, (jnp.zeros((FC, VOX), f32), jnp.zeros((FC, VF2), f32))
    )
    total = total.astype(bf16)
    grad_w3b = mm_nt(total, mean_two)
    grad_two = widen(mm_tn(w3b, total) * inverse)

    def back_two(i, carry):
        total, weight = carry
        dz = (part_of(d2_scr, i, 64) + valid_part(i, counts) * grad_two) * silu_slope(
            part_of(z2_scr, i, 64)
        )
        low = dz.astype(bf16)
        set_part(d1_scr, i, 16, mm_tn(w2a, low))
        return total + part_sum(dz), weight + mm_nt(low, part_of(j1_scr, i, 16))

    total, grad_w2a = lax.fori_loop(
        0, parts, back_two, (jnp.zeros((VF2, VOX), f32), jnp.zeros((VF2, VF1), f32))
    )
    total = total.astype(bf16)
    grad_w2b = mm_nt(total, mean_one)
    grad_one = widen(mm_tn(w2b, total) * inverse)

    def back_one(i, weight):
        dz = (part_of(d1_scr, i, 16) + valid_part(i, counts) * grad_one) * silu_slope(
            part_of(z1_scr, i, 16)
        )
        low = dz.astype(bf16)
        x = points_part(x_scr, i).astype(bf16)
        set_points_part(x_scr, i, mm_tn(w1, low))
        return weight + mm_nt(low, x)

    grad_w1 = lax.fori_loop(0, parts, back_one, jnp.zeros((VF1, 16), f32))
    for c in range(7):
        for b in range(VOX // LANES):
            out_ref[c, :, b * LANES : (b + 1) * LANES] = x_scr[b, pl.ds(c, PTS, stride=16), :]

    lane = lane_of((16, LANES))
    w1_scr[...] = jnp.concatenate([grad_w1, jnp.zeros((16, LANES - 16), f32)], 1)
    spread = jnp.where(lane < 7, w1_scr[...], 0.0)
    line = jnp.zeros((16, LANES), f32)
    row = row_of((16, LANES))
    for o in range(VF1):
        line = line + jnp.where(row == o, lane_roll(spread, 16 + 7 * o), 0.0)
    line = jnp.sum(line, axis=0, keepdims=True)
    weight_ref[0:16, :] = jnp.where(row == 15, line, 0.0)
    w2_scr[...] = jnp.concatenate([grad_w2a, grad_w2b, jnp.zeros((64, LANES - 32), f32)], 1)
    two = jnp.zeros((16, LANES), f32)
    for k in range(4):
        two = two + lane_roll(w2_scr[pl.ds(k, 16, stride=4), :], 32 * k)
    weight_ref[16:32, :] = two
    weight_ref[32:160, :] = jnp.concatenate([grad_w3a, grad_w3b], 1)


def encode_back(points, counts, rows, grad):
    return call(
        encode_back_kernel,
        (shape((7, PTS, VOX)), shape((160, LANES))),
        [vmem()] * 4,
        (vmem(), vmem()),
        VFE_SCRATCH
        + [
            pltpu.VMEM((PTS * 16, VOX), f32),
            pltpu.VMEM((PTS * 64, VOX), f32),
            pltpu.VMEM((PTS * 16, VOX), f32),
            pltpu.VMEM((PTS * 64, VOX), f32),
        ],
    )(points, counts, rows, grad)


R1W = (ROWS + 4) * GX
R2W = (ROWS + 2) * GX
R3W = ROWS * GX
RGW = (ROWS + 6) * GX


def cell_marks(places):
    value = places.astype(f32)
    high, low = value[0:1], value[1:2]
    column = lax.broadcasted_iota(jnp.int32, (GX, VOX), 0).astype(f32)
    return (column == low).astype(f32).astype(bf16), high


def layer_marks(column, high, depth, first_row):
    pieces = []
    for w in range(ROWS + 6):
        row = first_row - 3 + w
        inside = jnp.logical_and(row >= 0, row < GY)
        target = jnp.where(inside, depth * GY + row, -1).astype(f32)
        pieces.append(column * (high == target).astype(f32).astype(bf16))
    return jnp.concatenate(pieces, 0)


def conv_weights(rows_ref, start, taps, half, place, scr):
    lane = lane_of((half, LANES))
    left = lane < 64
    for t in range(taps):
        r = []
        for kx in range(3):
            base = start + (3 * t + kx) * half
            r.append(rows_ref[base : base + half, :].astype(f32))
        turned = [lane_roll(v, 64) for v in r]
        at = place(t)
        scr[0, pl.ds(at, half, stride=2), :] = jnp.where(left, r[1], turned[0])
        scr[0, pl.ds(at + 1, half, stride=2), :] = jnp.where(left, turned[1], r[0])
        scr[1, pl.ds(at, half, stride=2), :] = jnp.where(left, r[2], 0.0)
        scr[1, pl.ds(at + 1, half, stride=2), :] = jnp.where(left, turned[2], 0.0)


def conv_weight_grads(out_ref, start, taps, half, place, scr):
    lane = lane_of((half, LANES))
    left = lane < 64
    for t in range(taps):
        at = place(t)
        even = [scr[b, pl.ds(at, half, stride=2), :] for b in range(2)]
        odd = [scr[b, pl.ds(at + 1, half, stride=2), :] for b in range(2)]
        values = (
            jnp.where(left, lane_roll(even[0], 64), odd[0]),
            jnp.where(left, even[0], lane_roll(odd[0], 64)),
            jnp.where(left, even[1], lane_roll(odd[1], 64)),
        )
        for kx in range(3):
            base = start + (3 * t + kx) * half
            out_ref[base : base + half, :] = values[kx]


def both_halves(out_ref, scr):
    for b in range(2):
        out_ref[:, b * LANES : (b + 1) * LANES] = scr[b].astype(bf16)


def keep_halves(scr, value):
    for b in range(2):
        scr[b] = value[:, b * LANES : (b + 1) * LANES]


def tap_place(t):
    return 128 * t


def pair_place(t):
    kd, ky = t // 3, t % 3
    return 128 * ky + 64 * kd if kd < 2 else 384 + 128 * ky


def join_columns(p):
    first, last = p[:, 0:128], p[:, 128:256]
    left = lane_of(first.shape) < 64
    half = jnp.where(left, first + shift_in(last, -1, GX), shift_in(first, 1, GX))
    return half + lane_roll(half, 64)


def split_columns(d):
    left = lane_of(d.shape) < 64
    first = jnp.where(left, d, lane_roll(shift_in(d, -1, GX), 64))
    last = jnp.where(left, shift_in(d, 1, GX), 0.0)
    return jnp.concatenate([first, last], 1).astype(bf16)


def inside_rows(rows, first_row):
    place = first_row + row_of((rows, LANES)) // GX
    return jnp.logical_and(place >= 0, place < GY)


def grid_taps(grid_ref, k):
    return jnp.concatenate(
        [grid_ref[2 * k + kd, ky * GX : ky * GX + R1W, :] for kd in range(3) for ky in range(3)], 1
    )


def pair_taps(ref, at, rows):
    return jnp.concatenate(
        [ref[at, ky * GX : ky * GX + rows, :] for ky in range(3)]
        + [ref[at + 2, ky * GX : ky * GX + rows, :] for ky in range(3)],
        1,
    )


def volume_kernel(
    slab_ref, f_ref, rows_ref,
    bird_ref, grid_ref, first_ref, second_ref, z1_ref, z2_ref, z3_ref, w1_ref, w2_ref, w3_ref,
    w1_scr, w2_scr, bird_scr,
):
    w2_scr[...] = jnp.zeros_like(w2_scr)
    conv_weights(rows_ref, 0, 9, 64, tap_place, w1_scr)
    both_halves(w1_ref, w1_scr)
    conv_weights(rows_ref, 1728, 9, 32, pair_place, w2_scr)
    both_halves(w2_ref, w2_scr)
    conv_weights(rows_ref, 2592, 9, 32, pair_place, w2_scr)
    both_halves(w3_ref, w2_scr)

    first_row = slab_ref[0] * ROWS
    grid_ref[0] = jnp.zeros((RGW, FC), bf16)
    for t in range(SLABS):
        features = f_ref[t, 0:FC, :]
        column, high = cell_marks(f_ref[t, FC : FC + 16, :])
        for d in range(2):
            marks = layer_marks(column, high, d, first_row)
            grid_ref[1 + 2 * t + d] = mm_nt(marks, features).astype(bf16)

    first_ref[0] = jnp.zeros((R1W, LANES), bf16)
    first_ref[5] = jnp.zeros((R1W, LANES), bf16)
    keep = inside_rows(R1W, first_row - 2)
    for k in range(4):
        z = join_columns(mm(grid_taps(grid_ref, k), w1_ref[...]))
        z1_ref[k] = z
        value = jnp.where(keep, silu(z), 0.0).astype(bf16)
        first_ref[k + 1, :, 0:64] = value[:, 0:64]
        first_ref[k, :, 64:128] = value[:, 64:128]
    first_ref[4, :, 64:128] = jnp.zeros((R1W, 64), bf16)

    second_ref[0] = jnp.zeros((R2W, LANES), bf16)
    second_ref[5] = jnp.zeros((R2W, LANES), bf16)
    keep = inside_rows(R2W, first_row - 1)
    for k in range(4):
        z = join_columns(mm(pair_taps(first_ref, k, R2W), w2_ref[...]))
        z2_ref[k] = z
        value = jnp.where(keep, silu(z), 0.0).astype(bf16)
        second_ref[k + 1, :, 0:64] = value[:, 0:64]
        second_ref[k, :, 64:128] = value[:, 64:128]
    second_ref[4, :, 64:128] = jnp.zeros((R2W, 64), bf16)

    z3 = []
    for k in range(2):
        z3.append(join_columns(mm(pair_taps(second_ref, 2 * k, R3W), w3_ref[...])))
    z = jnp.where(lane_of((R3W, LANES)) < 64, z3[0], z3[1])
    z3_ref[...] = z
    bird_scr[...] = silu(z)
    for yp in range(2):
        for xp in range(2):
            for a in range(ROWS // 2):
                piece = bird_scr[pl.ds((2 * a + yp) * GX + xp, GX // 2, stride=2), :]
                bird_ref[2 * yp + xp, a * 32 : a * 32 + 32, :] = piece.astype(bf16)


def volume(slab, features, rows):
    return call(
        volume_kernel,
        (
            shape((4, 128, LANES), bf16),
            shape((9, RGW, LANES), bf16),
            shape((6, R1W, LANES), bf16),
            shape((6, R2W, LANES), bf16),
            shape((4, R1W, LANES)),
            shape((4, R2W, LANES)),
            shape((R3W, LANES)),
            shape((1152, 256), bf16),
            shape((768, 256), bf16),
            shape((768, 256), bf16),
        ),
        [smem(), vmem(), vmem()],
        (vmem(),) * 10,
        [pltpu.VMEM((2, 1152, LANES), f32), pltpu.VMEM((2, 768, LANES), f32), pltpu.VMEM((R3W, LANES), f32)],
    )(slab, features, rows)


def volume_back_kernel(
    slab_ref, f_ref, bird_ref, grid_ref, first_ref, second_ref, z1_ref, z2_ref, z3_ref, w1_ref, w2_ref, w3_ref,
    out_ref, weight_ref,
    bird_scr, acc2, acc1, accg, g1_scr, g2_scr,
):
    first_row = slab_ref[0] * ROWS
    for yp in range(2):
        for xp in range(2):
            for a in range(ROWS // 2):
                piece = bird_ref[2 * yp + xp, a * 32 : a * 32 + 32, :].astype(f32)
                bird_scr[pl.ds((2 * a + yp) * GX + xp, GX // 2, stride=2), :] = piece
    dz = bird_scr[...] * silu_slope(z3_ref[...])
    acc2[...] = jnp.zeros_like(acc2)
    acc1[...] = jnp.zeros_like(acc1)
    accg[...] = jnp.zeros_like(accg)

    def pair_back(acc, at, rows, spread, weight):
        back = mm_nt(spread, weight)
        for ky in range(3):
            acc[at, ky * GX : ky * GX + rows, :] += back[:, 128 * ky : 128 * ky + 128]
            acc[at + 2, ky * GX : ky * GX + rows, :] += back[:, 384 + 128 * ky : 512 + 128 * ky]

    def layer_grad(acc, m):
        return acc[m] + lane_roll(acc[m - 1], 64)

    total = jnp.zeros((768, 256), f32)
    for k in range(2):
        spread = split_columns(dz if k == 0 else lane_roll(dz, 64))
        total = total + mm_tn(pair_taps(second_ref, 2 * k, R3W), spread)
        pair_back(acc2, 2 * k, R3W, spread, w3_ref[...])
    keep_halves(g2_scr, total)
    conv_weight_grads(weight_ref, 2592, 9, 32, pair_place, g2_scr)

    keep = inside_rows(R2W, first_row - 1)
    total = jnp.zeros((768, 256), f32)
    for k in range(4):
        d = jnp.where(keep, layer_grad(acc2, k + 1) * silu_slope(z2_ref[k]), 0.0)
        spread = split_columns(d)
        total = total + mm_tn(pair_taps(first_ref, k, R2W), spread)
        pair_back(acc1, k, R2W, spread, w2_ref[...])
    keep_halves(g2_scr, total)
    conv_weight_grads(weight_ref, 1728, 9, 32, pair_place, g2_scr)

    keep = inside_rows(R1W, first_row - 2)
    total = jnp.zeros((1152, 256), f32)
    for k in range(4):
        d = jnp.where(keep, layer_grad(acc1, k + 1) * silu_slope(z1_ref[k]), 0.0)
        spread = split_columns(d)
        total = total + mm_tn(grid_taps(grid_ref, k), spread)
        back = mm_nt(spread, w1_ref[...])
        for kd in range(3):
            for ky in range(3):
                t = 3 * kd + ky
                accg[2 * k + kd, ky * GX : ky * GX + R1W, :] += back[:, 128 * t : 128 * t + 128]
    keep_halves(g1_scr, total)
    conv_weight_grads(weight_ref, 0, 9, 64, tap_place, g1_scr)

    for t in range(SLABS):
        column, high = cell_marks(f_ref[t, FC : FC + 16, :])
        value = jnp.zeros((FC, VOX), f32)
        for d in range(2):
            marks = layer_marks(column, high, d, first_row)
            value = value + mm_tn(accg[1 + 2 * t + d].astype(bf16), marks)
        out_ref[t] = value.astype(bf16)


def volume_back(slab, features, bird_grad, kept):
    return call(
        volume_back_kernel,
        (shape((SLABS, FC, VOX), bf16), shape((CONV_R, LANES))),
        [smem()] + [vmem()] * 11,
        (vmem(), vmem()),
        [
            pltpu.VMEM((R3W, LANES), f32),
            pltpu.VMEM((6, R2W, LANES), f32),
            pltpu.VMEM((6, R1W, LANES), f32),
            pltpu.VMEM((9, RGW, LANES), f32),
            pltpu.VMEM((2, 1152, LANES), f32),
            pltpu.VMEM((2, 768, LANES), f32),
        ],
    )(slab, features, bird_grad, *kept)


def split_planes(ref, height, width):
    planes = []
    for yp in range(2):
        for xp in range(2):
            planes.append(
                jnp.concatenate(
                    [
                        ref[pl.ds((2 * a + yp) * width + xp, width // 2, stride=2), :]
                        for a in range(height // 2)
                    ],
                    0,
                )
            )
    return planes


def merge_planes(ref, planes, height, width):
    half = width // 2
    for yp in range(2):
        for xp in range(2):
            for a in range(height // 2):
                ref[pl.ds((2 * a + yp) * width + xp, half, stride=2), :] = planes[2 * yp + xp][
                    a * half : a * half + half
                ]


def stride_taps(planes, width):
    pieces = []
    for ky in range(3):
        for kx in range(3):
            v = planes[2 * (ky != 1) + (kx != 1)]
            v = shift_in(v, 1, width) if kx == 0 else v
            pieces.append((shift_out(v, 1, width) if ky == 0 else v).astype(bf16))
    return jnp.concatenate(pieces, 1)


def stride_taps_back(grad, width):
    planes = [None] * 4
    channels = grad.shape[1] // 9
    for ky in range(3):
        for kx in range(3):
            t = 3 * ky + kx
            v = grad[:, t * channels : (t + 1) * channels]
            v = shift_out(v, -1, width) if ky == 0 else v
            v = shift_in(v, -1, width) if kx == 0 else v
            at = 2 * (ky != 1) + (kx != 1)
            planes[at] = v if planes[at] is None else planes[at] + v
    return planes


def full_taps(v, width):
    across = [shift_in(v, 1 - kx, width).astype(bf16) for kx in range(3)]
    return jnp.concatenate(
        [shift_out(across[kx], 1 - ky, width) for ky in range(3) for kx in range(3)], 1
    )


def full_taps_back(grad, width):
    channels = grad.shape[1] // 9
    total = None
    for kx in range(3):
        column = None
        for ky in range(3):
            t = 3 * ky + kx
            v = shift_out(grad[:, t * channels : (t + 1) * channels], ky - 1, width)
            column = v if column is None else column + v
        column = shift_in(column, kx - 1, width)
        total = column if total is None else total + column
    return total


HY = 16
HX = 32
CELLS = HY * HX


def region_kernel(
    slab_ref, counts_ref, bird_ref, anchors_ref, goals_ref, shards_ref,
    maps_ref, grad_ref, quarter_ref,
    wv, edge, gr, sems,
    l1_scr, l2_scr, z1_scr, zu1_scr, zu2_scr, zu3_scr, head_scr, maps_scr, two_scr, three_scr, plane_scr,
):
    slab = slab_ref[0]

    def local(tile, s):
        return PAD_T * s + tile - (STRIDE_T * s - 1)

    copies = []
    ends = [PLANE_T0] + [STRIDE_T * s - 1 for s in range(1, SLABS)] + [PLANE_T0 + PLANE_T]
    for s in range(SLABS):
        low = ends[s] + (2 if s > 0 else 0)
        size = ends[s + 1] - low
        copies.append(
            pltpu.make_async_copy(
                shards_ref.at[pl.ds(local(low, s), size)],
                wv.at[pl.ds(low - PLANE_T0, size)],
                sems.at[len(copies)],
            )
        )
    for s in range(1, SLABS):
        for k in range(2):
            copies.append(
                pltpu.make_async_copy(
                    shards_ref.at[pl.ds(local(ends[s], s - 1 + k), 2)],
                    edge.at[pl.ds(4 * (s - 1) + 2 * k, 2)],
                    sems.at[len(copies)],
                )
            )
    for c in copies:
        c.start()
    gr[0 : PLANE_T0 + 1] = jnp.zeros((PLANE_T0 + 1, TILE, LANES), f32)
    gr[PLANE_T0 + 1 + PLANE_T : GRAD_T] = jnp.zeros((GRAD_T - PLANE_T0 - 1 - PLANE_T, TILE, LANES), f32)
    for c in copies:
        c.wait()
    for s in range(1, SLABS):
        at = ends[s] - PLANE_T0
        wv[at : at + 2] = edge[4 * (s - 1) : 4 * s - 2] + edge[4 * s - 2 : 4 * s]

    def narrow(tile, rows):
        at = tile - PLANE_T0
        return wv[at : at + rows // 16].reshape(rows, LANES)

    def wide(tile, rows):
        at = tile - PLANE_T0
        both = wv[at : at + rows // 8].reshape(rows // 16, 2, TILE, LANES)
        return jnp.concatenate(
            [both[:, 0].reshape(rows, LANES), both[:, 1].reshape(rows, LANES)], 1
        )

    def keep_narrow(tile, value):
        at = tile + 1
        tiles = value.shape[0] // 16
        gr[at : at + tiles] = value.reshape(tiles, TILE, LANES)

    def keep_wide(tile, value):
        at = tile + 1
        tiles = value.shape[0] // 16
        left = value[:, 0:128].reshape(tiles, 1, TILE, LANES)
        right = value[:, 128:256].reshape(tiles, 1, TILE, LANES)
        gr[at : at + 2 * tiles] = jnp.concatenate([left, right], 1).reshape(2 * tiles, TILE, LANES)

    t_one, t_two, t_three, t_up1, t_up2, t_up3, t_head = 225, 297, 369, 513, 657, 721, 1233

    bird = [
        jnp.concatenate([bird_ref[s, p] for s in range(SLABS)], 0).astype(f32) for p in range(4)
    ]
    taps_one = stride_taps(bird, 32)
    z1 = mm(taps_one, narrow(t_one, 1152))
    z1_scr[...] = z1
    level_one = silu(z1).astype(bf16).astype(f32)
    l1_scr[...] = level_one
    taps_two = stride_taps(split_planes(l1_scr, 16, 32), 16)
    z2 = mm(taps_two, narrow(t_two, 1152))
    level_two = silu(z2).astype(bf16)
    l2_scr[...] = level_two.astype(f32)
    taps_three = stride_taps(split_planes(l2_scr, 8, 16), 8)
    z3 = mm(taps_three, wide(t_three, 1152))
    level_three = silu(z3).astype(bf16)

    taps_up = full_taps(level_one, 32)
    zu1_scr[...] = mm(taps_up, wide(t_up1, 1152))
    for g in range(4):
        zu2_scr[g] = mm(level_two, wide(t_up2 + 16 * g, 128))
    for g in range(16):
        zu3_scr[g] = mm(level_three, wide(t_up3 + 32 * g, 256))

    lane = lane_of((96, LANES))
    rows = narrow(t_head, 96).astype(f32)
    for c in range(8):
        head_scr[pl.ds(c, 96, stride=8), :] = jnp.where(lane < 16, lane_roll(rows, -16 * c), 0.0)
    head = head_scr[...].astype(bf16)
    head_a, head_b, head_c = head[0:256], head[256:512], head[512:768]
    joined_a = silu(zu1_scr[...]).astype(bf16)
    for g in range(4):
        p, q = g // 2, g % 2
        part = mm(silu(zu2_scr[g]).astype(bf16), head_b)
        for a in range(8):
            two_scr[pl.ds((2 * a + p) * HX + q, 16, stride=2), :] = part[16 * a : 16 * a + 16]
    for g in range(16):
        p, q = g // 4, g % 4
        part = mm(silu(zu3_scr[g]).astype(bf16), head_c)
        for a in range(4):
            three_scr[pl.ds((4 * a + p) * HX + q, 8, stride=4), :] = part[8 * a : 8 * a + 8]
    maps = mm(joined_a, head_a) + two_scr[...] + three_scr[...]
    maps = jnp.transpose(maps)[0:16]
    own = jnp.zeros((16, 128), f32)
    for s in range(SLABS):
        own = own + jnp.where(slab == s, maps[:, 128 * s : 128 * s + 128], 0.0)
    maps_ref[...] = own

    live_count = counts_ref[0]
    anchors = anchors_ref[...]
    slot = row_of((40, CELLS))
    place = lane_of((40, CELLS))
    positive = [
        jnp.sum(
            jnp.logical_and(anchors == place + k * CELLS, slot < live_count).astype(f32),
            axis=0,
            keepdims=True,
        )
        for k in range(2)
    ]
    row = row_of((16, CELLS))
    second = jnp.logical_or(row == 1, row >= 9)
    marked = jnp.where(second, positive[1], positive[0])
    share = 1.0 / jnp.maximum(live_count.astype(f32), 1.0)
    class_grad = (sigmoid(maps) - marked) * (1.0 / (2.0 * CELLS))
    box_grad = jnp.clip(maps - goals_ref[...], -1.0, 1.0) * marked * share
    dmaps = jnp.where(row < 2, class_grad, box_grad)
    dmaps = jnp.transpose(jnp.concatenate([dmaps, jnp.zeros((LANES - 16, CELLS), f32)], 0))
    maps_scr[...] = dmaps
    low = dmaps.astype(bf16)

    dhead_a = mm_tn(joined_a, low)
    dz = mm_nt(low, head_a) * silu_slope(zu1_scr[...])
    dz = dz.astype(bf16)
    keep_wide(t_up1, mm_tn(taps_up, dz))
    dlevel_one = full_taps_back(mm_nt(dz, wide(t_up1, 1152)), 32)

    dhead_b = jnp.zeros((256, LANES), f32)
    dlevel_two = jnp.zeros((128, 128), f32)
    for g in range(4):
        p, q = g // 2, g % 2
        part = jnp.concatenate(
            [maps_scr[pl.ds((2 * a + p) * HX + q, 16, stride=2), :] for a in range(8)], 0
        ).astype(bf16)
        z = zu2_scr[g]
        dhead_b = dhead_b + mm_tn(silu(z).astype(bf16), part)
        dz = (mm_nt(part, head_b) * silu_slope(z)).astype(bf16)
        keep_wide(t_up2 + 16 * g, mm_tn(level_two, dz))
        dlevel_two = dlevel_two + mm_nt(dz, wide(t_up2 + 16 * g, 128))
    dhead_c = jnp.zeros((256, LANES), f32)
    dlevel_three = jnp.zeros((32, 256), f32)
    for g in range(16):
        p, q = g // 4, g % 4
        part = jnp.concatenate(
            [maps_scr[pl.ds((4 * a + p) * HX + q, 8, stride=4), :] for a in range(4)], 0
        ).astype(bf16)
        z = zu3_scr[g]
        dhead_c = dhead_c + mm_tn(silu(z).astype(bf16), part)
        dz = (mm_nt(part, head_c) * silu_slope(z)).astype(bf16)
        keep_wide(t_up3 + 32 * g, mm_tn(level_three, dz))
        dlevel_three = dlevel_three + mm_nt(dz, wide(t_up3 + 32 * g, 256))

    head_scr[...] = jnp.concatenate([dhead_a, dhead_b, dhead_c], 0)
    rows = jnp.zeros((96, LANES), f32)
    for c in range(8):
        piece = jnp.where(lane < 16, head_scr[pl.ds(c, 96, stride=8), :], 0.0)
        rows = rows + lane_roll(piece, 16 * c)
    keep_narrow(t_head, rows)

    dz = (dlevel_three * silu_slope(z3)).astype(bf16)
    keep_wide(t_three, mm_tn(taps_three, dz))
    merge_planes(l2_scr, stride_taps_back(mm_nt(dz, wide(t_three, 1152)), 8), 8, 16)
    dlevel_two = dlevel_two + l2_scr[...]
    dz = (dlevel_two * silu_slope(z2)).astype(bf16)
    keep_narrow(t_two, mm_tn(taps_two, dz))
    merge_planes(l1_scr, stride_taps_back(mm_nt(dz, narrow(t_two, 1152)), 16), 16, 32)
    dlevel_one = dlevel_one + l1_scr[...]
    dz = (dlevel_one * silu_slope(z1_scr[...])).astype(bf16)
    keep_narrow(t_one, mm_tn(taps_one, dz))
    planes = stride_taps_back(mm_nt(dz, narrow(t_one, 1152)), 32)
    for p in range(4):
        plane_scr[p] = planes[p]
    at = pl.multiple_of(slab * 128, 128)
    for p in range(4):
        grad_ref[p] = plane_scr[p, pl.ds(at, 128), :].astype(bf16)
    out = pltpu.make_async_copy(gr.at[pl.ds(STRIDE_T * slab, SHARD_T)], quarter_ref, sems.at[0])
    out.start()
    out.wait()


def region(slab, counts, bird, anchors, goals, shards):
    return call(
        region_kernel,
        (
            shape((16, 128)),
            shape((4, 128, LANES), bf16),
            shape((SHARD_T, TILE, LANES)),
        ),
        [smem(), smem(), vmem(), vmem(), vmem(), anywhere()],
        (vmem(), vmem(), anywhere()),
        [
            pltpu.VMEM((PLANE_T, TILE, LANES), bf16),
            pltpu.VMEM((12, TILE, LANES), bf16),
            pltpu.VMEM((GRAD_T, TILE, LANES), f32),
            pltpu.SemaphoreType.DMA((10,)),
            pltpu.VMEM((512, 128), f32),
            pltpu.VMEM((128, 128), f32),
            pltpu.VMEM((512, 128), f32),
            pltpu.VMEM((512, 256), f32),
            pltpu.VMEM((4, 128, 256), f32),
            pltpu.VMEM((16, 32, 256), f32),
            pltpu.VMEM((768, LANES), f32),
            pltpu.VMEM((512, LANES), f32),
            pltpu.VMEM((512, LANES), f32),
            pltpu.VMEM((512, LANES), f32),
            pltpu.VMEM((4, 512, LANES), f32),
        ],
    )(slab, counts, bird, anchors, goals, shards)


def body(
    points, point_counts, voxel_cells, pos_anchors, pos_counts, reg_targets, params, moment1, moment2
):
    everyone = ("batch", "slab")
    batches = lax.axis_size("batch")
    devices = batches * SLABS
    slab = lax.axis_index("slab")
    slab_arg = slab.astype(jnp.int32).reshape(1)
    flat_rows = jnp.pad(params, (0, FLAT_R * LANES - SHARD)).reshape(FLAT_R, LANES)
    own = spread_shard(slab_arg, flat_rows)

    small = lax.all_gather(own[0:10], "slab", axis=0, tiled=True)[0:10]
    share = PAD_T // batches
    chunk = lax.dynamic_slice_in_dim(own, lax.axis_index("batch") * share, share, 0)
    shards = lax.all_gather(chunk, ("slab", "batch"), axis=0, tiled=True)
    conv_rows = shards[10 : 10 + CONV_R // TILE].reshape(CONV_R, LANES)

    counts = point_counts.reshape(1, VOX)
    features = encode(points, counts, voxel_cells.reshape(1, VOX), small)
    features = lax.all_gather(features, "slab", axis=0)
    bird, *kept = volume(slab_arg, features, conv_rows)
    birds = lax.all_gather(bird, "slab", axis=0)
    goals = jnp.pad(reg_targets.reshape(14, CELLS), ((2, 0), (0, 0)))
    maps, bird_grad, quarter = region(
        slab_arg, pos_counts, birds, pos_anchors.reshape(40, 1), goals, shards
    )
    quarter = lax.psum(quarter, "batch")
    feature_grad, conv_grad = volume_back(slab_arg, features, bird_grad, kept)
    feature_grad = lax.all_to_all(feature_grad, "slab", 0, 0, tiled=True)
    points_grad, vfe_grad = encode_back(points, counts, small, feature_grad)

    early = jnp.concatenate([vfe_grad, conv_grad], 0).astype(bf16)
    early = jnp.pad(early, ((0, CONV_T * TILE - early.shape[0]), (0, 0)))
    early = early.reshape(devices, CONV_T * TILE // devices, LANES)
    early = lax.all_to_all(early, everyone, 0, 0, tiled=True)
    early = jnp.sum(early.astype(f32), axis=0).astype(bf16)
    early = lax.all_gather(early, everyone, axis=0, tiled=True)
    grads, squares = gather_shard(slab_arg, quarter, early)
    grad_norm = jnp.sqrt(lax.psum(jnp.sum(squares), "slab"))
    own_grads = grads.reshape(-1)[0:SHARD]
    clipped = own_grads * (clip_level / jnp.maximum(grad_norm, clip_level))
    new_moment1 = beta_one * moment1 + (1.0 - beta_one) * clipped
    new_moment2 = beta_two * moment2 + (1.0 - beta_two) * clipped * clipped
    direction = (
        new_moment1
        / (1.0 - beta_one**STEP)
        / (jnp.sqrt(new_moment2 / (1.0 - beta_two**STEP)) + adam_eps)
    )
    new_params = params - learn_rate * (direction + weight_decay * params)
    head_maps = maps.reshape(1, 16, HY // SLABS, HX)
    return (head_maps, points_grad, new_moment1, new_moment2, new_params, grad_norm)


def solution(mesh):
    in_specs = (
        P(None, None, ("batch", "slab")),
        P(("batch", "slab")),
        P(("batch", "slab")),
        P("batch", None),
        P("batch"),
        P("batch", None, None, None),
        P("slab"),
        P("slab"),
        P("slab"),
    )
    out_specs = (
        P("batch", None, "slab", None),
        P(None, None, ("batch", "slab")),
        P("slab"),
        P("slab"),
        P("slab"),
        P(),
    )
    return jax.shard_map(body, mesh=mesh, in_specs=in_specs, out_specs=out_specs, check_vma=False)
```

```python
import functools
import math

import jax
import jax.numpy as jnp
from jax import lax
from jax.experimental import pallas as pl
from jax.experimental.pallas import tpu as pltpu
from jax.sharding import PartitionSpec as P

VF1 = 16
VF2 = 64
FC = 128
C3 = 64
STEP = 10
GY = 32
GX = 64
PTS = 35
VOX = 512
SLABS = 4
ROWS = GY // SLABS
LANES = 128
NPARAM = 2537584
SHARD = NPARAM // SLABS

TILE = 16
STRIDE_T = 310
SHARD_T = 312
PAD_T = 320
FLAT_R = 4960
EARLY_T = 288
EARLY_R = EARLY_T * TILE
VFE_T = 10
VFE_R = VFE_T * TILE
PLANE_T0 = 297
PLANE_T = 942
GRAD_T = 3 * STRIDE_T + PAD_T
CHUNK_T = PAD_T // 8
WIDE_T = (369, 1233)

beta_one = 0.9
beta_two = 0.999
adam_eps = 1e-08
learn_rate = 0.02
weight_decay = 0.01
clip_level = 0.002

f32 = jnp.float32
bf16 = jnp.bfloat16
VMEM_LIMIT = 56 * 1024 * 1024


def call(kernel, micros, out_shape, in_specs, out_specs, scratch=()):
    return pl.pallas_call(
        kernel,
        out_shape=out_shape,
        in_specs=in_specs,
        out_specs=out_specs,
        scratch_shapes=list(scratch),
        compiler_params=pltpu.CompilerParams(vmem_limit_bytes=VMEM_LIMIT),
        cost_estimate=pl.CostEstimate(
            flops=int(micros * 1e9), transcendentals=0, bytes_accessed=int(micros * 3e6)
        ),
    )


def vmem():
    return pl.BlockSpec(memory_space=pltpu.VMEM)


def smem():
    return pl.BlockSpec(memory_space=pltpu.SMEM)


def anywhere():
    return pl.BlockSpec(memory_space=pl.ANY)


def shape(dims, dtype=f32):
    return jax.ShapeDtypeStruct(dims, dtype)


def mm(a, b):
    return lax.dot_general(a, b, (((1,), (0,)), ((), ())), preferred_element_type=f32)


def mm_nt(a, b):
    return lax.dot_general(a, b, (((1,), (1,)), ((), ())), preferred_element_type=f32)


def mm_tn(a, b):
    return lax.dot_general(a, b, (((0,), (0,)), ((), ())), preferred_element_type=f32)


def sigmoid(z):
    return 0.5 * jnp.tanh(0.5 * z) + 0.5


def silu(z):
    return z * sigmoid(z)


def silu_slope(z):
    s = sigmoid(z)
    return s * (1.0 + z * (1.0 - s))


def lane_of(dims):
    return lax.broadcasted_iota(jnp.int32, dims, len(dims) - 1)


def row_of(dims):
    return lax.broadcasted_iota(jnp.int32, dims, 0)


def lane_roll(x, shift):
    shift = shift % x.shape[-1]
    return x if shift == 0 else pltpu.roll(x, shift, x.ndim - 1)


def shift_in(v, d, width):
    if d == 0:
        return v
    place = row_of(v.shape) % width
    keep = place > 0 if d > 0 else place < width - 1
    return jnp.where(keep, pltpu.roll(v, d % v.shape[0], 0), 0.0)


def shift_out(v, d, width):
    if d == 0:
        return v
    edge = jnp.zeros((width,) + v.shape[1:], v.dtype)
    if d > 0:
        return jnp.concatenate([edge, v[:-width]], 0)
    return jnp.concatenate([v[width:], edge], 0)


def batch_place(info_ref):
    return info_ref[1] // 2, info_ref[1] % 2


def chunk_start(chip, core, slot):
    return CHUNK_T * (2 * jnp.bitwise_xor(chip, slot) + core)


def join_chunks(info_ref, out_ref, own_ref, core_ref):
    chip, core = batch_place(info_ref)
    for slot in range(4):
        out_ref[pl.ds(chunk_start(chip, core, slot), CHUNK_T)] = own_ref[slot]
        out_ref[pl.ds(chunk_start(chip, 1 - core, slot), CHUNK_T)] = core_ref[slot]


def split_chunks(info_ref, scr, base, own_ref, core_ref):
    chip, core = batch_place(info_ref)
    for slot in range(4):
        own_ref[slot] = scr[pl.ds(base + chunk_start(chip, core, slot), CHUNK_T)].astype(bf16)
        core_ref[slot] = scr[pl.ds(base + chunk_start(chip, 1 - core, slot), CHUNK_T)].astype(bf16)


CHUNKS = (4, CHUNK_T, TILE, LANES)


def spread_kernel(slab_ref, flat_ref, out_ref, nat):
    nat[...] = jnp.zeros_like(nat)
    span = 480
    for s in range(SLABS):

        @pl.when(slab_ref[0] == s)
        def _(s=s):
            lanes, first = 16 + 28 * s, 15 - 4 * s
            lane = lane_of((span, LANES))
            count = FLAT_R // span + (FLAT_R % span > 0)
            for i in range(count):
                r0 = i * span
                n = min(span, FLAT_R - r0)
                rolled = lane_roll(flat_ref[r0 : r0 + n, :], lanes)
                nat[first + r0 : first + r0 + n, :] += jnp.where(lane[:n] >= lanes, rolled, 0.0)
                nat[first + r0 + 1 : first + r0 + 1 + n, :] += jnp.where(
                    lane[:n] < lanes, rolled, 0.0
                )
            low = max(0, min(SHARD_T // 2, (WIDE_T[0] - STRIDE_T * s + 1) // 2))
            high = max(low, min(SHARD_T // 2, (WIDE_T[1] - STRIDE_T * s + 1) // 2))
            for a, b, wide in ((0, low, False), (low, high, True), (high, SHARD_T // 2, False)):

                def block(i, carry, wide=wide):
                    base = pl.multiple_of(32 * i, 32)
                    if wide:
                        even = nat[pl.ds(base, 16, stride=2), :]
                        odd = nat[pl.ds(base + 1, 16, stride=2), :]
                    else:
                        even = nat[pl.ds(base, 16), :]
                        odd = nat[pl.ds(base + 16, 16), :]
                    out_ref[2 * i] = even.astype(bf16)
                    out_ref[2 * i + 1] = odd.astype(bf16)
                    return carry

                if b > a:
                    lax.fori_loop(a, b, block, 0, unroll=4)

    for t in range(SHARD_T, PAD_T):
        out_ref[t] = jnp.zeros((TILE, LANES), bf16)


def spread_shard(slab, flat_rows):
    return call(
        spread_kernel,
        4,
        shape((PAD_T, TILE, LANES), bf16),
        [smem(), vmem()],
        vmem(),
        [pltpu.VMEM((5120, LANES), f32)],
    )(slab, flat_rows)


def spread_first_kernel(flat_ref, out_ref, nat):
    lanes, first = 16, 15
    lane = lane_of((VFE_R, LANES))
    rolled = lane_roll(flat_ref[...], lanes)
    nat[...] = jnp.zeros_like(nat)
    nat[first : first + VFE_R, :] += jnp.where(lane >= lanes, rolled, 0.0)
    nat[first + 1 : first + 1 + VFE_R, :] += jnp.where(lane < lanes, rolled, 0.0)
    rows = nat[0:VFE_R, :].astype(bf16).reshape(VFE_T, TILE, LANES)
    out_ref[...] = rows


def spread_first(flat_rows):
    return call(
        spread_first_kernel,
        1,
        shape((VFE_T, TILE, LANES), bf16),
        [vmem()],
        vmem(),
        [pltpu.VMEM((VFE_R + 32, LANES), f32)],
    )(flat_rows)


def gather_kernel(slab_ref, own_ref, core_ref, vfe_ref, out_ref, quarter_ref, nat):
    join_chunks(slab_ref, quarter_ref, own_ref, core_ref)
    span = 480
    for s in range(SLABS):

        @pl.when(slab_ref[0] == s)
        def _(s=s):
            lanes, first = 16 + 28 * s, 15 - 4 * s
            low = max(0, min(SHARD_T // 2, (WIDE_T[0] - STRIDE_T * s + 1) // 2))
            high = max(low, min(SHARD_T // 2, (WIDE_T[1] - STRIDE_T * s + 1) // 2))
            for a, b, wide in ((0, low, False), (low, high, True), (high, SHARD_T // 2, False)):

                def block(i, carry, wide=wide):
                    base = pl.multiple_of(32 * i, 32)
                    even, odd = quarter_ref[2 * i].astype(f32), quarter_ref[2 * i + 1].astype(f32)
                    if wide:
                        nat[pl.ds(base, 16, stride=2), :] = even
                        nat[pl.ds(base + 1, 16, stride=2), :] = odd
                    else:
                        nat[pl.ds(base, 16), :] = even
                        nat[pl.ds(base + 16, 16), :] = odd
                    return carry

                if b > a:
                    lax.fori_loop(a, b, block, 0, unroll=4)
            if s == 0:
                nat[0:VFE_R, :] = vfe_ref[...]
            lane = lane_of((span, LANES))
            count = FLAT_R // span + (FLAT_R % span > 0)
            for i in range(count):
                r0 = i * span
                n = min(span, FLAT_R - r0)
                here = lane_roll(nat[first + r0 : first + r0 + n, :], -lanes)
                after = lane_roll(nat[first + r0 + 1 : first + r0 + 1 + n, :], -lanes)
                out_ref[r0 : r0 + n, :] = jnp.where(lane[:n] < LANES - lanes, here, after)


def gather_shard(info, own, core, vfe):
    return call(
        gather_kernel,
        5,
        shape((FLAT_R, LANES)),
        [smem(), vmem(), vmem(), vmem()],
        vmem(),
        [pltpu.VMEM((PAD_T, TILE, LANES), bf16), pltpu.VMEM((5120, LANES), f32)],
    )(info, own, core, vfe)


PART = 5
PARTS = PTS // PART
WIDE = PART * VOX
VFE_SCRATCH = [
    pltpu.VMEM((VOX // LANES, PTS * 16, LANES), f32),
    pltpu.VMEM((16, LANES), f32),
    pltpu.VMEM((64, LANES), f32),
]


def spread_points(points_ref, x_scr):
    x_scr[...] = jnp.zeros_like(x_scr)
    for c in range(7):
        plane = points_ref[c].astype(f32)
        for b in range(VOX // LANES):
            x_scr[b, pl.ds(c, PTS, stride=16), :] = plane[:, b * LANES : (b + 1) * LANES]


def vfe_weights(rows_ref, w1_scr, w2_scr):
    line = rows_ref[0].astype(f32)
    lane = lane_of((16, LANES))
    for o in range(VF1):
        w1_scr[o : o + 1, :] = jnp.where(lane < 7, lane_roll(line, -(16 + 7 * o)), 0.0)[15:16]
    two = rows_ref[1].astype(f32)
    for k in range(4):
        w2_scr[pl.ds(k, 16, stride=4), :] = jnp.where(lane < 32, lane_roll(two, -32 * k), 0.0)
    w1 = w1_scr[...].astype(bf16)[:, 0:16]
    w2 = w2_scr[...]
    w2a = w2.astype(bf16)[:, 0:16]
    w2b = lane_roll(w2, -16).astype(bf16)[:, 0:16]
    w3 = rows_ref[2:10].reshape(FC, LANES)
    w3a = w3[:, 0:64]
    w3b = lane_roll(w3.astype(f32), -64).astype(bf16)[:, 0:64]
    return w1, w2a, w2b, w3a, w3b


def points_part(ref, i):
    return jnp.concatenate(
        [
            ref[b, pl.ds(pl.multiple_of((PART * i + k) * 16, 16), 16), :]
            for k in range(PART)
            for b in range(VOX // LANES)
        ],
        1,
    )


def set_points_part(ref, i, value):
    for k in range(PART):
        for b in range(VOX // LANES):
            at = k * VOX + b * LANES
            ref[b, pl.ds(pl.multiple_of((PART * i + k) * 16, 16), 16), :] = value[:, at : at + LANES]


def part_sum(value):
    total = value[:, 0:VOX]
    for k in range(1, PART):
        total = total + value[:, k * VOX : (k + 1) * VOX]
    return total


def valid_part(i, counts):
    return jnp.concatenate([(PART * i + k < counts).astype(f32) for k in range(PART)], 1)


def widen(value):
    return jnp.concatenate([value] * PART, 1)


def vfe_front(weights, counts, inverse, x_scr, j1_ref, j2_ref, kept=None):
    w1, w2a, w2b, w3a, w3b = weights

    def layer_one(i, total):
        x = points_part(x_scr, i).astype(bf16)
        z = mm(w1, x)
        value = silu(z)
        j1_ref[i] = value.astype(bf16)
        if kept is not None:
            x_ref, s1_ref, s2_ref = kept
            x_ref[i] = x
            s1_ref[i] = silu_slope(z)
        return total + part_sum(value * valid_part(i, counts))

    total = lax.fori_loop(0, PARTS, layer_one, jnp.zeros((VF1, VOX), f32))
    mean_one = (total * inverse).astype(bf16)
    shared_two = widen(mm(w2b, mean_one))

    def layer_two(i, total):
        z = mm(w2a, j1_ref[i]) + shared_two
        value = silu(z)
        j2_ref[i] = value.astype(bf16)
        if kept is not None:
            kept[2][i] = silu_slope(z)
        return total + part_sum(value * valid_part(i, counts))

    total = lax.fori_loop(0, PARTS, layer_two, jnp.zeros((VF2, VOX), f32))
    mean_two = (total * inverse).astype(bf16)
    shared_three = widen(mm(w3b, mean_two))
    return mean_one, mean_two, shared_three


def encode_kernel(points_ref, counts_ref, cells_ref, rows_ref, out_ref, x_scr, w1_scr, w2_scr, j1_scr, j2_scr):
    spread_points(points_ref, x_scr)
    weights = vfe_weights(rows_ref, w1_scr, w2_scr)
    counts = counts_ref[...]
    inverse = 1.0 / counts.astype(f32)
    _, _, shared_three = vfe_front(weights, counts, inverse, x_scr, j1_scr, j2_scr)
    w3a = weights[3]

    def layer_three(i, total):
        value = silu(mm(w3a, j2_scr[i]) + shared_three)
        return total + part_sum(value * valid_part(i, counts))

    total = lax.fori_loop(0, PARTS, layer_three, jnp.zeros((FC, VOX), f32))
    features = (total * inverse).astype(bf16)
    cells = cells_ref[...]
    row = row_of((16, VOX))
    places = jnp.where(row == 0, cells // GX, cells % GX).astype(f32).astype(bf16)
    out_ref[0:FC, :] = features
    out_ref[FC : FC + 16, :] = places


def encode(points, counts, cells, rows):
    return call(
        encode_kernel,
        10,
        shape((FC + 16, VOX), bf16),
        [vmem()] * 4,
        vmem(),
        VFE_SCRATCH
        + [pltpu.VMEM((PARTS, 16, WIDE), bf16), pltpu.VMEM((PARTS, 64, WIDE), bf16)],
    )(points, counts, cells, rows)


def encode_slopes_kernel(
    points_ref, counts_ref, rows_ref,
    x_ref, j1_ref, j2_ref, s1_ref, s2_ref, s3_ref, m1_ref, m2_ref,
    x_scr, w1_scr, w2_scr,
):
    spread_points(points_ref, x_scr)
    weights = vfe_weights(rows_ref, w1_scr, w2_scr)
    counts = counts_ref[...]
    inverse = 1.0 / counts.astype(f32)
    mean_one, mean_two, shared_three = vfe_front(
        weights, counts, inverse, x_scr, j1_ref, j2_ref, (x_ref, s1_ref, s2_ref)
    )
    m1_ref[...] = mean_one
    m2_ref[...] = mean_two
    w3a = weights[3]
    scale = widen(inverse)

    def layer_three(i, carry):
        slope = silu_slope(mm(w3a, j2_ref[i]) + shared_three)
        s3_ref[i] = (slope * (valid_part(i, counts) * scale)).astype(bf16)
        return carry

    lax.fori_loop(0, PARTS, layer_three, 0)


def encode_slopes(points, counts, rows):
    return call(
        encode_slopes_kernel,
        15,
        (
            shape((PARTS, 16, WIDE), bf16),
            shape((PARTS, 16, WIDE), bf16),
            shape((PARTS, 64, WIDE), bf16),
            shape((PARTS, 16, WIDE)),
            shape((PARTS, 64, WIDE)),
            shape((PARTS, 128, WIDE), bf16),
            shape((VF1, VOX), bf16),
            shape((VF2, VOX), bf16),
        ),
        [vmem()] * 3,
        (vmem(),) * 8,
        VFE_SCRATCH,
    )(points, counts, rows)


def encode_back_kernel(
    counts_ref, rows_ref, g0_ref, g1_ref, g2_ref, g3_ref, x_ref, j1_ref, j2_ref, s1_ref, s2_ref, s3_ref, m1_ref, m2_ref,
    out_ref, weight_ref,
    x_scr, w1_scr, w2_scr, d1_scr, d2_scr,
):
    w1, w2a, w2b, w3a, w3b = vfe_weights(rows_ref, w1_scr, w2_scr)
    counts = counts_ref[...]
    inverse = 1.0 / counts.astype(f32)
    grad = g0_ref[...].astype(f32)
    for ref in (g1_ref, g2_ref, g3_ref):
        grad = grad + ref[...].astype(f32)
    grad_three = widen(grad)

    def back_three(i, carry):
        total, weight = carry
        dz = grad_three * s3_ref[i].astype(f32)
        low = dz.astype(bf16)
        d2_scr[i] = mm_tn(w3a, low)
        return total + part_sum(dz), weight + mm_nt(low, j2_ref[i])

    total, grad_w3a = lax.fori_loop(
        0, PARTS, back_three, (jnp.zeros((FC, VOX), f32), jnp.zeros((FC, VF2), f32))
    )
    total = total.astype(bf16)
    grad_w3b = mm_nt(total, m2_ref[...])
    grad_two = widen(mm_tn(w3b, total) * inverse)

    def back_two(i, carry):
        total, weight = carry
        dz = (d2_scr[i] + valid_part(i, counts) * grad_two) * s2_ref[i]
        low = dz.astype(bf16)
        d1_scr[i] = mm_tn(w2a, low)
        return total + part_sum(dz), weight + mm_nt(low, j1_ref[i])

    total, grad_w2a = lax.fori_loop(
        0, PARTS, back_two, (jnp.zeros((VF2, VOX), f32), jnp.zeros((VF2, VF1), f32))
    )
    total = total.astype(bf16)
    grad_w2b = mm_nt(total, m1_ref[...])
    grad_one = widen(mm_tn(w2b, total) * inverse)

    def back_one(i, weight):
        dz = (d1_scr[i] + valid_part(i, counts) * grad_one) * s1_ref[i]
        low = dz.astype(bf16)
        set_points_part(x_scr, i, mm_tn(w1, low))
        return weight + mm_nt(low, x_ref[i])

    grad_w1 = lax.fori_loop(0, PARTS, back_one, jnp.zeros((VF1, 16), f32))
    for c in range(7):
        for b in range(VOX // LANES):
            out_ref[c, :, b * LANES : (b + 1) * LANES] = x_scr[b, pl.ds(c, PTS, stride=16), :]

    lane = lane_of((16, LANES))
    w1_scr[...] = jnp.concatenate([grad_w1, jnp.zeros((16, LANES - 16), f32)], 1)
    spread = jnp.where(lane < 7, w1_scr[...], 0.0)
    line = jnp.zeros((16, LANES), f32)
    row = row_of((16, LANES))
    for o in range(VF1):
        line = line + jnp.where(row == o, lane_roll(spread, 16 + 7 * o), 0.0)
    line = jnp.sum(line, axis=0, keepdims=True)
    weight_ref[0:16, :] = jnp.where(row == 15, line, 0.0)
    w2_scr[...] = jnp.concatenate([grad_w2a, grad_w2b, jnp.zeros((64, LANES - 32), f32)], 1)
    two = jnp.zeros((16, LANES), f32)
    for k in range(4):
        two = two + lane_roll(w2_scr[pl.ds(k, 16, stride=4), :], 32 * k)
    weight_ref[16:32, :] = two
    weight_ref[32:160, :] = jnp.concatenate([grad_w3a, grad_w3b], 1)


def encode_back(counts, rows, grad, kept):
    return call(
        encode_back_kernel,
        15,
        (shape((7, PTS, VOX)), shape((VFE_R, LANES))),
        [vmem()] * 14,
        (vmem(), vmem()),
        VFE_SCRATCH + [pltpu.VMEM((PARTS, 16, WIDE), f32), pltpu.VMEM((PARTS, 64, WIDE), f32)],
    )(counts, rows, *grad, *kept)


R3 = ROWS + 1
R3W = R3 * GX
R2W = (R3 + 2) * GX
R1W = (R3 + 4) * GX
RG = R3 + 6
RGW = RG * GX
HX = GX // 2
L1_R = ROWS // 2 * HX


def cell_marks(places):
    value = places.astype(f32)
    high, low = value[0:1], value[1:2]
    column = lax.broadcasted_iota(jnp.int32, (GX, VOX), 0).astype(f32)
    return (column == low).astype(f32).astype(bf16), high


def layer_marks(column, high, depth, first_row):
    pieces = []
    for w in range(RG):
        row = first_row - 3 + w
        inside = jnp.logical_and(row >= 0, row < GY)
        target = jnp.where(inside, depth * GY + row, -1).astype(f32)
        pieces.append(column * (high == target).astype(f32).astype(bf16))
    return jnp.concatenate(pieces, 0)


def conv_weights(rows_ref, start, taps, half, place, scr):
    lane = lane_of((half, LANES))
    left = lane < 64
    for t in range(taps):
        r = []
        for kx in range(3):
            base = start + (3 * t + kx) * half
            r.append(rows_ref[base // TILE : (base + half) // TILE].reshape(half, LANES).astype(f32))
        turned = [lane_roll(v, 64) for v in r]
        at = place(t)
        scr[0, pl.ds(at, half, stride=2), :] = jnp.where(left, r[1], turned[0])
        scr[0, pl.ds(at + 1, half, stride=2), :] = jnp.where(left, turned[1], r[0])
        scr[1, pl.ds(at, half, stride=2), :] = jnp.where(left, r[2], 0.0)
        scr[1, pl.ds(at + 1, half, stride=2), :] = jnp.where(left, turned[2], 0.0)


def conv_weight_grads(out_ref, start, taps, half, place, scr):
    lane = lane_of((half, LANES))
    left = lane < 64
    for t in range(taps):
        at = place(t)
        even = [scr[b, pl.ds(at, half, stride=2), :] for b in range(2)]
        odd = [scr[b, pl.ds(at + 1, half, stride=2), :] for b in range(2)]
        values = (
            jnp.where(left, lane_roll(even[0], 64), odd[0]),
            jnp.where(left, even[0], lane_roll(odd[0], 64)),
            jnp.where(left, even[1], lane_roll(odd[1], 64)),
        )
        for kx in range(3):
            base = start + (3 * t + kx) * half
            out_ref[base // TILE : (base + half) // TILE] = (
                values[kx].astype(bf16).reshape(half // TILE, TILE, LANES)
            )


def both_halves(out_ref, scr):
    for b in range(2):
        out_ref[:, b * LANES : (b + 1) * LANES] = scr[b].astype(bf16)


def keep_halves(scr, value):
    for b in range(2):
        scr[b] = value[:, b * LANES : (b + 1) * LANES]


def tap_place(t):
    return 128 * t


def pair_place(t):
    kd, ky = t // 3, t % 3
    return 128 * ky + 64 * kd if kd < 2 else 384 + 128 * ky


def join_columns(p):
    first, last = p[:, 0:128], p[:, 128:256]
    left = lane_of(first.shape) < 64
    half = jnp.where(left, first + shift_in(last, -1, GX), shift_in(first, 1, GX))
    return half + lane_roll(half, 64)


def split_columns(d):
    left = lane_of(d.shape) < 64
    first = jnp.where(left, d, lane_roll(shift_in(d, -1, GX), 64))
    last = jnp.where(left, shift_in(d, 1, GX), 0.0)
    return jnp.concatenate([first, last], 1).astype(bf16)


def inside_rows(rows, first_row):
    place = first_row + row_of((rows, LANES)) // GX
    return jnp.logical_and(place >= 0, place < GY)


def grid_taps(grid_ref, k):
    return jnp.concatenate(
        [grid_ref[2 * k + kd, ky * GX : ky * GX + R1W, :] for kd in range(3) for ky in range(3)], 1
    )


def pair_taps(ref, at, rows):
    return jnp.concatenate(
        [ref[at, ky * GX : ky * GX + rows, :] for ky in range(3)]
        + [ref[at + 2, ky * GX : ky * GX + rows, :] for ky in range(3)],
        1,
    )


def level_taps(ref):
    planes = {}
    for xp in range(2):
        for yp in range(2):
            count = ROWS // 2 + 1 - yp
            planes[yp, xp] = jnp.concatenate(
                [ref[pl.ds((2 * a + yp) * GX + xp, HX, stride=2), :] for a in range(count)], 0
            )
    pieces = []
    for ky in range(3):
        for kx in range(3):
            v = planes[ky % 2, int(kx != 1)]
            v = v[HX:] if ky == 2 else v[0:L1_R]
            pieces.append((shift_in(v, 1, HX) if kx == 0 else v).astype(bf16))
    return jnp.concatenate(pieces, 1)


def level_taps_back(ref, grad):
    planes = {}
    edge = jnp.zeros((HX, LANES), f32)
    for ky in range(3):
        for kx in range(3):
            t = 3 * ky + kx
            v = grad[:, t * LANES : (t + 1) * LANES]
            v = shift_in(v, -1, HX) if kx == 0 else v
            if ky != 1:
                v = jnp.concatenate([edge, v] if ky == 2 else [v, edge], 0)
            at = (ky % 2, int(kx != 1))
            planes[at] = planes[at] + v if at in planes else v
    for (yp, xp), v in planes.items():
        for a in range(ROWS // 2 + 1 - yp):
            ref[pl.ds((2 * a + yp) * GX + xp, HX, stride=2), :] = v[a * HX : (a + 1) * HX]


def volume_kernel(
    slab_ref, f0_ref, f1_ref, f2_ref, f3_ref, own_ref, core_ref,
    level_ref, grid_ref, first_ref, second_ref, taps_ref, z1_ref, z2_ref, z3_ref, z4_ref, w1_ref, w2_ref, w3_ref, w4_ref,
    rows_ref, w1_scr, w2_scr, bird_scr,
):
    join_chunks(slab_ref, rows_ref, own_ref, core_ref)
    w4_ref[...] = rows_ref[LEVEL_T : LEVEL_T + 72].reshape(1152, LANES)
    w2_scr[...] = jnp.zeros_like(w2_scr)
    conv_weights(rows_ref, VFE_R, 9, 64, tap_place, w1_scr)
    both_halves(w1_ref, w1_scr)
    conv_weights(rows_ref, VFE_R + 1728, 9, 32, pair_place, w2_scr)
    both_halves(w2_ref, w2_scr)
    conv_weights(rows_ref, VFE_R + 2592, 9, 32, pair_place, w2_scr)
    both_halves(w3_ref, w2_scr)

    first_row = slab_ref[0] * ROWS - 1
    grid_ref[0] = jnp.zeros((RGW, FC), bf16)
    for slot, f_ref in enumerate((f0_ref, f1_ref, f2_ref, f3_ref)):
        t = jnp.bitwise_xor(slab_ref[0], slot)
        features = f_ref[0:FC, :]
        column, high = cell_marks(f_ref[FC : FC + 16, :])
        for d in range(2):
            marks = layer_marks(column, high, d, first_row)
            grid_ref[1 + 2 * t + d] = mm_nt(marks, features).astype(bf16)

    first_ref[0] = jnp.zeros((R1W, LANES), bf16)
    first_ref[5] = jnp.zeros((R1W, LANES), bf16)
    keep = inside_rows(R1W, first_row - 2)
    for k in range(4):
        z = join_columns(mm(grid_taps(grid_ref, k), w1_ref[...]))
        z1_ref[k] = z
        value = jnp.where(keep, silu(z), 0.0).astype(bf16)
        first_ref[k + 1, :, 0:64] = value[:, 0:64]
        first_ref[k, :, 64:128] = value[:, 64:128]
    first_ref[4, :, 64:128] = jnp.zeros((R1W, 64), bf16)

    second_ref[0] = jnp.zeros((R2W, LANES), bf16)
    second_ref[5] = jnp.zeros((R2W, LANES), bf16)
    keep = inside_rows(R2W, first_row - 1)
    for k in range(4):
        z = join_columns(mm(pair_taps(first_ref, k, R2W), w2_ref[...]))
        z2_ref[k] = z
        value = jnp.where(keep, silu(z), 0.0).astype(bf16)
        second_ref[k + 1, :, 0:64] = value[:, 0:64]
        second_ref[k, :, 64:128] = value[:, 64:128]
    second_ref[4, :, 64:128] = jnp.zeros((R2W, 64), bf16)

    z3 = []
    for k in range(2):
        z3.append(join_columns(mm(pair_taps(second_ref, 2 * k, R3W), w3_ref[...])))
    z = jnp.where(lane_of((R3W, LANES)) < 64, z3[0], z3[1])
    z3_ref[...] = z
    bird_scr[...] = jnp.where(inside_rows(R3W, first_row), silu(z), 0.0)
    taps = level_taps(bird_scr)
    taps_ref[...] = taps
    z = mm(taps, w4_ref[...])
    z4_ref[...] = z
    level_ref[...] = silu(z).astype(bf16)


LEVEL_T = VFE_T + 216


def volume(info, features, early):
    return call(
        volume_kernel,
        11,
        (
            shape((L1_R, LANES), bf16),
            shape((9, RGW, LANES), bf16),
            shape((6, R1W, LANES), bf16),
            shape((6, R2W, LANES), bf16),
            shape((L1_R, 1152), bf16),
            shape((4, R1W, LANES)),
            shape((4, R2W, LANES)),
            shape((R3W, LANES)),
            shape((L1_R, LANES)),
            shape((1152, 256), bf16),
            shape((768, 256), bf16),
            shape((768, 256), bf16),
            shape((1152, LANES), bf16),
        ),
        [smem()] + [vmem()] * 6,
        (vmem(),) * 13,
        [
            pltpu.VMEM((PAD_T, TILE, LANES), bf16),
            pltpu.VMEM((2, 1152, LANES), f32),
            pltpu.VMEM((2, 768, LANES), f32),
            pltpu.VMEM((R3W, LANES), f32),
        ],
    )(info, *features, *early)


def volume_back_kernel(
    slab_ref, f0_ref, f1_ref, f2_ref, f3_ref, level_ref,
    grid_ref, first_ref, second_ref, taps_ref, z1_ref, z2_ref, z3_ref, z4_ref, w1_ref, w2_ref, w3_ref, w4_ref,
    o0_ref, o1_ref, o2_ref, o3_ref, own_ref, core_ref,
    weight_ref, bird_scr, acc2, acc1, accg, g1_scr, g2_scr,
):
    first_row = slab_ref[0] * ROWS - 1
    dz = (level_ref[...] * silu_slope(z4_ref[...])).astype(bf16)
    weight_ref[0:VFE_T] = jnp.zeros((VFE_T, TILE, LANES), bf16)
    weight_ref[VFE_T + EARLY_T : PAD_T] = jnp.zeros((PAD_T - VFE_T - EARLY_T, TILE, LANES), bf16)
    weight_ref[LEVEL_T : LEVEL_T + 72] = mm_tn(taps_ref[...], dz).astype(bf16).reshape(72, TILE, LANES)
    level_taps_back(bird_scr, mm_nt(dz, w4_ref[...]))
    dz = jnp.where(inside_rows(R3W, first_row), bird_scr[...] * silu_slope(z3_ref[...]), 0.0)
    acc2[...] = jnp.zeros_like(acc2)
    acc1[...] = jnp.zeros_like(acc1)
    accg[...] = jnp.zeros_like(accg)

    def pair_back(acc, at, rows, spread, weight):
        back = mm_nt(spread, weight)
        for ky in range(3):
            acc[at, ky * GX : ky * GX + rows, :] += back[:, 128 * ky : 128 * ky + 128]
            acc[at + 2, ky * GX : ky * GX + rows, :] += back[:, 384 + 128 * ky : 512 + 128 * ky]

    def layer_grad(acc, m):
        return acc[m] + lane_roll(acc[m - 1], 64)

    total = jnp.zeros((768, 256), f32)
    for k in range(2):
        spread = split_columns(dz if k == 0 else lane_roll(dz, 64))
        total = total + mm_tn(pair_taps(second_ref, 2 * k, R3W), spread)
        pair_back(acc2, 2 * k, R3W, spread, w3_ref[...])
    keep_halves(g2_scr, total)
    conv_weight_grads(weight_ref, VFE_R + 2592, 9, 32, pair_place, g2_scr)

    keep = inside_rows(R2W, first_row - 1)
    total = jnp.zeros((768, 256), f32)
    for k in range(4):
        d = jnp.where(keep, layer_grad(acc2, k + 1) * silu_slope(z2_ref[k]), 0.0)
        spread = split_columns(d)
        total = total + mm_tn(pair_taps(first_ref, k, R2W), spread)
        pair_back(acc1, k, R2W, spread, w2_ref[...])
    keep_halves(g2_scr, total)
    conv_weight_grads(weight_ref, VFE_R + 1728, 9, 32, pair_place, g2_scr)

    keep = inside_rows(R1W, first_row - 2)
    total = jnp.zeros((1152, 256), f32)
    for k in range(4):
        d = jnp.where(keep, layer_grad(acc1, k + 1) * silu_slope(z1_ref[k]), 0.0)
        spread = split_columns(d)
        total = total + mm_tn(grid_taps(grid_ref, k), spread)
        back = mm_nt(spread, w1_ref[...])
        for kd in range(3):
            for ky in range(3):
                t = 3 * kd + ky
                accg[2 * k + kd, ky * GX : ky * GX + R1W, :] += back[:, 128 * t : 128 * t + 128]
    keep_halves(g1_scr, total)
    conv_weight_grads(weight_ref, VFE_R + 0, 9, 64, tap_place, g1_scr)

    pairs = zip((f0_ref, f1_ref, f2_ref, f3_ref), (o0_ref, o1_ref, o2_ref, o3_ref))
    for slot, (f_ref, out_ref) in enumerate(pairs):
        t = jnp.bitwise_xor(slab_ref[0], slot)
        column, high = cell_marks(f_ref[FC : FC + 16, :])
        value = jnp.zeros((FC, VOX), f32)
        for d in range(2):
            marks = layer_marks(column, high, d, first_row)
            value = value + mm_tn(accg[1 + 2 * t + d].astype(bf16), marks)
        out_ref[...] = value.astype(bf16)
    split_chunks(slab_ref, weight_ref, 0, own_ref, core_ref)


def volume_back(info, features, level_grad, kept):
    return call(
        volume_back_kernel,
        16,
        (shape((FC, VOX), bf16),) * 4 + (shape(CHUNKS, bf16),) * 2,
        [smem()] + [vmem()] * 17,
        (vmem(),) * 6,
        [
            pltpu.VMEM((PAD_T, TILE, LANES), bf16),
            pltpu.VMEM((R3W, LANES), f32),
            pltpu.VMEM((6, R2W, LANES), f32),
            pltpu.VMEM((6, R1W, LANES), f32),
            pltpu.VMEM((9, RGW, LANES), f32),
            pltpu.VMEM((2, 1152, LANES), f32),
            pltpu.VMEM((2, 768, LANES), f32),
        ],
    )(info, *features, level_grad, *kept)


def split_planes(ref, height, width):
    planes = []
    for yp in range(2):
        for xp in range(2):
            planes.append(
                jnp.concatenate(
                    [
                        ref[pl.ds((2 * a + yp) * width + xp, width // 2, stride=2), :]
                        for a in range(height // 2)
                    ],
                    0,
                )
            )
    return planes


def merge_planes(ref, planes, height, width):
    half = width // 2
    for yp in range(2):
        for xp in range(2):
            for a in range(height // 2):
                ref[pl.ds((2 * a + yp) * width + xp, half, stride=2), :] = planes[2 * yp + xp][
                    a * half : a * half + half
                ]


def stride_taps(planes, width):
    pieces = []
    for ky in range(3):
        for kx in range(3):
            v = planes[2 * (ky != 1) + (kx != 1)]
            v = shift_in(v, 1, width) if kx == 0 else v
            pieces.append((shift_out(v, 1, width) if ky == 0 else v).astype(bf16))
    return jnp.concatenate(pieces, 1)


def stride_taps_back(grad, width):
    planes = [None] * 4
    channels = grad.shape[1] // 9
    for ky in range(3):
        for kx in range(3):
            t = 3 * ky + kx
            v = grad[:, t * channels : (t + 1) * channels]
            v = shift_out(v, -1, width) if ky == 0 else v
            v = shift_in(v, -1, width) if kx == 0 else v
            at = 2 * (ky != 1) + (kx != 1)
            planes[at] = v if planes[at] is None else planes[at] + v
    return planes


def full_taps(v, width):
    across = [shift_in(v, 1 - kx, width).astype(bf16) for kx in range(3)]
    return jnp.concatenate(
        [shift_out(across[kx], 1 - ky, width) for ky in range(3) for kx in range(3)], 1
    )


def full_taps_back(grad, width):
    channels = grad.shape[1] // 9
    total = None
    for kx in range(3):
        column = None
        for ky in range(3):
            t = 3 * ky + kx
            v = shift_out(grad[:, t * channels : (t + 1) * channels], ky - 1, width)
            column = v if column is None else column + v
        column = shift_in(column, kx - 1, width)
        total = column if total is None else total + column
    return total


HY = 16
CELLS = HY * HX


def region_kernel(
    slab_ref, counts_ref, l0_ref, l1_ref, l2_ref, l3_ref, anchors_ref, goals_ref,
    s0_ref, s1_ref, s2_ref, s3_ref, s4_ref, s5_ref, s6_ref, s7_ref,
    maps_ref, grad_ref, own_ref, core_ref,
    wv, gr, sems,
    l1_scr, l2_scr, zu1_scr, zu2_scr, zu3_scr, head_scr, maps_scr, two_scr, three_scr,
):
    slab = slab_ref[0]
    chip, core = batch_place(slab_ref)
    copies = []
    shards = (s0_ref, s1_ref, s2_ref, s3_ref, s4_ref, s5_ref, s6_ref, s7_ref)
    for n, (ref, (chips, slots)) in enumerate(zip(shards, LATE_ORDER * 2)):
        for k in range(4):
            shard = jnp.bitwise_xor(slab_ref[2], slots[k])
            at = chunk_start(chip, core if n < 4 else 1 - core, chips[k])
            copies.append(
                pltpu.make_async_copy(
                    ref.at[k], wv.at[shard, pl.ds(at, CHUNK_T)], sems.at[len(copies)]
                )
            )
    for c in copies:
        c.start()
    gr[0 : PLANE_T0 + 1] = jnp.zeros((PLANE_T0 + 1, TILE, LANES), bf16)
    gr[PLANE_T0 + 1 + PLANE_T : GRAD_T] = jnp.zeros((GRAD_T - PLANE_T0 - 1 - PLANE_T, TILE, LANES), bf16)
    for slot, ref in enumerate((l0_ref, l1_ref, l2_ref, l3_ref)):
        at = pl.multiple_of(jnp.bitwise_xor(slab, slot) * L1_R, L1_R)
        l1_scr[pl.ds(at, L1_R), :] = ref[...].astype(f32)
    level_one = l1_scr[...]
    for c in copies:
        c.wait()
    for s in range(1, SLABS):
        wv[s, 0:2] = wv[s, 0:2] + wv[s - 1, STRIDE_T : STRIDE_T + 2]

    def tiles_of(tile, tiles):
        pieces = []
        while tiles:
            s = min((tile + 1) // STRIDE_T, SLABS - 1)
            at = tile + 1 - STRIDE_T * s
            size = min(tiles, STRIDE_T - at) if s < SLABS - 1 else tiles
            pieces.append(wv[s, at : at + size])
            tile, tiles = tile + size, tiles - size
        return pieces[0] if len(pieces) == 1 else jnp.concatenate(pieces, 0)

    def narrow(tile, rows):
        return tiles_of(tile, rows // 16).reshape(rows, LANES)

    def wide(tile, rows):
        both = tiles_of(tile, rows // 8).reshape(rows // 16, 2, TILE, LANES)
        return jnp.concatenate(
            [both[:, 0].reshape(rows, LANES), both[:, 1].reshape(rows, LANES)], 1
        )

    def keep_narrow(tile, value):
        at = tile + 1
        tiles = value.shape[0] // 16
        gr[at : at + tiles] = value.astype(bf16).reshape(tiles, TILE, LANES)

    def keep_wide(tile, value):
        at = tile + 1
        tiles = value.shape[0] // 16
        value = value.astype(bf16)
        left = value[:, 0:128].reshape(tiles, 1, TILE, LANES)
        right = value[:, 128:256].reshape(tiles, 1, TILE, LANES)
        gr[at : at + 2 * tiles] = jnp.concatenate([left, right], 1).reshape(2 * tiles, TILE, LANES)

    t_two, t_three, t_up1, t_up2, t_up3, t_head = 297, 369, 513, 657, 721, 1233

    taps_two = stride_taps(split_planes(l1_scr, 16, 32), 16)
    z2 = mm(taps_two, narrow(t_two, 1152))
    level_two = silu(z2).astype(bf16)
    l2_scr[...] = level_two.astype(f32)
    taps_three = stride_taps(split_planes(l2_scr, 8, 16), 8)
    z3 = mm(taps_three, wide(t_three, 1152))
    level_three = silu(z3).astype(bf16)

    taps_up = full_taps(level_one, 32)
    zu1_scr[...] = mm(taps_up, wide(t_up1, 1152))
    for g in range(4):
        zu2_scr[g] = mm(level_two, wide(t_up2 + 16 * g, 128))
    for g in range(16):
        zu3_scr[g] = mm(level_three, wide(t_up3 + 32 * g, 256))

    lane = lane_of((96, LANES))
    rows = narrow(t_head, 96).astype(f32)
    for c in range(8):
        head_scr[pl.ds(c, 96, stride=8), :] = jnp.where(lane < 16, lane_roll(rows, -16 * c), 0.0)
    head = head_scr[...].astype(bf16)
    head_a, head_b, head_c = head[0:256], head[256:512], head[512:768]
    joined_a = silu(zu1_scr[...]).astype(bf16)
    for g in range(4):
        p, q = g // 2, g % 2
        part = mm(silu(zu2_scr[g]).astype(bf16), head_b)
        for a in range(8):
            two_scr[pl.ds((2 * a + p) * HX + q, 16, stride=2), :] = part[16 * a : 16 * a + 16]
    for g in range(16):
        p, q = g // 4, g % 4
        part = mm(silu(zu3_scr[g]).astype(bf16), head_c)
        for a in range(4):
            three_scr[pl.ds((4 * a + p) * HX + q, 8, stride=4), :] = part[8 * a : 8 * a + 8]
    maps = mm(joined_a, head_a) + two_scr[...] + three_scr[...]
    maps = jnp.transpose(maps)[0:16]
    own = jnp.zeros((16, 128), f32)
    for s in range(SLABS):
        own = own + jnp.where(slab == s, maps[:, 128 * s : 128 * s + 128], 0.0)
    maps_ref[...] = own

    live_count = counts_ref[0]
    anchors = anchors_ref[...]
    slot = row_of((40, CELLS))
    place = lane_of((40, CELLS))
    positive = [
        jnp.sum(
            jnp.logical_and(anchors == place + k * CELLS, slot < live_count).astype(f32),
            axis=0,
            keepdims=True,
        )
        for k in range(2)
    ]
    row = row_of((16, CELLS))
    second = jnp.logical_or(row == 1, row >= 9)
    marked = jnp.where(second, positive[1], positive[0])
    share = 1.0 / jnp.maximum(live_count.astype(f32), 1.0)
    class_grad = (sigmoid(maps) - marked) * (1.0 / (2.0 * CELLS))
    box_grad = jnp.clip(maps - goals_ref[...], -1.0, 1.0) * marked * share
    dmaps = jnp.where(row < 2, class_grad, box_grad)
    dmaps = jnp.transpose(jnp.concatenate([dmaps, jnp.zeros((LANES - 16, CELLS), f32)], 0))
    maps_scr[...] = dmaps
    low = dmaps.astype(bf16)

    dhead_a = mm_tn(joined_a, low)
    dz = mm_nt(low, head_a) * silu_slope(zu1_scr[...])
    dz = dz.astype(bf16)
    keep_wide(t_up1, mm_tn(taps_up, dz))
    dlevel_one = full_taps_back(mm_nt(dz, wide(t_up1, 1152)), 32)

    dhead_b = jnp.zeros((256, LANES), f32)
    dlevel_two = jnp.zeros((128, 128), f32)
    for g in range(4):
        p, q = g // 2, g % 2
        part = jnp.concatenate(
            [maps_scr[pl.ds((2 * a + p) * HX + q, 16, stride=2), :] for a in range(8)], 0
        ).astype(bf16)
        z = zu2_scr[g]
        dhead_b = dhead_b + mm_tn(silu(z).astype(bf16), part)
        dz = (mm_nt(part, head_b) * silu_slope(z)).astype(bf16)
        keep_wide(t_up2 + 16 * g, mm_tn(level_two, dz))
        dlevel_two = dlevel_two + mm_nt(dz, wide(t_up2 + 16 * g, 128))
    dhead_c = jnp.zeros((256, LANES), f32)
    dlevel_three = jnp.zeros((32, 256), f32)
    for g in range(16):
        p, q = g // 4, g % 4
        part = jnp.concatenate(
            [maps_scr[pl.ds((4 * a + p) * HX + q, 8, stride=4), :] for a in range(4)], 0
        ).astype(bf16)
        z = zu3_scr[g]
        dhead_c = dhead_c + mm_tn(silu(z).astype(bf16), part)
        dz = (mm_nt(part, head_c) * silu_slope(z)).astype(bf16)
        keep_wide(t_up3 + 32 * g, mm_tn(level_three, dz))
        dlevel_three = dlevel_three + mm_nt(dz, wide(t_up3 + 32 * g, 256))

    head_scr[...] = jnp.concatenate([dhead_a, dhead_b, dhead_c], 0)
    rows = jnp.zeros((96, LANES), f32)
    for c in range(8):
        piece = jnp.where(lane < 16, head_scr[pl.ds(c, 96, stride=8), :], 0.0)
        rows = rows + lane_roll(piece, 16 * c)
    keep_narrow(t_head, rows)

    dz = (dlevel_three * silu_slope(z3)).astype(bf16)
    keep_wide(t_three, mm_tn(taps_three, dz))
    merge_planes(l2_scr, stride_taps_back(mm_nt(dz, wide(t_three, 1152)), 8), 8, 16)
    dlevel_two = dlevel_two + l2_scr[...]
    dz = (dlevel_two * silu_slope(z2)).astype(bf16)
    keep_narrow(t_two, mm_tn(taps_two, dz))
    merge_planes(l1_scr, stride_taps_back(mm_nt(dz, narrow(t_two, 1152)), 16), 16, 32)
    dlevel_one = dlevel_one + l1_scr[...]
    l1_scr[...] = dlevel_one
    grad_ref[...] = l1_scr[pl.ds(pl.multiple_of(slab * L1_R, L1_R), L1_R), :]
    for s in range(SLABS):

        @pl.when(slab == s)
        def _(s=s):
            start = (15 - 4 * s) * LANES + 16 + 28 * s
            for t in (0, 1) + tuple(range(SHARD_T - 4, PAD_T)):
                tile = STRIDE_T * s - 1 + t
                row = row_of((TILE, LANES))
                if t >= SHARD_T:
                    gr[STRIDE_T * s + t] = jnp.zeros((TILE, LANES), bf16)
                    continue
                if WIDE_T[0] <= tile < WIDE_T[1]:
                    row = 32 * (t // 2) + 2 * row + t % 2
                else:
                    row = TILE * t + row
                at = row * LANES + lane_of((TILE, LANES)) - start
                inside = jnp.logical_and(at >= 0, at < SHARD)
                gr[STRIDE_T * s + t] = jnp.where(
                    inside, gr[STRIDE_T * s + t].astype(f32), 0.0
                ).astype(bf16)

    split_chunks(slab_ref, gr, STRIDE_T * slab, own_ref, core_ref)


LATE_ORDER = (
    ((0, 0, 2, 2), (0, 1, 0, 1)),
    ((1, 1, 3, 3), (0, 1, 0, 1)),
    ((0, 0, 1, 1), (2, 3, 2, 3)),
    ((2, 2, 3, 3), (2, 3, 2, 3)),
)


def region(info, counts, levels, anchors, goals, late):
    return call(
        region_kernel,
        12,
        (shape((16, 128)), shape((L1_R, LANES)), shape(CHUNKS, bf16), shape(CHUNKS, bf16)),
        [smem(), smem()] + [vmem()] * 6 + [anywhere()] * 8,
        (vmem(),) * 4,
        [
            pltpu.VMEM((SLABS, PAD_T, TILE, LANES), bf16),
            pltpu.VMEM((GRAD_T, TILE, LANES), bf16),
            pltpu.SemaphoreType.DMA((32,)),
            pltpu.VMEM((512, 128), f32),
            pltpu.VMEM((128, 128), f32),
            pltpu.VMEM((512, 256), f32),
            pltpu.VMEM((4, 128, 256), f32),
            pltpu.VMEM((16, 32, 256), f32),
            pltpu.VMEM((768, LANES), f32),
            pltpu.VMEM((512, LANES), f32),
            pltpu.VMEM((512, LANES), f32),
            pltpu.VMEM((512, LANES), f32),
        ],
    )(info, counts, *levels, anchors, goals, *late)


def swap(x, axis, bit):
    count = lax.axis_size(axis)
    return lax.ppermute(x, axis, [(i, i ^ bit) for i in range(count)])


def slab_all(x):
    return [x] + [swap(x, "slab", k) for k in range(1, SLABS)]


def plane_all(x):
    return [x] + [swap(x, "batch", 2 * k) for k in range(1, 4)]


def share_chunk(x):
    own = jnp.stack(plane_all(x))
    return own, swap(own, "batch", 1)


def share_late(pieces):
    first, second = jnp.stack(pieces[0:2]), jnp.stack(pieces[2:4])
    first = jnp.concatenate([first, swap(first, "batch", 4)], 0)
    second = jnp.concatenate([second, swap(second, "batch", 2)], 0)
    parts = [first, swap(first, "batch", 2), second, swap(second, "batch", 4)]
    return parts + [swap(x, "batch", 1) for x in parts]


def sum_chunks(own, core):
    other = swap(core, "batch", 1)
    parts = [(own[k].astype(f32) + other[k].astype(f32)).astype(bf16) for k in range(4)]
    total = parts[0].astype(f32)
    for k in range(1, 4):
        total = total + swap(parts[k], "batch", 2 * k).astype(f32)
    return total


def to_first(x):
    total = x
    for k in range(1, SLABS):
        total = total + lax.ppermute(x.astype(bf16), "slab", [(k, 0)]).astype(f32)
    return total


def even_odd(whole):
    both = whole.reshape(4, 2, CHUNK_T, TILE, LANES)
    return both[:, 0], both[:, 1]


def gathered_shards(own):
    batches = lax.axis_size("batch")
    share = PAD_T // batches
    chunk = lax.dynamic_slice_in_dim(own, lax.axis_index("batch") * share, share, 0)
    shards = lax.all_gather(chunk, ("slab", "batch"), axis=0, tiled=True)
    shards = shards.reshape(SLABS, 4, 2, CHUNK_T, TILE, LANES)
    late = []
    for core in range(2):
        for chips, slots in LATE_ORDER:
            late.append(jnp.stack([shards[s, c, core] for c, s in zip(chips, slots)]))
    return (shards[0, :, 0], shards[0, :, 1]), late


def body(
    points, point_counts, voxel_cells, pos_anchors, pos_counts, reg_targets, params, moment1, moment2
):
    batches = lax.axis_size("batch")
    slab, batch = lax.axis_index("slab"), lax.axis_index("batch")
    direct = batches == 8
    zero = jnp.zeros_like(slab)
    info = jnp.stack([slab, batch if direct else zero, slab if direct else zero]).astype(jnp.int32)
    counts = point_counts.reshape(1, VOX)

    small = spread_first(params[0 : VFE_R * LANES].reshape(VFE_R, LANES))
    arrived = [lax.ppermute(small, "slab", [(0, k)]) for k in range(1, SLABS)]
    small = jnp.where(slab == 0, small, arrived[0] + arrived[1] + arrived[2])
    flat_rows = jnp.pad(params, (0, FLAT_R * LANES - SHARD)).reshape(FLAT_R, LANES)
    own = spread_shard(info, flat_rows)
    if direct:
        chunk = lax.dynamic_slice_in_dim(own, batch * CHUNK_T, CHUNK_T, 0)
        pieces = slab_all(chunk)
        early = share_chunk(
            jnp.where(
                slab < 2,
                jnp.where(slab == 0, pieces[0], pieces[1]),
                jnp.where(slab == 2, pieces[2], pieces[3]),
            )
        )
        late = share_late(pieces)
    else:
        early, late = gathered_shards(own)

    features = slab_all(encode(points, counts, voxel_cells.reshape(1, VOX), small))
    slopes = encode_slopes(points, counts, small)
    level, *kept = volume(info, features, early)
    goals = jnp.pad(reg_targets.reshape(14, CELLS), ((2, 0), (0, 0)))
    maps, level_grad, *quarter = region(
        info, pos_counts, slab_all(level), pos_anchors.reshape(40, 1), goals, late
    )
    *feature_grad, own_early, core_early = volume_back(info, features, level_grad, kept)
    feature_grad = feature_grad[0:1] + [swap(feature_grad[k], "slab", k) for k in range(1, SLABS)]
    if direct:
        chunk = sum_chunks(*quarter)
        early_chunk = to_first(sum_chunks(own_early, core_early))
        chunk = (chunk + jnp.where(slab == 0, early_chunk, 0.0)).astype(bf16)
        squares = jnp.sum(jnp.square(chunk.astype(f32)))
        final = share_chunk(chunk)
    else:
        whole = jnp.stack(quarter, 1).astype(f32)
        whole_early = lax.psum(jnp.stack([own_early, core_early], 1).astype(f32), "slab")
        whole = lax.psum(whole + jnp.where(slab == 0, whole_early, 0.0), "batch").astype(bf16)
        squares = jnp.sum(jnp.square(whole.astype(f32))) / batches
        final = even_odd(whole)

    points_grad, vfe_grad = encode_back(counts, small, feature_grad, slopes)
    total = jnp.concatenate([vfe_grad, jnp.broadcast_to(squares, (8, LANES))], 0)
    for axis, size in (("batch", batches), ("slab", SLABS)):
        bit = 1
        while bit < size:
            total = total + swap(total, axis, bit)
            bit *= 2
    vfe_grad = total[0:VFE_R]
    grad_norm = jnp.sqrt(total[VFE_R, 0] + jnp.sum(vfe_grad * vfe_grad))
    grads = gather_shard(info, *final, vfe_grad)
    own_grads = grads.reshape(-1)[0:SHARD]
    clipped = own_grads * (clip_level / jnp.maximum(grad_norm, clip_level))
    new_moment1 = beta_one * moment1 + (1.0 - beta_one) * clipped
    new_moment2 = beta_two * moment2 + (1.0 - beta_two) * clipped * clipped
    direction = (
        new_moment1
        / (1.0 - beta_one**STEP)
        / (jnp.sqrt(new_moment2 / (1.0 - beta_two**STEP)) + adam_eps)
    )
    new_params = params - learn_rate * (direction + weight_decay * params)
    head_maps = maps.reshape(1, 16, HY // SLABS, HX)
    return (head_maps, points_grad, new_moment1, new_moment2, new_params, grad_norm)


def solution(mesh):
    in_specs = (
        P(None, None, ("batch", "slab")),
        P(("batch", "slab")),
        P(("batch", "slab")),
        P("batch", None),
        P("batch"),
        P("batch", None, None, None),
        P("slab"),
        P("slab"),
        P("slab"),
    )
    out_specs = (
        P("batch", None, "slab", None),
        P(None, None, ("batch", "slab")),
        P("slab"),
        P("slab"),
        P("slab"),
        P(),
    )
    return jax.shard_map(body, mesh=mesh, in_specs=in_specs, out_specs=out_specs, check_vma=False)
```

```python
import functools
import math

import jax
import jax.numpy as jnp
from jax import lax
from jax.experimental import pallas as pl
from jax.experimental.pallas import tpu as pltpu
from jax.sharding import PartitionSpec as P

VF1 = 16
VF2 = 64
FC = 128
C3 = 64
STEP = 10
GY = 32
GX = 64
PTS = 35
VOX = 512
SLABS = 4
ROWS = GY // SLABS
LANES = 128
NPARAM = 2537584
SHARD = NPARAM // SLABS

TILE = 16
STRIDE_T = 310
SHARD_T = 312
PAD_T = 320
FLAT_R = 4960
EARLY_T = 288
EARLY_R = EARLY_T * TILE
VFE_T = 10
VFE_R = VFE_T * TILE
PLANE_T0 = 297
PLANE_T = 942
GRAD_T = 3 * STRIDE_T + PAD_T
CHUNK_T = PAD_T // 8
WIDE_T = (369, 1233)

beta_one = 0.9
beta_two = 0.999
adam_eps = 1e-08
learn_rate = 0.02
weight_decay = 0.01
clip_level = 0.002

f32 = jnp.float32
bf16 = jnp.bfloat16
VMEM_LIMIT = 56 * 1024 * 1024


def call(kernel, micros, out_shape, in_specs, out_specs, scratch=()):
    return pl.pallas_call(
        kernel,
        out_shape=out_shape,
        in_specs=in_specs,
        out_specs=out_specs,
        scratch_shapes=list(scratch),
        compiler_params=pltpu.CompilerParams(vmem_limit_bytes=VMEM_LIMIT),
        cost_estimate=pl.CostEstimate(
            flops=int(micros * 1e9), transcendentals=0, bytes_accessed=int(micros * 3e6)
        ),
    )


def vmem():
    return pl.BlockSpec(memory_space=pltpu.VMEM)


def smem():
    return pl.BlockSpec(memory_space=pltpu.SMEM)


def anywhere():
    return pl.BlockSpec(memory_space=pl.ANY)


def shape(dims, dtype=f32):
    return jax.ShapeDtypeStruct(dims, dtype)


def mm(a, b):
    return lax.dot_general(a, b, (((1,), (0,)), ((), ())), preferred_element_type=f32)


def mm_nt(a, b):
    return lax.dot_general(a, b, (((1,), (1,)), ((), ())), preferred_element_type=f32)


def mm_tn(a, b):
    return lax.dot_general(a, b, (((0,), (0,)), ((), ())), preferred_element_type=f32)


def sigmoid(z):
    return 0.5 * jnp.tanh(0.5 * z) + 0.5


def silu(z):
    return z * sigmoid(z)


def silu_slope(z):
    s = sigmoid(z)
    return s * (1.0 + z * (1.0 - s))


def lane_of(dims):
    return lax.broadcasted_iota(jnp.int32, dims, len(dims) - 1)


def row_of(dims):
    return lax.broadcasted_iota(jnp.int32, dims, 0)


def lane_roll(x, shift):
    shift = shift % x.shape[-1]
    return x if shift == 0 else pltpu.roll(x, shift, x.ndim - 1)


def shift_in(v, d, width):
    if d == 0:
        return v
    place = row_of(v.shape) % width
    keep = place > 0 if d > 0 else place < width - 1
    return jnp.where(keep, pltpu.roll(v, d % v.shape[0], 0), 0.0)


def shift_out(v, d, width):
    if d == 0:
        return v
    edge = jnp.zeros((width,) + v.shape[1:], v.dtype)
    if d > 0:
        return jnp.concatenate([edge, v[:-width]], 0)
    return jnp.concatenate([v[width:], edge], 0)


def batch_place(info_ref):
    return info_ref[1] // 2, info_ref[1] % 2


def chunk_start(chip, core, slot):
    return CHUNK_T * (2 * jnp.bitwise_xor(chip, slot) + core)


def join_chunks(info_ref, out_ref, own_ref, core_ref):
    chip, core = batch_place(info_ref)
    for slot in range(4):
        out_ref[pl.ds(chunk_start(chip, core, slot), CHUNK_T)] = own_ref[slot]
        out_ref[pl.ds(chunk_start(chip, 1 - core, slot), CHUNK_T)] = core_ref[slot]


def split_chunks(info_ref, scr, base, own_ref, core_ref):
    chip, core = batch_place(info_ref)
    for slot in range(4):
        own_ref[slot] = scr[pl.ds(base + chunk_start(chip, core, slot), CHUNK_T)].astype(bf16)
        core_ref[slot] = scr[pl.ds(base + chunk_start(chip, 1 - core, slot), CHUNK_T)].astype(bf16)


CHUNKS = (4, CHUNK_T, TILE, LANES)


def spread_kernel(slab_ref, flat_ref, out_ref, nat):
    nat[...] = jnp.zeros_like(nat)
    span = 480
    for s in range(SLABS):

        @pl.when(slab_ref[0] == s)
        def _(s=s):
            lanes, first = 16 + 28 * s, 15 - 4 * s
            lane = lane_of((span, LANES))
            count = FLAT_R // span + (FLAT_R % span > 0)
            for i in range(count):
                r0 = i * span
                n = min(span, FLAT_R - r0)
                rolled = lane_roll(flat_ref[r0 : r0 + n, :], lanes)
                nat[first + r0 : first + r0 + n, :] += jnp.where(lane[:n] >= lanes, rolled, 0.0)
                nat[first + r0 + 1 : first + r0 + 1 + n, :] += jnp.where(
                    lane[:n] < lanes, rolled, 0.0
                )
            low = max(0, min(SHARD_T // 2, (WIDE_T[0] - STRIDE_T * s + 1) // 2))
            high = max(low, min(SHARD_T // 2, (WIDE_T[1] - STRIDE_T * s + 1) // 2))
            for a, b, wide in ((0, low, False), (low, high, True), (high, SHARD_T // 2, False)):

                def block(i, carry, wide=wide):
                    base = pl.multiple_of(32 * i, 32)
                    if wide:
                        even = nat[pl.ds(base, 16, stride=2), :]
                        odd = nat[pl.ds(base + 1, 16, stride=2), :]
                    else:
                        even = nat[pl.ds(base, 16), :]
                        odd = nat[pl.ds(base + 16, 16), :]
                    out_ref[2 * i] = even.astype(bf16)
                    out_ref[2 * i + 1] = odd.astype(bf16)
                    return carry

                if b > a:
                    lax.fori_loop(a, b, block, 0, unroll=4)

    for t in range(SHARD_T, PAD_T):
        out_ref[t] = jnp.zeros((TILE, LANES), bf16)


def spread_shard(slab, flat_rows):
    return call(
        spread_kernel,
        4,
        shape((PAD_T, TILE, LANES), bf16),
        [smem(), vmem()],
        vmem(),
        [pltpu.VMEM((5120, LANES), f32)],
    )(slab, flat_rows)


CHUNK_R = CHUNK_T * TILE
CHUNK_N = CHUNK_R * LANES
WHOLE_R = SHARD // LANES // 8 * 8
REST = SHARD - SHARD // LANES * LANES


def flat_tail(flat_ref):
    rest_r = SHARD // LANES - WHOLE_R
    rows = flat_ref[pl.ds(WHOLE_R * LANES, rest_r * LANES)].reshape(rest_r, LANES)
    return rows, flat_ref[pl.ds(SHARD - REST, REST)].reshape(1, REST)


def spread_own_kernel(info_ref, flat_ref, chunk_ref, first_ref, x_scr, nat):
    batch = info_ref[1]

    @pl.when(batch == 0)
    def _():
        x_scr[0:TILE, :] = jnp.zeros((TILE, LANES), f32)
        x_scr[TILE:, :] = flat_ref[pl.ds(0, CHUNK_N)].reshape(CHUNK_R, LANES)

    @pl.when(jnp.logical_and(batch > 0, batch < 7))
    def _():
        start = pl.multiple_of(batch * CHUNK_N - TILE * LANES, 1024)
        rows = CHUNK_R + TILE
        x_scr[...] = flat_ref[pl.ds(start, rows * LANES)].reshape(rows, LANES)

    @pl.when(batch == 7)
    def _():
        first_r = 7 * CHUNK_R - TILE
        whole = WHOLE_R - first_r
        x_scr[0:whole, :] = flat_ref[pl.ds(first_r * LANES, whole * LANES)].reshape(whole, LANES)
        x_scr[whole:, :] = jnp.zeros((CHUNK_R + TILE - whole, LANES), f32)
        rows, last = flat_tail(flat_ref)
        x_scr[whole : whole + rows.shape[0], :] = rows
        x_scr[whole + rows.shape[0] : whole + rows.shape[0] + 1, 0:REST] = last

    def shifted(first, lanes, rows):
        lane = lane_of((rows, LANES))
        here = lane_roll(x_scr[TILE - first : TILE - first + rows, :], lanes)
        above = lane_roll(x_scr[TILE - 1 - first : TILE - 1 - first + rows, :], lanes)
        return jnp.where(lane >= lanes, here, above)

    for s in range(SLABS):

        @pl.when(info_ref[0] == s)
        def _(s=s):
            nat[...] = shifted(15 - 4 * s, 16 + 28 * s, CHUNK_R)
            low = max(0, min(SHARD_T // 2, (WIDE_T[0] - STRIDE_T * s + 1) // 2))
            high = max(low, min(SHARD_T // 2, (WIDE_T[1] - STRIDE_T * s + 1) // 2))
            for i in range(CHUNK_T // 2):
                block = batch * (CHUNK_T // 2) + i
                wide = jnp.logical_and(block >= low, block < high)
                even = nat[pl.ds(32 * i, 16, stride=2), :]
                odd = nat[pl.ds(32 * i + 1, 16, stride=2), :]
                top, bottom = nat[32 * i : 32 * i + 16, :], nat[32 * i + 16 : 32 * i + 32, :]
                chunk_ref[2 * i] = jnp.where(wide, even, top).astype(bf16)
                chunk_ref[2 * i + 1] = jnp.where(wide, odd, bottom).astype(bf16)

    first_ref[VFE_T : VFE_T + CHUNK_T] = chunk_ref[...]
    x_scr[0:TILE, :] = jnp.zeros((TILE, LANES), f32)
    x_scr[TILE : TILE + VFE_R, :] = flat_ref[pl.ds(0, VFE_R * LANES)].reshape(VFE_R, LANES)
    rows = shifted(15, 16, VFE_R).astype(bf16)
    first_ref[0:VFE_T] = rows.reshape(VFE_T, TILE, LANES)


def spread_own(info, params):
    return call(
        spread_own_kernel,
        3,
        (shape((CHUNK_T, TILE, LANES), bf16), shape((VFE_T + CHUNK_T, TILE, LANES), bf16)),
        [smem(), vmem()],
        (vmem(), vmem()),
        [pltpu.VMEM((CHUNK_R + TILE, LANES), f32), pltpu.VMEM((CHUNK_R, LANES), f32)],
    )(info, params)


def spread_first_kernel(flat_ref, out_ref, nat):
    lanes, first = 16, 15
    lane = lane_of((VFE_R, LANES))
    rolled = lane_roll(flat_ref[...], lanes)
    nat[...] = jnp.zeros_like(nat)
    nat[first : first + VFE_R, :] += jnp.where(lane >= lanes, rolled, 0.0)
    nat[first + 1 : first + 1 + VFE_R, :] += jnp.where(lane < lanes, rolled, 0.0)
    out_ref[...] = nat[0:VFE_R, :].astype(bf16).reshape(VFE_T, TILE, LANES)


def spread_first(flat_rows):
    return call(
        spread_first_kernel,
        1,
        shape((VFE_T, TILE, LANES), bf16),
        [vmem()],
        vmem(),
        [pltpu.VMEM((VFE_R + 32, LANES), f32)],
    )(flat_rows)


def update_kernel(
    slab_ref, own_ref, core_ref, vfe_ref, params_ref, moment1_ref, moment2_ref,
    new_params_ref, new_moment1_ref, new_moment2_ref, norm_ref,
    quarter_ref, nat, grads,
):
    join_chunks(slab_ref, quarter_ref, own_ref, core_ref)
    vfe = vfe_ref[0:VFE_R, :]
    squares = vfe_ref[VFE_R : VFE_R + 1, :][0, 0] + jnp.sum(vfe * vfe)
    norm = jnp.sqrt(jnp.broadcast_to(squares, (8, LANES)))
    norm_ref[...] = norm
    scale = (clip_level / jnp.maximum(norm, clip_level))[0:1, :]
    span = 480
    for s in range(SLABS):

        @pl.when(slab_ref[0] == s)
        def _(s=s):
            lanes, first = 16 + 28 * s, 15 - 4 * s
            low = max(0, min(SHARD_T // 2, (WIDE_T[0] - STRIDE_T * s + 1) // 2))
            high = max(low, min(SHARD_T // 2, (WIDE_T[1] - STRIDE_T * s + 1) // 2))
            for a, b, wide in ((0, low, False), (low, high, True), (high, SHARD_T // 2, False)):

                def block(i, carry, wide=wide):
                    base = pl.multiple_of(32 * i, 32)
                    even, odd = quarter_ref[2 * i].astype(f32), quarter_ref[2 * i + 1].astype(f32)
                    if wide:
                        nat[pl.ds(base, 16, stride=2), :] = even
                        nat[pl.ds(base + 1, 16, stride=2), :] = odd
                    else:
                        nat[pl.ds(base, 16), :] = even
                        nat[pl.ds(base + 16, 16), :] = odd
                    return carry

                if b > a:
                    lax.fori_loop(a, b, block, 0, unroll=4)
            if s == 0:
                nat[0:VFE_R, :] = vfe
            lane = lane_of((span, LANES))
            count = FLAT_R // span + (FLAT_R % span > 0)
            for i in range(count):
                r0 = i * span
                n = min(span, FLAT_R - r0)
                here = lane_roll(nat[first + r0 : first + r0 + n, :], -lanes)
                after = lane_roll(nat[first + r0 + 1 : first + r0 + 1 + n, :], -lanes)
                grads[r0 : r0 + n, :] = jnp.where(lane[:n] < LANES - lanes, here, after) * scale

    def update(start, count, clipped):
        at = pl.ds(start, count)
        param = params_ref[at]
        moment1 = beta_one * moment1_ref[at] + (1.0 - beta_one) * clipped
        moment2 = beta_two * moment2_ref[at] + (1.0 - beta_two) * clipped * clipped
        direction = (
            moment1
            / (1.0 - beta_one**STEP)
            / (jnp.sqrt(moment2 / (1.0 - beta_two**STEP)) + adam_eps)
        )
        new_moment1_ref[at] = moment1
        new_moment2_ref[at] = moment2
        new_params_ref[at] = param - learn_rate * (direction + weight_decay * param)

    span = 512
    for r0 in range(0, WHOLE_R, span):
        n = min(span, WHOLE_R - r0)
        update(r0 * LANES, n * LANES, grads[r0 : r0 + n, :].reshape(n * LANES))
    rest_r = SHARD // LANES - WHOLE_R
    update(WHOLE_R * LANES, rest_r * LANES, grads[WHOLE_R : WHOLE_R + rest_r, :].reshape(rest_r * LANES))
    last = WHOLE_R + rest_r
    update(SHARD - REST, REST, grads[last : last + 1, 0:REST].reshape(REST))


def update_shard(info, own, core, vfe, params, moment1, moment2):
    return call(
        update_kernel,
        7,
        (shape((SHARD,)),) * 3 + (shape((8, LANES)),),
        [smem()] + [vmem()] * 6,
        (vmem(),) * 4,
        [
            pltpu.VMEM((PAD_T, TILE, LANES), bf16),
            pltpu.VMEM((5120, LANES), f32),
            pltpu.VMEM((FLAT_R, LANES), f32),
        ],
    )(info, own, core, vfe, params, moment1, moment2)


PART = 5
PARTS = PTS // PART
WIDE = PART * VOX
VFE_SCRATCH = [
    pltpu.VMEM((VOX // LANES, PTS * 16, LANES), f32),
    pltpu.VMEM((16, LANES), f32),
    pltpu.VMEM((64, LANES), f32),
]


def spread_points(points_ref, x_scr):
    x_scr[...] = jnp.zeros_like(x_scr)
    for c in range(7):
        plane = points_ref[c].astype(f32)
        for b in range(VOX // LANES):
            x_scr[b, pl.ds(c, PTS, stride=16), :] = plane[:, b * LANES : (b + 1) * LANES]


def vfe_weights(rows_ref, w1_scr, w2_scr):
    line = rows_ref[0].astype(f32)
    lane = lane_of((16, LANES))
    for o in range(VF1):
        w1_scr[o : o + 1, :] = jnp.where(lane < 7, lane_roll(line, -(16 + 7 * o)), 0.0)[15:16]
    two = rows_ref[1].astype(f32)
    for k in range(4):
        w2_scr[pl.ds(k, 16, stride=4), :] = jnp.where(lane < 32, lane_roll(two, -32 * k), 0.0)
    w1 = w1_scr[...].astype(bf16)[:, 0:16]
    w2 = w2_scr[...]
    w2a = w2.astype(bf16)[:, 0:16]
    w2b = lane_roll(w2, -16).astype(bf16)[:, 0:16]
    w3 = rows_ref[2:10].reshape(FC, LANES)
    w3a = w3[:, 0:64]
    w3b = lane_roll(w3.astype(f32), -64).astype(bf16)[:, 0:64]
    return w1, w2a, w2b, w3a, w3b


def points_part(ref, i):
    return jnp.concatenate(
        [
            ref[b, pl.ds(pl.multiple_of((PART * i + k) * 16, 16), 16), :]
            for k in range(PART)
            for b in range(VOX // LANES)
        ],
        1,
    )


def set_points_part(ref, i, value):
    for k in range(PART):
        for b in range(VOX // LANES):
            at = k * VOX + b * LANES
            ref[b, pl.ds(pl.multiple_of((PART * i + k) * 16, 16), 16), :] = value[:, at : at + LANES]


def part_sum(value):
    total = value[:, 0:VOX]
    for k in range(1, PART):
        total = total + value[:, k * VOX : (k + 1) * VOX]
    return total


def valid_part(i, counts):
    return jnp.concatenate([(PART * i + k < counts).astype(f32) for k in range(PART)], 1)


def widen(value):
    return jnp.concatenate([value] * PART, 1)


def vfe_front(weights, counts, inverse, x_scr, j1_ref, j2_ref, kept=None):
    w1, w2a, w2b, w3a, w3b = weights

    def layer_one(i, total):
        x = points_part(x_scr, i).astype(bf16)
        z = mm(w1, x)
        value = silu(z)
        j1_ref[i] = value.astype(bf16)
        if kept is not None:
            x_ref, s1_ref, s2_ref = kept
            x_ref[i] = x
            s1_ref[i] = silu_slope(z)
        return total + part_sum(value * valid_part(i, counts))

    total = lax.fori_loop(0, PARTS, layer_one, jnp.zeros((VF1, VOX), f32), unroll=PARTS)
    mean_one = (total * inverse).astype(bf16)
    shared_two = widen(mm(w2b, mean_one))

    def layer_two(i, total):
        z = mm(w2a, j1_ref[i]) + shared_two
        value = silu(z)
        j2_ref[i] = value.astype(bf16)
        if kept is not None:
            kept[2][i] = silu_slope(z)
        return total + part_sum(value * valid_part(i, counts))

    total = lax.fori_loop(0, PARTS, layer_two, jnp.zeros((VF2, VOX), f32), unroll=PARTS)
    mean_two = (total * inverse).astype(bf16)
    shared_three = widen(mm(w3b, mean_two))
    return mean_one, mean_two, shared_three


def encode_kernel(
    points_ref, counts_ref, cells_ref, rows_ref, out_ref, s3_ref, x_scr, w1_scr, w2_scr, j1_scr, j2_scr
):
    spread_points(points_ref, x_scr)
    weights = vfe_weights(rows_ref, w1_scr, w2_scr)
    counts = counts_ref[...]
    inverse = 1.0 / counts.astype(f32)
    _, _, shared_three = vfe_front(weights, counts, inverse, x_scr, j1_scr, j2_scr)
    w3a = weights[3]

    wide_inverse = widen(inverse)

    def layer_three(i, total):
        z = mm(w3a, j2_scr[i]) + shared_three
        gate = sigmoid(z)
        value = z * gate
        share = valid_part(i, counts) * wide_inverse
        s3_ref[i] = ((gate + value - value * gate) * share).astype(bf16)
        return total + part_sum(value * share)

    total = lax.fori_loop(0, PARTS, layer_three, jnp.zeros((FC, VOX), f32), unroll=PARTS)
    features = total.astype(bf16)
    cells = cells_ref[...]
    row = row_of((16, VOX))
    places = jnp.where(row == 0, cells // GX, cells % GX).astype(f32).astype(bf16)
    for t in range(SLABS):
        out_ref[t, 0:FC, :] = features
        out_ref[t, FC : FC + 16, :] = places


def encode(points, counts, cells, rows):
    return call(
        encode_kernel,
        10,
        (shape((SLABS, FC + 16, VOX), bf16), shape((PARTS, 128, WIDE), bf16)),
        [vmem()] * 4,
        (vmem(), vmem()),
        VFE_SCRATCH
        + [pltpu.VMEM((PARTS, 16, WIDE), bf16), pltpu.VMEM((PARTS, 64, WIDE), bf16)],
    )(points, counts, cells, rows)


def encode_slopes_kernel(
    points_ref, counts_ref, rows_ref,
    x_ref, j1_ref, j2_ref, s1_ref, s2_ref, m1_ref, m2_ref,
    x_scr, w1_scr, w2_scr,
):
    spread_points(points_ref, x_scr)
    weights = vfe_weights(rows_ref, w1_scr, w2_scr)
    counts = counts_ref[...]
    inverse = 1.0 / counts.astype(f32)
    mean_one, mean_two, _ = vfe_front(
        weights, counts, inverse, x_scr, j1_ref, j2_ref, (x_ref, s1_ref, s2_ref)
    )
    m1_ref[...] = mean_one
    m2_ref[...] = mean_two


def encode_slopes(points, counts, rows):
    return call(
        encode_slopes_kernel,
        7,
        (
            shape((PARTS, 16, WIDE), bf16),
            shape((PARTS, 16, WIDE), bf16),
            shape((PARTS, 64, WIDE), bf16),
            shape((PARTS, 16, WIDE)),
            shape((PARTS, 64, WIDE)),
            shape((VF1, VOX), bf16),
            shape((VF2, VOX), bf16),
        ),
        [vmem()] * 3,
        (vmem(),) * 7,
        VFE_SCRATCH,
    )(points, counts, rows)


def encode_back_kernel(
    counts_ref, rows_ref, grad_ref, j2_ref, s3_ref, m2_ref,
    d2_ref, shared_ref, weight_ref,
    w1_scr, w2_scr,
):
    _, _, _, w3a, w3b = vfe_weights(rows_ref, w1_scr, w2_scr)
    inverse = 1.0 / counts_ref[...].astype(f32)
    grad = grad_ref[0].astype(f32)
    for t in range(1, SLABS):
        grad = grad + grad_ref[t].astype(f32)
    grad_three = widen(grad)

    def back_three(i, carry):
        total, weight = carry
        dz = grad_three * s3_ref[i].astype(f32)
        low = dz.astype(bf16)
        d2_ref[i] = mm_tn(w3a, low).astype(bf16)
        return total + part_sum(dz), weight + mm_nt(low, j2_ref[i])

    total, grad_w3a = lax.fori_loop(
        0, PARTS, back_three, (jnp.zeros((FC, VOX), f32), jnp.zeros((FC, VF2), f32)), unroll=PARTS
    )
    total = total.astype(bf16)
    weight_ref[...] = jnp.concatenate([grad_w3a, mm_nt(total, m2_ref[...])], 1)
    shared_ref[...] = mm_tn(w3b, total) * inverse


def encode_back(counts, rows, grad, j2, s3, m2):
    return call(
        encode_back_kernel,
        8,
        (shape((PARTS, 64, WIDE), bf16), shape((VF2, VOX)), shape((FC, LANES))),
        [vmem()] * 6,
        (vmem(),) * 3,
        VFE_SCRATCH[1:],
    )(counts, rows, grad, j2, s3, m2)


def points_back_kernel(
    counts_ref, rows_ref, d2_ref, shared_ref, w3_ref, x_ref, j1_ref, s1_ref, s2_ref, m1_ref,
    out_ref, weight_ref,
    x_scr, w1_scr, w2_scr, d1_scr,
):
    w1, w2a, w2b, _, _ = vfe_weights(rows_ref, w1_scr, w2_scr)
    counts = counts_ref[...]
    inverse = 1.0 / counts.astype(f32)
    grad_two = widen(shared_ref[...])

    def back_two(i, carry):
        total, weight = carry
        dz = (d2_ref[i].astype(f32) + valid_part(i, counts) * grad_two) * s2_ref[i]
        low = dz.astype(bf16)
        d1_scr[i] = mm_tn(w2a, low)
        return total + part_sum(dz), weight + mm_nt(low, j1_ref[i])

    total, grad_w2a = lax.fori_loop(
        0, PARTS, back_two, (jnp.zeros((VF2, VOX), f32), jnp.zeros((VF2, VF1), f32)), unroll=PARTS
    )
    total = total.astype(bf16)
    grad_w2b = mm_nt(total, m1_ref[...])
    grad_one = widen(mm_tn(w2b, total) * inverse)

    def back_one(i, weight):
        dz = (d1_scr[i] + valid_part(i, counts) * grad_one) * s1_ref[i]
        low = dz.astype(bf16)
        set_points_part(x_scr, i, mm_tn(w1, low))
        return weight + mm_nt(low, x_ref[i])

    grad_w1 = lax.fori_loop(0, PARTS, back_one, jnp.zeros((VF1, 16), f32), unroll=PARTS)
    for c in range(7):
        for b in range(VOX // LANES):
            out_ref[c, :, b * LANES : (b + 1) * LANES] = x_scr[b, pl.ds(c, PTS, stride=16), :]

    lane = lane_of((16, LANES))
    w1_scr[...] = jnp.concatenate([grad_w1, jnp.zeros((16, LANES - 16), f32)], 1)
    spread = jnp.where(lane < 7, w1_scr[...], 0.0)
    line = jnp.zeros((16, LANES), f32)
    row = row_of((16, LANES))
    for o in range(VF1):
        line = line + jnp.where(row == o, lane_roll(spread, 16 + 7 * o), 0.0)
    line = jnp.sum(line, axis=0, keepdims=True)
    weight_ref[0:16, :] = jnp.where(row == 15, line, 0.0)
    w2_scr[...] = jnp.concatenate([grad_w2a, grad_w2b, jnp.zeros((64, LANES - 32), f32)], 1)
    two = jnp.zeros((16, LANES), f32)
    for k in range(4):
        two = two + lane_roll(w2_scr[pl.ds(k, 16, stride=4), :], 32 * k)
    weight_ref[16:32, :] = two
    weight_ref[32:160, :] = w3_ref[...]
    weight_ref[160:168, :] = jnp.zeros((8, LANES), f32)


def points_back(counts, rows, back, kept):
    return call(
        points_back_kernel,
        7,
        (shape((7, PTS, VOX)), shape((VFE_R + 8, LANES))),
        [vmem()] * 10,
        (vmem(), vmem()),
        VFE_SCRATCH + [pltpu.VMEM((PARTS, 16, WIDE), f32)],
    )(counts, rows, *back, *kept)


R3 = ROWS + 1
R3W = R3 * GX
R2W = (R3 + 2) * GX
R1W = (R3 + 4) * GX
RG = R3 + 6
RGW = RG * GX
HX = GX // 2
L1_R = ROWS // 2 * HX


def cell_marks(places):
    value = places.astype(f32)
    high, low = value[0:1], value[1:2]
    column = lax.broadcasted_iota(jnp.int32, (GX, VOX), 0).astype(f32)
    return (column == low).astype(f32).astype(bf16), high


def layer_marks(column, high, depth, first_row):
    pieces = []
    for w in range(RG):
        row = first_row - 3 + w
        inside = jnp.logical_and(row >= 0, row < GY)
        target = jnp.where(inside, depth * GY + row, -1).astype(f32)
        pieces.append(column * (high == target).astype(f32).astype(bf16))
    return jnp.concatenate(pieces, 0)


def conv_weights(rows_ref, start, taps, half, place, scr):
    lane = lane_of((half, LANES))
    left = lane < 64
    for t in range(taps):
        r = []
        for kx in range(3):
            base = start + (3 * t + kx) * half
            r.append(rows_ref[base // TILE : (base + half) // TILE].reshape(half, LANES).astype(f32))
        turned = [lane_roll(v, 64) for v in r]
        at = place(t)
        scr[0, pl.ds(at, half, stride=2), :] = jnp.where(left, r[1], turned[0])
        scr[0, pl.ds(at + 1, half, stride=2), :] = jnp.where(left, turned[1], r[0])
        scr[1, pl.ds(at, half, stride=2), :] = jnp.where(left, r[2], 0.0)
        scr[1, pl.ds(at + 1, half, stride=2), :] = jnp.where(left, turned[2], 0.0)


def conv_weight_grads(out_ref, start, taps, half, place, scr):
    lane = lane_of((half, LANES))
    left = lane < 64
    for t in range(taps):
        at = place(t)
        even = [scr[b, pl.ds(at, half, stride=2), :] for b in range(2)]
        odd = [scr[b, pl.ds(at + 1, half, stride=2), :] for b in range(2)]
        values = (
            jnp.where(left, lane_roll(even[0], 64), odd[0]),
            jnp.where(left, even[0], lane_roll(odd[0], 64)),
            jnp.where(left, even[1], lane_roll(odd[1], 64)),
        )
        for kx in range(3):
            base = start + (3 * t + kx) * half
            out_ref[base // TILE : (base + half) // TILE] = (
                values[kx].astype(bf16).reshape(half // TILE, TILE, LANES)
            )


def both_halves(out_ref, scr):
    for b in range(2):
        out_ref[:, b * LANES : (b + 1) * LANES] = scr[b].astype(bf16)


def keep_halves(scr, value):
    for b in range(2):
        scr[b] = value[:, b * LANES : (b + 1) * LANES]


def tap_place(t):
    return 128 * t


def pair_place(t):
    kd, ky = t // 3, t % 3
    return 128 * ky + 64 * kd if kd < 2 else 384 + 128 * ky


def join_columns(p):
    first, last = p[:, 0:128], p[:, 128:256]
    left = lane_of(first.shape) < 64
    half = jnp.where(left, first + shift_in(last, -1, GX), shift_in(first, 1, GX))
    return half + lane_roll(half, 64)


def split_columns(d):
    left = lane_of(d.shape) < 64
    first = jnp.where(left, d, lane_roll(shift_in(d, -1, GX), 64))
    last = jnp.where(left, shift_in(d, 1, GX), 0.0)
    return jnp.concatenate([first, last], 1).astype(bf16)


def inside_rows(rows, first_row):
    place = first_row + row_of((rows, LANES)) // GX
    return jnp.logical_and(place >= 0, place < GY)


def grid_taps(grid_ref, k):
    return jnp.concatenate(
        [grid_ref[2 * k + kd, ky * GX : ky * GX + R1W, :] for kd in range(3) for ky in range(3)], 1
    )


def pair_taps(ref, at, rows):
    return jnp.concatenate(
        [ref[at, ky * GX : ky * GX + rows, :] for ky in range(3)]
        + [ref[at + 2, ky * GX : ky * GX + rows, :] for ky in range(3)],
        1,
    )


def level_taps(ref):
    planes = {}
    for xp in range(2):
        for yp in range(2):
            count = ROWS // 2 + 1 - yp
            planes[yp, xp] = jnp.concatenate(
                [ref[pl.ds((2 * a + yp) * GX + xp, HX, stride=2), :] for a in range(count)], 0
            )
    pieces = []
    for ky in range(3):
        for kx in range(3):
            v = planes[ky % 2, int(kx != 1)]
            v = v[HX:] if ky == 2 else v[0:L1_R]
            pieces.append((shift_in(v, 1, HX) if kx == 0 else v).astype(bf16))
    return jnp.concatenate(pieces, 1)


def level_taps_back(ref, grad):
    planes = {}
    edge = jnp.zeros((HX, LANES), f32)
    for ky in range(3):
        for kx in range(3):
            t = 3 * ky + kx
            v = grad[:, t * LANES : (t + 1) * LANES]
            v = shift_in(v, -1, HX) if kx == 0 else v
            if ky != 1:
                v = jnp.concatenate([edge, v] if ky == 2 else [v, edge], 0)
            at = (ky % 2, int(kx != 1))
            planes[at] = planes[at] + v if at in planes else v
    for (yp, xp), v in planes.items():
        for a in range(ROWS // 2 + 1 - yp):
            ref[pl.ds((2 * a + yp) * GX + xp, HX, stride=2), :] = v[a * HX : (a + 1) * HX]


def volume_kernel(
    slab_ref, f_ref, own_ref, core_ref,
    level_ref, grid_ref, first_ref, second_ref, taps_ref, z1_ref, z2_ref, z3_ref, z4_ref, w1_ref, w2_ref, w3_ref, w4_ref,
    rows_ref, w1_scr, w2_scr, bird_scr,
):
    join_chunks(slab_ref, rows_ref, own_ref, core_ref)
    w4_ref[...] = rows_ref[LEVEL_T : LEVEL_T + 72].reshape(1152, LANES)
    w2_scr[...] = jnp.zeros_like(w2_scr)
    conv_weights(rows_ref, VFE_R, 9, 64, tap_place, w1_scr)
    both_halves(w1_ref, w1_scr)
    conv_weights(rows_ref, VFE_R + 1728, 9, 32, pair_place, w2_scr)
    both_halves(w2_ref, w2_scr)
    conv_weights(rows_ref, VFE_R + 2592, 9, 32, pair_place, w2_scr)
    both_halves(w3_ref, w2_scr)

    first_row = slab_ref[0] * ROWS - 1
    grid_ref[0] = jnp.zeros((RGW, FC), bf16)
    for t in range(SLABS):
        features = f_ref[t, 0:FC, :]
        column, high = cell_marks(f_ref[t, FC : FC + 16, :])
        for d in range(2):
            marks = layer_marks(column, high, d, first_row)
            grid_ref[1 + 2 * t + d] = mm_nt(marks, features).astype(bf16)

    first_ref[0] = jnp.zeros((R1W, LANES), bf16)
    first_ref[5] = jnp.zeros((R1W, LANES), bf16)
    keep = inside_rows(R1W, first_row - 2)
    for k in range(4):
        z = join_columns(mm(grid_taps(grid_ref, k), w1_ref[...]))
        z1_ref[k] = z
        value = jnp.where(keep, silu(z), 0.0).astype(bf16)
        first_ref[k + 1, :, 0:64] = value[:, 0:64]
        first_ref[k, :, 64:128] = value[:, 64:128]
    first_ref[4, :, 64:128] = jnp.zeros((R1W, 64), bf16)

    second_ref[0] = jnp.zeros((R2W, LANES), bf16)
    second_ref[5] = jnp.zeros((R2W, LANES), bf16)
    keep = inside_rows(R2W, first_row - 1)
    for k in range(4):
        z = join_columns(mm(pair_taps(first_ref, k, R2W), w2_ref[...]))
        z2_ref[k] = z
        value = jnp.where(keep, silu(z), 0.0).astype(bf16)
        second_ref[k + 1, :, 0:64] = value[:, 0:64]
        second_ref[k, :, 64:128] = value[:, 64:128]
    second_ref[4, :, 64:128] = jnp.zeros((R2W, 64), bf16)

    z3 = []
    for k in range(2):
        z3.append(join_columns(mm(pair_taps(second_ref, 2 * k, R3W), w3_ref[...])))
    z = jnp.where(lane_of((R3W, LANES)) < 64, z3[0], z3[1])
    z3_ref[...] = z
    bird_scr[...] = jnp.where(inside_rows(R3W, first_row), silu(z), 0.0)
    taps = level_taps(bird_scr)
    taps_ref[...] = taps
    z = mm(taps, w4_ref[...])
    z4_ref[...] = z
    level_ref[...] = silu(z).astype(bf16)


LEVEL_T = VFE_T + 216


def volume(info, features, early):
    return call(
        volume_kernel,
        11,
        (
            shape((L1_R, LANES), bf16),
            shape((9, RGW, LANES), bf16),
            shape((6, R1W, LANES), bf16),
            shape((6, R2W, LANES), bf16),
            shape((L1_R, 1152), bf16),
            shape((4, R1W, LANES)),
            shape((4, R2W, LANES)),
            shape((R3W, LANES)),
            shape((L1_R, LANES)),
            shape((1152, 256), bf16),
            shape((768, 256), bf16),
            shape((768, 256), bf16),
            shape((1152, LANES), bf16),
        ),
        [smem()] + [vmem()] * 3,
        (vmem(),) * 13,
        [
            pltpu.VMEM((PAD_T, TILE, LANES), bf16),
            pltpu.VMEM((2, 1152, LANES), f32),
            pltpu.VMEM((2, 768, LANES), f32),
            pltpu.VMEM((R3W, LANES), f32),
        ],
    )(info, features, *early)


def volume_back_kernel(
    slab_ref, f_ref, level_ref, z1_ref, z2_ref, z3_ref, z4_ref, w1_ref, w2_ref, w3_ref, w4_ref,
    out_ref, d4_ref, sp3_ref, sp2_ref, sp1_ref,
    bird_scr, acc2, acc1, accg,
):
    first_row = slab_ref[0] * ROWS - 1
    dz = (level_ref[...] * silu_slope(z4_ref[...])).astype(bf16)
    d4_ref[...] = dz
    level_taps_back(bird_scr, mm_nt(dz, w4_ref[...]))
    dz = jnp.where(inside_rows(R3W, first_row), bird_scr[...] * silu_slope(z3_ref[...]), 0.0)
    acc2[...] = jnp.zeros_like(acc2)
    acc1[...] = jnp.zeros_like(acc1)
    accg[...] = jnp.zeros_like(accg)

    def pair_back(acc, at, rows, spread, weight):
        back = mm_nt(spread, weight)
        for ky in range(3):
            acc[at, ky * GX : ky * GX + rows, :] += back[:, 128 * ky : 128 * ky + 128]
            acc[at + 2, ky * GX : ky * GX + rows, :] += back[:, 384 + 128 * ky : 512 + 128 * ky]

    def layer_grad(acc, m):
        return acc[m] + lane_roll(acc[m - 1], 64)

    for k in range(2):
        spread = split_columns(dz if k == 0 else lane_roll(dz, 64))
        sp3_ref[k] = spread
        pair_back(acc2, 2 * k, R3W, spread, w3_ref[...])

    keep = inside_rows(R2W, first_row - 1)
    for k in range(4):
        d = jnp.where(keep, layer_grad(acc2, k + 1) * silu_slope(z2_ref[k]), 0.0)
        spread = split_columns(d)
        sp2_ref[k] = spread
        pair_back(acc1, k, R2W, spread, w2_ref[...])

    keep = inside_rows(R1W, first_row - 2)
    for k in range(4):
        d = jnp.where(keep, layer_grad(acc1, k + 1) * silu_slope(z1_ref[k]), 0.0)
        spread = split_columns(d)
        sp1_ref[k] = spread
        back = mm_nt(spread, w1_ref[...])
        for kd in range(3):
            for ky in range(3):
                t = 3 * kd + ky
                accg[2 * k + kd, ky * GX : ky * GX + R1W, :] += back[:, 128 * t : 128 * t + 128]

    for t in range(SLABS):
        column, high = cell_marks(f_ref[t, FC : FC + 16, :])
        value = jnp.zeros((FC, VOX), f32)
        for d in range(2):
            marks = layer_marks(column, high, d, first_row)
            value = value + mm_tn(accg[1 + 2 * t + d].astype(bf16), marks)
        out_ref[t] = value.astype(bf16)


def volume_back(info, features, level_grad, kept):
    return call(
        volume_back_kernel,
        9,
        (
            shape((SLABS, FC, VOX), bf16),
            shape((L1_R, LANES), bf16),
            shape((2, R3W, 256), bf16),
            shape((4, R2W, 256), bf16),
            shape((4, R1W, 256), bf16),
        ),
        [smem()] + [vmem()] * 10,
        (vmem(),) * 5,
        [
            pltpu.VMEM((R3W, LANES), f32),
            pltpu.VMEM((6, R2W, LANES), f32),
            pltpu.VMEM((6, R1W, LANES), f32),
            pltpu.VMEM((9, RGW, LANES), f32),
        ],
    )(info, features, level_grad, *kept)


def volume_weights_kernel(
    info_ref, grid_ref, first_ref, second_ref, taps_ref, d4_ref, sp3_ref, sp2_ref, sp1_ref,
    own_ref, core_ref,
    weight_ref, g1_scr, g2_scr,
):
    weight_ref[0:VFE_T] = jnp.zeros((VFE_T, TILE, LANES), bf16)
    weight_ref[VFE_T + EARLY_T : PAD_T] = jnp.zeros((PAD_T - VFE_T - EARLY_T, TILE, LANES), bf16)
    total = mm_tn(taps_ref[...], d4_ref[...])
    weight_ref[LEVEL_T : LEVEL_T + 72] = total.astype(bf16).reshape(72, TILE, LANES)
    total = mm_tn(pair_taps(second_ref, 0, R3W), sp3_ref[0])
    keep_halves(g2_scr, total + mm_tn(pair_taps(second_ref, 2, R3W), sp3_ref[1]))
    conv_weight_grads(weight_ref, VFE_R + 2592, 9, 32, pair_place, g2_scr)
    total = jnp.zeros((768, 256), f32)
    for k in range(4):
        total = total + mm_tn(pair_taps(first_ref, k, R2W), sp2_ref[k])
    keep_halves(g2_scr, total)
    conv_weight_grads(weight_ref, VFE_R + 1728, 9, 32, pair_place, g2_scr)
    total = jnp.zeros((1152, 256), f32)
    for k in range(4):
        total = total + mm_tn(grid_taps(grid_ref, k), sp1_ref[k])
    keep_halves(g1_scr, total)
    conv_weight_grads(weight_ref, VFE_R, 9, 64, tap_place, g1_scr)
    split_chunks(info_ref, weight_ref, 0, own_ref, core_ref)


def volume_weights(info, kept, grads):
    return call(
        volume_weights_kernel,
        8,
        (shape(CHUNKS, bf16),) * 2,
        [smem()] + [vmem()] * 8,
        (vmem(),) * 2,
        [
            pltpu.VMEM((PAD_T, TILE, LANES), bf16),
            pltpu.VMEM((2, 1152, LANES), f32),
            pltpu.VMEM((2, 768, LANES), f32),
        ],
    )(info, *kept, *grads)


def split_planes(ref, height, width):
    planes = []
    for yp in range(2):
        for xp in range(2):
            planes.append(
                jnp.concatenate(
                    [
                        ref[pl.ds((2 * a + yp) * width + xp, width // 2, stride=2), :]
                        for a in range(height // 2)
                    ],
                    0,
                )
            )
    return planes


def merge_planes(ref, planes, height, width):
    half = width // 2
    for yp in range(2):
        for xp in range(2):
            for a in range(height // 2):
                ref[pl.ds((2 * a + yp) * width + xp, half, stride=2), :] = planes[2 * yp + xp][
                    a * half : a * half + half
                ]


def stride_taps(planes, width):
    pieces = []
    for ky in range(3):
        for kx in range(3):
            v = planes[2 * (ky != 1) + (kx != 1)]
            v = shift_in(v, 1, width) if kx == 0 else v
            pieces.append((shift_out(v, 1, width) if ky == 0 else v).astype(bf16))
    return jnp.concatenate(pieces, 1)


def stride_taps_back(grad, width):
    planes = [None] * 4
    channels = grad.shape[1] // 9
    for ky in range(3):
        for kx in range(3):
            t = 3 * ky + kx
            v = grad[:, t * channels : (t + 1) * channels]
            v = shift_out(v, -1, width) if ky == 0 else v
            v = shift_in(v, -1, width) if kx == 0 else v
            at = 2 * (ky != 1) + (kx != 1)
            planes[at] = v if planes[at] is None else planes[at] + v
    return planes


def full_taps(v, width):
    across = [shift_in(v, 1 - kx, width).astype(bf16) for kx in range(3)]
    return jnp.concatenate(
        [shift_out(across[kx], 1 - ky, width) for ky in range(3) for kx in range(3)], 1
    )


def full_taps_back(grad, width):
    channels = grad.shape[1] // 9
    total = None
    for kx in range(3):
        column = None
        for ky in range(3):
            t = 3 * ky + kx
            v = shift_out(grad[:, t * channels : (t + 1) * channels], ky - 1, width)
            column = v if column is None else column + v
        column = shift_in(column, kx - 1, width)
        total = column if total is None else total + column
    return total


HY = 16
CELLS = HY * HX


def region_kernel(
    slab_ref, counts_ref, l0_ref, l1_ref, l2_ref, l3_ref, anchors_ref, goals_ref,
    s0_ref, s1_ref, s2_ref, s3_ref, s4_ref, s5_ref, s6_ref, s7_ref,
    maps_ref, grad_ref, own_ref, core_ref,
    wv, gr, sems,
    l1_scr, l2_scr, zu1_scr, zu2_scr, zu3_scr, head_scr, maps_scr, two_scr, three_scr,
):
    slab = slab_ref[0]
    chip, core = batch_place(slab_ref)
    copies = []
    late = (s0_ref, s1_ref, s2_ref, s3_ref, s4_ref, s5_ref, s6_ref, s7_ref)
    for n, (ref, (chips, slots)) in enumerate(zip(late, LATE_ORDER * 2)):
        for k in range(4):
            shard = jnp.bitwise_xor(slab_ref[2], slots[k])
            at = chunk_start(chip, core if n < 4 else 1 - core, chips[k])
            copies.append(
                pltpu.make_async_copy(
                    ref.at[k // 2, k % 2],
                    wv.at[shard, pl.ds(at, CHUNK_T)],
                    sems.at[len(copies)],
                )
            )
    for c in copies:
        c.start()
    gr[0 : PLANE_T0 + 1] = jnp.zeros((PLANE_T0 + 1, TILE, LANES), bf16)
    gr[PLANE_T0 + 1 + PLANE_T : GRAD_T] = jnp.zeros((GRAD_T - PLANE_T0 - 1 - PLANE_T, TILE, LANES), bf16)
    for slot, ref in enumerate((l0_ref, l1_ref, l2_ref, l3_ref)):
        at = pl.multiple_of(jnp.bitwise_xor(slab, slot) * L1_R, L1_R)
        l1_scr[pl.ds(at, L1_R), :] = ref[...].astype(f32)
    level_one = l1_scr[...]
    for c in copies:
        c.wait()
    for s in range(1, SLABS):
        wv[s, 0:2] = wv[s, 0:2] + wv[s - 1, STRIDE_T : STRIDE_T + 2]

    def tiles_of(tile, tiles):
        pieces = []
        while tiles:
            s = min((tile + 1) // STRIDE_T, SLABS - 1)
            at = tile + 1 - STRIDE_T * s
            size = min(tiles, STRIDE_T - at) if s < SLABS - 1 else tiles
            pieces.append(wv[s, at : at + size])
            tile, tiles = tile + size, tiles - size
        return pieces[0] if len(pieces) == 1 else jnp.concatenate(pieces, 0)

    def narrow(tile, rows):
        return tiles_of(tile, rows // 16).reshape(rows, LANES)

    def wide(tile, rows):
        both = tiles_of(tile, rows // 8).reshape(rows // 16, 2, TILE, LANES)
        return jnp.concatenate(
            [both[:, 0].reshape(rows, LANES), both[:, 1].reshape(rows, LANES)], 1
        )

    def keep_narrow(tile, value):
        at = tile + 1
        tiles = value.shape[0] // 16
        gr[at : at + tiles] = value.astype(bf16).reshape(tiles, TILE, LANES)

    def keep_wide(tile, value):
        at = tile + 1
        tiles = value.shape[0] // 16
        value = value.astype(bf16)
        left = value[:, 0:128].reshape(tiles, 1, TILE, LANES)
        right = value[:, 128:256].reshape(tiles, 1, TILE, LANES)
        gr[at : at + 2 * tiles] = jnp.concatenate([left, right], 1).reshape(2 * tiles, TILE, LANES)

    t_two, t_three, t_up1, t_up2, t_up3, t_head = 297, 369, 513, 657, 721, 1233

    taps_two = stride_taps(split_planes(l1_scr, 16, 32), 16)
    z2 = mm(taps_two, narrow(t_two, 1152))
    level_two = silu(z2).astype(bf16)
    l2_scr[...] = level_two.astype(f32)
    taps_three = stride_taps(split_planes(l2_scr, 8, 16), 8)
    z3 = mm(taps_three, wide(t_three, 1152))
    level_three = silu(z3).astype(bf16)

    taps_up = full_taps(level_one, 32)
    zu1_scr[...] = mm(taps_up, wide(t_up1, 1152))
    for g in range(4):
        zu2_scr[g] = mm(level_two, wide(t_up2 + 16 * g, 128))
    for g in range(16):
        zu3_scr[g] = mm(level_three, wide(t_up3 + 32 * g, 256))

    lane = lane_of((96, LANES))
    rows = narrow(t_head, 96).astype(f32)
    for c in range(8):
        head_scr[pl.ds(c, 96, stride=8), :] = jnp.where(lane < 16, lane_roll(rows, -16 * c), 0.0)
    head = head_scr[...].astype(bf16)
    head_a, head_b, head_c = head[0:256], head[256:512], head[512:768]
    joined_a = silu(zu1_scr[...]).astype(bf16)
    for g in range(4):
        p, q = g // 2, g % 2
        part = mm(silu(zu2_scr[g]).astype(bf16), head_b)
        for a in range(8):
            two_scr[pl.ds((2 * a + p) * HX + q, 16, stride=2), :] = part[16 * a : 16 * a + 16]
    for g in range(16):
        p, q = g // 4, g % 4
        part = mm(silu(zu3_scr[g]).astype(bf16), head_c)
        for a in range(4):
            three_scr[pl.ds((4 * a + p) * HX + q, 8, stride=4), :] = part[8 * a : 8 * a + 8]
    maps = mm(joined_a, head_a) + two_scr[...] + three_scr[...]
    maps = jnp.transpose(maps)[0:16]
    own = jnp.zeros((16, 128), f32)
    for s in range(SLABS):
        own = own + jnp.where(slab == s, maps[:, 128 * s : 128 * s + 128], 0.0)
    for i in range(HY // SLABS):
        maps_ref[0, :, i, :] = own[:, HX * i : HX * i + HX]

    live_count = counts_ref[0]
    anchors = anchors_ref[...]
    slot = row_of((40, CELLS))
    place = lane_of((40, CELLS))
    positive = [
        jnp.sum(
            jnp.logical_and(anchors == place + k * CELLS, slot < live_count).astype(f32),
            axis=0,
            keepdims=True,
        )
        for k in range(2)
    ]
    row = row_of((16, CELLS))
    second = jnp.logical_or(row == 1, row >= 9)
    marked = jnp.where(second, positive[1], positive[0])
    share = 1.0 / jnp.maximum(live_count.astype(f32), 1.0)
    class_grad = (sigmoid(maps) - marked) * (1.0 / (2.0 * CELLS))
    box_grad = jnp.clip(maps - goals_ref[...], -1.0, 1.0) * marked * share
    dmaps = jnp.where(row < 2, class_grad, box_grad)
    dmaps = jnp.transpose(jnp.concatenate([dmaps, jnp.zeros((LANES - 16, CELLS), f32)], 0))
    maps_scr[...] = dmaps
    low = dmaps.astype(bf16)

    dhead_a = mm_tn(joined_a, low)
    dz = mm_nt(low, head_a) * silu_slope(zu1_scr[...])
    dz = dz.astype(bf16)
    keep_wide(t_up1, mm_tn(taps_up, dz))
    dlevel_one = full_taps_back(mm_nt(dz, wide(t_up1, 1152)), 32)

    dhead_b = jnp.zeros((256, LANES), f32)
    dlevel_two = jnp.zeros((128, 128), f32)
    for g in range(4):
        p, q = g // 2, g % 2
        part = jnp.concatenate(
            [maps_scr[pl.ds((2 * a + p) * HX + q, 16, stride=2), :] for a in range(8)], 0
        ).astype(bf16)
        z = zu2_scr[g]
        dhead_b = dhead_b + mm_tn(silu(z).astype(bf16), part)
        dz = (mm_nt(part, head_b) * silu_slope(z)).astype(bf16)
        keep_wide(t_up2 + 16 * g, mm_tn(level_two, dz))
        dlevel_two = dlevel_two + mm_nt(dz, wide(t_up2 + 16 * g, 128))
    dhead_c = jnp.zeros((256, LANES), f32)
    dlevel_three = jnp.zeros((32, 256), f32)
    for g in range(16):
        p, q = g // 4, g % 4
        part = jnp.concatenate(
            [maps_scr[pl.ds((4 * a + p) * HX + q, 8, stride=4), :] for a in range(4)], 0
        ).astype(bf16)
        z = zu3_scr[g]
        dhead_c = dhead_c + mm_tn(silu(z).astype(bf16), part)
        dz = (mm_nt(part, head_c) * silu_slope(z)).astype(bf16)
        keep_wide(t_up3 + 32 * g, mm_tn(level_three, dz))
        dlevel_three = dlevel_three + mm_nt(dz, wide(t_up3 + 32 * g, 256))

    head_scr[...] = jnp.concatenate([dhead_a, dhead_b, dhead_c], 0)
    rows = jnp.zeros((96, LANES), f32)
    for c in range(8):
        piece = jnp.where(lane < 16, head_scr[pl.ds(c, 96, stride=8), :], 0.0)
        rows = rows + lane_roll(piece, 16 * c)
    keep_narrow(t_head, rows)

    dz = (dlevel_three * silu_slope(z3)).astype(bf16)
    keep_wide(t_three, mm_tn(taps_three, dz))
    merge_planes(l2_scr, stride_taps_back(mm_nt(dz, wide(t_three, 1152)), 8), 8, 16)
    dlevel_two = dlevel_two + l2_scr[...]
    dz = (dlevel_two * silu_slope(z2)).astype(bf16)
    keep_narrow(t_two, mm_tn(taps_two, dz))
    merge_planes(l1_scr, stride_taps_back(mm_nt(dz, narrow(t_two, 1152)), 16), 16, 32)
    dlevel_one = dlevel_one + l1_scr[...]
    l1_scr[...] = dlevel_one
    grad_ref[...] = l1_scr[pl.ds(pl.multiple_of(slab * L1_R, L1_R), L1_R), :]
    for s in range(SLABS):

        @pl.when(slab == s)
        def _(s=s):
            start = (15 - 4 * s) * LANES + 16 + 28 * s
            for t in (0, 1) + tuple(range(SHARD_T - 4, PAD_T)):
                tile = STRIDE_T * s - 1 + t
                row = row_of((TILE, LANES))
                if t >= SHARD_T:
                    gr[STRIDE_T * s + t] = jnp.zeros((TILE, LANES), bf16)
                    continue
                if WIDE_T[0] <= tile < WIDE_T[1]:
                    row = 32 * (t // 2) + 2 * row + t % 2
                else:
                    row = TILE * t + row
                at = row * LANES + lane_of((TILE, LANES)) - start
                inside = jnp.logical_and(at >= 0, at < SHARD)
                gr[STRIDE_T * s + t] = jnp.where(
                    inside, gr[STRIDE_T * s + t].astype(f32), 0.0
                ).astype(bf16)

    split_chunks(slab_ref, gr, STRIDE_T * slab, own_ref, core_ref)


LATE_ORDER = (
    ((0, 0, 2, 2), (0, 1, 0, 1)),
    ((1, 1, 3, 3), (0, 1, 0, 1)),
    ((0, 0, 1, 1), (2, 3, 2, 3)),
    ((2, 2, 3, 3), (2, 3, 2, 3)),
)


def region(info, counts, levels, anchors, goals, late):
    return call(
        region_kernel,
        12,
        (shape((1, 16, HY // SLABS, HX)), shape((L1_R, LANES)), shape(CHUNKS, bf16), shape(CHUNKS, bf16)),
        [smem(), smem()] + [vmem()] * 6 + [anywhere()] * 8,
        (vmem(),) * 4,
        [
            pltpu.VMEM((SLABS, PAD_T, TILE, LANES), bf16),
            pltpu.VMEM((GRAD_T, TILE, LANES), bf16),
            pltpu.SemaphoreType.DMA((32,)),
            pltpu.VMEM((512, 128), f32),
            pltpu.VMEM((128, 128), f32),
            pltpu.VMEM((512, 256), f32),
            pltpu.VMEM((4, 128, 256), f32),
            pltpu.VMEM((16, 32, 256), f32),
            pltpu.VMEM((768, LANES), f32),
            pltpu.VMEM((512, LANES), f32),
            pltpu.VMEM((512, LANES), f32),
            pltpu.VMEM((512, LANES), f32),
        ],
    )(info, counts, *levels, anchors, goals, *late)


def swap(x, axis, bit):
    count = lax.axis_size(axis)
    return lax.ppermute(x, axis, [(i, i ^ bit) for i in range(count)])


def after(x, *earlier):
    return lax.optimization_barrier((x,) + earlier)[0]


def slab_all(x):
    return [x] + [swap(x, "slab", k) for k in range(1, SLABS)]


def plane_all(x):
    return [x] + [swap(x, "batch", 2 * k) for k in range(1, 4)]


def sum_cores(own, other):
    return [(own[k].astype(f32) + other[k].astype(f32)).astype(bf16) for k in range(4)]


def sum_chips(parts):
    total = parts[0].astype(f32)
    for k in range(1, 4):
        total = total + parts[k].astype(f32)
    return total


def send_parts(parts):
    return parts[0:1] + [swap(parts[k], "batch", 2 * k) for k in range(1, 4)]


def to_first(total, low):
    for k in range(1, SLABS):
        total = total + lax.ppermute(low, "slab", [(k, 0)]).astype(f32)
    return total


def from_first(x, slab):
    x = jnp.where(slab == 2, lax.ppermute(x, "slab", [(0, 2)]), x)
    near = lax.ppermute(x, "slab", [(0, 1), (2, 3)])
    return jnp.where(slab % 2 == 1, near, x)


def gathered_shards(own):
    batches = lax.axis_size("batch")
    share = PAD_T // batches
    chunk = lax.dynamic_slice_in_dim(own, lax.axis_index("batch") * share, share, 0)
    shards = lax.all_gather(chunk, ("slab", "batch"), axis=0, tiled=True)
    shards = shards.reshape(SLABS, 4, 2, CHUNK_T, TILE, LANES)
    late = []
    for core in range(2):
        for chips, slots in LATE_ORDER:
            part = jnp.stack([shards[s, c, core] for c, s in zip(chips, slots)])
            late.append(part.reshape((2, 2) + part.shape[1:]))
    return (shards[0, :, 0], shards[0, :, 1]), late


def even_odd(whole):
    both = whole.reshape(4, 2, CHUNK_T, TILE, LANES)
    return both[:, 0], both[:, 1]


def body(
    points, point_counts, voxel_cells, pos_anchors, pos_counts, reg_targets, params, moment1, moment2
):
    batches = lax.axis_size("batch")
    slab, batch = lax.axis_index("slab"), lax.axis_index("batch")
    direct = batches == 8
    zero = jnp.zeros_like(slab)
    info = jnp.stack([slab, batch if direct else zero, slab if direct else zero]).astype(jnp.int32)
    counts = point_counts.reshape(1, VOX)

    if direct:
        chunk, first = spread_own(info, params)
        near = jnp.stack([chunk, swap(chunk, "slab", 1)])
        far = swap(near, "slab", 2)
        first = from_first(first, slab)
        small, early = first, first[VFE_T:]
        early = plane_all(early)
    else:
        flat_rows = jnp.pad(params, (0, FLAT_R * LANES - SHARD)).reshape(FLAT_R, LANES)
        first = spread_first(flat_rows[0:VFE_R])
        small = from_first(first, slab)
        early, late = gathered_shards(spread_shard(info, flat_rows))
    encoded, s3 = encode(points, counts, voxel_cells.reshape(1, VOX), small)
    features = lax.all_to_all(encoded, "slab", 0, 0)
    if direct:
        early = jnp.stack(lax.optimization_barrier((*early, encoded))[0:4])
        early = (early, swap(early, "batch", 1))
        near, far = lax.optimization_barrier((near, far, early[0]))[0:2]
        later, near, far = lax.optimization_barrier((points, near, far))
        late = [near, swap(near, "batch", 4), far, swap(far, "batch", 2)]
        x, j1, j2, s1, s2, m1, m2 = encode_slopes(later, counts, small)
        near, near_y, far, far_x = lax.optimization_barrier((*late, x))[0:4]
        near, far = jnp.stack([near, near_y]), jnp.stack([far, far_x])
        late = [near, swap(near, "batch", 2), far, swap(far, "batch", 4)]
        features = after(features, x, near, far)
    else:
        x, j1, j2, s1, s2, m1, m2 = encode_slopes(points, counts, small)
    level, grid, first_pad, second_pad, taps, *kept = volume(info, features, early)
    if direct:
        late = list(lax.optimization_barrier((*late, level))[0:4])
        late = late + [swap(x, "batch", 1) for x in late]
    goals = jnp.pad(reg_targets.reshape(14, CELLS), ((2, 0), (0, 0)))
    levels = slab_all(level)
    maps, level_grad, quarter_own, quarter_core = region(
        info, pos_counts, levels, pos_anchors.reshape(40, 1), goals, late
    )
    feature_back, *spreads = volume_back(info, features, level_grad, kept)
    feature_grad = lax.all_to_all(feature_back, "slab", 0, 0)
    if direct:
        quarter_other = swap(quarter_core, "batch", 1)
        quarter = lax.optimization_barrier((quarter_own, quarter_other, feature_back))[0:2]
        quarter = sum_cores(*quarter)
        spreads[0], *quarter = lax.optimization_barrier((spreads[0], *quarter))
        quarter = send_parts(quarter)
    early_own, early_core = volume_weights(info, (grid, first_pad, second_pad, taps), spreads)
    if direct:
        feature_grad, early_own, early_core, *quarter = lax.optimization_barrier(
            (feature_grad, early_own, early_core, *quarter)
        )
        parts = sum_cores(early_own, swap(early_core, "batch", 1))
        feature_grad, *parts = lax.optimization_barrier((feature_grad, *parts))
        parts = send_parts(parts)
    back = encode_back(counts, small, feature_grad, j2, s3, m2)
    if direct:
        chunk = sum_chips(quarter)
        early_chunk = sum_chips(lax.optimization_barrier((*parts, back[0]))[0:4])
        early_low = early_chunk.astype(bf16)
        d2, early_low, chunk = lax.optimization_barrier((back[0], early_low, chunk))
        back = [d2] + list(back[1:])
        early_chunk = to_first(early_chunk, early_low)
    points_grad, vfe_grad = points_back(counts, small, back, (x, j1, s1, s2, m1))
    if direct:
        early_chunk, vfe_grad = lax.optimization_barrier((early_chunk, vfe_grad))
        chunk = (chunk + jnp.where(slab == 0, early_chunk, 0.0)).astype(bf16)
        squares = jnp.sum(jnp.square(chunk.astype(f32)))
        final = plane_all(chunk)
    else:
        whole = jnp.stack([quarter_own, quarter_core], 1).astype(f32)
        whole_early = lax.psum(jnp.stack([early_own, early_core], 1).astype(f32), "slab")
        whole = lax.psum(whole + jnp.where(slab == 0, whole_early, 0.0), "batch").astype(bf16)
        squares = jnp.sum(jnp.square(whole.astype(f32))) / batches
        final = even_odd(whole)

    total = vfe_grad + jnp.pad(jnp.broadcast_to(squares, (8, LANES)), ((VFE_R, 0), (0, 0)))
    for axis, size in (("slab", SLABS), ("batch", batches)):
        bit = 1
        while bit < size:
            total = total + swap(total, axis, bit)
            if direct and axis == "batch" and bit == 1:
                *final, total = lax.optimization_barrier((*final, total))
                final = jnp.stack(final)
                final = (final, swap(final, "batch", 1))
            bit *= 2
    new_params, new_moment1, new_moment2, norm = update_shard(
        info, *final, total, params, moment1, moment2
    )
    return (maps, points_grad, new_moment1, new_moment2, new_params, norm[0, 0])


def solution(mesh):
    in_specs = (
        P(None, None, ("batch", "slab")),
        P(("batch", "slab")),
        P(("batch", "slab")),
        P("batch", None),
        P("batch"),
        P("batch", None, None, None),
        P("slab"),
        P("slab"),
        P("slab"),
    )
    out_specs = (
        P("batch", None, "slab", None),
        P(None, None, ("batch", "slab")),
        P("slab"),
        P("slab"),
        P("slab"),
        P(),
    )
    return jax.shard_map(body, mesh=mesh, in_specs=in_specs, out_specs=out_specs, check_vma=False)
```

```python
import functools
import math

import jax
import jax.numpy as jnp
from jax import lax
from jax.experimental import pallas as pl
from jax.experimental.pallas import tpu as pltpu
from jax.sharding import PartitionSpec as P

VF1 = 16
VF2 = 64
FC = 128
C3 = 64
STEP = 10
GY = 32
GX = 64
PTS = 35
VOX = 512
SLABS = 4
ROWS = GY // SLABS
LANES = 128
NPARAM = 2537584
SHARD = NPARAM // SLABS

TILE = 16
STRIDE_T = 310
SHARD_T = 312
PAD_T = 320
FLAT_R = 4960
EARLY_T = 288
EARLY_R = EARLY_T * TILE
VFE_T = 10
VFE_R = VFE_T * TILE
PLANE_T0 = 297
PLANE_T = 942
GRAD_T = 3 * STRIDE_T + PAD_T
CHUNK_T = PAD_T // 8
WIDE_T = (369, 1233)

beta_one = 0.9
beta_two = 0.999
adam_eps = 1e-08
learn_rate = 0.02
weight_decay = 0.01
clip_level = 0.002

f32 = jnp.float32
bf16 = jnp.bfloat16


def call(kernel, micros, megabytes, out_shape, in_specs, out_specs, scratch=()):
    return pl.pallas_call(
        kernel,
        out_shape=out_shape,
        in_specs=in_specs,
        out_specs=out_specs,
        scratch_shapes=list(scratch),
        compiler_params=pltpu.CompilerParams(vmem_limit_bytes=megabytes * 1024 * 1024),
        cost_estimate=pl.CostEstimate(
            flops=int(micros * 1e9), transcendentals=0, bytes_accessed=int(micros * 3e6)
        ),
    )


def vmem():
    return pl.BlockSpec(memory_space=pltpu.VMEM)


def smem():
    return pl.BlockSpec(memory_space=pltpu.SMEM)


def anywhere():
    return pl.BlockSpec(memory_space=pl.ANY)


def shape(dims, dtype=f32):
    return jax.ShapeDtypeStruct(dims, dtype)


def mm(a, b):
    return lax.dot_general(a, b, (((1,), (0,)), ((), ())), preferred_element_type=f32)


def mm_nt(a, b):
    return lax.dot_general(a, b, (((1,), (1,)), ((), ())), preferred_element_type=f32)


def mm_tn(a, b):
    return lax.dot_general(a, b, (((0,), (0,)), ((), ())), preferred_element_type=f32)


def sigmoid(z):
    return 0.5 * jnp.tanh(0.5 * z) + 0.5


def silu(z):
    return z * sigmoid(z)


def silu_slope(z):
    s = sigmoid(z)
    return s * (1.0 + z * (1.0 - s))


def lane_of(dims):
    return lax.broadcasted_iota(jnp.int32, dims, len(dims) - 1)


def row_of(dims):
    return lax.broadcasted_iota(jnp.int32, dims, 0)


def lane_roll(x, shift):
    shift = shift % x.shape[-1]
    return x if shift == 0 else pltpu.roll(x, shift, x.ndim - 1)


def shift_in(v, d, width):
    if d == 0:
        return v
    place = row_of(v.shape) % width
    keep = place > 0 if d > 0 else place < width - 1
    return jnp.where(keep, pltpu.roll(v, d % v.shape[0], 0), 0.0)


def shift_out(v, d, width):
    if d == 0:
        return v
    edge = jnp.zeros((width,) + v.shape[1:], v.dtype)
    if d > 0:
        return jnp.concatenate([edge, v[:-width]], 0)
    return jnp.concatenate([v[width:], edge], 0)


def begin(sources, targets, sems, first=0):
    copies = [
        pltpu.make_async_copy(a, b, sems.at[first + n])
        for n, (a, b) in enumerate(zip(sources, targets))
    ]
    for c in copies:
        c.start()
    return copies


def finish(copies):
    for c in copies:
        c.wait()


def batch_place(info_ref):
    return info_ref[1] // 2, info_ref[1] % 2


def chunk_start(chip, core, slot):
    return CHUNK_T * (2 * jnp.bitwise_xor(chip, slot) + core)


def join_chunks(info_ref, out_ref, own_ref, core_ref):
    chip, core = batch_place(info_ref)
    for slot in range(4):
        out_ref[pl.ds(chunk_start(chip, core, slot), CHUNK_T)] = own_ref[slot]
        out_ref[pl.ds(chunk_start(chip, 1 - core, slot), CHUNK_T)] = core_ref[slot]


def split_chunks(info_ref, scr, base, own_ref, core_ref):
    chip, core = batch_place(info_ref)
    for slot in range(4):
        own_ref[slot] = scr[pl.ds(base + chunk_start(chip, core, slot), CHUNK_T)].astype(bf16)
        core_ref[slot] = scr[pl.ds(base + chunk_start(chip, 1 - core, slot), CHUNK_T)].astype(bf16)


CHUNKS = (4, CHUNK_T, TILE, LANES)


def spread_kernel(slab_ref, flat_ref, out_ref, nat):
    nat[...] = jnp.zeros_like(nat)
    span = 480
    for s in range(SLABS):

        @pl.when(slab_ref[0] == s)
        def _(s=s):
            lanes, first = 16 + 28 * s, 15 - 4 * s
            lane = lane_of((span, LANES))
            count = FLAT_R // span + (FLAT_R % span > 0)
            for i in range(count):
                r0 = i * span
                n = min(span, FLAT_R - r0)
                rolled = lane_roll(flat_ref[r0 : r0 + n, :], lanes)
                nat[first + r0 : first + r0 + n, :] += jnp.where(lane[:n] >= lanes, rolled, 0.0)
                nat[first + r0 + 1 : first + r0 + 1 + n, :] += jnp.where(
                    lane[:n] < lanes, rolled, 0.0
                )
            low = max(0, min(SHARD_T // 2, (WIDE_T[0] - STRIDE_T * s + 1) // 2))
            high = max(low, min(SHARD_T // 2, (WIDE_T[1] - STRIDE_T * s + 1) // 2))
            for a, b, wide in ((0, low, False), (low, high, True), (high, SHARD_T // 2, False)):

                def block(i, carry, wide=wide):
                    base = pl.multiple_of(32 * i, 32)
                    if wide:
                        even = nat[pl.ds(base, 16, stride=2), :]
                        odd = nat[pl.ds(base + 1, 16, stride=2), :]
                    else:
                        even = nat[pl.ds(base, 16), :]
                        odd = nat[pl.ds(base + 16, 16), :]
                    out_ref[2 * i] = even.astype(bf16)
                    out_ref[2 * i + 1] = odd.astype(bf16)
                    return carry

                if b > a:
                    lax.fori_loop(a, b, block, 0, unroll=4)

    for t in range(SHARD_T, PAD_T):
        out_ref[t] = jnp.zeros((TILE, LANES), bf16)


def spread_shard(slab, flat_rows):
    return call(
        spread_kernel,
        4,
        56,
        shape((PAD_T, TILE, LANES), bf16),
        [smem(), vmem()],
        vmem(),
        [pltpu.VMEM((5120, LANES), f32)],
    )(slab, flat_rows)


CHUNK_R = CHUNK_T * TILE
CHUNK_N = CHUNK_R * LANES
WHOLE_R = SHARD // LANES // 8 * 8
REST = SHARD - SHARD // LANES * LANES


def flat_tail(flat_ref):
    rest_r = SHARD // LANES - WHOLE_R
    rows = flat_ref[pl.ds(WHOLE_R * LANES, rest_r * LANES)].reshape(rest_r, LANES)
    return rows, flat_ref[pl.ds(SHARD - REST, REST)].reshape(1, REST)


def spread_own_kernel(info_ref, flat_ref, chunk_ref, first_ref, x_scr, nat):
    batch = info_ref[1]

    @pl.when(batch == 0)
    def _():
        x_scr[0:TILE, :] = jnp.zeros((TILE, LANES), f32)
        x_scr[TILE:, :] = flat_ref[pl.ds(0, CHUNK_N)].reshape(CHUNK_R, LANES)

    @pl.when(jnp.logical_and(batch > 0, batch < 7))
    def _():
        start = pl.multiple_of(batch * CHUNK_N - TILE * LANES, 1024)
        rows = CHUNK_R + TILE
        x_scr[...] = flat_ref[pl.ds(start, rows * LANES)].reshape(rows, LANES)

    @pl.when(batch == 7)
    def _():
        first_r = 7 * CHUNK_R - TILE
        whole = WHOLE_R - first_r
        x_scr[0:whole, :] = flat_ref[pl.ds(first_r * LANES, whole * LANES)].reshape(whole, LANES)
        x_scr[whole:, :] = jnp.zeros((CHUNK_R + TILE - whole, LANES), f32)
        rows, last = flat_tail(flat_ref)
        x_scr[whole : whole + rows.shape[0], :] = rows
        x_scr[whole + rows.shape[0] : whole + rows.shape[0] + 1, 0:REST] = last

    def shifted(first, lanes, rows):
        lane = lane_of((rows, LANES))
        here = lane_roll(x_scr[TILE - first : TILE - first + rows, :], lanes)
        above = lane_roll(x_scr[TILE - 1 - first : TILE - 1 - first + rows, :], lanes)
        return jnp.where(lane >= lanes, here, above)

    for s in range(SLABS):

        @pl.when(info_ref[0] == s)
        def _(s=s):
            nat[...] = shifted(15 - 4 * s, 16 + 28 * s, CHUNK_R)
            low = max(0, min(SHARD_T // 2, (WIDE_T[0] - STRIDE_T * s + 1) // 2))
            high = max(low, min(SHARD_T // 2, (WIDE_T[1] - STRIDE_T * s + 1) // 2))
            for i in range(CHUNK_T // 2):
                block = batch * (CHUNK_T // 2) + i
                wide = jnp.logical_and(block >= low, block < high)
                even = nat[pl.ds(32 * i, 16, stride=2), :]
                odd = nat[pl.ds(32 * i + 1, 16, stride=2), :]
                top, bottom = nat[32 * i : 32 * i + 16, :], nat[32 * i + 16 : 32 * i + 32, :]
                chunk_ref[2 * i] = jnp.where(wide, even, top).astype(bf16)
                chunk_ref[2 * i + 1] = jnp.where(wide, odd, bottom).astype(bf16)

    first_ref[VFE_T : VFE_T + CHUNK_T] = chunk_ref[...]
    x_scr[0:TILE, :] = jnp.zeros((TILE, LANES), f32)
    x_scr[TILE : TILE + VFE_R, :] = flat_ref[pl.ds(0, VFE_R * LANES)].reshape(VFE_R, LANES)
    rows = shifted(15, 16, VFE_R).astype(bf16)
    first_ref[0:VFE_T] = rows.reshape(VFE_T, TILE, LANES)


def spread_own(info, params):
    return call(
        spread_own_kernel,
        3,
        56,
        (shape((CHUNK_T, TILE, LANES), bf16), shape((VFE_T + CHUNK_T, TILE, LANES), bf16)),
        [smem(), vmem()],
        (vmem(), vmem()),
        [pltpu.VMEM((CHUNK_R + TILE, LANES), f32), pltpu.VMEM((CHUNK_R, LANES), f32)],
    )(info, params)


def spread_first_kernel(flat_ref, out_ref, nat):
    lanes, first = 16, 15
    lane = lane_of((VFE_R, LANES))
    rolled = lane_roll(flat_ref[...], lanes)
    nat[...] = jnp.zeros_like(nat)
    nat[first : first + VFE_R, :] += jnp.where(lane >= lanes, rolled, 0.0)
    nat[first + 1 : first + 1 + VFE_R, :] += jnp.where(lane < lanes, rolled, 0.0)
    out_ref[...] = nat[0:VFE_R, :].astype(bf16).reshape(VFE_T, TILE, LANES)


def spread_first(flat_rows):
    return call(
        spread_first_kernel,
        1,
        56,
        shape((VFE_T, TILE, LANES), bf16),
        [vmem()],
        vmem(),
        [pltpu.VMEM((VFE_R + 32, LANES), f32)],
    )(flat_rows)


UPDATE_R = 1024
UPDATE_N = UPDATE_R * LANES


def update_kernel(
    slab_ref, own_ref, core_ref, vfe_ref, params_ref, moment1_ref, moment2_ref,
    new_params_ref, new_moment1_ref, new_moment2_ref, norm_ref,
    quarter_ref, nat, grads,
):
    step = pl.program_id(0)

    @pl.when(step == 0)
    def _():
        gather_grads(slab_ref, own_ref, core_ref, vfe_ref, norm_ref, quarter_ref, nat, grads)

    def update(source, target, clipped):
        param = params_ref[source]
        moment1 = beta_one * moment1_ref[source] + (1.0 - beta_one) * clipped
        moment2 = beta_two * moment2_ref[source] + (1.0 - beta_two) * clipped * clipped
        direction = (
            moment1
            * (1.0 / (1.0 - beta_one**STEP))
            / (jnp.sqrt(moment2 * (1.0 / (1.0 - beta_two**STEP))) + adam_eps)
        )
        new_moment1_ref[target] = moment1
        new_moment2_ref[target] = moment2
        new_params_ref[target] = param - learn_rate * (direction + weight_decay * param)

    last = SHARD // UPDATE_N

    @pl.when(step < last)
    def _():
        rows = pl.ds(pl.multiple_of(step * UPDATE_R, UPDATE_R), UPDATE_R)
        at = pl.ds(pl.multiple_of(step * UPDATE_N, UPDATE_N), UPDATE_N)
        update(at, pl.ds(0, UPDATE_N), grads[rows, :].reshape(UPDATE_N))

    @pl.when(step == last)
    def _():
        first = last * UPDATE_R
        whole = WHOLE_R - first
        rest = SHARD // LANES - WHOLE_R
        for r0, n in ((0, whole), (whole, rest)):
            update(
                pl.ds((first + r0) * LANES, n * LANES),
                pl.ds(r0 * LANES, n * LANES),
                grads[first + r0 : first + r0 + n, :].reshape(n * LANES),
            )
        r0 = whole + rest
        update(
            pl.ds(SHARD - REST, REST),
            pl.ds(r0 * LANES, REST),
            grads[first + r0 : first + r0 + 1, 0:REST].reshape(REST),
        )


def gather_grads(slab_ref, own_ref, core_ref, vfe_ref, norm_ref, quarter_ref, nat, grads):
    join_chunks(slab_ref, quarter_ref, own_ref, core_ref)
    vfe = vfe_ref[0:VFE_R, :]
    squares = vfe_ref[VFE_R : VFE_R + 1, :][0, 0] + jnp.sum(vfe * vfe)
    norm = jnp.sqrt(jnp.broadcast_to(squares, (8, LANES)))
    norm_ref[0, 0] = norm[0, 0]
    scale = (clip_level / jnp.maximum(norm, clip_level))[0:1, :]
    grads[FLAT_R:, :] = jnp.zeros((grads.shape[0] - FLAT_R, LANES), f32)
    span = 480
    for s in range(SLABS):

        @pl.when(slab_ref[0] == s)
        def _(s=s):
            lanes, first = 16 + 28 * s, 15 - 4 * s
            low = max(0, min(SHARD_T // 2, (WIDE_T[0] - STRIDE_T * s + 1) // 2))
            high = max(low, min(SHARD_T // 2, (WIDE_T[1] - STRIDE_T * s + 1) // 2))
            for a, b, wide in ((0, low, False), (low, high, True), (high, SHARD_T // 2, False)):

                def block(i, carry, wide=wide):
                    base = pl.multiple_of(32 * i, 32)
                    even, odd = quarter_ref[2 * i].astype(f32), quarter_ref[2 * i + 1].astype(f32)
                    if wide:
                        nat[pl.ds(base, 16, stride=2), :] = even
                        nat[pl.ds(base + 1, 16, stride=2), :] = odd
                    else:
                        nat[pl.ds(base, 16), :] = even
                        nat[pl.ds(base + 16, 16), :] = odd
                    return carry

                if b > a:
                    lax.fori_loop(a, b, block, 0, unroll=4)
            if s == 0:
                nat[0:VFE_R, :] = vfe
            lane = lane_of((span, LANES))
            count = FLAT_R // span + (FLAT_R % span > 0)
            for i in range(count):
                r0 = i * span
                n = min(span, FLAT_R - r0)
                here = lane_roll(nat[first + r0 : first + r0 + n, :], -lanes)
                after = lane_roll(nat[first + r0 + 1 : first + r0 + 1 + n, :], -lanes)
                grads[r0 : r0 + n, :] = jnp.where(lane[:n] < LANES - lanes, here, after) * scale


def update_shard(info, own, core, vfe, params, moment1, moment2):
    block = pl.BlockSpec((UPDATE_N,), lambda i: (i,))
    steps = pl.cdiv(SHARD, UPDATE_N)
    return pl.pallas_call(
        update_kernel,
        grid=(steps,),
        out_shape=(shape((SHARD,)),) * 3 + (shape((1, 1)),),
        in_specs=[smem()] + [vmem()] * 6,
        out_specs=(block,) * 3 + (smem(),),
        scratch_shapes=[
            pltpu.VMEM((PAD_T, TILE, LANES), bf16),
            pltpu.VMEM((5120, LANES), f32),
            pltpu.VMEM((steps * UPDATE_R, LANES), f32),
        ],
        compiler_params=pltpu.CompilerParams(vmem_limit_bytes=24 * 1024 * 1024),
    )(info, own, core, vfe, params, moment1, moment2)


PART = 5
PARTS = PTS // PART
WIDE = PART * VOX
VFE_SCRATCH = [
    pltpu.VMEM((VOX // LANES, PTS * 16, LANES), f32),
    pltpu.VMEM((16, LANES), f32),
    pltpu.VMEM((64, LANES), f32),
]


def spread_points(points_ref, x_scr):
    x_scr[...] = jnp.zeros_like(x_scr)
    for c in range(7):
        plane = points_ref[c].astype(f32)
        for b in range(VOX // LANES):
            x_scr[b, pl.ds(c, PTS, stride=16), :] = plane[:, b * LANES : (b + 1) * LANES]


def vfe_weights(rows_ref, w1_scr, w2_scr):
    line = rows_ref[0].astype(f32)
    lane = lane_of((16, LANES))
    for o in range(VF1):
        w1_scr[o : o + 1, :] = jnp.where(lane < 7, lane_roll(line, -(16 + 7 * o)), 0.0)[15:16]
    two = rows_ref[1].astype(f32)
    for k in range(4):
        w2_scr[pl.ds(k, 16, stride=4), :] = jnp.where(lane < 32, lane_roll(two, -32 * k), 0.0)
    w1 = w1_scr[...].astype(bf16)[:, 0:16]
    w2 = w2_scr[...]
    w2a = w2.astype(bf16)[:, 0:16]
    w2b = lane_roll(w2, -16).astype(bf16)[:, 0:16]
    w3 = rows_ref[2:10].reshape(FC, LANES)
    w3a = w3[:, 0:64]
    w3b = lane_roll(w3.astype(f32), -64).astype(bf16)[:, 0:64]
    return w1, w2a, w2b, w3a, w3b


def points_part(ref, i):
    return jnp.concatenate(
        [
            ref[b, pl.ds(pl.multiple_of((PART * i + k) * 16, 16), 16), :]
            for k in range(PART)
            for b in range(VOX // LANES)
        ],
        1,
    )


def set_points_part(ref, i, value):
    for k in range(PART):
        for b in range(VOX // LANES):
            at = k * VOX + b * LANES
            ref[b, pl.ds(pl.multiple_of((PART * i + k) * 16, 16), 16), :] = value[:, at : at + LANES]


def part_sum(value):
    total = value[:, 0:VOX]
    for k in range(1, PART):
        total = total + value[:, k * VOX : (k + 1) * VOX]
    return total


def valid_part(i, counts):
    return jnp.concatenate([(PART * i + k < counts).astype(f32) for k in range(PART)], 1)


def widen(value):
    return jnp.concatenate([value] * PART, 1)


def vfe_front(weights, counts, inverse, x_scr, j1_ref, j2_ref, kept=None, done=None):
    w1, w2a, w2b, w3a, w3b = weights
    total = jnp.zeros((VF1, VOX), f32)
    for i in range(PARTS):
        x = points_part(x_scr, i).astype(bf16)
        z = mm(w1, x)
        value = silu(z)
        j1_ref[i] = value.astype(bf16)
        if kept is not None:
            kept[0][i] = x
            kept[1][i] = silu_slope(z).astype(bf16)
        total = total + part_sum(value * valid_part(i, counts))
    mean_one = (total * inverse).astype(bf16)
    shared_two = widen(mm(w2b, mean_one))
    total = jnp.zeros((VF2, VOX), f32)
    for i in range(PARTS):
        z = mm(w2a, j1_ref[i]) + shared_two
        value = silu(z)
        j2_ref[i] = value.astype(bf16)
        if kept is not None:
            kept[2][i] = silu_slope(z).astype(bf16)
            done(i)
        total = total + part_sum(value * valid_part(i, counts))
    mean_two = (total * inverse).astype(bf16)
    shared_three = widen(mm(w3b, mean_two))
    return mean_one, mean_two, shared_three


def encode_kernel(
    points_ref, counts_ref, cells_ref, rows_ref, out_ref, s3_ref,
    x_scr, w1_scr, w2_scr, j1_scr, j2_scr, s3_scr, sems,
):
    spread_points(points_ref, x_scr)
    weights = vfe_weights(rows_ref, w1_scr, w2_scr)
    counts = counts_ref[...]
    inverse = 1.0 / counts.astype(f32)
    _, _, shared_three = vfe_front(weights, counts, inverse, x_scr, j1_scr, j2_scr)
    w3a = weights[3]
    wide_inverse = widen(inverse)
    total = jnp.zeros((FC, VOX), f32)
    copies = []
    for i in range(PARTS):
        z = mm(w3a, j2_scr[i]) + shared_three
        gate = sigmoid(z)
        value = z * gate
        share = valid_part(i, counts) * wide_inverse
        s3_scr[i] = ((gate + value - value * gate) * share).astype(bf16)
        copies += begin([s3_scr.at[i]], [s3_ref.at[i]], sems, i)
        total = total + part_sum(value * share)
    features = total.astype(bf16)
    cells = cells_ref[...]
    row = row_of((16, VOX))
    places = jnp.where(row == 0, cells // GX, cells % GX).astype(f32).astype(bf16)
    for t in range(SLABS):
        out_ref[t, 0:FC, :] = features
        out_ref[t, FC : FC + 16, :] = places
    finish(copies)


def encode(points, counts, cells, rows):
    return call(
        encode_kernel,
        10,
        56,
        (shape((SLABS, FC + 16, VOX), bf16), shape((PARTS, 128, WIDE), bf16)),
        [vmem()] * 4,
        (vmem(), anywhere()),
        VFE_SCRATCH
        + [
            pltpu.VMEM((PARTS, 16, WIDE), bf16),
            pltpu.VMEM((PARTS, 64, WIDE), bf16),
            pltpu.VMEM((PARTS, 128, WIDE), bf16),
            pltpu.SemaphoreType.DMA((PARTS,)),
        ],
    )(points, counts, cells, rows)


def encode_slopes_kernel(
    points_ref, counts_ref, rows_ref,
    x_ref, j1_ref, j2_ref, s1_ref, s2_ref, m1_ref, m2_ref,
    x_scr, w1_scr, w2_scr, xs_scr, j1_scr, j2_scr, s1_scr, s2_scr, sems,
):
    spread_points(points_ref, x_scr)
    weights = vfe_weights(rows_ref, w1_scr, w2_scr)
    counts = counts_ref[...]
    inverse = 1.0 / counts.astype(f32)
    copies = []

    def done(i):
        if i == 0:
            copies.extend(begin((xs_scr, j1_scr, s1_scr), (x_ref, j1_ref, s1_ref), sems, 0))
        copies.extend(
            begin((j2_scr.at[i], s2_scr.at[i]), (j2_ref.at[i], s2_ref.at[i]), sems, 3 + 2 * i)
        )

    mean_one, mean_two, _ = vfe_front(
        weights, counts, inverse, x_scr, j1_scr, j2_scr, (xs_scr, s1_scr, s2_scr), done
    )
    m1_ref[...] = mean_one
    m2_ref[...] = mean_two
    finish(copies)


LOW = (PARTS, 16, WIDE)
MID = (PARTS, 64, WIDE)
HIGH = (PARTS, 128, WIDE)


def encode_slopes(points, counts, rows):
    return call(
        encode_slopes_kernel,
        7,
        56,
        tuple(shape(d, bf16) for d in (LOW, LOW, MID, LOW, MID, (VF1, VOX), (VF2, VOX))),
        [vmem()] * 3,
        (anywhere(),) * 5 + (vmem(),) * 2,
        VFE_SCRATCH
        + [pltpu.VMEM(d, bf16) for d in (LOW, LOW, MID, LOW, MID)]
        + [pltpu.SemaphoreType.DMA((3 + 2 * PARTS,))],
    )(points, counts, rows)


def encode_back_kernel(
    counts_ref, rows_ref, grad_ref, j2_ref, s3_ref, m2_ref,
    d2_ref, shared_ref, weight_ref,
    w1_scr, w2_scr, j2_scr, s3_scr, d2_scr, sems,
):
    arrive = []
    for i in range(PARTS):
        arrive.append(
            begin((s3_ref.at[i], j2_ref.at[i]), (s3_scr.at[i], j2_scr.at[i]), sems, 3 * i)
        )
    _, _, _, w3a, w3b = vfe_weights(rows_ref, w1_scr, w2_scr)
    inverse = 1.0 / counts_ref[...].astype(f32)
    grad = grad_ref[0].astype(f32)
    for t in range(1, SLABS):
        grad = grad + grad_ref[t].astype(f32)
    grad_three = widen(grad)
    total = jnp.zeros((FC, VOX), f32)
    weight = jnp.zeros((FC, VF2), f32)
    leave = []
    for i in range(PARTS):
        finish(arrive[i])
        dz = grad_three * s3_scr[i].astype(f32)
        low = dz.astype(bf16)
        d2_scr[i] = mm_tn(w3a, low).astype(bf16)
        leave += begin([d2_scr.at[i]], [d2_ref.at[i]], sems, 3 * i + 2)
        total = total + part_sum(dz)
        weight = weight + mm_nt(low, j2_scr[i])
    total = total.astype(bf16)
    weight_ref[...] = jnp.concatenate([weight, mm_nt(total, m2_ref[...])], 1)
    shared_ref[...] = mm_tn(w3b, total) * inverse
    finish(leave)


def encode_back(counts, rows, grad, j2, s3, m2):
    return call(
        encode_back_kernel,
        8,
        56,
        (shape(MID, bf16), shape((VF2, VOX)), shape((FC, LANES))),
        [vmem()] * 3 + [anywhere()] * 2 + [vmem()],
        (anywhere(), vmem(), vmem()),
        VFE_SCRATCH[1:]
        + [pltpu.VMEM(d, bf16) for d in (MID, HIGH, MID)]
        + [pltpu.SemaphoreType.DMA((3 * PARTS,))],
    )(counts, rows, grad, j2, s3, m2)


def points_back_kernel(
    counts_ref, rows_ref, d2_ref, shared_ref, w3_ref, x_ref, j1_ref, s1_ref, s2_ref, m1_ref,
    out_ref, weight_ref,
    x_scr, w1_scr, w2_scr, d1_scr, d2_scr, s2_scr, j1_scr, s1_scr, xs_scr, sems,
):
    arrive = []
    for i in range(PARTS):
        arrive.append(
            begin(
                (d2_ref.at[i], s2_ref.at[i], j1_ref.at[i]),
                (d2_scr.at[i], s2_scr.at[i], j1_scr.at[i]),
                sems,
                3 * i,
            )
        )
    late = begin((s1_ref, x_ref), (s1_scr, xs_scr), sems, 3 * PARTS)
    w1, w2a, w2b, _, _ = vfe_weights(rows_ref, w1_scr, w2_scr)
    counts = counts_ref[...]
    inverse = 1.0 / counts.astype(f32)
    grad_two = widen(shared_ref[...])
    total = jnp.zeros((VF2, VOX), f32)
    grad_w2a = jnp.zeros((VF2, VF1), f32)
    for i in range(PARTS):
        finish(arrive[i])
        dz = d2_scr[i].astype(f32) + valid_part(i, counts) * grad_two
        dz = dz * s2_scr[i].astype(f32)
        low = dz.astype(bf16)
        d1_scr[i] = mm_tn(w2a, low)
        total = total + part_sum(dz)
        grad_w2a = grad_w2a + mm_nt(low, j1_scr[i])
    total = total.astype(bf16)
    grad_w2b = mm_nt(total, m1_ref[...])
    grad_one = widen(mm_tn(w2b, total) * inverse)
    grad_w1 = jnp.zeros((VF1, 16), f32)
    finish(late)
    for i in range(PARTS):
        dz = (d1_scr[i] + valid_part(i, counts) * grad_one) * s1_scr[i].astype(f32)
        low = dz.astype(bf16)
        set_points_part(x_scr, i, mm_tn(w1, low))
        grad_w1 = grad_w1 + mm_nt(low, xs_scr[i])
    for c in range(7):
        for b in range(VOX // LANES):
            out_ref[c, :, b * LANES : (b + 1) * LANES] = x_scr[b, pl.ds(c, PTS, stride=16), :]

    lane = lane_of((16, LANES))
    w1_scr[...] = jnp.concatenate([grad_w1, jnp.zeros((16, LANES - 16), f32)], 1)
    spread = jnp.where(lane < 7, w1_scr[...], 0.0)
    line = jnp.zeros((16, LANES), f32)
    row = row_of((16, LANES))
    for o in range(VF1):
        line = line + jnp.where(row == o, lane_roll(spread, 16 + 7 * o), 0.0)
    line = jnp.sum(line, axis=0, keepdims=True)
    weight_ref[0:16, :] = jnp.where(row == 15, line, 0.0)
    w2_scr[...] = jnp.concatenate([grad_w2a, grad_w2b, jnp.zeros((64, LANES - 32), f32)], 1)
    two = jnp.zeros((16, LANES), f32)
    for k in range(4):
        two = two + lane_roll(w2_scr[pl.ds(k, 16, stride=4), :], 32 * k)
    weight_ref[16:32, :] = two
    weight_ref[32:160, :] = w3_ref[...]
    weight_ref[160:168, :] = jnp.zeros((8, LANES), f32)


def points_back(counts, rows, back, kept):
    return call(
        points_back_kernel,
        7,
        56,
        (shape((7, PTS, VOX)), shape((VFE_R + 8, LANES))),
        [vmem(), vmem(), anywhere(), vmem(), vmem()] + [anywhere()] * 4 + [vmem()],
        (vmem(), vmem()),
        VFE_SCRATCH
        + [pltpu.VMEM(LOW, f32)]
        + [pltpu.VMEM(d, bf16) for d in (MID, MID, LOW, LOW, LOW)]
        + [pltpu.SemaphoreType.DMA((3 * PARTS + 2,))],
    )(counts, rows, *back, *kept)


R3 = ROWS + 1
R3W = R3 * GX
R2W = (R3 + 2) * GX
R1W = (R3 + 4) * GX
RG = R3 + 6
RGW = RG * GX
HX = GX // 2
L1_R = ROWS // 2 * HX


def cell_marks(places):
    value = places.astype(f32)
    high, low = value[0:1], value[1:2]
    column = lax.broadcasted_iota(jnp.int32, (GX, VOX), 0).astype(f32)
    return (column == low).astype(f32).astype(bf16), high


def layer_marks(column, high, depth, first_row):
    pieces = []
    for w in range(RG):
        row = first_row - 3 + w
        inside = jnp.logical_and(row >= 0, row < GY)
        target = jnp.where(inside, depth * GY + row, -1).astype(f32)
        pieces.append(column * (high == target).astype(f32).astype(bf16))
    return jnp.concatenate(pieces, 0)


def conv_weights(rows_ref, start, taps, half, place, scr):
    lane = lane_of((half, LANES))
    left = lane < 64
    for t in range(taps):
        r = []
        for kx in range(3):
            base = start + (3 * t + kx) * half
            r.append(rows_ref[base // TILE : (base + half) // TILE].reshape(half, LANES).astype(f32))
        turned = [lane_roll(v, 64) for v in r]
        at = place(t)
        scr[0, pl.ds(at, half, stride=2), :] = jnp.where(left, r[1], turned[0])
        scr[0, pl.ds(at + 1, half, stride=2), :] = jnp.where(left, turned[1], r[0])
        scr[1, pl.ds(at, half, stride=2), :] = jnp.where(left, r[2], 0.0)
        scr[1, pl.ds(at + 1, half, stride=2), :] = jnp.where(left, turned[2], 0.0)


def conv_weight_grads(out_ref, start, taps, half, place, scr):
    lane = lane_of((half, LANES))
    left = lane < 64
    for t in range(taps):
        at = place(t)
        even = [scr[b, pl.ds(at, half, stride=2), :] for b in range(2)]
        odd = [scr[b, pl.ds(at + 1, half, stride=2), :] for b in range(2)]
        values = (
            jnp.where(left, lane_roll(even[0], 64), odd[0]),
            jnp.where(left, even[0], lane_roll(odd[0], 64)),
            jnp.where(left, even[1], lane_roll(odd[1], 64)),
        )
        for kx in range(3):
            base = start + (3 * t + kx) * half
            out_ref[base // TILE : (base + half) // TILE] = (
                values[kx].astype(bf16).reshape(half // TILE, TILE, LANES)
            )


def both_halves(out_ref, scr):
    for b in range(2):
        out_ref[:, b * LANES : (b + 1) * LANES] = scr[b].astype(bf16)


def keep_halves(scr, value):
    for b in range(2):
        scr[b] = value[:, b * LANES : (b + 1) * LANES]


def tap_place(t):
    return 128 * t


def pair_place(t):
    kd, ky = t // 3, t % 3
    return 128 * ky + 64 * kd if kd < 2 else 384 + 128 * ky


def join_columns(p):
    first, last = p[:, 0:128], p[:, 128:256]
    left = lane_of(first.shape) < 64
    half = jnp.where(left, first + shift_in(last, -1, GX), shift_in(first, 1, GX))
    return half + lane_roll(half, 64)


def split_columns(d):
    left = lane_of(d.shape) < 64
    first = jnp.where(left, d, lane_roll(shift_in(d, -1, GX), 64))
    last = jnp.where(left, shift_in(d, 1, GX), 0.0)
    return jnp.concatenate([first, last], 1).astype(bf16)


def inside_rows(rows, first_row):
    place = first_row + row_of((rows, LANES)) // GX
    return jnp.logical_and(place >= 0, place < GY)


def grid_taps(grid_ref, k):
    return jnp.concatenate(
        [grid_ref[2 * k + kd, ky * GX : ky * GX + R1W, :] for kd in range(3) for ky in range(3)], 1
    )


def pair_taps(ref, at, rows):
    return jnp.concatenate(
        [ref[at, ky * GX : ky * GX + rows, :] for ky in range(3)]
        + [ref[at + 2, ky * GX : ky * GX + rows, :] for ky in range(3)],
        1,
    )


def level_taps(ref):
    planes = {}
    for xp in range(2):
        for yp in range(2):
            count = ROWS // 2 + 1 - yp
            planes[yp, xp] = jnp.concatenate(
                [ref[pl.ds((2 * a + yp) * GX + xp, HX, stride=2), :] for a in range(count)], 0
            )
    pieces = []
    for ky in range(3):
        for kx in range(3):
            v = planes[ky % 2, int(kx != 1)]
            v = v[HX:] if ky == 2 else v[0:L1_R]
            pieces.append((shift_in(v, 1, HX) if kx == 0 else v).astype(bf16))
    return jnp.concatenate(pieces, 1)


def level_taps_back(ref, grad):
    planes = {}
    edge = jnp.zeros((HX, LANES), f32)
    for ky in range(3):
        for kx in range(3):
            t = 3 * ky + kx
            v = grad[:, t * LANES : (t + 1) * LANES]
            v = shift_in(v, -1, HX) if kx == 0 else v
            if ky != 1:
                v = jnp.concatenate([edge, v] if ky == 2 else [v, edge], 0)
            at = (ky % 2, int(kx != 1))
            planes[at] = planes[at] + v if at in planes else v
    for (yp, xp), v in planes.items():
        for a in range(ROWS // 2 + 1 - yp):
            ref[pl.ds((2 * a + yp) * GX + xp, HX, stride=2), :] = v[a * HX : (a + 1) * HX]


GRID = (9, RGW, LANES)
FIRST = (6, R1W, LANES)
SECOND = (6, R2W, LANES)


def volume_kernel(
    slab_ref, f_ref, own_ref, core_ref,
    level_ref, grid_out, first_out, second_out, taps_ref, z1_out, z2_out, z3_ref, z4_ref, w1_ref, w2_ref, w3_ref, w4_ref,
    rows_ref, w1_scr, w2_scr, bird_scr, grid_ref, first_ref, second_ref, z1_ref, z2_ref, sems,
):
    join_chunks(slab_ref, rows_ref, own_ref, core_ref)
    w4_ref[...] = rows_ref[LEVEL_T : LEVEL_T + 72].reshape(1152, LANES)
    w2_scr[...] = jnp.zeros_like(w2_scr)
    conv_weights(rows_ref, VFE_R, 9, 64, tap_place, w1_scr)
    both_halves(w1_ref, w1_scr)
    conv_weights(rows_ref, VFE_R + 1728, 9, 32, pair_place, w2_scr)
    both_halves(w2_ref, w2_scr)
    conv_weights(rows_ref, VFE_R + 2592, 9, 32, pair_place, w2_scr)
    both_halves(w3_ref, w2_scr)

    first_row = slab_ref[0] * ROWS - 1
    grid_ref[0] = jnp.zeros((RGW, FC), bf16)
    for t in range(SLABS):
        features = f_ref[t, 0:FC, :]
        column, high = cell_marks(f_ref[t, FC : FC + 16, :])
        for d in range(2):
            marks = layer_marks(column, high, d, first_row)
            grid_ref[1 + 2 * t + d] = mm_nt(marks, features).astype(bf16)
    copies = begin([grid_ref], [grid_out], sems, 0)

    first_ref[0] = jnp.zeros((R1W, LANES), bf16)
    first_ref[5] = jnp.zeros((R1W, LANES), bf16)
    keep = inside_rows(R1W, first_row - 2)
    for k in range(4):
        z = join_columns(mm(grid_taps(grid_ref, k), w1_ref[...]))
        z1_ref[k] = jnp.where(keep, silu_slope(z), 0.0).astype(bf16)
        value = jnp.where(keep, silu(z), 0.0).astype(bf16)
        first_ref[k + 1, :, 0:64] = value[:, 0:64]
        first_ref[k, :, 64:128] = value[:, 64:128]
    first_ref[4, :, 64:128] = jnp.zeros((R1W, 64), bf16)
    copies += begin((first_ref, z1_ref), (first_out, z1_out), sems, 1)

    second_ref[0] = jnp.zeros((R2W, LANES), bf16)
    second_ref[5] = jnp.zeros((R2W, LANES), bf16)
    keep = inside_rows(R2W, first_row - 1)
    for k in range(4):
        z = join_columns(mm(pair_taps(first_ref, k, R2W), w2_ref[...]))
        z2_ref[k] = jnp.where(keep, silu_slope(z), 0.0).astype(bf16)
        value = jnp.where(keep, silu(z), 0.0).astype(bf16)
        second_ref[k + 1, :, 0:64] = value[:, 0:64]
        second_ref[k, :, 64:128] = value[:, 64:128]
    second_ref[4, :, 64:128] = jnp.zeros((R2W, 64), bf16)
    copies += begin((second_ref, z2_ref), (second_out, z2_out), sems, 3)

    z3 = []
    for k in range(2):
        z3.append(join_columns(mm(pair_taps(second_ref, 2 * k, R3W), w3_ref[...])))
    z = jnp.where(lane_of((R3W, LANES)) < 64, z3[0], z3[1])
    keep = inside_rows(R3W, first_row)
    z3_ref[...] = jnp.where(keep, silu_slope(z), 0.0).astype(bf16)
    bird_scr[...] = jnp.where(keep, silu(z), 0.0)
    taps = level_taps(bird_scr)
    taps_ref[...] = taps
    z = mm(taps, w4_ref[...])
    z4_ref[...] = silu_slope(z).astype(bf16)
    level_ref[...] = silu(z).astype(bf16)
    finish(copies)


LEVEL_T = VFE_T + 216


def volume(info, features, early):
    return call(
        volume_kernel,
        11,
        56,
        (
            shape((L1_R, LANES), bf16),
            shape(GRID, bf16),
            shape(FIRST, bf16),
            shape(SECOND, bf16),
            shape((L1_R, 1152), bf16),
            shape((4, R1W, LANES), bf16),
            shape((4, R2W, LANES), bf16),
            shape((R3W, LANES), bf16),
            shape((L1_R, LANES), bf16),
            shape((1152, 256), bf16),
            shape((768, 256), bf16),
            shape((768, 256), bf16),
            shape((1152, LANES), bf16),
        ),
        [smem()] + [vmem()] * 3,
        (vmem(),) + (anywhere(),) * 3 + (vmem(),) + (anywhere(),) * 2 + (vmem(),) * 6,
        [
            pltpu.VMEM((PAD_T, TILE, LANES), bf16),
            pltpu.VMEM((2, 1152, LANES), f32),
            pltpu.VMEM((2, 768, LANES), f32),
            pltpu.VMEM((R3W, LANES), f32),
            pltpu.VMEM(GRID, bf16),
            pltpu.VMEM(FIRST, bf16),
            pltpu.VMEM(SECOND, bf16),
            pltpu.VMEM((4, R1W, LANES), bf16),
            pltpu.VMEM((4, R2W, LANES), bf16),
            pltpu.SemaphoreType.DMA((5,)),
        ],
    )(info, features, *early)


def volume_back(
    first_row, f_ref, level_grad, z1_ref, z2_ref, z3_ref, z4_ref, w1_ref, w2_ref, w3_ref, w4_ref,
    out_ref, d4_ref, sp3_ref, sp2_ref, sp1_ref,
    bird_scr, acc2, acc1, accg, leave,
):
    dz = (level_grad * z4_ref[...].astype(f32)).astype(bf16)
    d4_ref[...] = dz
    leave(0)
    level_taps_back(bird_scr, mm_nt(dz, w4_ref[...]))
    dz = bird_scr[...] * z3_ref[...].astype(f32)
    acc2[...] = jnp.zeros_like(acc2)
    acc1[...] = jnp.zeros_like(acc1)
    accg[...] = jnp.zeros_like(accg)

    def pair_back(acc, at, rows, spread, weight):
        back = mm_nt(spread, weight)
        for ky in range(3):
            acc[at, ky * GX : ky * GX + rows, :] += back[:, 128 * ky : 128 * ky + 128]
            acc[at + 2, ky * GX : ky * GX + rows, :] += back[:, 384 + 128 * ky : 512 + 128 * ky]

    def layer_grad(acc, m):
        return acc[m] + lane_roll(acc[m - 1], 64)

    for k in range(2):
        spread = split_columns(dz if k == 0 else lane_roll(dz, 64))
        sp3_ref[k] = spread
        pair_back(acc2, 2 * k, R3W, spread, w3_ref[...])
    leave(1)
    for k in range(4):
        spread = split_columns(layer_grad(acc2, k + 1) * z2_ref[k].astype(f32))
        sp2_ref[k] = spread
        pair_back(acc1, k, R2W, spread, w2_ref[...])
    leave(2)
    for k in range(4):
        spread = split_columns(layer_grad(acc1, k + 1) * z1_ref[k].astype(f32))
        sp1_ref[k] = spread
        back = mm_nt(spread, w1_ref[...])
        for kd in range(3):
            for ky in range(3):
                t = 3 * kd + ky
                accg[2 * k + kd, ky * GX : ky * GX + R1W, :] += back[:, 128 * t : 128 * t + 128]
    leave(3)
    for t in range(SLABS):
        column, high = cell_marks(f_ref[t, FC : FC + 16, :])
        value = jnp.zeros((FC, VOX), f32)
        for d in range(2):
            marks = layer_marks(column, high, d, first_row)
            value = value + mm_tn(accg[1 + 2 * t + d].astype(bf16), marks)
        out_ref[t] = value.astype(bf16)


SPREADS = ((L1_R, LANES), (2, R3W, 256), (4, R2W, 256), (4, R1W, 256))
BACK_IN = (
    (SLABS, FC + 16, VOX),
    (4, R1W, LANES),
    (4, R2W, LANES),
    (R3W, LANES),
    (L1_R, LANES),
    (1152, 256),
    (768, 256),
    (768, 256),
    (1152, LANES),
)


def volume_weights_kernel(
    info_ref, taps_ref, d4_ref, second_ref, sp3_ref, first_ref, sp2_ref, grid_ref, sp1_ref,
    own_ref, core_ref,
    weight_ref, g1_scr, g2_scr,
):
    weight_ref[0:VFE_T] = jnp.zeros((VFE_T, TILE, LANES), bf16)
    weight_ref[VFE_T + EARLY_T : PAD_T] = jnp.zeros((PAD_T - VFE_T - EARLY_T, TILE, LANES), bf16)
    total = mm_tn(taps_ref[...], d4_ref[...])
    weight_ref[LEVEL_T : LEVEL_T + 72] = total.astype(bf16).reshape(72, TILE, LANES)
    total = mm_tn(pair_taps(second_ref, 0, R3W), sp3_ref[0])
    keep_halves(g2_scr, total + mm_tn(pair_taps(second_ref, 2, R3W), sp3_ref[1]))
    conv_weight_grads(weight_ref, VFE_R + 2592, 9, 32, pair_place, g2_scr)
    total = jnp.zeros((768, 256), f32)
    for k in range(4):
        total = total + mm_tn(pair_taps(first_ref, k, R2W), sp2_ref[k])
    keep_halves(g2_scr, total)
    conv_weight_grads(weight_ref, VFE_R + 1728, 9, 32, pair_place, g2_scr)
    total = jnp.zeros((1152, 256), f32)
    for k in range(4):
        total = total + mm_tn(grid_taps(grid_ref, k), sp1_ref[k])
    keep_halves(g1_scr, total)
    conv_weight_grads(weight_ref, VFE_R, 9, 64, tap_place, g1_scr)
    split_chunks(info_ref, weight_ref, 0, own_ref, core_ref)


def volume_weights(info, kept, grads):
    grid, first, second, taps = kept
    d4, sp3, sp2, sp1 = grads
    return call(
        volume_weights_kernel,
        8,
        56,
        (shape(CHUNKS, bf16),) * 2,
        [smem()] + [vmem()] * 8,
        (vmem(),) * 2,
        [
            pltpu.VMEM((PAD_T, TILE, LANES), bf16),
            pltpu.VMEM((2, 1152, LANES), f32),
            pltpu.VMEM((2, 768, LANES), f32),
        ],
    )(info, taps, d4, second, sp3, first, sp2, grid, sp1)


def split_planes(ref, height, width):
    planes = []
    for yp in range(2):
        for xp in range(2):
            planes.append(
                jnp.concatenate(
                    [
                        ref[pl.ds((2 * a + yp) * width + xp, width // 2, stride=2), :]
                        for a in range(height // 2)
                    ],
                    0,
                )
            )
    return planes


def merge_planes(ref, planes, height, width):
    half = width // 2
    for yp in range(2):
        for xp in range(2):
            for a in range(height // 2):
                ref[pl.ds((2 * a + yp) * width + xp, half, stride=2), :] = planes[2 * yp + xp][
                    a * half : a * half + half
                ]


def stride_taps(planes, width):
    pieces = []
    for ky in range(3):
        for kx in range(3):
            v = planes[2 * (ky != 1) + (kx != 1)]
            v = shift_in(v, 1, width) if kx == 0 else v
            pieces.append((shift_out(v, 1, width) if ky == 0 else v).astype(bf16))
    return jnp.concatenate(pieces, 1)


def stride_taps_back(grad, width):
    planes = [None] * 4
    channels = grad.shape[1] // 9
    for ky in range(3):
        for kx in range(3):
            t = 3 * ky + kx
            v = grad[:, t * channels : (t + 1) * channels]
            v = shift_out(v, -1, width) if ky == 0 else v
            v = shift_in(v, -1, width) if kx == 0 else v
            at = 2 * (ky != 1) + (kx != 1)
            planes[at] = v if planes[at] is None else planes[at] + v
    return planes


def full_taps(v, width):
    across = [shift_in(v, 1 - kx, width).astype(bf16) for kx in range(3)]
    return jnp.concatenate(
        [shift_out(across[kx], 1 - ky, width) for ky in range(3) for kx in range(3)], 1
    )


def full_taps_back(grad, width):
    channels = grad.shape[1] // 9
    total = None
    for kx in range(3):
        column = None
        for ky in range(3):
            t = 3 * ky + kx
            v = shift_out(grad[:, t * channels : (t + 1) * channels], ky - 1, width)
            column = v if column is None else column + v
        column = shift_in(column, kx - 1, width)
        total = column if total is None else total + column
    return total


HY = 16
CELLS = HY * HX


def region_kernel(
    slab_ref, counts_ref, l0_ref, l1_ref, l2_ref, l3_ref, anchors_ref, goals_ref,
    s0_ref, s1_ref, s2_ref, s3_ref, s4_ref, s5_ref, s6_ref, s7_ref,
    f_in, z1_in, z2_in, z3_in, z4_in, w1_in, w2_in, w3_in, w4_in,
    maps_ref, own_ref, core_ref, out_ref, d4_out, sp3_out, sp2_out, sp1_out,
    f_ref, z1_ref, z2_ref, z3_ref, z4_ref, w1_ref, w2_ref, w3_ref, w4_ref,
    d4_ref, sp3_ref, sp2_ref, sp1_ref, bird_scr, acc2, acc1, accg, back_sems,
    wv, gr, sems,
    l1_scr, l2_scr, zu1_scr, zu2_scr, zu3_scr, head_scr, maps_scr, two_scr, three_scr,
):
    slab = slab_ref[0]
    chip, core = batch_place(slab_ref)
    copies = []
    late = (s0_ref, s1_ref, s2_ref, s3_ref, s4_ref, s5_ref, s6_ref, s7_ref)
    for n, (ref, (chips, slots)) in enumerate(zip(late, LATE_ORDER * 2)):
        for k in range(4):
            shard = jnp.bitwise_xor(slab_ref[2], slots[k])
            at = chunk_start(chip, core if n < 4 else 1 - core, chips[k])
            copies.append(
                pltpu.make_async_copy(
                    ref.at[k // 2, k % 2],
                    wv.at[shard, pl.ds(at, CHUNK_T)],
                    sems.at[len(copies)],
                )
            )
    for c in copies:
        c.start()
    arrive = begin(
        (f_in, z1_in, z2_in, z3_in, z4_in, w1_in, w2_in, w3_in, w4_in),
        (f_ref, z1_ref, z2_ref, z3_ref, z4_ref, w1_ref, w2_ref, w3_ref, w4_ref),
        back_sems,
    )
    gr[0 : PLANE_T0 + 1] = jnp.zeros((PLANE_T0 + 1, TILE, LANES), bf16)
    gr[PLANE_T0 + 1 + PLANE_T : GRAD_T] = jnp.zeros((GRAD_T - PLANE_T0 - 1 - PLANE_T, TILE, LANES), bf16)
    for slot, ref in enumerate((l0_ref, l1_ref, l2_ref, l3_ref)):
        at = pl.multiple_of(jnp.bitwise_xor(slab, slot) * L1_R, L1_R)
        l1_scr[pl.ds(at, L1_R), :] = ref[...].astype(f32)
    level_one = l1_scr[...]
    for c in copies:
        c.wait()
    for s in range(1, SLABS):
        wv[s, 0:2] = wv[s, 0:2] + wv[s - 1, STRIDE_T : STRIDE_T + 2]

    def tiles_of(tile, tiles):
        pieces = []
        while tiles:
            s = min((tile + 1) // STRIDE_T, SLABS - 1)
            at = tile + 1 - STRIDE_T * s
            size = min(tiles, STRIDE_T - at) if s < SLABS - 1 else tiles
            pieces.append(wv[s, at : at + size])
            tile, tiles = tile + size, tiles - size
        return pieces[0] if len(pieces) == 1 else jnp.concatenate(pieces, 0)

    def narrow(tile, rows):
        return tiles_of(tile, rows // 16).reshape(rows, LANES)

    def wide(tile, rows):
        both = tiles_of(tile, rows // 8).reshape(rows // 16, 2, TILE, LANES)
        return jnp.concatenate(
            [both[:, 0].reshape(rows, LANES), both[:, 1].reshape(rows, LANES)], 1
        )

    def keep_narrow(tile, value):
        at = tile + 1
        tiles = value.shape[0] // 16
        gr[at : at + tiles] = value.astype(bf16).reshape(tiles, TILE, LANES)

    def keep_wide(tile, value):
        at = tile + 1
        tiles = value.shape[0] // 16
        value = value.astype(bf16)
        left = value[:, 0:128].reshape(tiles, 1, TILE, LANES)
        right = value[:, 128:256].reshape(tiles, 1, TILE, LANES)
        gr[at : at + 2 * tiles] = jnp.concatenate([left, right], 1).reshape(2 * tiles, TILE, LANES)

    t_two, t_three, t_up1, t_up2, t_up3, t_head = 297, 369, 513, 657, 721, 1233

    taps_two = stride_taps(split_planes(l1_scr, 16, 32), 16)
    z2 = mm(taps_two, narrow(t_two, 1152))
    level_two = silu(z2).astype(bf16)
    l2_scr[...] = level_two.astype(f32)
    taps_three = stride_taps(split_planes(l2_scr, 8, 16), 8)
    z3 = mm(taps_three, wide(t_three, 1152))
    level_three = silu(z3).astype(bf16)

    taps_up = full_taps(level_one, 32)
    zu1_scr[...] = mm(taps_up, wide(t_up1, 1152))
    for g in range(4):
        zu2_scr[g] = mm(level_two, wide(t_up2 + 16 * g, 128))
    for g in range(16):
        zu3_scr[g] = mm(level_three, wide(t_up3 + 32 * g, 256))

    lane = lane_of((96, LANES))
    rows = narrow(t_head, 96).astype(f32)
    for c in range(8):
        head_scr[pl.ds(c, 96, stride=8), :] = jnp.where(lane < 16, lane_roll(rows, -16 * c), 0.0)
    head = head_scr[...].astype(bf16)
    head_a, head_b, head_c = head[0:256], head[256:512], head[512:768]
    joined_a = silu(zu1_scr[...]).astype(bf16)
    for g in range(4):
        p, q = g // 2, g % 2
        part = mm(silu(zu2_scr[g]).astype(bf16), head_b)
        for a in range(8):
            two_scr[pl.ds((2 * a + p) * HX + q, 16, stride=2), :] = part[16 * a : 16 * a + 16]
    for g in range(16):
        p, q = g // 4, g % 4
        part = mm(silu(zu3_scr[g]).astype(bf16), head_c)
        for a in range(4):
            three_scr[pl.ds((4 * a + p) * HX + q, 8, stride=4), :] = part[8 * a : 8 * a + 8]
    maps = mm(joined_a, head_a) + two_scr[...] + three_scr[...]
    maps = jnp.transpose(maps)[0:16]
    own = jnp.zeros((16, 128), f32)
    for s in range(SLABS):
        own = own + jnp.where(slab == s, maps[:, 128 * s : 128 * s + 128], 0.0)
    for i in range(HY // SLABS):
        maps_ref[0, :, i, :] = own[:, HX * i : HX * i + HX]

    live_count = counts_ref[0]
    anchors = anchors_ref[...]
    slot = row_of((40, CELLS))
    place = lane_of((40, CELLS))
    positive = [
        jnp.sum(
            jnp.logical_and(anchors == place + k * CELLS, slot < live_count).astype(f32),
            axis=0,
            keepdims=True,
        )
        for k in range(2)
    ]
    row = row_of((16, CELLS))
    second = jnp.logical_or(row == 1, row >= 9)
    marked = jnp.where(second, positive[1], positive[0])
    share = 1.0 / jnp.maximum(live_count.astype(f32), 1.0)
    class_grad = (sigmoid(maps) - marked) * (1.0 / (2.0 * CELLS))
    box_grad = jnp.clip(maps - goals_ref[...], -1.0, 1.0) * marked * share
    dmaps = jnp.where(row < 2, class_grad, box_grad)
    dmaps = jnp.transpose(jnp.concatenate([dmaps, jnp.zeros((LANES - 16, CELLS), f32)], 0))
    maps_scr[...] = dmaps
    low = dmaps.astype(bf16)

    dhead_a = mm_tn(joined_a, low)
    dz = mm_nt(low, head_a) * silu_slope(zu1_scr[...])
    dz = dz.astype(bf16)
    keep_wide(t_up1, mm_tn(taps_up, dz))
    dlevel_one = full_taps_back(mm_nt(dz, wide(t_up1, 1152)), 32)

    dhead_b = jnp.zeros((256, LANES), f32)
    dlevel_two = jnp.zeros((128, 128), f32)
    for g in range(4):
        p, q = g // 2, g % 2
        part = jnp.concatenate(
            [maps_scr[pl.ds((2 * a + p) * HX + q, 16, stride=2), :] for a in range(8)], 0
        ).astype(bf16)
        z = zu2_scr[g]
        dhead_b = dhead_b + mm_tn(silu(z).astype(bf16), part)
        dz = (mm_nt(part, head_b) * silu_slope(z)).astype(bf16)
        keep_wide(t_up2 + 16 * g, mm_tn(level_two, dz))
        dlevel_two = dlevel_two + mm_nt(dz, wide(t_up2 + 16 * g, 128))
    dhead_c = jnp.zeros((256, LANES), f32)
    dlevel_three = jnp.zeros((32, 256), f32)
    for g in range(16):
        p, q = g // 4, g % 4
        part = jnp.concatenate(
            [maps_scr[pl.ds((4 * a + p) * HX + q, 8, stride=4), :] for a in range(4)], 0
        ).astype(bf16)
        z = zu3_scr[g]
        dhead_c = dhead_c + mm_tn(silu(z).astype(bf16), part)
        dz = (mm_nt(part, head_c) * silu_slope(z)).astype(bf16)
        keep_wide(t_up3 + 32 * g, mm_tn(level_three, dz))
        dlevel_three = dlevel_three + mm_nt(dz, wide(t_up3 + 32 * g, 256))

    head_scr[...] = jnp.concatenate([dhead_a, dhead_b, dhead_c], 0)
    rows = jnp.zeros((96, LANES), f32)
    for c in range(8):
        piece = jnp.where(lane < 16, head_scr[pl.ds(c, 96, stride=8), :], 0.0)
        rows = rows + lane_roll(piece, 16 * c)
    keep_narrow(t_head, rows)

    dz = (dlevel_three * silu_slope(z3)).astype(bf16)
    keep_wide(t_three, mm_tn(taps_three, dz))
    merge_planes(l2_scr, stride_taps_back(mm_nt(dz, wide(t_three, 1152)), 8), 8, 16)
    dlevel_two = dlevel_two + l2_scr[...]
    dz = (dlevel_two * silu_slope(z2)).astype(bf16)
    keep_narrow(t_two, mm_tn(taps_two, dz))
    merge_planes(l1_scr, stride_taps_back(mm_nt(dz, narrow(t_two, 1152)), 16), 16, 32)
    dlevel_one = dlevel_one + l1_scr[...]
    l1_scr[...] = dlevel_one
    level_grad = l1_scr[pl.ds(pl.multiple_of(slab * L1_R, L1_R), L1_R), :]
    for s in range(SLABS):

        @pl.when(slab == s)
        def _(s=s):
            start = (15 - 4 * s) * LANES + 16 + 28 * s
            for t in (0, 1) + tuple(range(SHARD_T - 4, PAD_T)):
                tile = STRIDE_T * s - 1 + t
                row = row_of((TILE, LANES))
                if t >= SHARD_T:
                    gr[STRIDE_T * s + t] = jnp.zeros((TILE, LANES), bf16)
                    continue
                if WIDE_T[0] <= tile < WIDE_T[1]:
                    row = 32 * (t // 2) + 2 * row + t % 2
                else:
                    row = TILE * t + row
                at = row * LANES + lane_of((TILE, LANES)) - start
                inside = jnp.logical_and(at >= 0, at < SHARD)
                gr[STRIDE_T * s + t] = jnp.where(
                    inside, gr[STRIDE_T * s + t].astype(f32), 0.0
                ).astype(bf16)

    split_chunks(slab_ref, gr, STRIDE_T * slab, own_ref, core_ref)
    finish(arrive)
    spreads = (d4_ref, sp3_ref, sp2_ref, sp1_ref)
    outs = (d4_out, sp3_out, sp2_out, sp1_out)
    copies = []

    def leave(n):
        copies.extend(begin([spreads[n]], [outs[n]], back_sems, 9 + n))

    volume_back(
        slab * ROWS - 1, f_ref, level_grad, z1_ref, z2_ref, z3_ref, z4_ref, w1_ref, w2_ref, w3_ref, w4_ref,
        out_ref, *spreads, bird_scr, acc2, acc1, accg, leave,
    )
    finish(copies)


LATE_ORDER = (
    ((0, 0, 2, 2), (0, 1, 0, 1)),
    ((1, 1, 3, 3), (0, 1, 0, 1)),
    ((0, 0, 1, 1), (2, 3, 2, 3)),
    ((2, 2, 3, 3), (2, 3, 2, 3)),
)


def region(info, counts, levels, anchors, goals, late, features, kept):
    return call(
        region_kernel,
        20,
        56,
        (
            shape((1, 16, HY // SLABS, HX)),
            shape(CHUNKS, bf16),
            shape(CHUNKS, bf16),
            shape((SLABS, FC, VOX), bf16),
        )
        + tuple(shape(d, bf16) for d in SPREADS),
        [smem(), smem()] + [vmem()] * 6 + [anywhere()] * 17,
        (vmem(),) * 4 + (anywhere(),) * 4,
        [pltpu.VMEM(d, bf16) for d in BACK_IN + SPREADS]
        + [
            pltpu.VMEM((R3W, LANES), f32),
            pltpu.VMEM((6, R2W, LANES), f32),
            pltpu.VMEM((6, R1W, LANES), f32),
            pltpu.VMEM((9, RGW, LANES), f32),
            pltpu.SemaphoreType.DMA((13,)),
            pltpu.VMEM((SLABS, PAD_T, TILE, LANES), bf16),
            pltpu.VMEM((GRAD_T, TILE, LANES), bf16),
            pltpu.SemaphoreType.DMA((32,)),
            pltpu.VMEM((512, 128), f32),
            pltpu.VMEM((128, 128), f32),
            pltpu.VMEM((512, 256), f32),
            pltpu.VMEM((4, 128, 256), f32),
            pltpu.VMEM((16, 32, 256), f32),
            pltpu.VMEM((768, LANES), f32),
            pltpu.VMEM((512, LANES), f32),
            pltpu.VMEM((512, LANES), f32),
            pltpu.VMEM((512, LANES), f32),
        ],
    )(info, counts, *levels, anchors, goals, *late, features, *kept)


def swap(x, axis, bit):
    count = lax.axis_size(axis)
    return lax.ppermute(x, axis, [(i, i ^ bit) for i in range(count)])


def after(x, *earlier):
    return lax.optimization_barrier((x,) + earlier)[0]


def slab_all(x):
    return [x] + [swap(x, "slab", k) for k in range(1, SLABS)]


def plane_all(x):
    return [x] + [swap(x, "batch", 2 * k) for k in range(1, 4)]


def sum_cores(own, other):
    return [(own[k].astype(f32) + other[k].astype(f32)).astype(bf16) for k in range(4)]


def sum_chips(parts):
    total = parts[0].astype(f32)
    for k in range(1, 4):
        total = total + parts[k].astype(f32)
    return total


def send_parts(parts):
    return parts[0:1] + [swap(parts[k], "batch", 2 * k) for k in range(1, 4)]


def to_first(total, low):
    for k in range(1, SLABS):
        total = total + lax.ppermute(low, "slab", [(k, 0)]).astype(f32)
    return total


def from_first(x, slab):
    x = jnp.where(slab == 2, lax.ppermute(x, "slab", [(0, 2)]), x)
    near = lax.ppermute(x, "slab", [(0, 1), (2, 3)])
    return jnp.where(slab % 2 == 1, near, x)


def gathered_shards(own):
    batches = lax.axis_size("batch")
    share = PAD_T // batches
    chunk = lax.dynamic_slice_in_dim(own, lax.axis_index("batch") * share, share, 0)
    shards = lax.all_gather(chunk, ("slab", "batch"), axis=0, tiled=True)
    shards = shards.reshape(SLABS, 4, 2, CHUNK_T, TILE, LANES)
    late = []
    for core in range(2):
        for chips, slots in LATE_ORDER:
            part = jnp.stack([shards[s, c, core] for c, s in zip(chips, slots)])
            late.append(part.reshape((2, 2) + part.shape[1:]))
    return (shards[0, :, 0], shards[0, :, 1]), late


def even_odd(whole):
    both = whole.reshape(4, 2, CHUNK_T, TILE, LANES)
    return both[:, 0], both[:, 1]


def body(
    points, point_counts, voxel_cells, pos_anchors, pos_counts, reg_targets, params, moment1, moment2
):
    batches = lax.axis_size("batch")
    slab, batch = lax.axis_index("slab"), lax.axis_index("batch")
    direct = batches == 8
    zero = jnp.zeros_like(slab)
    info = jnp.stack([slab, batch if direct else zero, slab if direct else zero]).astype(jnp.int32)
    counts = point_counts.reshape(1, VOX)

    if direct:
        chunk, first = spread_own(info, params)
        near = jnp.stack([chunk, swap(chunk, "slab", 1)])
        far = swap(near, "slab", 2)
        first = from_first(first, slab)
        small, early = first, first[VFE_T:]
        early = plane_all(early)
    else:
        flat_rows = jnp.pad(params, (0, FLAT_R * LANES - SHARD)).reshape(FLAT_R, LANES)
        first = spread_first(flat_rows[0:VFE_R])
        small = from_first(first, slab)
        early, late = gathered_shards(spread_shard(info, flat_rows))
    encoded, s3 = encode(points, counts, voxel_cells.reshape(1, VOX), small)
    features = lax.all_to_all(encoded, "slab", 0, 0)
    if direct:
        early = jnp.stack(lax.optimization_barrier((*early, encoded))[0:4])
        early = (early, swap(early, "batch", 1))
        near, far = lax.optimization_barrier((near, far, early[0]))[0:2]
        later, near, far = lax.optimization_barrier((points, near, far))
        late = [near, swap(near, "batch", 4), far, swap(far, "batch", 2)]
        x, j1, j2, s1, s2, m1, m2 = encode_slopes(later, counts, small)
        near, near_y, far, far_x = lax.optimization_barrier((*late, x))[0:4]
        near, far = jnp.stack([near, near_y]), jnp.stack([far, far_x])
        late = [near, swap(near, "batch", 2), far, swap(far, "batch", 4)]
        features = after(features, x, near, far)
        late = late + [swap(near, "batch", 1), swap(far, "batch", 1)]
    else:
        x, j1, j2, s1, s2, m1, m2 = encode_slopes(points, counts, small)
    level, grid, first_pad, second_pad, taps, *kept = volume(info, features, early)
    if direct:
        near, near_x, far, far_y, near_c, far_c = late
        near_x, far_y, near_c, far_c = lax.optimization_barrier(
            (near_x, far_y, near_c, far_c, level)
        )[0:4]
        late = [near, near_x, far, far_y, near_c, swap(near_x, "batch", 1), far_c, swap(far_y, "batch", 1)]
    goals = jnp.pad(reg_targets.reshape(14, CELLS), ((2, 0), (0, 0)))
    levels = slab_all(level)
    maps, quarter_own, quarter_core, feature_back, *spreads = region(
        info, pos_counts, levels, pos_anchors.reshape(40, 1), goals, late, features, kept
    )
    feature_grad = lax.all_to_all(feature_back, "slab", 0, 0)
    if direct:
        quarter_other = swap(quarter_core, "batch", 1)
        quarter = lax.optimization_barrier((quarter_own, quarter_other, feature_back))[0:2]
        quarter = sum_cores(*quarter)
        spreads[0], *quarter = lax.optimization_barrier((spreads[0], *quarter))
        quarter = send_parts(quarter)
    early_own, early_core = volume_weights(info, (grid, first_pad, second_pad, taps), spreads)
    if direct:
        feature_grad, early_own, early_core, *quarter = lax.optimization_barrier(
            (feature_grad, early_own, early_core, *quarter)
        )
        parts = sum_cores(early_own, swap(early_core, "batch", 1))
        feature_grad, *parts = lax.optimization_barrier((feature_grad, *parts))
        parts = send_parts(parts)
    back = encode_back(counts, small, feature_grad, j2, s3, m2)
    if direct:
        chunk = sum_chips(quarter)
        early_chunk = sum_chips(lax.optimization_barrier((*parts, back[0]))[0:4])
        early_low = early_chunk.astype(bf16)
        d2, early_low, chunk = lax.optimization_barrier((back[0], early_low, chunk))
        back = [d2] + list(back[1:])
        early_chunk = to_first(early_chunk, early_low)
    points_grad, vfe_grad = points_back(counts, small, back, (x, j1, s1, s2, m1))
    if direct:
        early_chunk, vfe_grad = lax.optimization_barrier((early_chunk, vfe_grad))
        chunk = (chunk + jnp.where(slab == 0, early_chunk, 0.0)).astype(bf16)
        squares = jnp.sum(jnp.square(chunk.astype(f32)))
        final = plane_all(chunk)
    else:
        whole = jnp.stack([quarter_own, quarter_core], 1).astype(f32)
        whole_early = lax.psum(jnp.stack([early_own, early_core], 1).astype(f32), "slab")
        whole = lax.psum(whole + jnp.where(slab == 0, whole_early, 0.0), "batch").astype(bf16)
        squares = jnp.sum(jnp.square(whole.astype(f32))) / batches
        final = even_odd(whole)

    total = vfe_grad + jnp.pad(jnp.broadcast_to(squares, (8, LANES)), ((VFE_R, 0), (0, 0)))
    for axis, size in (("slab", SLABS), ("batch", batches)):
        bit = 1
        while bit < size:
            total = total + swap(total, axis, bit)
            if direct and axis == "batch" and bit == 1:
                *final, total = lax.optimization_barrier((*final, total))
                final = jnp.stack(final)
                final = (final, swap(final, "batch", 1))
            bit *= 2
    new_params, new_moment1, new_moment2, norm = update_shard(
        info, *final, total, params, moment1, moment2
    )
    return (maps, points_grad, new_moment1, new_moment2, new_params, norm.reshape(()))


def solution(mesh):
    in_specs = (
        P(None, None, ("batch", "slab")),
        P(("batch", "slab")),
        P(("batch", "slab")),
        P("batch", None),
        P("batch"),
        P("batch", None, None, None),
        P("slab"),
        P("slab"),
        P("slab"),
    )
    out_specs = (
        P("batch", None, "slab", None),
        P(None, None, ("batch", "slab")),
        P("slab"),
        P("slab"),
        P("slab"),
        P(),
    )
    return jax.shard_map(body, mesh=mesh, in_specs=in_specs, out_specs=out_specs, check_vma=False)
```

```python
import functools
import math

import jax
import jax.numpy as jnp
from jax import lax
from jax.experimental import pallas as pl
from jax.experimental.pallas import tpu as pltpu
from jax.sharding import PartitionSpec as P

VF1 = 16
VF2 = 64
FC = 128
C3 = 64
STEP = 10
GY = 32
GX = 64
PTS = 35
VOX = 512
SLABS = 4
ROWS = GY // SLABS
LANES = 128
NPARAM = 2537584
SHARD = NPARAM // SLABS

TILE = 16
STRIDE_T = 310
SHARD_T = 312
PAD_T = 320
FLAT_R = 4960
EARLY_T = 288
EARLY_R = EARLY_T * TILE
VFE_T = 10
VFE_R = VFE_T * TILE
PLANE_T0 = 297
PLANE_T = 942
GRAD_T = 3 * STRIDE_T + PAD_T
CHUNK_T = PAD_T // 8
WIDE_T = (369, 1233)

beta_one = 0.9
beta_two = 0.999
adam_eps = 1e-08
learn_rate = 0.02
weight_decay = 0.01
clip_level = 0.002

f32 = jnp.float32
bf16 = jnp.bfloat16


def call(kernel, micros, megabytes, out_shape, in_specs, out_specs, scratch=()):
    return pl.pallas_call(
        kernel,
        out_shape=out_shape,
        in_specs=in_specs,
        out_specs=out_specs,
        scratch_shapes=list(scratch),
        compiler_params=pltpu.CompilerParams(vmem_limit_bytes=megabytes * 1024 * 1024),
        cost_estimate=pl.CostEstimate(
            flops=int(micros * 1e9), transcendentals=0, bytes_accessed=int(micros * 3e6)
        ),
    )


def vmem():
    return pl.BlockSpec(memory_space=pltpu.VMEM)


def smem():
    return pl.BlockSpec(memory_space=pltpu.SMEM)


def anywhere():
    return pl.BlockSpec(memory_space=pl.ANY)


def held(dims, dtype=bf16):
    return pltpu.VMEM(dims, dtype)


def shape(dims, dtype=f32):
    return jax.ShapeDtypeStruct(dims, dtype)


def mm(a, b):
    return lax.dot_general(a, b, (((1,), (0,)), ((), ())), preferred_element_type=f32)


def mm_nt(a, b):
    return lax.dot_general(a, b, (((1,), (1,)), ((), ())), preferred_element_type=f32)


def mm_tn(a, b):
    return lax.dot_general(a, b, (((0,), (0,)), ((), ())), preferred_element_type=f32)


def sigmoid(z):
    return 0.5 * jnp.tanh(0.5 * z) + 0.5


def silu(z):
    return z * sigmoid(z)


def silu_slope(z):
    s = sigmoid(z)
    return s * (1.0 + z * (1.0 - s))


def lane_of(dims):
    return lax.broadcasted_iota(jnp.int32, dims, len(dims) - 1)


def row_of(dims):
    return lax.broadcasted_iota(jnp.int32, dims, 0)


def lane_roll(x, shift):
    shift = shift % x.shape[-1]
    return x if shift == 0 else pltpu.roll(x, shift, x.ndim - 1)


def shift_in(v, d, width):
    if d == 0:
        return v
    place = row_of(v.shape) % width
    keep = place > 0 if d > 0 else place < width - 1
    return jnp.where(keep, pltpu.roll(v, d % v.shape[0], 0), 0.0)


def shift_out(v, d, width):
    if d == 0:
        return v
    edge = jnp.zeros((width,) + v.shape[1:], v.dtype)
    if d > 0:
        return jnp.concatenate([edge, v[:-width]], 0)
    return jnp.concatenate([v[width:], edge], 0)


def begin(sources, targets, sems, first=0):
    copies = [
        pltpu.make_async_copy(a, b, sems.at[first + n])
        for n, (a, b) in enumerate(zip(sources, targets))
    ]
    for c in copies:
        c.start()
    return copies


def finish(copies):
    for c in copies:
        c.wait()


def batch_place(info_ref):
    return info_ref[1] // 2, info_ref[1] % 2


def chunk_start(chip, core, slot):
    return CHUNK_T * (2 * jnp.bitwise_xor(chip, slot) + core)


def join_chunks(info_ref, out_ref, own_ref, core_ref):
    chip, core = batch_place(info_ref)
    for slot in range(4):
        out_ref[pl.ds(chunk_start(chip, core, slot), CHUNK_T)] = own_ref[slot]
        out_ref[pl.ds(chunk_start(chip, 1 - core, slot), CHUNK_T)] = core_ref[slot]


def split_chunks(info_ref, scr, base, own_ref, core_ref):
    chip, core = batch_place(info_ref)
    for slot in range(4):
        own_ref[slot] = scr[pl.ds(base + chunk_start(chip, core, slot), CHUNK_T)].astype(bf16)
        core_ref[slot] = scr[pl.ds(base + chunk_start(chip, 1 - core, slot), CHUNK_T)].astype(bf16)


CHUNKS = (4, CHUNK_T, TILE, LANES)


def spread_kernel(slab_ref, flat_ref, out_ref, nat):
    nat[...] = jnp.zeros_like(nat)
    span = 480
    for s in range(SLABS):

        @pl.when(slab_ref[0] == s)
        def _(s=s):
            lanes, first = 16 + 28 * s, 15 - 4 * s
            lane = lane_of((span, LANES))
            count = FLAT_R // span + (FLAT_R % span > 0)
            for i in range(count):
                r0 = i * span
                n = min(span, FLAT_R - r0)
                rolled = lane_roll(flat_ref[r0 : r0 + n, :], lanes)
                nat[first + r0 : first + r0 + n, :] += jnp.where(lane[:n] >= lanes, rolled, 0.0)
                nat[first + r0 + 1 : first + r0 + 1 + n, :] += jnp.where(
                    lane[:n] < lanes, rolled, 0.0
                )
            low = max(0, min(SHARD_T // 2, (WIDE_T[0] - STRIDE_T * s + 1) // 2))
            high = max(low, min(SHARD_T // 2, (WIDE_T[1] - STRIDE_T * s + 1) // 2))
            for a, b, wide in ((0, low, False), (low, high, True), (high, SHARD_T // 2, False)):

                def block(i, carry, wide=wide):
                    base = pl.multiple_of(32 * i, 32)
                    if wide:
                        even = nat[pl.ds(base, 16, stride=2), :]
                        odd = nat[pl.ds(base + 1, 16, stride=2), :]
                    else:
                        even = nat[pl.ds(base, 16), :]
                        odd = nat[pl.ds(base + 16, 16), :]
                    out_ref[2 * i] = even.astype(bf16)
                    out_ref[2 * i + 1] = odd.astype(bf16)
                    return carry

                if b > a:
                    lax.fori_loop(a, b, block, 0, unroll=4)

    for t in range(SHARD_T, PAD_T):
        out_ref[t] = jnp.zeros((TILE, LANES), bf16)


def spread_shard(slab, flat_rows):
    return call(
        spread_kernel,
        4,
        56,
        shape((PAD_T, TILE, LANES), bf16),
        [smem(), vmem()],
        vmem(),
        [pltpu.VMEM((5120, LANES), f32)],
    )(slab, flat_rows)


CHUNK_R = CHUNK_T * TILE
CHUNK_N = CHUNK_R * LANES
WHOLE_R = SHARD // LANES // 8 * 8
REST = SHARD - SHARD // LANES * LANES


def flat_tail(flat_ref):
    rest_r = SHARD // LANES - WHOLE_R
    rows = flat_ref[pl.ds(WHOLE_R * LANES, rest_r * LANES)].reshape(rest_r, LANES)
    return rows, flat_ref[pl.ds(SHARD - REST, REST)].reshape(1, REST)


def spread_own_kernel(info_ref, flat_ref, chunk_ref, first_ref, x_scr, nat):
    batch = info_ref[1]

    @pl.when(batch == 0)
    def _():
        x_scr[0:TILE, :] = jnp.zeros((TILE, LANES), f32)
        x_scr[TILE:, :] = flat_ref[pl.ds(0, CHUNK_N)].reshape(CHUNK_R, LANES)

    @pl.when(jnp.logical_and(batch > 0, batch < 7))
    def _():
        start = pl.multiple_of(batch * CHUNK_N - TILE * LANES, 1024)
        rows = CHUNK_R + TILE
        x_scr[...] = flat_ref[pl.ds(start, rows * LANES)].reshape(rows, LANES)

    @pl.when(batch == 7)
    def _():
        first_r = 7 * CHUNK_R - TILE
        whole = WHOLE_R - first_r
        x_scr[0:whole, :] = flat_ref[pl.ds(first_r * LANES, whole * LANES)].reshape(whole, LANES)
        x_scr[whole:, :] = jnp.zeros((CHUNK_R + TILE - whole, LANES), f32)
        rows, last = flat_tail(flat_ref)
        x_scr[whole : whole + rows.shape[0], :] = rows
        x_scr[whole + rows.shape[0] : whole + rows.shape[0] + 1, 0:REST] = last

    def shifted(first, lanes, rows):
        lane = lane_of((rows, LANES))
        here = lane_roll(x_scr[TILE - first : TILE - first + rows, :], lanes)
        above = lane_roll(x_scr[TILE - 1 - first : TILE - 1 - first + rows, :], lanes)
        return jnp.where(lane >= lanes, here, above)

    for s in range(SLABS):

        @pl.when(info_ref[0] == s)
        def _(s=s):
            nat[...] = shifted(15 - 4 * s, 16 + 28 * s, CHUNK_R)
            low = max(0, min(SHARD_T // 2, (WIDE_T[0] - STRIDE_T * s + 1) // 2))
            high = max(low, min(SHARD_T // 2, (WIDE_T[1] - STRIDE_T * s + 1) // 2))
            for i in range(CHUNK_T // 2):
                block = batch * (CHUNK_T // 2) + i
                wide = jnp.logical_and(block >= low, block < high)
                even = nat[pl.ds(32 * i, 16, stride=2), :]
                odd = nat[pl.ds(32 * i + 1, 16, stride=2), :]
                top, bottom = nat[32 * i : 32 * i + 16, :], nat[32 * i + 16 : 32 * i + 32, :]
                chunk_ref[2 * i] = jnp.where(wide, even, top).astype(bf16)
                chunk_ref[2 * i + 1] = jnp.where(wide, odd, bottom).astype(bf16)

    first_ref[VFE_T : VFE_T + CHUNK_T] = chunk_ref[...]
    x_scr[0:TILE, :] = jnp.zeros((TILE, LANES), f32)
    x_scr[TILE : TILE + VFE_R, :] = flat_ref[pl.ds(0, VFE_R * LANES)].reshape(VFE_R, LANES)
    rows = shifted(15, 16, VFE_R).astype(bf16)
    first_ref[0:VFE_T] = rows.reshape(VFE_T, TILE, LANES)


def spread_own(info, params):
    return call(
        spread_own_kernel,
        3,
        56,
        (shape((CHUNK_T, TILE, LANES), bf16), shape((VFE_T + CHUNK_T, TILE, LANES), bf16)),
        [smem(), vmem()],
        (vmem(), vmem()),
        [pltpu.VMEM((CHUNK_R + TILE, LANES), f32), pltpu.VMEM((CHUNK_R, LANES), f32)],
    )(info, params)


def spread_first_kernel(flat_ref, out_ref, nat):
    lanes, first = 16, 15
    lane = lane_of((VFE_R, LANES))
    rolled = lane_roll(flat_ref[...], lanes)
    nat[...] = jnp.zeros_like(nat)
    nat[first : first + VFE_R, :] += jnp.where(lane >= lanes, rolled, 0.0)
    nat[first + 1 : first + 1 + VFE_R, :] += jnp.where(lane < lanes, rolled, 0.0)
    out_ref[...] = nat[0:VFE_R, :].astype(bf16).reshape(VFE_T, TILE, LANES)


def spread_first(flat_rows):
    return call(
        spread_first_kernel,
        1,
        56,
        shape((VFE_T, TILE, LANES), bf16),
        [vmem()],
        vmem(),
        [pltpu.VMEM((VFE_R + 32, LANES), f32)],
    )(flat_rows)


UPDATE_R = 1024
UPDATE_N = UPDATE_R * LANES


def update_kernel(
    slab_ref, own_ref, core_ref, vfe_ref, params_ref, moment1_ref, moment2_ref,
    new_params_ref, new_moment1_ref, new_moment2_ref, norm_ref,
    quarter_ref, nat, grads,
):
    step = pl.program_id(0)

    @pl.when(step == 0)
    def _():
        gather_grads(slab_ref, own_ref, core_ref, vfe_ref, norm_ref, quarter_ref, nat, grads)

    def update(source, target, clipped):
        param = params_ref[source]
        moment1 = beta_one * moment1_ref[source] + (1.0 - beta_one) * clipped
        moment2 = beta_two * moment2_ref[source] + (1.0 - beta_two) * clipped * clipped
        direction = (
            moment1
            * (1.0 / (1.0 - beta_one**STEP))
            / (jnp.sqrt(moment2 * (1.0 / (1.0 - beta_two**STEP))) + adam_eps)
        )
        new_moment1_ref[target] = moment1
        new_moment2_ref[target] = moment2
        new_params_ref[target] = param - learn_rate * (direction + weight_decay * param)

    last = SHARD // UPDATE_N

    @pl.when(step < last)
    def _():
        rows = pl.ds(pl.multiple_of(step * UPDATE_R, UPDATE_R), UPDATE_R)
        at = pl.ds(pl.multiple_of(step * UPDATE_N, UPDATE_N), UPDATE_N)
        update(at, pl.ds(0, UPDATE_N), grads[rows, :].reshape(UPDATE_N))

    @pl.when(step == last)
    def _():
        first = last * UPDATE_R
        whole = WHOLE_R - first
        rest = SHARD // LANES - WHOLE_R
        for r0, n in ((0, whole), (whole, rest)):
            update(
                pl.ds((first + r0) * LANES, n * LANES),
                pl.ds(r0 * LANES, n * LANES),
                grads[first + r0 : first + r0 + n, :].reshape(n * LANES),
            )
        r0 = whole + rest
        update(
            pl.ds(SHARD - REST, REST),
            pl.ds(r0 * LANES, REST),
            grads[first + r0 : first + r0 + 1, 0:REST].reshape(REST),
        )


def gather_grads(slab_ref, own_ref, core_ref, vfe_ref, norm_ref, quarter_ref, nat, grads):
    join_chunks(slab_ref, quarter_ref, own_ref, core_ref)
    vfe = vfe_ref[0:VFE_R, :]
    squares = vfe_ref[VFE_R : VFE_R + 1, :][0, 0] + jnp.sum(vfe * vfe)
    norm = jnp.sqrt(jnp.broadcast_to(squares, (8, LANES)))
    norm_ref[0, 0] = norm[0, 0]
    scale = (clip_level / jnp.maximum(norm, clip_level))[0:1, :]
    grads[FLAT_R:, :] = jnp.zeros((grads.shape[0] - FLAT_R, LANES), f32)
    span = 480
    for s in range(SLABS):

        @pl.when(slab_ref[0] == s)
        def _(s=s):
            lanes, first = 16 + 28 * s, 15 - 4 * s
            low = max(0, min(SHARD_T // 2, (WIDE_T[0] - STRIDE_T * s + 1) // 2))
            high = max(low, min(SHARD_T // 2, (WIDE_T[1] - STRIDE_T * s + 1) // 2))
            for a, b, wide in ((0, low, False), (low, high, True), (high, SHARD_T // 2, False)):

                def block(i, carry, wide=wide):
                    base = pl.multiple_of(32 * i, 32)
                    even, odd = quarter_ref[2 * i].astype(f32), quarter_ref[2 * i + 1].astype(f32)
                    if wide:
                        nat[pl.ds(base, 16, stride=2), :] = even
                        nat[pl.ds(base + 1, 16, stride=2), :] = odd
                    else:
                        nat[pl.ds(base, 16), :] = even
                        nat[pl.ds(base + 16, 16), :] = odd
                    return carry

                if b > a:
                    lax.fori_loop(a, b, block, 0, unroll=4)
            if s == 0:
                nat[0:VFE_R, :] = vfe
            lane = lane_of((span, LANES))
            count = FLAT_R // span + (FLAT_R % span > 0)
            for i in range(count):
                r0 = i * span
                n = min(span, FLAT_R - r0)
                here = lane_roll(nat[first + r0 : first + r0 + n, :], -lanes)
                after = lane_roll(nat[first + r0 + 1 : first + r0 + 1 + n, :], -lanes)
                grads[r0 : r0 + n, :] = jnp.where(lane[:n] < LANES - lanes, here, after) * scale


def update_shard(info, own, core, vfe, params, moment1, moment2):
    block = pl.BlockSpec((UPDATE_N,), lambda i: (i,))
    steps = pl.cdiv(SHARD, UPDATE_N)
    return pl.pallas_call(
        update_kernel,
        grid=(steps,),
        out_shape=(shape((SHARD,)),) * 3 + (shape((1, 1)),),
        in_specs=[smem()] + [vmem()] * 6,
        out_specs=(block,) * 3 + (smem(),),
        scratch_shapes=[
            pltpu.VMEM((PAD_T, TILE, LANES), bf16),
            pltpu.VMEM((5120, LANES), f32),
            pltpu.VMEM((steps * UPDATE_R, LANES), f32),
        ],
        compiler_params=pltpu.CompilerParams(vmem_limit_bytes=24 * 1024 * 1024),
    )(info, own, core, vfe, params, moment1, moment2)


PART = 5
PARTS = PTS // PART
WIDE = PART * VOX
VFE_SCRATCH = [
    pltpu.VMEM((VOX // LANES, PTS * 16, LANES), f32),
    pltpu.VMEM((16, LANES), f32),
    pltpu.VMEM((64, LANES), f32),
]


def spread_points(points_ref, x_scr):
    x_scr[...] = jnp.zeros_like(x_scr)
    for c in range(7):
        plane = points_ref[c].astype(f32)
        for b in range(VOX // LANES):
            x_scr[b, pl.ds(c, PTS, stride=16), :] = plane[:, b * LANES : (b + 1) * LANES]


def vfe_weights(rows_ref, w1_scr, w2_scr):
    line = rows_ref[0].astype(f32)
    lane = lane_of((16, LANES))
    for o in range(VF1):
        w1_scr[o : o + 1, :] = jnp.where(lane < 7, lane_roll(line, -(16 + 7 * o)), 0.0)[15:16]
    two = rows_ref[1].astype(f32)
    for k in range(4):
        w2_scr[pl.ds(k, 16, stride=4), :] = jnp.where(lane < 32, lane_roll(two, -32 * k), 0.0)
    w1 = w1_scr[...].astype(bf16)[:, 0:16]
    w2 = w2_scr[...]
    w2a = w2.astype(bf16)[:, 0:16]
    w2b = lane_roll(w2, -16).astype(bf16)[:, 0:16]
    w3 = rows_ref[2:10].reshape(FC, LANES)
    w3a = w3[:, 0:64]
    w3b = lane_roll(w3.astype(f32), -64).astype(bf16)[:, 0:64]
    return w1, w2a, w2b, w3a, w3b


def points_part(ref, i):
    return jnp.concatenate(
        [
            ref[b, pl.ds(pl.multiple_of((PART * i + k) * 16, 16), 16), :]
            for k in range(PART)
            for b in range(VOX // LANES)
        ],
        1,
    )


def set_points_part(ref, i, value):
    for k in range(PART):
        for b in range(VOX // LANES):
            at = k * VOX + b * LANES
            ref[b, pl.ds(pl.multiple_of((PART * i + k) * 16, 16), 16), :] = value[:, at : at + LANES]


def part_sum(value):
    total = value[:, 0:VOX]
    for k in range(1, PART):
        total = total + value[:, k * VOX : (k + 1) * VOX]
    return total


def valid_part(i, counts):
    return jnp.concatenate([(PART * i + k < counts).astype(f32) for k in range(PART)], 1)


def widen(value):
    return jnp.concatenate([value] * PART, 1)


def vfe_front(weights, counts, inverse, x_scr, j1_ref, j2_ref, kept=None, done=None):
    w1, w2a, w2b, w3a, w3b = weights
    total = jnp.zeros((VF1, VOX), f32)
    for i in range(PARTS):
        x = points_part(x_scr, i).astype(bf16)
        z = mm(w1, x)
        value = silu(z)
        j1_ref[i] = value.astype(bf16)
        if kept is not None:
            kept[0][i] = x
            kept[1][i] = silu_slope(z).astype(bf16)
        total = total + part_sum(value * valid_part(i, counts))
    mean_one = (total * inverse).astype(bf16)
    shared_two = widen(mm(w2b, mean_one))
    total = jnp.zeros((VF2, VOX), f32)
    for i in range(PARTS):
        z = mm(w2a, j1_ref[i]) + shared_two
        value = silu(z)
        j2_ref[i] = value.astype(bf16)
        if kept is not None:
            kept[2][i] = silu_slope(z).astype(bf16)
            done(i)
        total = total + part_sum(value * valid_part(i, counts))
    mean_two = (total * inverse).astype(bf16)
    shared_three = widen(mm(w3b, mean_two))
    return mean_one, mean_two, shared_three


def encode_kernel(
    points_ref, counts_ref, cells_ref, rows_ref, out_ref, s3_ref,
    x_scr, w1_scr, w2_scr, j1_scr, j2_scr, s3_scr, sems,
):
    spread_points(points_ref, x_scr)
    weights = vfe_weights(rows_ref, w1_scr, w2_scr)
    counts = counts_ref[...]
    inverse = 1.0 / counts.astype(f32)
    _, _, shared_three = vfe_front(weights, counts, inverse, x_scr, j1_scr, j2_scr)
    w3a = weights[3]
    wide_inverse = widen(inverse)
    total = jnp.zeros((FC, VOX), f32)
    copies = []
    for i in range(PARTS):
        z = mm(w3a, j2_scr[i]) + shared_three
        gate = sigmoid(z)
        value = z * gate
        share = valid_part(i, counts) * wide_inverse
        s3_scr[i] = ((gate + value - value * gate) * share).astype(bf16)
        copies += begin([s3_scr.at[i]], [s3_ref.at[i]], sems, i)
        total = total + part_sum(value * share)
    features = total.astype(bf16)
    cells = cells_ref[...]
    row = row_of((16, VOX))
    places = jnp.where(row == 0, cells // GX, cells % GX).astype(f32).astype(bf16)
    out_ref[0:FC, :] = features
    out_ref[FC : FC + 16, :] = places
    finish(copies)


def encode(points, counts, cells, rows):
    return call(
        encode_kernel,
        10,
        56,
        (shape((FC + 16, VOX), bf16), shape((PARTS, 128, WIDE), bf16)),
        [vmem()] * 4,
        (vmem(), anywhere()),
        VFE_SCRATCH
        + [
            pltpu.VMEM((PARTS, 16, WIDE), bf16),
            pltpu.VMEM((PARTS, 64, WIDE), bf16),
            pltpu.VMEM((PARTS, 128, WIDE), bf16),
            pltpu.SemaphoreType.DMA((PARTS,)),
        ],
    )(points, counts, cells, rows)


def encode_slopes_kernel(
    points_ref, counts_ref, rows_ref,
    x_ref, j1_ref, j2_ref, s1_ref, s2_ref, m1_ref, m2_ref,
    x_scr, w1_scr, w2_scr, xs_scr, j1_scr, j2_scr, s1_scr, s2_scr, sems,
):
    spread_points(points_ref, x_scr)
    weights = vfe_weights(rows_ref, w1_scr, w2_scr)
    counts = counts_ref[...]
    inverse = 1.0 / counts.astype(f32)
    copies = []

    def done(i):
        if i == 0:
            copies.extend(begin((xs_scr, j1_scr, s1_scr), (x_ref, j1_ref, s1_ref), sems, 0))
        copies.extend(
            begin((j2_scr.at[i], s2_scr.at[i]), (j2_ref.at[i], s2_ref.at[i]), sems, 3 + 2 * i)
        )

    mean_one, mean_two, _ = vfe_front(
        weights, counts, inverse, x_scr, j1_scr, j2_scr, (xs_scr, s1_scr, s2_scr), done
    )
    m1_ref[...] = mean_one
    m2_ref[...] = mean_two
    finish(copies)


LOW = (PARTS, 16, WIDE)
MID = (PARTS, 64, WIDE)
HIGH = (PARTS, 128, WIDE)


def encode_slopes(points, counts, rows):
    return call(
        encode_slopes_kernel,
        7,
        56,
        tuple(shape(d, bf16) for d in (LOW, LOW, MID, LOW, MID, (VF1, VOX), (VF2, VOX))),
        [vmem()] * 3,
        (anywhere(),) * 5 + (vmem(),) * 2,
        VFE_SCRATCH
        + [pltpu.VMEM(d, bf16) for d in (LOW, LOW, MID, LOW, MID)]
        + [pltpu.SemaphoreType.DMA((3 + 2 * PARTS,))],
    )(points, counts, rows)


def encode_back_kernel(
    counts_ref, rows_ref, g0_ref, g1_ref, g2_ref, g3_ref, j2_ref, s3_ref, m2_ref,
    d2_ref, shared_ref, weight_ref,
    w1_scr, w2_scr, j2_scr, s3_scr, d2_scr, sems,
):
    arrive = []
    for i in range(PARTS):
        arrive.append(
            begin((s3_ref.at[i], j2_ref.at[i]), (s3_scr.at[i], j2_scr.at[i]), sems, 3 * i)
        )
    _, _, _, w3a, w3b = vfe_weights(rows_ref, w1_scr, w2_scr)
    inverse = 1.0 / counts_ref[...].astype(f32)
    grad = g0_ref[...].astype(f32)
    for ref in (g1_ref, g2_ref, g3_ref):
        grad = grad + ref[...].astype(f32)
    grad_three = widen(grad)
    total = jnp.zeros((FC, VOX), f32)
    weight = jnp.zeros((FC, VF2), f32)
    leave = []
    for i in range(PARTS):
        finish(arrive[i])
        dz = grad_three * s3_scr[i].astype(f32)
        low = dz.astype(bf16)
        d2_scr[i] = mm_tn(w3a, low).astype(bf16)
        leave += begin([d2_scr.at[i]], [d2_ref.at[i]], sems, 3 * i + 2)
        total = total + part_sum(dz)
        weight = weight + mm_nt(low, j2_scr[i])
    total = total.astype(bf16)
    weight_ref[...] = jnp.concatenate([weight, mm_nt(total, m2_ref[...])], 1)
    shared_ref[...] = mm_tn(w3b, total) * inverse
    finish(leave)


def encode_back(counts, rows, grad, j2, s3, m2):
    return call(
        encode_back_kernel,
        8,
        56,
        (shape(MID, bf16), shape((VF2, VOX)), shape((FC, LANES))),
        [vmem()] * 6 + [anywhere()] * 2 + [vmem()],
        (anywhere(), vmem(), vmem()),
        VFE_SCRATCH[1:]
        + [pltpu.VMEM(d, bf16) for d in (MID, HIGH, MID)]
        + [pltpu.SemaphoreType.DMA((3 * PARTS,))],
    )(counts, rows, *grad, j2, s3, m2)


def points_back_kernel(
    counts_ref, rows_ref, d2_ref, shared_ref, w3_ref, x_ref, j1_ref, s1_ref, s2_ref, m1_ref,
    out_ref, weight_ref,
    x_scr, w1_scr, w2_scr, d1_scr, d2_scr, s2_scr, j1_scr, s1_scr, xs_scr, sems,
):
    arrive = []
    for i in range(PARTS):
        arrive.append(
            begin(
                (d2_ref.at[i], s2_ref.at[i], j1_ref.at[i]),
                (d2_scr.at[i], s2_scr.at[i], j1_scr.at[i]),
                sems,
                3 * i,
            )
        )
    late = begin((s1_ref, x_ref), (s1_scr, xs_scr), sems, 3 * PARTS)
    w1, w2a, w2b, _, _ = vfe_weights(rows_ref, w1_scr, w2_scr)
    counts = counts_ref[...]
    inverse = 1.0 / counts.astype(f32)
    grad_two = widen(shared_ref[...])
    total = jnp.zeros((VF2, VOX), f32)
    grad_w2a = jnp.zeros((VF2, VF1), f32)
    for i in range(PARTS):
        finish(arrive[i])
        dz = d2_scr[i].astype(f32) + valid_part(i, counts) * grad_two
        dz = dz * s2_scr[i].astype(f32)
        low = dz.astype(bf16)
        d1_scr[i] = mm_tn(w2a, low)
        total = total + part_sum(dz)
        grad_w2a = grad_w2a + mm_nt(low, j1_scr[i])
    total = total.astype(bf16)
    grad_w2b = mm_nt(total, m1_ref[...])
    grad_one = widen(mm_tn(w2b, total) * inverse)
    grad_w1 = jnp.zeros((VF1, 16), f32)
    finish(late)
    for i in range(PARTS):
        dz = (d1_scr[i] + valid_part(i, counts) * grad_one) * s1_scr[i].astype(f32)
        low = dz.astype(bf16)
        set_points_part(x_scr, i, mm_tn(w1, low))
        grad_w1 = grad_w1 + mm_nt(low, xs_scr[i])
    for c in range(7):
        for b in range(VOX // LANES):
            out_ref[c, :, b * LANES : (b + 1) * LANES] = x_scr[b, pl.ds(c, PTS, stride=16), :]

    lane = lane_of((16, LANES))
    w1_scr[...] = jnp.concatenate([grad_w1, jnp.zeros((16, LANES - 16), f32)], 1)
    spread = jnp.where(lane < 7, w1_scr[...], 0.0)
    line = jnp.zeros((16, LANES), f32)
    row = row_of((16, LANES))
    for o in range(VF1):
        line = line + jnp.where(row == o, lane_roll(spread, 16 + 7 * o), 0.0)
    line = jnp.sum(line, axis=0, keepdims=True)
    weight_ref[0:16, :] = jnp.where(row == 15, line, 0.0)
    w2_scr[...] = jnp.concatenate([grad_w2a, grad_w2b, jnp.zeros((64, LANES - 32), f32)], 1)
    two = jnp.zeros((16, LANES), f32)
    for k in range(4):
        two = two + lane_roll(w2_scr[pl.ds(k, 16, stride=4), :], 32 * k)
    weight_ref[16:32, :] = two
    weight_ref[32:160, :] = w3_ref[...]
    weight_ref[160:168, :] = jnp.zeros((8, LANES), f32)


def points_back(counts, rows, back, kept):
    return call(
        points_back_kernel,
        7,
        56,
        (shape((7, PTS, VOX)), shape((VFE_R + 8, LANES))),
        [vmem(), vmem(), anywhere(), vmem(), vmem()] + [anywhere()] * 4 + [vmem()],
        (vmem(), vmem()),
        VFE_SCRATCH
        + [pltpu.VMEM(LOW, f32)]
        + [pltpu.VMEM(d, bf16) for d in (MID, MID, LOW, LOW, LOW)]
        + [pltpu.SemaphoreType.DMA((3 * PARTS + 2,))],
    )(counts, rows, *back, *kept)


R3 = ROWS + 1
R3W = R3 * GX
R2W = (R3 + 2) * GX
R1W = (R3 + 4) * GX
RG = R3 + 6
RGW = RG * GX
HX = GX // 2
L1_R = ROWS // 2 * HX


def cell_marks(places, first_row):
    value = places.astype(f32)
    high, low = value[0:1], value[1:2]
    upper = high >= GY
    row = jnp.where(upper, high - GY, high)
    column = lax.broadcasted_iota(jnp.int32, (GX, VOX), 0).astype(f32)
    column = (column == low).astype(f32).astype(bf16)
    pieces = []
    for w in range(RG):
        target = first_row - 3 + w
        inside = jnp.logical_and(target >= 0, target < GY)
        target = jnp.where(inside, target, -1).astype(f32)
        pieces.append(column * (row == target).astype(f32).astype(bf16))
    upper = upper.astype(f32)
    return jnp.concatenate(pieces, 0), 1.0 - upper, upper


def conv_weights(rows_ref, start, taps, half, place, scr):
    lane = lane_of((half, LANES))
    left = lane < 64
    for t in range(taps):
        r = []
        for kx in range(3):
            base = start + (3 * t + kx) * half
            r.append(rows_ref[base // TILE : (base + half) // TILE].reshape(half, LANES).astype(f32))
        turned = [lane_roll(v, 64) for v in r]
        at = place(t)
        scr[0, pl.ds(at, half, stride=2), :] = jnp.where(left, r[1], turned[0])
        scr[0, pl.ds(at + 1, half, stride=2), :] = jnp.where(left, turned[1], r[0])
        scr[1, pl.ds(at, half, stride=2), :] = jnp.where(left, r[2], 0.0)
        scr[1, pl.ds(at + 1, half, stride=2), :] = jnp.where(left, turned[2], 0.0)


def conv_weight_grads(out_ref, start, taps, half, place, scr):
    lane = lane_of((half, LANES))
    left = lane < 64
    for t in range(taps):
        at = place(t)
        even = [scr[b, pl.ds(at, half, stride=2), :] for b in range(2)]
        odd = [scr[b, pl.ds(at + 1, half, stride=2), :] for b in range(2)]
        values = (
            jnp.where(left, lane_roll(even[0], 64), odd[0]),
            jnp.where(left, even[0], lane_roll(odd[0], 64)),
            jnp.where(left, even[1], lane_roll(odd[1], 64)),
        )
        for kx in range(3):
            base = start + (3 * t + kx) * half
            out_ref[base // TILE : (base + half) // TILE] = (
                values[kx].astype(bf16).reshape(half // TILE, TILE, LANES)
            )


def both_halves(out_ref, scr):
    for b in range(2):
        out_ref[:, b * LANES : (b + 1) * LANES] = scr[b].astype(bf16)


def keep_halves(scr, value):
    for b in range(2):
        scr[b] = value[:, b * LANES : (b + 1) * LANES]


def tap_place(t):
    return 128 * t


def pair_place(t):
    kd, ky = t // 3, t % 3
    return 128 * ky + 64 * kd if kd < 2 else 384 + 128 * ky


def join_columns(p):
    first, last = p[:, 0:128], p[:, 128:256]
    left = lane_of(first.shape) < 64
    half = jnp.where(left, first + shift_in(last, -1, GX), shift_in(first, 1, GX))
    return half + lane_roll(half, 64)


def split_columns(d):
    left = lane_of(d.shape) < 64
    first = jnp.where(left, d, lane_roll(shift_in(d, -1, GX), 64))
    last = jnp.where(left, shift_in(d, 1, GX), 0.0)
    return jnp.concatenate([first, last], 1).astype(bf16)


def inside_rows(rows, first_row):
    place = first_row + row_of((rows, LANES)) // GX
    return jnp.logical_and(place >= 0, place < GY)


def grid_taps(grid_ref, k):
    return jnp.concatenate(
        [grid_ref[2 * k + kd, ky * GX : ky * GX + R1W, :] for kd in range(3) for ky in range(3)], 1
    )


def pair_taps(ref, at, rows):
    return jnp.concatenate(
        [ref[at, ky * GX : ky * GX + rows, :] for ky in range(3)]
        + [ref[at + 2, ky * GX : ky * GX + rows, :] for ky in range(3)],
        1,
    )


def level_taps(ref):
    planes = {}
    for xp in range(2):
        for yp in range(2):
            count = ROWS // 2 + 1 - yp
            planes[yp, xp] = jnp.concatenate(
                [ref[pl.ds((2 * a + yp) * GX + xp, HX, stride=2), :] for a in range(count)], 0
            )
    pieces = []
    for ky in range(3):
        for kx in range(3):
            v = planes[ky % 2, int(kx != 1)]
            v = v[HX:] if ky == 2 else v[0:L1_R]
            pieces.append((shift_in(v, 1, HX) if kx == 0 else v).astype(bf16))
    return jnp.concatenate(pieces, 1)


def level_taps_back(ref, grad):
    planes = {}
    edge = jnp.zeros((HX, LANES), f32)
    for ky in range(3):
        for kx in range(3):
            t = 3 * ky + kx
            v = grad[:, t * LANES : (t + 1) * LANES]
            v = shift_in(v, -1, HX) if kx == 0 else v
            if ky != 1:
                v = jnp.concatenate([edge, v] if ky == 2 else [v, edge], 0)
            at = (ky % 2, int(kx != 1))
            planes[at] = planes[at] + v if at in planes else v
    for (yp, xp), v in planes.items():
        for a in range(ROWS // 2 + 1 - yp):
            ref[pl.ds((2 * a + yp) * GX + xp, HX, stride=2), :] = v[a * HX : (a + 1) * HX]


GRID = (9, RGW, LANES)
FIRST = (6, R1W, LANES)
SECOND = (6, R2W, LANES)


def volume_kernel(
    slab_ref, f0_ref, f1_ref, f2_ref, f3_ref, own_ref, core_ref,
    level_ref, grid_ref, first_ref, second_ref, taps_ref, z1_ref, z2_ref, z3_ref, z4_ref, w1_ref, w2_ref, w3_ref, w4_ref,
    rows_ref, w1_scr, w2_scr, bird_scr,
):
    join_chunks(slab_ref, rows_ref, own_ref, core_ref)
    w4_ref[...] = rows_ref[LEVEL_T : LEVEL_T + 72].reshape(1152, LANES)
    w2_scr[...] = jnp.zeros_like(w2_scr)
    conv_weights(rows_ref, VFE_R, 9, 64, tap_place, w1_scr)
    both_halves(w1_ref, w1_scr)
    conv_weights(rows_ref, VFE_R + 1728, 9, 32, pair_place, w2_scr)
    both_halves(w2_ref, w2_scr)
    conv_weights(rows_ref, VFE_R + 2592, 9, 32, pair_place, w2_scr)
    both_halves(w3_ref, w2_scr)

    first_row = slab_ref[0] * ROWS - 1
    grid_ref[0] = jnp.zeros((RGW, FC), bf16)
    for slot, f_ref in enumerate((f0_ref, f1_ref, f2_ref, f3_ref)):
        t = jnp.bitwise_xor(slab_ref[0], slot)
        features = f_ref[0:FC, :]
        marks, lower, upper = cell_marks(f_ref[FC : FC + 16, :], first_row)
        both = jnp.concatenate([features * lower.astype(bf16), features * upper.astype(bf16)], 0)
        cells = mm_nt(marks, both).astype(bf16)
        grid_ref[1 + 2 * t] = cells[:, 0:FC]
        grid_ref[2 + 2 * t] = cells[:, FC:]

    first_ref[0] = jnp.zeros((R1W, LANES), bf16)
    first_ref[5] = jnp.zeros((R1W, LANES), bf16)
    keep = inside_rows(R1W, first_row - 2)
    for k in range(4):
        z = join_columns(mm(grid_taps(grid_ref, k), w1_ref[...]))
        z1_ref[k] = jnp.where(keep, silu_slope(z), 0.0).astype(bf16)
        value = jnp.where(keep, silu(z), 0.0).astype(bf16)
        first_ref[k + 1, :, 0:64] = value[:, 0:64]
        first_ref[k, :, 64:128] = value[:, 64:128]
    first_ref[4, :, 64:128] = jnp.zeros((R1W, 64), bf16)

    second_ref[0] = jnp.zeros((R2W, LANES), bf16)
    second_ref[5] = jnp.zeros((R2W, LANES), bf16)
    keep = inside_rows(R2W, first_row - 1)
    for k in range(4):
        z = join_columns(mm(pair_taps(first_ref, k, R2W), w2_ref[...]))
        z2_ref[k] = jnp.where(keep, silu_slope(z), 0.0).astype(bf16)
        value = jnp.where(keep, silu(z), 0.0).astype(bf16)
        second_ref[k + 1, :, 0:64] = value[:, 0:64]
        second_ref[k, :, 64:128] = value[:, 64:128]
    second_ref[4, :, 64:128] = jnp.zeros((R2W, 64), bf16)

    z3 = []
    for k in range(2):
        z3.append(join_columns(mm(pair_taps(second_ref, 2 * k, R3W), w3_ref[...])))
    z = jnp.where(lane_of((R3W, LANES)) < 64, z3[0], z3[1])
    keep = inside_rows(R3W, first_row)
    z3_ref[...] = jnp.where(keep, silu_slope(z), 0.0).astype(bf16)
    bird_scr[...] = jnp.where(keep, silu(z), 0.0)
    taps = level_taps(bird_scr)
    taps_ref[...] = taps
    z = mm(taps, w4_ref[...])
    z4_ref[...] = silu_slope(z).astype(bf16)
    level_ref[...] = silu(z).astype(bf16)


LEVEL_T = VFE_T + 216


def volume(info, features, early):
    return call(
        volume_kernel,
        11,
        56,
        (
            shape((L1_R, LANES), bf16),
            shape(GRID, bf16),
            shape(FIRST, bf16),
            shape(SECOND, bf16),
            shape((L1_R, 1152), bf16),
            shape((4, R1W, LANES), bf16),
            shape((4, R2W, LANES), bf16),
            shape((R3W, LANES), bf16),
            shape((L1_R, LANES), bf16),
            shape((1152, 256), bf16),
            shape((768, 256), bf16),
            shape((768, 256), bf16),
            shape((1152, LANES), bf16),
        ),
        [smem()] + [vmem()] * 6,
        (vmem(),) * 13,
        [
            pltpu.VMEM((PAD_T, TILE, LANES), bf16),
            pltpu.VMEM((2, 1152, LANES), f32),
            pltpu.VMEM((2, 768, LANES), f32),
            pltpu.VMEM((R3W, LANES), f32),
        ],
    )(info, *features, *early)


def volume_back(
    slab, f_ref, level_grad, z1_ref, z2_ref, z3_ref, z4_ref, w1_ref, w2_ref, w3_ref, w4_ref,
    out_refs, d4_ref, sp3_ref, sp2_ref, sp1_ref,
    bird_scr, acc2, acc1, accg,
):
    dz = (level_grad * z4_ref[...].astype(f32)).astype(bf16)
    d4_ref[...] = dz
    level_taps_back(bird_scr, mm_nt(dz, w4_ref[...]))
    dz = bird_scr[...] * z3_ref[...].astype(f32)
    acc2[...] = jnp.zeros_like(acc2)
    acc1[...] = jnp.zeros_like(acc1)
    accg[...] = jnp.zeros_like(accg)

    def pair_back(acc, at, rows, spread, weight):
        back = mm_nt(spread, weight)
        for ky in range(3):
            acc[at, ky * GX : ky * GX + rows, :] += back[:, 128 * ky : 128 * ky + 128]
            acc[at + 2, ky * GX : ky * GX + rows, :] += back[:, 384 + 128 * ky : 512 + 128 * ky]

    def layer_grad(acc, m):
        return acc[m] + lane_roll(acc[m - 1], 64)

    for k in range(2):
        spread = split_columns(dz if k == 0 else lane_roll(dz, 64))
        sp3_ref[k] = spread
        pair_back(acc2, 2 * k, R3W, spread, w3_ref[...])
    for k in range(4):
        spread = split_columns(layer_grad(acc2, k + 1) * z2_ref[k].astype(f32))
        sp2_ref[k] = spread
        pair_back(acc1, k, R2W, spread, w2_ref[...])
    for k in range(4):
        spread = split_columns(layer_grad(acc1, k + 1) * z1_ref[k].astype(f32))
        sp1_ref[k] = spread
        back = mm_nt(spread, w1_ref[...])
        for kd in range(3):
            for ky in range(3):
                t = 3 * kd + ky
                accg[2 * k + kd, ky * GX : ky * GX + R1W, :] += back[:, 128 * t : 128 * t + 128]
    for slot in range(SLABS):
        t = jnp.bitwise_xor(slab, slot)
        marks, lower, upper = cell_marks(f_ref[slot, FC : FC + 16, :], slab * ROWS - 1)
        both = jnp.concatenate([accg[1 + 2 * t].astype(bf16), accg[2 + 2 * t].astype(bf16)], 1)
        both = mm_tn(both, marks)
        value = both[0:FC] * lower + both[FC:] * upper
        out_refs[slot][...] = value.astype(bf16)


SPREADS = ((L1_R, LANES), (2, R3W, 256), (4, R2W, 256), (4, R1W, 256))
BACK_IN = (
    (SLABS, FC + 16, VOX),
    (4, R1W, LANES),
    (4, R2W, LANES),
    (R3W, LANES),
    (L1_R, LANES),
    (1152, 256),
    (768, 256),
    (768, 256),
    (1152, LANES),
)


def volume_weights_kernel(
    info_ref, taps_ref, d4_ref, second_ref, sp3_ref, first_ref, sp2_ref, grid_ref, sp1_ref,
    own_ref, core_ref,
    weight_ref, g1_scr, g2_scr,
):
    weight_ref[0:VFE_T] = jnp.zeros((VFE_T, TILE, LANES), bf16)
    weight_ref[VFE_T + EARLY_T : PAD_T] = jnp.zeros((PAD_T - VFE_T - EARLY_T, TILE, LANES), bf16)
    total = mm_tn(taps_ref[...], d4_ref[...])
    weight_ref[LEVEL_T : LEVEL_T + 72] = total.astype(bf16).reshape(72, TILE, LANES)
    total = mm_tn(pair_taps(second_ref, 0, R3W), sp3_ref[0])
    keep_halves(g2_scr, total + mm_tn(pair_taps(second_ref, 2, R3W), sp3_ref[1]))
    conv_weight_grads(weight_ref, VFE_R + 2592, 9, 32, pair_place, g2_scr)
    total = jnp.zeros((768, 256), f32)
    for k in range(4):
        total = total + mm_tn(pair_taps(first_ref, k, R2W), sp2_ref[k])
    keep_halves(g2_scr, total)
    conv_weight_grads(weight_ref, VFE_R + 1728, 9, 32, pair_place, g2_scr)
    total = jnp.zeros((1152, 256), f32)
    for k in range(4):
        total = total + mm_tn(grid_taps(grid_ref, k), sp1_ref[k])
    keep_halves(g1_scr, total)
    conv_weight_grads(weight_ref, VFE_R, 9, 64, tap_place, g1_scr)
    split_chunks(info_ref, weight_ref, 0, own_ref, core_ref)


def volume_weights(info, kept, grads):
    grid, first, second, taps = kept
    d4, sp3, sp2, sp1 = grads
    return call(
        volume_weights_kernel,
        8,
        14,
        (shape(CHUNKS, bf16),) * 2,
        [smem()] + [vmem()] * 8,
        (vmem(),) * 2,
        [
            pltpu.VMEM((PAD_T, TILE, LANES), bf16),
            pltpu.VMEM((2, 1152, LANES), f32),
            pltpu.VMEM((2, 768, LANES), f32),
        ],
    )(info, taps, d4, second, sp3, first, sp2, grid, sp1)


def split_planes(ref, height, width):
    planes = []
    for yp in range(2):
        for xp in range(2):
            planes.append(
                jnp.concatenate(
                    [
                        ref[pl.ds((2 * a + yp) * width + xp, width // 2, stride=2), :]
                        for a in range(height // 2)
                    ],
                    0,
                )
            )
    return planes


def merge_planes(ref, planes, height, width):
    half = width // 2
    for yp in range(2):
        for xp in range(2):
            for a in range(height // 2):
                ref[pl.ds((2 * a + yp) * width + xp, half, stride=2), :] = planes[2 * yp + xp][
                    a * half : a * half + half
                ]


def stride_taps(planes, width):
    pieces = []
    for ky in range(3):
        for kx in range(3):
            v = planes[2 * (ky != 1) + (kx != 1)]
            v = shift_in(v, 1, width) if kx == 0 else v
            pieces.append((shift_out(v, 1, width) if ky == 0 else v).astype(bf16))
    return jnp.concatenate(pieces, 1)


def stride_taps_back(grad, width):
    planes = [None] * 4
    channels = grad.shape[1] // 9
    for ky in range(3):
        for kx in range(3):
            t = 3 * ky + kx
            v = grad[:, t * channels : (t + 1) * channels]
            v = shift_out(v, -1, width) if ky == 0 else v
            v = shift_in(v, -1, width) if kx == 0 else v
            at = 2 * (ky != 1) + (kx != 1)
            planes[at] = v if planes[at] is None else planes[at] + v
    return planes


def full_taps(v, width):
    across = [shift_in(v, 1 - kx, width).astype(bf16) for kx in range(3)]
    return jnp.concatenate(
        [shift_out(across[kx], 1 - ky, width) for ky in range(3) for kx in range(3)], 1
    )


def full_taps_back(grad, width):
    channels = grad.shape[1] // 9
    total = None
    for kx in range(3):
        column = None
        for ky in range(3):
            t = 3 * ky + kx
            v = shift_out(grad[:, t * channels : (t + 1) * channels], ky - 1, width)
            column = v if column is None else column + v
        column = shift_in(column, kx - 1, width)
        total = column if total is None else total + column
    return total


HY = 16
CELLS = HY * HX


def region_kernel(
    slab_ref, counts_ref, l0_ref, l1_ref, l2_ref, l3_ref, anchors_ref, goals_ref,
    s0_ref, s1_ref, s2_ref, s3_ref, s4_ref, s5_ref, s6_ref, s7_ref,
    f0_in, f1_in, f2_in, f3_in, z1_in, z2_in, z3_in, z4_in, w1_in, w2_in, w3_in, w4_in,
    maps_ref, own_ref, core_ref, o0_ref, o1_ref, o2_ref, o3_ref, d4_ref, sp3_ref, sp2_ref, sp1_ref,
    f_ref, z1_ref, z2_ref, z3_ref, z4_ref, w1_ref, w2_ref, w3_ref, w4_ref,
    bird_scr, acc2, acc1, accg, back_sems,
    wv, gr, sems,
    l1_scr, l2_scr, zu1_scr, zu2_scr, zu3_scr, head_scr, maps_scr, two_scr, three_scr,
):
    slab = slab_ref[0]
    chip, core = batch_place(slab_ref)
    copies = []
    late = (s0_ref, s1_ref, s2_ref, s3_ref, s4_ref, s5_ref, s6_ref, s7_ref)
    for n, (ref, (chips, slots)) in enumerate(zip(late, LATE_ORDER * 2)):
        for k in range(4):
            shard = jnp.bitwise_xor(slab_ref[2], slots[k])
            at = chunk_start(chip, core if n < 4 else 1 - core, chips[k])
            copies.append(
                pltpu.make_async_copy(
                    ref.at[k // 2, k % 2],
                    wv.at[shard, pl.ds(at, CHUNK_T)],
                    sems.at[len(copies)],
                )
            )
    for c in copies:
        c.start()
    gr[0 : PLANE_T0 + 1] = jnp.zeros((PLANE_T0 + 1, TILE, LANES), bf16)
    gr[PLANE_T0 + 1 + PLANE_T : GRAD_T] = jnp.zeros((GRAD_T - PLANE_T0 - 1 - PLANE_T, TILE, LANES), bf16)
    for slot, ref in enumerate((l0_ref, l1_ref, l2_ref, l3_ref)):
        at = pl.multiple_of(jnp.bitwise_xor(slab, slot) * L1_R, L1_R)
        l1_scr[pl.ds(at, L1_R), :] = ref[...].astype(f32)
    level_one = l1_scr[...]
    finish(copies)
    arrive = begin(
        (f0_in, f1_in, f2_in, f3_in, z1_in, z2_in, z3_in, z4_in, w1_in, w2_in, w3_in, w4_in),
        (f_ref.at[0], f_ref.at[1], f_ref.at[2], f_ref.at[3], z1_ref, z2_ref, z3_ref, z4_ref, w1_ref, w2_ref, w3_ref, w4_ref),
        back_sems,
    )
    for s in range(1, SLABS):
        wv[s, 0:2] = wv[s, 0:2] + wv[s - 1, STRIDE_T : STRIDE_T + 2]

    def tiles_of(tile, tiles):
        pieces = []
        while tiles:
            s = min((tile + 1) // STRIDE_T, SLABS - 1)
            at = tile + 1 - STRIDE_T * s
            size = min(tiles, STRIDE_T - at) if s < SLABS - 1 else tiles
            pieces.append(wv[s, at : at + size])
            tile, tiles = tile + size, tiles - size
        return pieces[0] if len(pieces) == 1 else jnp.concatenate(pieces, 0)

    def narrow(tile, rows):
        return tiles_of(tile, rows // 16).reshape(rows, LANES)

    def wide(tile, rows):
        both = tiles_of(tile, rows // 8).reshape(rows // 16, 2, TILE, LANES)
        return jnp.concatenate(
            [both[:, 0].reshape(rows, LANES), both[:, 1].reshape(rows, LANES)], 1
        )

    def keep_narrow(tile, value):
        at = tile + 1
        tiles = value.shape[0] // 16
        gr[at : at + tiles] = value.astype(bf16).reshape(tiles, TILE, LANES)

    def keep_wide(tile, value):
        at = tile + 1
        tiles = value.shape[0] // 16
        value = value.astype(bf16)
        left = value[:, 0:128].reshape(tiles, 1, TILE, LANES)
        right = value[:, 128:256].reshape(tiles, 1, TILE, LANES)
        gr[at : at + 2 * tiles] = jnp.concatenate([left, right], 1).reshape(2 * tiles, TILE, LANES)

    t_two, t_three, t_up1, t_up2, t_up3, t_head = 297, 369, 513, 657, 721, 1233

    taps_two = stride_taps(split_planes(l1_scr, 16, 32), 16)
    z2 = mm(taps_two, narrow(t_two, 1152))
    level_two = silu(z2).astype(bf16)
    l2_scr[...] = level_two.astype(f32)
    taps_three = stride_taps(split_planes(l2_scr, 8, 16), 8)
    z3 = mm(taps_three, wide(t_three, 1152))
    level_three = silu(z3).astype(bf16)

    taps_up = full_taps(level_one, 32)
    zu1_scr[...] = mm(taps_up, wide(t_up1, 1152))
    for g in range(4):
        zu2_scr[g] = mm(level_two, wide(t_up2 + 16 * g, 128))
    for g in range(16):
        zu3_scr[g] = mm(level_three, wide(t_up3 + 32 * g, 256))

    lane = lane_of((96, LANES))
    rows = narrow(t_head, 96).astype(f32)
    for c in range(8):
        head_scr[pl.ds(c, 96, stride=8), :] = jnp.where(lane < 16, lane_roll(rows, -16 * c), 0.0)
    head = head_scr[...].astype(bf16)
    head_a, head_b, head_c = head[0:256], head[256:512], head[512:768]
    joined_a = silu(zu1_scr[...]).astype(bf16)
    for g in range(4):
        p, q = g // 2, g % 2
        part = mm(silu(zu2_scr[g]).astype(bf16), head_b)
        for a in range(8):
            two_scr[pl.ds((2 * a + p) * HX + q, 16, stride=2), :] = part[16 * a : 16 * a + 16]
    for g in range(16):
        p, q = g // 4, g % 4
        part = mm(silu(zu3_scr[g]).astype(bf16), head_c)
        for a in range(4):
            three_scr[pl.ds((4 * a + p) * HX + q, 8, stride=4), :] = part[8 * a : 8 * a + 8]
    maps = mm(joined_a, head_a) + two_scr[...] + three_scr[...]
    maps = jnp.transpose(maps)[0:16]
    own = jnp.zeros((16, 128), f32)
    for s in range(SLABS):
        own = own + jnp.where(slab == s, maps[:, 128 * s : 128 * s + 128], 0.0)
    for i in range(HY // SLABS):
        maps_ref[0, :, i, :] = own[:, HX * i : HX * i + HX]

    live_count = counts_ref[0]
    anchors = anchors_ref[...]
    slot = row_of((40, CELLS))
    place = lane_of((40, CELLS))
    positive = [
        jnp.sum(
            jnp.logical_and(anchors == place + k * CELLS, slot < live_count).astype(f32),
            axis=0,
            keepdims=True,
        )
        for k in range(2)
    ]
    row = row_of((16, CELLS))
    second = jnp.logical_or(row == 1, row >= 9)
    marked = jnp.where(second, positive[1], positive[0])
    share = 1.0 / jnp.maximum(live_count.astype(f32), 1.0)
    class_grad = (sigmoid(maps) - marked) * (1.0 / (2.0 * CELLS))
    box_grad = jnp.clip(maps - goals_ref[...], -1.0, 1.0) * marked * share
    dmaps = jnp.where(row < 2, class_grad, box_grad)
    dmaps = jnp.transpose(jnp.concatenate([dmaps, jnp.zeros((LANES - 16, CELLS), f32)], 0))
    maps_scr[...] = dmaps
    low = dmaps.astype(bf16)

    dhead_a = mm_tn(joined_a, low)
    dz = mm_nt(low, head_a) * silu_slope(zu1_scr[...])
    dz = dz.astype(bf16)
    keep_wide(t_up1, mm_tn(taps_up, dz))
    dlevel_one = full_taps_back(mm_nt(dz, wide(t_up1, 1152)), 32)

    dhead_b = jnp.zeros((256, LANES), f32)
    dlevel_two = jnp.zeros((128, 128), f32)
    for g in range(4):
        p, q = g // 2, g % 2
        part = jnp.concatenate(
            [maps_scr[pl.ds((2 * a + p) * HX + q, 16, stride=2), :] for a in range(8)], 0
        ).astype(bf16)
        z = zu2_scr[g]
        dhead_b = dhead_b + mm_tn(silu(z).astype(bf16), part)
        dz = (mm_nt(part, head_b) * silu_slope(z)).astype(bf16)
        keep_wide(t_up2 + 16 * g, mm_tn(level_two, dz))
        dlevel_two = dlevel_two + mm_nt(dz, wide(t_up2 + 16 * g, 128))
    dhead_c = jnp.zeros((256, LANES), f32)
    dlevel_three = jnp.zeros((32, 256), f32)
    for g in range(16):
        p, q = g // 4, g % 4
        part = jnp.concatenate(
            [maps_scr[pl.ds((4 * a + p) * HX + q, 8, stride=4), :] for a in range(4)], 0
        ).astype(bf16)
        z = zu3_scr[g]
        dhead_c = dhead_c + mm_tn(silu(z).astype(bf16), part)
        dz = (mm_nt(part, head_c) * silu_slope(z)).astype(bf16)
        keep_wide(t_up3 + 32 * g, mm_tn(level_three, dz))
        dlevel_three = dlevel_three + mm_nt(dz, wide(t_up3 + 32 * g, 256))

    head_scr[...] = jnp.concatenate([dhead_a, dhead_b, dhead_c], 0)
    rows = jnp.zeros((96, LANES), f32)
    for c in range(8):
        piece = jnp.where(lane < 16, head_scr[pl.ds(c, 96, stride=8), :], 0.0)
        rows = rows + lane_roll(piece, 16 * c)
    keep_narrow(t_head, rows)

    dz = (dlevel_three * silu_slope(z3)).astype(bf16)
    keep_wide(t_three, mm_tn(taps_three, dz))
    merge_planes(l2_scr, stride_taps_back(mm_nt(dz, wide(t_three, 1152)), 8), 8, 16)
    dlevel_two = dlevel_two + l2_scr[...]
    dz = (dlevel_two * silu_slope(z2)).astype(bf16)
    keep_narrow(t_two, mm_tn(taps_two, dz))
    merge_planes(l1_scr, stride_taps_back(mm_nt(dz, narrow(t_two, 1152)), 16), 16, 32)
    dlevel_one = dlevel_one + l1_scr[...]
    l1_scr[...] = dlevel_one
    level_grad = l1_scr[pl.ds(pl.multiple_of(slab * L1_R, L1_R), L1_R), :]
    for s in range(SLABS):

        @pl.when(slab == s)
        def _(s=s):
            start = (15 - 4 * s) * LANES + 16 + 28 * s
            for t in (0, 1) + tuple(range(SHARD_T - 4, PAD_T)):
                tile = STRIDE_T * s - 1 + t
                row = row_of((TILE, LANES))
                if t >= SHARD_T:
                    gr[STRIDE_T * s + t] = jnp.zeros((TILE, LANES), bf16)
                    continue
                if WIDE_T[0] <= tile < WIDE_T[1]:
                    row = 32 * (t // 2) + 2 * row + t % 2
                else:
                    row = TILE * t + row
                at = row * LANES + lane_of((TILE, LANES)) - start
                inside = jnp.logical_and(at >= 0, at < SHARD)
                gr[STRIDE_T * s + t] = jnp.where(
                    inside, gr[STRIDE_T * s + t].astype(f32), 0.0
                ).astype(bf16)

    split_chunks(slab_ref, gr, STRIDE_T * slab, own_ref, core_ref)
    finish(arrive)
    spreads = (d4_ref, sp3_ref, sp2_ref, sp1_ref)
    volume_back(
        slab, f_ref, level_grad, z1_ref, z2_ref, z3_ref, z4_ref, w1_ref, w2_ref, w3_ref, w4_ref,
        (o0_ref, o1_ref, o2_ref, o3_ref), *spreads, bird_scr, acc2, acc1, accg,
    )


LATE_ORDER = (
    ((0, 0, 2, 2), (0, 1, 0, 1)),
    ((1, 1, 3, 3), (0, 1, 0, 1)),
    ((0, 0, 1, 1), (2, 3, 2, 3)),
    ((2, 2, 3, 3), (2, 3, 2, 3)),
)


def region(info, counts, levels, anchors, goals, late, features, kept):
    return call(
        region_kernel,
        20,
        56,
        (
            shape((1, 16, HY // SLABS, HX)),
            shape(CHUNKS, bf16),
            shape(CHUNKS, bf16),
            shape((FC, VOX), bf16),
            shape((FC, VOX), bf16),
            shape((FC, VOX), bf16),
            shape((FC, VOX), bf16),
        )
        + (shape(SPREADS[0], bf16),)
        + tuple(held(d) for d in SPREADS[1:]),
        [smem(), smem()] + [vmem()] * 6 + [anywhere()] * 20,
        (vmem(),) * 11,
        [pltpu.VMEM(d, bf16) for d in BACK_IN]
        + [
            pltpu.VMEM((R3W, LANES), f32),
            pltpu.VMEM((6, R2W, LANES), f32),
            pltpu.VMEM((6, R1W, LANES), f32),
            pltpu.VMEM((9, RGW, LANES), f32),
            pltpu.SemaphoreType.DMA((12,)),
            pltpu.VMEM((SLABS, PAD_T, TILE, LANES), bf16),
            pltpu.VMEM((GRAD_T, TILE, LANES), bf16),
            pltpu.SemaphoreType.DMA((32,)),
            pltpu.VMEM((512, 128), f32),
            pltpu.VMEM((128, 128), f32),
            pltpu.VMEM((512, 256), f32),
            pltpu.VMEM((4, 128, 256), f32),
            pltpu.VMEM((16, 32, 256), f32),
            pltpu.VMEM((768, LANES), f32),
            pltpu.VMEM((512, LANES), f32),
            pltpu.VMEM((512, LANES), f32),
            pltpu.VMEM((512, LANES), f32),
        ],
    )(info, counts, *levels, anchors, goals, *late, *features, *kept)


def swap(x, axis, bit):
    count = lax.axis_size(axis)
    return lax.ppermute(x, axis, [(i, i ^ bit) for i in range(count)])


def after(x, *earlier):
    return lax.optimization_barrier((x,) + earlier)[0]


def slab_all(x):
    return [x] + [swap(x, "slab", k) for k in range(1, SLABS)]


def plane_all(x):
    return [x] + [swap(x, "batch", 2 * k) for k in range(1, 4)]


def sum_cores(own, other):
    return [(own[k].astype(f32) + other[k].astype(f32)).astype(bf16) for k in range(4)]


def sum_chips(parts):
    total = parts[0].astype(f32)
    for k in range(1, 4):
        total = total + parts[k].astype(f32)
    return total


def send_parts(parts):
    return parts[0:1] + [swap(parts[k], "batch", 2 * k) for k in range(1, 4)]


def send_half(parts):
    return parts[0], parts[1], swap(jnp.stack(parts[2:4]), "batch", 4)


def send_rest(first, second, arrived):
    first = first.astype(f32) + arrived[0].astype(f32)
    second = (second.astype(f32) + arrived[1].astype(f32)).astype(bf16)
    return first, swap(second, "batch", 2)


def to_first(total, low):
    for k in range(1, SLABS):
        total = total + lax.ppermute(low, "slab", [(k, 0)]).astype(f32)
    return total


def from_first(x, slab):
    x = jnp.where(slab == 2, lax.ppermute(x, "slab", [(0, 2)]), x)
    near = lax.ppermute(x, "slab", [(0, 1), (2, 3)])
    return jnp.where(slab % 2 == 1, near, x)


def gathered_shards(own):
    batches = lax.axis_size("batch")
    share = PAD_T // batches
    chunk = lax.dynamic_slice_in_dim(own, lax.axis_index("batch") * share, share, 0)
    shards = lax.all_gather(chunk, ("slab", "batch"), axis=0, tiled=True)
    shards = shards.reshape(SLABS, 4, 2, CHUNK_T, TILE, LANES)
    late = []
    for core in range(2):
        for chips, slots in LATE_ORDER:
            part = jnp.stack([shards[s, c, core] for c, s in zip(chips, slots)])
            late.append(part.reshape((2, 2) + part.shape[1:]))
    return (shards[0, :, 0], shards[0, :, 1]), late


def even_odd(whole):
    both = whole.reshape(4, 2, CHUNK_T, TILE, LANES)
    return both[:, 0], both[:, 1]


def body(
    points, point_counts, voxel_cells, pos_anchors, pos_counts, reg_targets, params, moment1, moment2
):
    batches = lax.axis_size("batch")
    slab, batch = lax.axis_index("slab"), lax.axis_index("batch")
    direct = batches == 8
    zero = jnp.zeros_like(slab)
    info = jnp.stack([slab, batch if direct else zero, slab if direct else zero]).astype(jnp.int32)
    counts = point_counts.reshape(1, VOX)

    if direct:
        chunk, first = spread_own(info, params)
        near = jnp.stack([chunk, swap(chunk, "slab", 1)])
        far = swap(near, "slab", 2)
        first = from_first(first, slab)
        small, early = first, first[VFE_T:]
        early = plane_all(early)
    else:
        flat_rows = jnp.pad(params, (0, FLAT_R * LANES - SHARD)).reshape(FLAT_R, LANES)
        first = spread_first(flat_rows[0:VFE_R])
        small = from_first(first, slab)
        early, late = gathered_shards(spread_shard(info, flat_rows))
    encoded, s3 = encode(points, counts, voxel_cells.reshape(1, VOX), small)
    features = slab_all(encoded)
    if direct:
        early = jnp.stack(lax.optimization_barrier((*early, encoded))[0:4])
        early = (early, swap(early, "batch", 1))
        near, far = lax.optimization_barrier((near, far, early[0]))[0:2]
        later, near, far = lax.optimization_barrier((points, near, far))
        late = [near, swap(near, "batch", 4), far, swap(far, "batch", 2)]
        x, j1, j2, s1, s2, m1, m2 = encode_slopes(later, counts, small)
        near, near_y, far, far_x = lax.optimization_barrier((*late, x))[0:4]
        near, far = jnp.stack([near, near_y]), jnp.stack([far, far_x])
        late = [near, swap(near, "batch", 2), far, swap(far, "batch", 4)]
        features[0] = after(features[0], x, near, far)
        late = late + [swap(near, "batch", 1), swap(far, "batch", 1)]
    else:
        x, j1, j2, s1, s2, m1, m2 = encode_slopes(points, counts, small)
    level, grid, first_pad, second_pad, taps, *kept = volume(info, features, early)
    if direct:
        near, near_x, far, far_y, near_c, far_c = late
        near_c, far_c, level = lax.optimization_barrier((near_c, far_c, level))
        levels = slab_all(level)
        near_x, far_y, *levels = lax.optimization_barrier((near_x, far_y, *levels))
        late = [near, near_x, far, far_y, near_c, swap(near_x, "batch", 1), far_c, swap(far_y, "batch", 1)]
    goals = jnp.pad(reg_targets.reshape(14, CELLS), ((2, 0), (0, 0)))
    if not direct:
        levels = slab_all(level)
    maps, quarter_own, quarter_core, *feature_back = region(
        info, pos_counts, levels, pos_anchors.reshape(40, 1), goals, late, features, kept
    )
    feature_back, spreads = feature_back[0:4], feature_back[4:]
    feature_grad = feature_back[0:1] + [swap(feature_back[k], "slab", k) for k in range(1, SLABS)]
    if direct:
        quarter_other = swap(quarter_core, "batch", 1)
        quarter = lax.optimization_barrier((quarter_own, quarter_other, feature_back[0]))[0:2]
        quarter = sum_cores(*quarter)
        spreads[0], *quarter = lax.optimization_barrier((spreads[0], *quarter))
        quarter = send_half(quarter)
    early_own, early_core = volume_weights(info, (grid, first_pad, second_pad, taps), spreads)
    if direct:
        early_own, early_core, *rest = lax.optimization_barrier(
            (early_own, early_core, *feature_grad, *quarter)
        )
        feature_grad, quarter = rest[0:4], rest[4:]
        parts = sum_cores(early_own, swap(early_core, "batch", 1))
        *parts, feature_grad[0] = lax.optimization_barrier((*parts, feature_grad[0]))
        parts = send_parts(parts)
    back = encode_back(counts, small, feature_grad, j2, s3, m2)
    if direct:
        quarter = lax.optimization_barrier((*quarter, back[0]))[0:3]
        chunk, chunk_far = send_rest(*quarter)
        early_chunk = sum_chips(lax.optimization_barrier((*parts, back[0]))[0:4])
        early_low = early_chunk.astype(bf16)
        d2, early_low, chunk = lax.optimization_barrier((back[0], early_low, chunk))
        back = [d2] + list(back[1:])
        early_chunk = to_first(early_chunk, early_low)
    points_grad, vfe_grad = points_back(counts, small, back, (x, j1, s1, s2, m1))
    if direct:
        early_chunk, chunk_far, vfe_grad = lax.optimization_barrier(
            (early_chunk, chunk_far, vfe_grad)
        )
        chunk = chunk + chunk_far.astype(f32)
        chunk = (chunk + jnp.where(slab == 0, early_chunk, 0.0)).astype(bf16)
        squares = jnp.sum(jnp.square(chunk.astype(f32)))
        final = plane_all(chunk)
    else:
        whole = jnp.stack([quarter_own, quarter_core], 1).astype(f32)
        whole_early = lax.psum(jnp.stack([early_own, early_core], 1).astype(f32), "slab")
        whole = lax.psum(whole + jnp.where(slab == 0, whole_early, 0.0), "batch").astype(bf16)
        squares = jnp.sum(jnp.square(whole.astype(f32))) / batches
        final = even_odd(whole)

    total = vfe_grad + jnp.pad(jnp.broadcast_to(squares, (8, LANES)), ((VFE_R, 0), (0, 0)))
    for axis, size in (("slab", SLABS), ("batch", batches)):
        bit = 1
        while bit < size:
            total = total + swap(total, axis, bit)
            if direct and axis == "batch" and bit == 1:
                *final, total = lax.optimization_barrier((*final, total))
                final = jnp.stack(final)
                final = (final, swap(final, "batch", 1))
            bit *= 2
    new_params, new_moment1, new_moment2, norm = update_shard(
        info, *final, total, params, moment1, moment2
    )
    return (maps, points_grad, new_moment1, new_moment2, new_params, norm.reshape(()))


def solution(mesh):
    in_specs = (
        P(None, None, ("batch", "slab")),
        P(("batch", "slab")),
        P(("batch", "slab")),
        P("batch", None),
        P("batch"),
        P("batch", None, None, None),
        P("slab"),
        P("slab"),
        P("slab"),
    )
    out_specs = (
        P("batch", None, "slab", None),
        P(None, None, ("batch", "slab")),
        P("slab"),
        P("slab"),
        P("slab"),
        P(),
    )
    return jax.shard_map(body, mesh=mesh, in_specs=in_specs, out_specs=out_specs, check_vma=False)
```

```python
import functools
import math

import jax
import jax.numpy as jnp
from jax import lax
from jax.experimental import pallas as pl
from jax.experimental.pallas import tpu as pltpu
from jax.sharding import PartitionSpec as P

VF1 = 16
VF2 = 64
FC = 128
C3 = 64
STEP = 10
GY = 32
GX = 64
PTS = 35
VOX = 512
SLABS = 4
ROWS = GY // SLABS
LANES = 128
NPARAM = 2537584
SHARD = NPARAM // SLABS

TILE = 16
STRIDE_T = 310
SHARD_T = 312
PAD_T = 320
FLAT_R = 4960
EARLY_T = 288
EARLY_R = EARLY_T * TILE
VFE_T = 10
VFE_R = VFE_T * TILE
PLANE_T0 = 297
PLANE_T = 942
GRAD_T = 3 * STRIDE_T + PAD_T
CHUNK_T = PAD_T // 8
WIDE_T = (369, 1233)

beta_one = 0.9
beta_two = 0.999
adam_eps = 1e-08
learn_rate = 0.02
weight_decay = 0.01
clip_level = 0.002

f32 = jnp.float32
bf16 = jnp.bfloat16


def call(kernel, micros, megabytes, out_shape, in_specs, out_specs, scratch=()):
    return pl.pallas_call(
        kernel,
        out_shape=out_shape,
        in_specs=in_specs,
        out_specs=out_specs,
        scratch_shapes=list(scratch),
        compiler_params=pltpu.CompilerParams(vmem_limit_bytes=megabytes * 1024 * 1024),
        cost_estimate=pl.CostEstimate(
            flops=int(micros * 1e9), transcendentals=0, bytes_accessed=int(micros * 3e6)
        ),
    )


def vmem():
    return pl.BlockSpec(memory_space=pltpu.VMEM)


def smem():
    return pl.BlockSpec(memory_space=pltpu.SMEM)


def anywhere():
    return pl.BlockSpec(memory_space=pl.ANY)


def held(dims, dtype=bf16):
    return pltpu.VMEM(dims, dtype)


def shape(dims, dtype=f32):
    return jax.ShapeDtypeStruct(dims, dtype)


def mm(a, b):
    return lax.dot_general(a, b, (((1,), (0,)), ((), ())), preferred_element_type=f32)


def mm_nt(a, b):
    return lax.dot_general(a, b, (((1,), (1,)), ((), ())), preferred_element_type=f32)


def mm_tn(a, b):
    return lax.dot_general(a, b, (((0,), (0,)), ((), ())), preferred_element_type=f32)


def sigmoid(z):
    return 0.5 * jnp.tanh(0.5 * z) + 0.5


def silu(z):
    return z * sigmoid(z)


def silu_slope(z):
    s = sigmoid(z)
    return s * (1.0 + z * (1.0 - s))


def lane_of(dims):
    return lax.broadcasted_iota(jnp.int32, dims, len(dims) - 1)


def row_of(dims):
    return lax.broadcasted_iota(jnp.int32, dims, 0)


def lane_roll(x, shift):
    shift = shift % x.shape[-1]
    return x if shift == 0 else pltpu.roll(x, shift, x.ndim - 1)


def shift_in(v, d, width):
    if d == 0:
        return v
    place = row_of(v.shape) % width
    keep = place > 0 if d > 0 else place < width - 1
    return jnp.where(keep, pltpu.roll(v, d % v.shape[0], 0), 0.0)


def shift_out(v, d, width):
    if d == 0:
        return v
    edge = jnp.zeros((width,) + v.shape[1:], v.dtype)
    if d > 0:
        return jnp.concatenate([edge, v[:-width]], 0)
    return jnp.concatenate([v[width:], edge], 0)


def begin(sources, targets, sems, first=0):
    copies = [
        pltpu.make_async_copy(a, b, sems.at[first + n])
        for n, (a, b) in enumerate(zip(sources, targets))
    ]
    for c in copies:
        c.start()
    return copies


def finish(copies):
    for c in copies:
        c.wait()


def batch_place(info_ref):
    return info_ref[1] // 2, info_ref[1] % 2


def chunk_start(chip, core, slot):
    return CHUNK_T * (2 * jnp.bitwise_xor(chip, slot) + core)


def join_chunks(info_ref, out_ref, own_ref, core_ref):
    chip, core = batch_place(info_ref)
    for slot in range(4):
        out_ref[pl.ds(chunk_start(chip, core, slot), CHUNK_T)] = own_ref[slot]
        out_ref[pl.ds(chunk_start(chip, 1 - core, slot), CHUNK_T)] = core_ref[slot]


def split_chunks(info_ref, scr, base, own_ref, core_ref):
    chip, core = batch_place(info_ref)
    for slot in range(4):
        own_ref[slot] = scr[pl.ds(base + chunk_start(chip, core, slot), CHUNK_T)].astype(bf16)
        core_ref[slot] = scr[pl.ds(base + chunk_start(chip, 1 - core, slot), CHUNK_T)].astype(bf16)


CHUNKS = (4, CHUNK_T, TILE, LANES)


def spread_kernel(slab_ref, flat_ref, out_ref, nat):
    nat[...] = jnp.zeros_like(nat)
    span = 480
    for s in range(SLABS):

        @pl.when(slab_ref[0] == s)
        def _(s=s):
            lanes, first = 16 + 28 * s, 15 - 4 * s
            lane = lane_of((span, LANES))
            count = FLAT_R // span + (FLAT_R % span > 0)
            for i in range(count):
                r0 = i * span
                n = min(span, FLAT_R - r0)
                rolled = lane_roll(flat_ref[r0 : r0 + n, :], lanes)
                nat[first + r0 : first + r0 + n, :] += jnp.where(lane[:n] >= lanes, rolled, 0.0)
                nat[first + r0 + 1 : first + r0 + 1 + n, :] += jnp.where(
                    lane[:n] < lanes, rolled, 0.0
                )
            low = max(0, min(SHARD_T // 2, (WIDE_T[0] - STRIDE_T * s + 1) // 2))
            high = max(low, min(SHARD_T // 2, (WIDE_T[1] - STRIDE_T * s + 1) // 2))
            for a, b, wide in ((0, low, False), (low, high, True), (high, SHARD_T // 2, False)):

                def block(i, carry, wide=wide):
                    base = pl.multiple_of(32 * i, 32)
                    if wide:
                        even = nat[pl.ds(base, 16, stride=2), :]
                        odd = nat[pl.ds(base + 1, 16, stride=2), :]
                    else:
                        even = nat[pl.ds(base, 16), :]
                        odd = nat[pl.ds(base + 16, 16), :]
                    out_ref[2 * i] = even.astype(bf16)
                    out_ref[2 * i + 1] = odd.astype(bf16)
                    return carry

                if b > a:
                    lax.fori_loop(a, b, block, 0, unroll=4)

    for t in range(SHARD_T, PAD_T):
        out_ref[t] = jnp.zeros((TILE, LANES), bf16)


def spread_shard(slab, flat_rows):
    return call(
        spread_kernel,
        4,
        56,
        shape((PAD_T, TILE, LANES), bf16),
        [smem(), vmem()],
        vmem(),
        [pltpu.VMEM((5120, LANES), f32)],
    )(slab, flat_rows)


CHUNK_R = CHUNK_T * TILE
CHUNK_N = CHUNK_R * LANES
WHOLE_R = SHARD // LANES // 8 * 8
REST = SHARD - SHARD // LANES * LANES


def flat_tail(flat_ref):
    rest_r = SHARD // LANES - WHOLE_R
    rows = flat_ref[pl.ds(WHOLE_R * LANES, rest_r * LANES)].reshape(rest_r, LANES)
    return rows, flat_ref[pl.ds(SHARD - REST, REST)].reshape(1, REST)


def spread_own_kernel(info_ref, flat_ref, chunk_ref, first_ref, x_scr, nat):
    batch = info_ref[1]

    @pl.when(batch == 0)
    def _():
        x_scr[0:TILE, :] = jnp.zeros((TILE, LANES), f32)
        x_scr[TILE:, :] = flat_ref[pl.ds(0, CHUNK_N)].reshape(CHUNK_R, LANES)

    @pl.when(jnp.logical_and(batch > 0, batch < 7))
    def _():
        start = pl.multiple_of(batch * CHUNK_N - TILE * LANES, 1024)
        rows = CHUNK_R + TILE
        x_scr[...] = flat_ref[pl.ds(start, rows * LANES)].reshape(rows, LANES)

    @pl.when(batch == 7)
    def _():
        first_r = 7 * CHUNK_R - TILE
        whole = WHOLE_R - first_r
        x_scr[0:whole, :] = flat_ref[pl.ds(first_r * LANES, whole * LANES)].reshape(whole, LANES)
        x_scr[whole:, :] = jnp.zeros((CHUNK_R + TILE - whole, LANES), f32)
        rows, last = flat_tail(flat_ref)
        x_scr[whole : whole + rows.shape[0], :] = rows
        x_scr[whole + rows.shape[0] : whole + rows.shape[0] + 1, 0:REST] = last

    def shifted(first, lanes, rows):
        lane = lane_of((rows, LANES))
        here = lane_roll(x_scr[TILE - first : TILE - first + rows, :], lanes)
        above = lane_roll(x_scr[TILE - 1 - first : TILE - 1 - first + rows, :], lanes)
        return jnp.where(lane >= lanes, here, above)

    for s in range(SLABS):

        @pl.when(info_ref[0] == s)
        def _(s=s):
            nat[...] = shifted(15 - 4 * s, 16 + 28 * s, CHUNK_R)
            low = max(0, min(SHARD_T // 2, (WIDE_T[0] - STRIDE_T * s + 1) // 2))
            high = max(low, min(SHARD_T // 2, (WIDE_T[1] - STRIDE_T * s + 1) // 2))
            for i in range(CHUNK_T // 2):
                block = batch * (CHUNK_T // 2) + i
                wide = jnp.logical_and(block >= low, block < high)
                even = nat[pl.ds(32 * i, 16, stride=2), :]
                odd = nat[pl.ds(32 * i + 1, 16, stride=2), :]
                top, bottom = nat[32 * i : 32 * i + 16, :], nat[32 * i + 16 : 32 * i + 32, :]
                chunk_ref[2 * i] = jnp.where(wide, even, top).astype(bf16)
                chunk_ref[2 * i + 1] = jnp.where(wide, odd, bottom).astype(bf16)

    first_ref[VFE_T : VFE_T + CHUNK_T] = chunk_ref[...]
    x_scr[0:TILE, :] = jnp.zeros((TILE, LANES), f32)
    x_scr[TILE : TILE + VFE_R, :] = flat_ref[pl.ds(0, VFE_R * LANES)].reshape(VFE_R, LANES)
    rows = shifted(15, 16, VFE_R).astype(bf16)
    first_ref[0:VFE_T] = rows.reshape(VFE_T, TILE, LANES)


def spread_own(info, params):
    return call(
        spread_own_kernel,
        3,
        56,
        (shape((CHUNK_T, TILE, LANES), bf16), shape((VFE_T + CHUNK_T, TILE, LANES), bf16)),
        [smem(), vmem()],
        (vmem(), vmem()),
        [pltpu.VMEM((CHUNK_R + TILE, LANES), f32), pltpu.VMEM((CHUNK_R, LANES), f32)],
    )(info, params)


def spread_first_kernel(flat_ref, out_ref, nat):
    lanes, first = 16, 15
    lane = lane_of((VFE_R, LANES))
    rolled = lane_roll(flat_ref[...], lanes)
    nat[...] = jnp.zeros_like(nat)
    nat[first : first + VFE_R, :] += jnp.where(lane >= lanes, rolled, 0.0)
    nat[first + 1 : first + 1 + VFE_R, :] += jnp.where(lane < lanes, rolled, 0.0)
    out_ref[...] = nat[0:VFE_R, :].astype(bf16).reshape(VFE_T, TILE, LANES)


def spread_first(flat_rows):
    return call(
        spread_first_kernel,
        1,
        56,
        shape((VFE_T, TILE, LANES), bf16),
        [vmem()],
        vmem(),
        [pltpu.VMEM((VFE_R + 32, LANES), f32)],
    )(flat_rows)


UPDATE_R = 1024
UPDATE_N = UPDATE_R * LANES


def update_kernel(
    slab_ref, own_ref, core_ref, vfe_ref, params_ref, moment1_ref, moment2_ref,
    new_params_ref, new_moment1_ref, new_moment2_ref, norm_ref,
    quarter_ref, nat, grads,
):
    step = pl.program_id(0)

    @pl.when(step == 0)
    def _():
        gather_grads(slab_ref, own_ref, core_ref, vfe_ref, norm_ref, quarter_ref, nat, grads)

    def update(source, target, clipped):
        param = params_ref[source]
        moment1 = beta_one * moment1_ref[source] + (1.0 - beta_one) * clipped
        moment2 = beta_two * moment2_ref[source] + (1.0 - beta_two) * clipped * clipped
        root = jnp.sqrt(moment2) + adam_eps * (1.0 - beta_two**STEP) ** 0.5
        rate = learn_rate * (1.0 - beta_two**STEP) ** 0.5 / (1.0 - beta_one**STEP)
        new_moment1_ref[target] = moment1
        new_moment2_ref[target] = moment2
        new_params_ref[target] = (1.0 - learn_rate * weight_decay) * param - rate * (moment1 / root)

    last = SHARD // UPDATE_N

    @pl.when(step < last)
    def _():
        rows = pl.ds(pl.multiple_of(step * UPDATE_R, UPDATE_R), UPDATE_R)
        at = pl.ds(pl.multiple_of(step * UPDATE_N, UPDATE_N), UPDATE_N)
        update(at, pl.ds(0, UPDATE_N), grads[rows, :].reshape(UPDATE_N))

    @pl.when(step == last)
    def _():
        first = last * UPDATE_R
        whole = WHOLE_R - first
        rest = SHARD // LANES - WHOLE_R
        for r0, n in ((0, whole), (whole, rest)):
            update(
                pl.ds((first + r0) * LANES, n * LANES),
                pl.ds(r0 * LANES, n * LANES),
                grads[first + r0 : first + r0 + n, :].reshape(n * LANES),
            )
        r0 = whole + rest
        update(
            pl.ds(SHARD - REST, REST),
            pl.ds(r0 * LANES, REST),
            grads[first + r0 : first + r0 + 1, 0:REST].reshape(REST),
        )


def gather_grads(slab_ref, own_ref, core_ref, vfe_ref, norm_ref, quarter_ref, nat, grads):
    join_chunks(slab_ref, quarter_ref, own_ref, core_ref)
    vfe = vfe_ref[0:VFE_R, :]
    squares = vfe_ref[VFE_R : VFE_R + 1, :][0, 0] + jnp.sum(vfe * vfe)
    norm = jnp.sqrt(jnp.broadcast_to(squares, (8, LANES)))
    norm_ref[0, 0] = norm[0, 0]
    scale = (clip_level / jnp.maximum(norm, clip_level))[0:1, :]
    grads[FLAT_R:, :] = jnp.zeros((grads.shape[0] - FLAT_R, LANES), f32)
    span = 480
    for s in range(SLABS):

        @pl.when(slab_ref[0] == s)
        def _(s=s):
            lanes, first = 16 + 28 * s, 15 - 4 * s
            low = max(0, min(SHARD_T // 2, (WIDE_T[0] - STRIDE_T * s + 1) // 2))
            high = max(low, min(SHARD_T // 2, (WIDE_T[1] - STRIDE_T * s + 1) // 2))
            for a, b, wide in ((0, low, False), (low, high, True), (high, SHARD_T // 2, False)):

                def block(i, carry, wide=wide):
                    base = pl.multiple_of(32 * i, 32)
                    even, odd = quarter_ref[2 * i].astype(f32), quarter_ref[2 * i + 1].astype(f32)
                    if wide:
                        nat[pl.ds(base, 16, stride=2), :] = even
                        nat[pl.ds(base + 1, 16, stride=2), :] = odd
                    else:
                        nat[pl.ds(base, 16), :] = even
                        nat[pl.ds(base + 16, 16), :] = odd
                    return carry

                if b > a:
                    lax.fori_loop(a, b, block, 0, unroll=4)
            if s == 0:
                nat[0:VFE_R, :] = vfe
            lane = lane_of((span, LANES))
            count = FLAT_R // span + (FLAT_R % span > 0)
            for i in range(count):
                r0 = i * span
                n = min(span, FLAT_R - r0)
                here = lane_roll(nat[first + r0 : first + r0 + n, :], -lanes)
                after = lane_roll(nat[first + r0 + 1 : first + r0 + 1 + n, :], -lanes)
                grads[r0 : r0 + n, :] = jnp.where(lane[:n] < LANES - lanes, here, after) * scale


def update_shard(info, own, core, vfe, params, moment1, moment2):
    block = pl.BlockSpec((UPDATE_N,), lambda i: (i,))
    steps = pl.cdiv(SHARD, UPDATE_N)
    return pl.pallas_call(
        update_kernel,
        grid=(steps,),
        out_shape=(shape((SHARD,)),) * 3 + (shape((1, 1)),),
        in_specs=[smem()] + [vmem()] * 6,
        out_specs=(block,) * 3 + (smem(),),
        scratch_shapes=[
            pltpu.VMEM((PAD_T, TILE, LANES), bf16),
            pltpu.VMEM((5120, LANES), f32),
            pltpu.VMEM((steps * UPDATE_R, LANES), f32),
        ],
        compiler_params=pltpu.CompilerParams(vmem_limit_bytes=24 * 1024 * 1024),
    )(info, own, core, vfe, params, moment1, moment2)


PART = 5
PARTS = PTS // PART
WIDE = PART * VOX
VFE_SCRATCH = [
    pltpu.VMEM((VOX // LANES, PTS * 16, LANES), f32),
    pltpu.VMEM((16, LANES), f32),
    pltpu.VMEM((64, LANES), f32),
]


def spread_points(points_ref, x_scr):
    x_scr[...] = jnp.zeros_like(x_scr)
    for c in range(7):
        plane = points_ref[c].astype(f32)
        for b in range(VOX // LANES):
            x_scr[b, pl.ds(c, PTS, stride=16), :] = plane[:, b * LANES : (b + 1) * LANES]


def vfe_weights(rows_ref, w1_scr, w2_scr):
    line = rows_ref[0].astype(f32)
    lane = lane_of((16, LANES))
    for o in range(VF1):
        w1_scr[o : o + 1, :] = jnp.where(lane < 7, lane_roll(line, -(16 + 7 * o)), 0.0)[15:16]
    two = rows_ref[1].astype(f32)
    for k in range(4):
        w2_scr[pl.ds(k, 16, stride=4), :] = jnp.where(lane < 32, lane_roll(two, -32 * k), 0.0)
    w1 = w1_scr[...].astype(bf16)[:, 0:16]
    w2 = w2_scr[...]
    w2a = w2.astype(bf16)[:, 0:16]
    w2b = lane_roll(w2, -16).astype(bf16)[:, 0:16]
    w3 = rows_ref[2:10].reshape(FC, LANES)
    w3a = w3[:, 0:64]
    w3b = lane_roll(w3.astype(f32), -64).astype(bf16)[:, 0:64]
    return w1, w2a, w2b, w3a, w3b


def points_part(ref, i):
    return jnp.concatenate(
        [
            ref[b, pl.ds(pl.multiple_of((PART * i + k) * 16, 16), 16), :]
            for k in range(PART)
            for b in range(VOX // LANES)
        ],
        1,
    )


def set_points_part(ref, i, value):
    for k in range(PART):
        for b in range(VOX // LANES):
            at = k * VOX + b * LANES
            ref[b, pl.ds(pl.multiple_of((PART * i + k) * 16, 16), 16), :] = value[:, at : at + LANES]


def part_sum(value):
    total = value[:, 0:VOX]
    for k in range(1, PART):
        total = total + value[:, k * VOX : (k + 1) * VOX]
    return total


def valid_part(i, counts):
    return jnp.concatenate([(PART * i + k < counts).astype(f32) for k in range(PART)], 1)


def widen(value):
    return jnp.concatenate([value] * PART, 1)


def vfe_front(weights, counts, inverse, x_scr, j1_ref, j2_ref, kept=None, done=None):
    w1, w2a, w2b, w3a, w3b = weights
    total = jnp.zeros((VF1, VOX), f32)
    for i in range(PARTS):
        x = points_part(x_scr, i).astype(bf16)
        z = mm(w1, x)
        value = silu(z)
        j1_ref[i] = value.astype(bf16)
        if kept is not None:
            kept[0][i] = x
            kept[1][i] = silu_slope(z).astype(bf16)
        total = total + part_sum(value * valid_part(i, counts))
    mean_one = (total * inverse).astype(bf16)
    shared_two = widen(mm(w2b, mean_one))
    total = jnp.zeros((VF2, VOX), f32)
    for i in range(PARTS):
        z = mm(w2a, j1_ref[i]) + shared_two
        value = silu(z)
        j2_ref[i] = value.astype(bf16)
        if kept is not None:
            kept[2][i] = silu_slope(z).astype(bf16)
            done(i)
        total = total + part_sum(value * valid_part(i, counts))
    mean_two = (total * inverse).astype(bf16)
    shared_three = widen(mm(w3b, mean_two))
    return mean_one, mean_two, shared_three


def encode_kernel(
    points_ref, counts_ref, cells_ref, rows_ref, out_ref, s3_ref,
    x_scr, w1_scr, w2_scr, j1_scr, j2_scr, s3_scr, sems,
):
    spread_points(points_ref, x_scr)
    weights = vfe_weights(rows_ref, w1_scr, w2_scr)
    counts = counts_ref[...]
    inverse = 1.0 / counts.astype(f32)
    _, _, shared_three = vfe_front(weights, counts, inverse, x_scr, j1_scr, j2_scr)
    w3a = weights[3]
    wide_inverse = widen(inverse)
    total = jnp.zeros((FC, VOX), f32)
    copies = []
    for i in range(PARTS):
        z = mm(w3a, j2_scr[i]) + shared_three
        gate = sigmoid(z)
        value = z * gate
        share = valid_part(i, counts) * wide_inverse
        s3_scr[i] = ((gate + value - value * gate) * share).astype(bf16)
        copies += begin([s3_scr.at[i]], [s3_ref.at[i]], sems, i)
        total = total + part_sum(value * share)
    features = total.astype(bf16)
    cells = cells_ref[...]
    row = row_of((16, VOX))
    places = jnp.where(row == 0, cells // GX, cells % GX).astype(f32).astype(bf16)
    out_ref[0:FC, :] = features
    out_ref[FC : FC + 16, :] = places
    finish(copies)


def encode(points, counts, cells, rows):
    return call(
        encode_kernel,
        10,
        56,
        (shape((FC + 16, VOX), bf16), shape((PARTS, 128, WIDE), bf16)),
        [vmem()] * 4,
        (vmem(), anywhere()),
        VFE_SCRATCH
        + [
            pltpu.VMEM((PARTS, 16, WIDE), bf16),
            pltpu.VMEM((PARTS, 64, WIDE), bf16),
            pltpu.VMEM((PARTS, 128, WIDE), bf16),
            pltpu.SemaphoreType.DMA((PARTS,)),
        ],
    )(points, counts, cells, rows)


def encode_slopes_kernel(
    points_ref, counts_ref, rows_ref,
    x_ref, j1_ref, j2_ref, s1_ref, s2_ref, m1_ref, m2_ref,
    x_scr, w1_scr, w2_scr, xs_scr, j1_scr, j2_scr, s1_scr, s2_scr, sems,
):
    spread_points(points_ref, x_scr)
    weights = vfe_weights(rows_ref, w1_scr, w2_scr)
    counts = counts_ref[...]
    inverse = 1.0 / counts.astype(f32)
    copies = []

    def done(i):
        if i == 0:
            copies.extend(begin((xs_scr, j1_scr, s1_scr), (x_ref, j1_ref, s1_ref), sems, 0))
        copies.extend(
            begin((j2_scr.at[i], s2_scr.at[i]), (j2_ref.at[i], s2_ref.at[i]), sems, 3 + 2 * i)
        )

    mean_one, mean_two, _ = vfe_front(
        weights, counts, inverse, x_scr, j1_scr, j2_scr, (xs_scr, s1_scr, s2_scr), done
    )
    m1_ref[...] = mean_one
    m2_ref[...] = mean_two
    finish(copies)


LOW = (PARTS, 16, WIDE)
MID = (PARTS, 64, WIDE)
HIGH = (PARTS, 128, WIDE)


def encode_slopes(points, counts, rows):
    return call(
        encode_slopes_kernel,
        7,
        56,
        tuple(shape(d, bf16) for d in (LOW, LOW, MID, LOW, MID, (VF1, VOX), (VF2, VOX))),
        [vmem()] * 3,
        (anywhere(),) * 5 + (vmem(),) * 2,
        VFE_SCRATCH
        + [pltpu.VMEM(d, bf16) for d in (LOW, LOW, MID, LOW, MID)]
        + [pltpu.SemaphoreType.DMA((3 + 2 * PARTS,))],
    )(points, counts, rows)


def encode_back_kernel(
    counts_ref, rows_ref, g0_ref, g1_ref, g2_ref, g3_ref, j2_scr, s3_scr, m2_ref,
    d2_scr, shared_ref, weight_ref,
    w1_scr, w2_scr,
):
    _, _, _, w3a, w3b = vfe_weights(rows_ref, w1_scr, w2_scr)
    inverse = 1.0 / counts_ref[...].astype(f32)
    grad = g0_ref[...].astype(f32)
    for ref in (g1_ref, g2_ref, g3_ref):
        grad = grad + ref[...].astype(f32)
    grad_three = widen(grad)
    total = jnp.zeros((FC, VOX), f32)
    weight = jnp.zeros((FC, VF2), f32)
    for i in range(PARTS):
        dz = grad_three * s3_scr[i].astype(f32)
        low = dz.astype(bf16)
        d2_scr[i] = mm_tn(w3a, low).astype(bf16)
        total = total + part_sum(dz)
        weight = weight + mm_nt(low, j2_scr[i])
    total = total.astype(bf16)
    weight_ref[...] = jnp.concatenate([weight, mm_nt(total, m2_ref[...])], 1)
    shared_ref[...] = mm_tn(w3b, total) * inverse


def encode_back(counts, rows, grad, j2, s3, m2):
    return call(
        encode_back_kernel,
        8,
        16,
        (held(MID), shape((VF2, VOX)), shape((FC, LANES))),
        [vmem()] * 9,
        (vmem(),) * 3,
        VFE_SCRATCH[1:],
    )(counts, rows, *grad, j2, s3, m2)


def points_back_kernel(
    counts_ref, rows_ref, d2_scr, shared_ref, w3_ref, xs_scr, j1_scr, s1_scr, s2_scr, m1_ref,
    out_ref, weight_ref,
    x_scr, w1_scr, w2_scr, d1_scr,
):
    w1, w2a, w2b, _, _ = vfe_weights(rows_ref, w1_scr, w2_scr)
    counts = counts_ref[...]
    inverse = 1.0 / counts.astype(f32)
    grad_two = widen(shared_ref[...])
    total = jnp.zeros((VF2, VOX), f32)
    grad_w2a = jnp.zeros((VF2, VF1), f32)
    for i in range(PARTS):
        dz = d2_scr[i].astype(f32) + valid_part(i, counts) * grad_two
        dz = dz * s2_scr[i].astype(f32)
        low = dz.astype(bf16)
        d1_scr[i] = mm_tn(w2a, low)
        total = total + part_sum(dz)
        grad_w2a = grad_w2a + mm_nt(low, j1_scr[i])
    total = total.astype(bf16)
    grad_w2b = mm_nt(total, m1_ref[...])
    grad_one = widen(mm_tn(w2b, total) * inverse)
    grad_w1 = jnp.zeros((VF1, 16), f32)
    for i in range(PARTS):
        dz = (d1_scr[i] + valid_part(i, counts) * grad_one) * s1_scr[i].astype(f32)
        low = dz.astype(bf16)
        set_points_part(x_scr, i, mm_tn(w1, low))
        grad_w1 = grad_w1 + mm_nt(low, xs_scr[i])
    for c in range(7):
        for b in range(VOX // LANES):
            out_ref[c, :, b * LANES : (b + 1) * LANES] = x_scr[b, pl.ds(c, PTS, stride=16), :]

    lane = lane_of((16, LANES))
    w1_scr[...] = jnp.concatenate([grad_w1, jnp.zeros((16, LANES - 16), f32)], 1)
    spread = jnp.where(lane < 7, w1_scr[...], 0.0)
    line = jnp.zeros((16, LANES), f32)
    row = row_of((16, LANES))
    for o in range(VF1):
        line = line + jnp.where(row == o, lane_roll(spread, 16 + 7 * o), 0.0)
    line = jnp.sum(line, axis=0, keepdims=True)
    weight_ref[0:16, :] = jnp.where(row == 15, line, 0.0)
    w2_scr[...] = jnp.concatenate([grad_w2a, grad_w2b, jnp.zeros((64, LANES - 32), f32)], 1)
    two = jnp.zeros((16, LANES), f32)
    for k in range(4):
        two = two + lane_roll(w2_scr[pl.ds(k, 16, stride=4), :], 32 * k)
    weight_ref[16:32, :] = two
    weight_ref[32:160, :] = w3_ref[...]
    weight_ref[160:168, :] = jnp.zeros((8, LANES), f32)


def points_back(counts, rows, back, kept):
    return call(
        points_back_kernel,
        7,
        14,
        (shape((7, PTS, VOX)), shape((VFE_R + 8, LANES))),
        [vmem()] * 10,
        (vmem(), vmem()),
        VFE_SCRATCH + [pltpu.VMEM(LOW, f32)],
    )(counts, rows, *back, *kept)


R3 = ROWS + 1
R3W = R3 * GX
R2W = (R3 + 2) * GX
R1W = (R3 + 4) * GX
RG = R3 + 6
RGW = RG * GX
HX = GX // 2
L1_R = ROWS // 2 * HX


def cell_marks(places, first_row):
    value = places.astype(f32)
    high, low = value[0:1], value[1:2]
    upper = high >= GY
    row = jnp.where(upper, high - GY, high)
    column = lax.broadcasted_iota(jnp.int32, (GX, VOX), 0).astype(f32)
    column = (column == low).astype(f32).astype(bf16)
    pieces = []
    for w in range(RG):
        target = first_row - 3 + w
        inside = jnp.logical_and(target >= 0, target < GY)
        target = jnp.where(inside, target, -1).astype(f32)
        pieces.append(column * (row == target).astype(f32).astype(bf16))
    upper = upper.astype(f32)
    return jnp.concatenate(pieces, 0), 1.0 - upper, upper


def conv_weights(rows_ref, start, taps, half, place, scr):
    lane = lane_of((half, LANES))
    left = lane < 64
    for t in range(taps):
        r = []
        for kx in range(3):
            base = start + (3 * t + kx) * half
            r.append(rows_ref[base // TILE : (base + half) // TILE].reshape(half, LANES).astype(f32))
        turned = [lane_roll(v, 64) for v in r]
        at = place(t)
        scr[0, pl.ds(at, half, stride=2), :] = jnp.where(left, r[1], turned[0])
        scr[0, pl.ds(at + 1, half, stride=2), :] = jnp.where(left, turned[1], r[0])
        scr[1, pl.ds(at, half, stride=2), :] = jnp.where(left, r[2], 0.0)
        scr[1, pl.ds(at + 1, half, stride=2), :] = jnp.where(left, turned[2], 0.0)


def conv_weight_grads(out_ref, start, taps, half, place, scr):
    lane = lane_of((half, LANES))
    left = lane < 64
    for t in range(taps):
        at = place(t)
        even = [scr[b, pl.ds(at, half, stride=2), :] for b in range(2)]
        odd = [scr[b, pl.ds(at + 1, half, stride=2), :] for b in range(2)]
        values = (
            jnp.where(left, lane_roll(even[0], 64), odd[0]),
            jnp.where(left, even[0], lane_roll(odd[0], 64)),
            jnp.where(left, even[1], lane_roll(odd[1], 64)),
        )
        for kx in range(3):
            base = start + (3 * t + kx) * half
            out_ref[base // TILE : (base + half) // TILE] = (
                values[kx].astype(bf16).reshape(half // TILE, TILE, LANES)
            )


def both_halves(out_ref, scr):
    for b in range(2):
        out_ref[:, b * LANES : (b + 1) * LANES] = scr[b].astype(bf16)


def keep_halves(scr, value):
    for b in range(2):
        scr[b] = value[:, b * LANES : (b + 1) * LANES]


def tap_place(t):
    return 128 * t


def pair_place(t):
    kd, ky = t // 3, t % 3
    return 128 * ky + 64 * kd if kd < 2 else 384 + 128 * ky


def join_columns(p):
    first, last = p[:, 0:128], p[:, 128:256]
    left = lane_of(first.shape) < 64
    half = jnp.where(left, first + shift_in(last, -1, GX), shift_in(first, 1, GX))
    return half + lane_roll(half, 64)


def split_columns(d):
    left = lane_of(d.shape) < 64
    first = jnp.where(left, d, lane_roll(shift_in(d, -1, GX), 64))
    last = jnp.where(left, shift_in(d, 1, GX), 0.0)
    return jnp.concatenate([first, last], 1).astype(bf16)


def inside_rows(rows, first_row):
    place = first_row + row_of((rows, LANES)) // GX
    return jnp.logical_and(place >= 0, place < GY)


def grid_taps(grid_ref, k):
    return jnp.concatenate(
        [grid_ref[2 * k + kd, ky * GX : ky * GX + R1W, :] for kd in range(3) for ky in range(3)], 1
    )


def pair_taps(ref, at, rows):
    return jnp.concatenate(
        [ref[at, ky * GX : ky * GX + rows, :] for ky in range(3)]
        + [ref[at + 2, ky * GX : ky * GX + rows, :] for ky in range(3)],
        1,
    )


def level_taps(ref):
    planes = {}
    for xp in range(2):
        for yp in range(2):
            count = ROWS // 2 + 1 - yp
            planes[yp, xp] = jnp.concatenate(
                [ref[pl.ds((2 * a + yp) * GX + xp, HX, stride=2), :] for a in range(count)], 0
            )
    pieces = []
    for ky in range(3):
        for kx in range(3):
            v = planes[ky % 2, int(kx != 1)]
            v = v[HX:] if ky == 2 else v[0:L1_R]
            pieces.append((shift_in(v, 1, HX) if kx == 0 else v).astype(bf16))
    return jnp.concatenate(pieces, 1)


def level_taps_back(ref, grad):
    planes = {}
    edge = jnp.zeros((HX, LANES), f32)
    for ky in range(3):
        for kx in range(3):
            t = 3 * ky + kx
            v = grad[:, t * LANES : (t + 1) * LANES]
            v = shift_in(v, -1, HX) if kx == 0 else v
            if ky != 1:
                v = jnp.concatenate([edge, v] if ky == 2 else [v, edge], 0)
            at = (ky % 2, int(kx != 1))
            planes[at] = planes[at] + v if at in planes else v
    for (yp, xp), v in planes.items():
        for a in range(ROWS // 2 + 1 - yp):
            ref[pl.ds((2 * a + yp) * GX + xp, HX, stride=2), :] = v[a * HX : (a + 1) * HX]


GRID = (9, RGW, LANES)
FIRST = (6, R1W, LANES)
SECOND = (6, R2W, LANES)


def volume_kernel(
    slab_ref, f0_ref, f1_ref, f2_ref, f3_ref, own_ref, core_ref,
    level_ref, grid_ref, first_ref, second_ref, taps_ref, z1_ref, z2_ref, z3_ref, z4_ref, w1_ref, w2_ref, w3_ref, w4_ref,
    rows_ref, w1_scr, w2_scr, bird_scr,
):
    join_chunks(slab_ref, rows_ref, own_ref, core_ref)
    w4_ref[...] = rows_ref[LEVEL_T : LEVEL_T + 72].reshape(1152, LANES)
    w2_scr[...] = jnp.zeros_like(w2_scr)
    conv_weights(rows_ref, VFE_R, 9, 64, tap_place, w1_scr)
    both_halves(w1_ref, w1_scr)
    conv_weights(rows_ref, VFE_R + 1728, 9, 32, pair_place, w2_scr)
    both_halves(w2_ref, w2_scr)
    conv_weights(rows_ref, VFE_R + 2592, 9, 32, pair_place, w2_scr)
    both_halves(w3_ref, w2_scr)

    first_row = slab_ref[0] * ROWS - 1
    grid_ref[0] = jnp.zeros((RGW, FC), bf16)
    for slot, f_ref in enumerate((f0_ref, f1_ref, f2_ref, f3_ref)):
        t = jnp.bitwise_xor(slab_ref[0], slot)
        features = f_ref[0:FC, :]
        marks, lower, upper = cell_marks(f_ref[FC : FC + 16, :], first_row)
        both = jnp.concatenate([features * lower.astype(bf16), features * upper.astype(bf16)], 0)
        cells = mm_nt(marks, both).astype(bf16)
        grid_ref[1 + 2 * t] = cells[:, 0:FC]
        grid_ref[2 + 2 * t] = cells[:, FC:]

    first_ref[0] = jnp.zeros((R1W, LANES), bf16)
    first_ref[5] = jnp.zeros((R1W, LANES), bf16)
    keep = inside_rows(R1W, first_row - 2)
    for k in range(4):
        z = join_columns(mm(grid_taps(grid_ref, k), w1_ref[...]))
        z1_ref[k] = jnp.where(keep, silu_slope(z), 0.0).astype(bf16)
        value = jnp.where(keep, silu(z), 0.0).astype(bf16)
        first_ref[k + 1, :, 0:64] = value[:, 0:64]
        first_ref[k, :, 64:128] = value[:, 64:128]
    first_ref[4, :, 64:128] = jnp.zeros((R1W, 64), bf16)

    second_ref[0] = jnp.zeros((R2W, LANES), bf16)
    second_ref[5] = jnp.zeros((R2W, LANES), bf16)
    keep = inside_rows(R2W, first_row - 1)
    for k in range(4):
        z = join_columns(mm(pair_taps(first_ref, k, R2W), w2_ref[...]))
        z2_ref[k] = jnp.where(keep, silu_slope(z), 0.0).astype(bf16)
        value = jnp.where(keep, silu(z), 0.0).astype(bf16)
        second_ref[k + 1, :, 0:64] = value[:, 0:64]
        second_ref[k, :, 64:128] = value[:, 64:128]
    second_ref[4, :, 64:128] = jnp.zeros((R2W, 64), bf16)

    z3 = []
    for k in range(2):
        z3.append(join_columns(mm(pair_taps(second_ref, 2 * k, R3W), w3_ref[...])))
    z = jnp.where(lane_of((R3W, LANES)) < 64, z3[0], z3[1])
    keep = inside_rows(R3W, first_row)
    z3_ref[...] = jnp.where(keep, silu_slope(z), 0.0).astype(bf16)
    bird_scr[...] = jnp.where(keep, silu(z), 0.0)
    taps = level_taps(bird_scr)
    taps_ref[...] = taps
    z = mm(taps, w4_ref[...])
    z4_ref[...] = silu_slope(z).astype(bf16)
    level_ref[...] = silu(z).astype(bf16)


LEVEL_T = VFE_T + 216


def volume(info, features, early):
    return call(
        volume_kernel,
        11,
        56,
        (
            shape((L1_R, LANES), bf16),
            shape(GRID, bf16),
            shape(FIRST, bf16),
            shape(SECOND, bf16),
            shape((L1_R, 1152), bf16),
            shape((4, R1W, LANES), bf16),
            shape((4, R2W, LANES), bf16),
            shape((R3W, LANES), bf16),
            shape((L1_R, LANES), bf16),
            shape((1152, 256), bf16),
            shape((768, 256), bf16),
            shape((768, 256), bf16),
            shape((1152, LANES), bf16),
        ),
        [smem()] + [vmem()] * 6,
        (vmem(),) * 13,
        [
            pltpu.VMEM((PAD_T, TILE, LANES), bf16),
            pltpu.VMEM((2, 1152, LANES), f32),
            pltpu.VMEM((2, 768, LANES), f32),
            pltpu.VMEM((R3W, LANES), f32),
        ],
    )(info, *features, *early)


def volume_back(
    slab, f_ref, level_grad, z1_ref, z2_ref, z3_ref, z4_ref, w1_ref, w2_ref, w3_ref, w4_ref,
    out_refs, d4_ref, sp3_ref, sp2_ref, sp1_ref,
    bird_scr, acc2, acc1, accg,
):
    dz = (level_grad * z4_ref[...].astype(f32)).astype(bf16)
    d4_ref[...] = dz
    level_taps_back(bird_scr, mm_nt(dz, w4_ref[...]))
    dz = bird_scr[...] * z3_ref[...].astype(f32)
    acc2[...] = jnp.zeros_like(acc2)
    acc1[...] = jnp.zeros_like(acc1)
    accg[...] = jnp.zeros_like(accg)

    def pair_back(acc, at, rows, spread, weight):
        back = mm_nt(spread, weight)
        for ky in range(3):
            acc[at, ky * GX : ky * GX + rows, :] += back[:, 128 * ky : 128 * ky + 128]
            acc[at + 2, ky * GX : ky * GX + rows, :] += back[:, 384 + 128 * ky : 512 + 128 * ky]

    def layer_grad(acc, m):
        return acc[m] + lane_roll(acc[m - 1], 64)

    for k in range(2):
        spread = split_columns(dz if k == 0 else lane_roll(dz, 64))
        sp3_ref[k] = spread
        pair_back(acc2, 2 * k, R3W, spread, w3_ref[...])
    for k in range(4):
        spread = split_columns(layer_grad(acc2, k + 1) * z2_ref[k].astype(f32))
        sp2_ref[k] = spread
        pair_back(acc1, k, R2W, spread, w2_ref[...])
    for k in range(4):
        spread = split_columns(layer_grad(acc1, k + 1) * z1_ref[k].astype(f32))
        sp1_ref[k] = spread
        back = mm_nt(spread, w1_ref[...])
        for kd in range(3):
            for ky in range(3):
                t = 3 * kd + ky
                accg[2 * k + kd, ky * GX : ky * GX + R1W, :] += back[:, 128 * t : 128 * t + 128]
    for slot in range(SLABS):
        t = jnp.bitwise_xor(slab, slot)
        marks, lower, upper = cell_marks(f_ref[slot, FC : FC + 16, :], slab * ROWS - 1)
        both = jnp.concatenate([accg[1 + 2 * t].astype(bf16), accg[2 + 2 * t].astype(bf16)], 1)
        both = mm_tn(both, marks)
        value = both[0:FC] * lower + both[FC:] * upper
        out_refs[slot][...] = value.astype(bf16)


SPREADS = ((L1_R, LANES), (2, R3W, 256), (4, R2W, 256), (4, R1W, 256))
BACK_IN = (
    (SLABS, FC + 16, VOX),
    (4, R1W, LANES),
    (4, R2W, LANES),
    (R3W, LANES),
    (L1_R, LANES),
    (1152, 256),
    (768, 256),
    (768, 256),
    (1152, LANES),
)


def volume_weights_kernel(
    info_ref, taps_ref, d4_ref, second_ref, sp3_ref, first_ref, sp2_ref, grid_ref, sp1_ref,
    own_ref, core_ref,
    weight_ref, g1_scr, g2_scr,
):
    weight_ref[0:VFE_T] = jnp.zeros((VFE_T, TILE, LANES), bf16)
    weight_ref[VFE_T + EARLY_T : PAD_T] = jnp.zeros((PAD_T - VFE_T - EARLY_T, TILE, LANES), bf16)
    total = mm_tn(taps_ref[...], d4_ref[...])
    weight_ref[LEVEL_T : LEVEL_T + 72] = total.astype(bf16).reshape(72, TILE, LANES)
    total = mm_tn(pair_taps(second_ref, 0, R3W), sp3_ref[0])
    keep_halves(g2_scr, total + mm_tn(pair_taps(second_ref, 2, R3W), sp3_ref[1]))
    conv_weight_grads(weight_ref, VFE_R + 2592, 9, 32, pair_place, g2_scr)
    total = jnp.zeros((768, 256), f32)
    for k in range(4):
        total = total + mm_tn(pair_taps(first_ref, k, R2W), sp2_ref[k])
    keep_halves(g2_scr, total)
    conv_weight_grads(weight_ref, VFE_R + 1728, 9, 32, pair_place, g2_scr)
    total = jnp.zeros((1152, 256), f32)
    for k in range(4):
        total = total + mm_tn(grid_taps(grid_ref, k), sp1_ref[k])
    keep_halves(g1_scr, total)
    conv_weight_grads(weight_ref, VFE_R, 9, 64, tap_place, g1_scr)
    split_chunks(info_ref, weight_ref, 0, own_ref, core_ref)


def volume_weights(info, kept, grads):
    grid, first, second, taps = kept
    d4, sp3, sp2, sp1 = grads
    return call(
        volume_weights_kernel,
        8,
        14,
        (shape(CHUNKS, bf16),) * 2,
        [smem()] + [vmem()] * 8,
        (vmem(),) * 2,
        [
            pltpu.VMEM((PAD_T, TILE, LANES), bf16),
            pltpu.VMEM((2, 1152, LANES), f32),
            pltpu.VMEM((2, 768, LANES), f32),
        ],
    )(info, taps, d4, second, sp3, first, sp2, grid, sp1)


def split_planes(ref, height, width):
    planes = []
    for yp in range(2):
        for xp in range(2):
            planes.append(
                jnp.concatenate(
                    [
                        ref[pl.ds((2 * a + yp) * width + xp, width // 2, stride=2), :]
                        for a in range(height // 2)
                    ],
                    0,
                )
            )
    return planes


def merge_planes(ref, planes, height, width):
    half = width // 2
    for yp in range(2):
        for xp in range(2):
            for a in range(height // 2):
                ref[pl.ds((2 * a + yp) * width + xp, half, stride=2), :] = planes[2 * yp + xp][
                    a * half : a * half + half
                ]


def stride_taps(planes, width):
    pieces = []
    for ky in range(3):
        for kx in range(3):
            v = planes[2 * (ky != 1) + (kx != 1)]
            v = shift_in(v, 1, width) if kx == 0 else v
            pieces.append((shift_out(v, 1, width) if ky == 0 else v).astype(bf16))
    return jnp.concatenate(pieces, 1)


def stride_taps_back(grad, width):
    planes = [None] * 4
    channels = grad.shape[1] // 9
    for ky in range(3):
        for kx in range(3):
            t = 3 * ky + kx
            v = grad[:, t * channels : (t + 1) * channels]
            v = shift_out(v, -1, width) if ky == 0 else v
            v = shift_in(v, -1, width) if kx == 0 else v
            at = 2 * (ky != 1) + (kx != 1)
            planes[at] = v if planes[at] is None else planes[at] + v
    return planes


def full_taps(v, width):
    across = [shift_in(v, 1 - kx, width).astype(bf16) for kx in range(3)]
    return jnp.concatenate(
        [shift_out(across[kx], 1 - ky, width) for ky in range(3) for kx in range(3)], 1
    )


def full_taps_back(grad, width):
    channels = grad.shape[1] // 9
    total = None
    for kx in range(3):
        column = None
        for ky in range(3):
            t = 3 * ky + kx
            v = shift_out(grad[:, t * channels : (t + 1) * channels], ky - 1, width)
            column = v if column is None else column + v
        column = shift_in(column, kx - 1, width)
        total = column if total is None else total + column
    return total


HY = 16
CELLS = HY * HX


def region_kernel(
    slab_ref, counts_ref, l0_ref, l1_ref, l2_ref, l3_ref, anchors_ref, goals_ref,
    s0_ref, s1_ref, s2_ref, s3_ref, s4_ref, s5_ref, s6_ref, s7_ref,
    f0_in, f1_in, f2_in, f3_in, z1_in, z2_in, z3_in, z4_in, w1_in, w2_in, w3_in, w4_in,
    maps_ref, own_ref, core_ref, o0_ref, o1_ref, o2_ref, o3_ref, d4_ref, sp3_ref, sp2_ref, sp1_ref,
    f_ref, z1_ref, z2_ref, z3_ref, z4_ref, w1_ref, w2_ref, w3_ref, w4_ref,
    bird_scr, acc2, acc1, accg, back_sems,
    wv, gr,
    l1_scr, l2_scr, zu1_scr, zu2_scr, zu3_scr, head_scr, maps_scr, two_scr, three_scr,
):
    slab = slab_ref[0]
    chip, core = batch_place(slab_ref)
    late = (s0_ref, s1_ref, s2_ref, s3_ref, s4_ref, s5_ref, s6_ref, s7_ref)
    for n, (ref, (chips, slots)) in enumerate(zip(late, LATE_ORDER * 2)):
        for k in range(4):
            shard = jnp.bitwise_xor(slab_ref[2], slots[k])
            at = chunk_start(chip, core if n < 4 else 1 - core, chips[k])
            wv[shard, pl.ds(at, CHUNK_T)] = ref[k // 2, k % 2]
    gr[0 : PLANE_T0 + 1] = jnp.zeros((PLANE_T0 + 1, TILE, LANES), bf16)
    gr[PLANE_T0 + 1 + PLANE_T : GRAD_T] = jnp.zeros((GRAD_T - PLANE_T0 - 1 - PLANE_T, TILE, LANES), bf16)
    for slot, ref in enumerate((l0_ref, l1_ref, l2_ref, l3_ref)):
        at = pl.multiple_of(jnp.bitwise_xor(slab, slot) * L1_R, L1_R)
        l1_scr[pl.ds(at, L1_R), :] = ref[...].astype(f32)
    level_one = l1_scr[...]
    arrive = begin(
        (f0_in, f1_in, f2_in, f3_in, z1_in, z2_in, z3_in, z4_in, w1_in, w2_in, w3_in, w4_in),
        (f_ref.at[0], f_ref.at[1], f_ref.at[2], f_ref.at[3], z1_ref, z2_ref, z3_ref, z4_ref, w1_ref, w2_ref, w3_ref, w4_ref),
        back_sems,
    )
    for s in range(1, SLABS):
        wv[s, 0:2] = wv[s, 0:2] + wv[s - 1, STRIDE_T : STRIDE_T + 2]

    def tiles_of(tile, tiles):
        pieces = []
        while tiles:
            s = min((tile + 1) // STRIDE_T, SLABS - 1)
            at = tile + 1 - STRIDE_T * s
            size = min(tiles, STRIDE_T - at) if s < SLABS - 1 else tiles
            pieces.append(wv[s, at : at + size])
            tile, tiles = tile + size, tiles - size
        return pieces[0] if len(pieces) == 1 else jnp.concatenate(pieces, 0)

    def narrow(tile, rows):
        return tiles_of(tile, rows // 16).reshape(rows, LANES)

    def wide(tile, rows):
        both = tiles_of(tile, rows // 8).reshape(rows // 16, 2, TILE, LANES)
        return jnp.concatenate(
            [both[:, 0].reshape(rows, LANES), both[:, 1].reshape(rows, LANES)], 1
        )

    def keep_narrow(tile, value):
        at = tile + 1
        tiles = value.shape[0] // 16
        gr[at : at + tiles] = value.astype(bf16).reshape(tiles, TILE, LANES)

    def keep_wide(tile, value):
        at = tile + 1
        tiles = value.shape[0] // 16
        value = value.astype(bf16)
        left = value[:, 0:128].reshape(tiles, 1, TILE, LANES)
        right = value[:, 128:256].reshape(tiles, 1, TILE, LANES)
        gr[at : at + 2 * tiles] = jnp.concatenate([left, right], 1).reshape(2 * tiles, TILE, LANES)

    t_two, t_three, t_up1, t_up2, t_up3, t_head = 297, 369, 513, 657, 721, 1233

    taps_two = stride_taps(split_planes(l1_scr, 16, 32), 16)
    z2 = mm(taps_two, narrow(t_two, 1152))
    level_two = silu(z2).astype(bf16)
    l2_scr[...] = level_two.astype(f32)
    taps_three = stride_taps(split_planes(l2_scr, 8, 16), 8)
    z3 = mm(taps_three, wide(t_three, 1152))
    level_three = silu(z3).astype(bf16)

    taps_up = full_taps(level_one, 32)
    zu1_scr[...] = mm(taps_up, wide(t_up1, 1152))
    for g in range(4):
        zu2_scr[g] = mm(level_two, wide(t_up2 + 16 * g, 128))
    for g in range(16):
        zu3_scr[g] = mm(level_three, wide(t_up3 + 32 * g, 256))

    lane = lane_of((96, LANES))
    rows = narrow(t_head, 96).astype(f32)
    for c in range(8):
        head_scr[pl.ds(c, 96, stride=8), :] = jnp.where(lane < 16, lane_roll(rows, -16 * c), 0.0)
    head = head_scr[...].astype(bf16)
    head_a, head_b, head_c = head[0:256], head[256:512], head[512:768]
    joined_a = silu(zu1_scr[...]).astype(bf16)
    for g in range(4):
        p, q = g // 2, g % 2
        part = mm(silu(zu2_scr[g]).astype(bf16), head_b)
        for a in range(8):
            two_scr[pl.ds((2 * a + p) * HX + q, 16, stride=2), :] = part[16 * a : 16 * a + 16]
    for g in range(16):
        p, q = g // 4, g % 4
        part = mm(silu(zu3_scr[g]).astype(bf16), head_c)
        for a in range(4):
            three_scr[pl.ds((4 * a + p) * HX + q, 8, stride=4), :] = part[8 * a : 8 * a + 8]
    maps = mm(joined_a, head_a) + two_scr[...] + three_scr[...]
    maps = jnp.transpose(maps)[0:16]
    own = jnp.zeros((16, 128), f32)
    for s in range(SLABS):
        own = own + jnp.where(slab == s, maps[:, 128 * s : 128 * s + 128], 0.0)
    for i in range(HY // SLABS):
        maps_ref[0, :, i, :] = own[:, HX * i : HX * i + HX]

    live_count = counts_ref[0]
    anchors = anchors_ref[...]
    slot = row_of((40, CELLS))
    place = lane_of((40, CELLS))
    positive = [
        jnp.sum(
            jnp.logical_and(anchors == place + k * CELLS, slot < live_count).astype(f32),
            axis=0,
            keepdims=True,
        )
        for k in range(2)
    ]
    row = row_of((16, CELLS))
    second = jnp.logical_or(row == 1, row >= 9)
    marked = jnp.where(second, positive[1], positive[0])
    share = 1.0 / jnp.maximum(live_count.astype(f32), 1.0)
    class_grad = (sigmoid(maps) - marked) * (1.0 / (2.0 * CELLS))
    box_grad = jnp.clip(maps - goals_ref[...], -1.0, 1.0) * marked * share
    dmaps = jnp.where(row < 2, class_grad, box_grad)
    dmaps = jnp.transpose(jnp.concatenate([dmaps, jnp.zeros((LANES - 16, CELLS), f32)], 0))
    maps_scr[...] = dmaps
    low = dmaps.astype(bf16)

    dhead_a = mm_tn(joined_a, low)
    dz = mm_nt(low, head_a) * silu_slope(zu1_scr[...])
    dz = dz.astype(bf16)
    keep_wide(t_up1, mm_tn(taps_up, dz))
    dlevel_one = full_taps_back(mm_nt(dz, wide(t_up1, 1152)), 32)

    dhead_b = jnp.zeros((256, LANES), f32)
    dlevel_two = jnp.zeros((128, 128), f32)
    for g in range(4):
        p, q = g // 2, g % 2
        part = jnp.concatenate(
            [maps_scr[pl.ds((2 * a + p) * HX + q, 16, stride=2), :] for a in range(8)], 0
        ).astype(bf16)
        z = zu2_scr[g]
        dhead_b = dhead_b + mm_tn(silu(z).astype(bf16), part)
        dz = (mm_nt(part, head_b) * silu_slope(z)).astype(bf16)
        keep_wide(t_up2 + 16 * g, mm_tn(level_two, dz))
        dlevel_two = dlevel_two + mm_nt(dz, wide(t_up2 + 16 * g, 128))
    dhead_c = jnp.zeros((256, LANES), f32)
    dlevel_three = jnp.zeros((32, 256), f32)
    for g in range(16):
        p, q = g // 4, g % 4
        part = jnp.concatenate(
            [maps_scr[pl.ds((4 * a + p) * HX + q, 8, stride=4), :] for a in range(4)], 0
        ).astype(bf16)
        z = zu3_scr[g]
        dhead_c = dhead_c + mm_tn(silu(z).astype(bf16), part)
        dz = (mm_nt(part, head_c) * silu_slope(z)).astype(bf16)
        keep_wide(t_up3 + 32 * g, mm_tn(level_three, dz))
        dlevel_three = dlevel_three + mm_nt(dz, wide(t_up3 + 32 * g, 256))

    head_scr[...] = jnp.concatenate([dhead_a, dhead_b, dhead_c], 0)
    rows = jnp.zeros((96, LANES), f32)
    for c in range(8):
        piece = jnp.where(lane < 16, head_scr[pl.ds(c, 96, stride=8), :], 0.0)
        rows = rows + lane_roll(piece, 16 * c)
    keep_narrow(t_head, rows)

    dz = (dlevel_three * silu_slope(z3)).astype(bf16)
    keep_wide(t_three, mm_tn(taps_three, dz))
    merge_planes(l2_scr, stride_taps_back(mm_nt(dz, wide(t_three, 1152)), 8), 8, 16)
    dlevel_two = dlevel_two + l2_scr[...]
    dz = (dlevel_two * silu_slope(z2)).astype(bf16)
    keep_narrow(t_two, mm_tn(taps_two, dz))
    merge_planes(l1_scr, stride_taps_back(mm_nt(dz, narrow(t_two, 1152)), 16), 16, 32)
    dlevel_one = dlevel_one + l1_scr[...]
    l1_scr[...] = dlevel_one
    level_grad = l1_scr[pl.ds(pl.multiple_of(slab * L1_R, L1_R), L1_R), :]
    for s in range(SLABS):

        @pl.when(slab == s)
        def _(s=s):
            start = (15 - 4 * s) * LANES + 16 + 28 * s
            for t in (0, 1) + tuple(range(SHARD_T - 4, PAD_T)):
                tile = STRIDE_T * s - 1 + t
                row = row_of((TILE, LANES))
                if t >= SHARD_T:
                    gr[STRIDE_T * s + t] = jnp.zeros((TILE, LANES), bf16)
                    continue
                if WIDE_T[0] <= tile < WIDE_T[1]:
                    row = 32 * (t // 2) + 2 * row + t % 2
                else:
                    row = TILE * t + row
                at = row * LANES + lane_of((TILE, LANES)) - start
                inside = jnp.logical_and(at >= 0, at < SHARD)
                gr[STRIDE_T * s + t] = jnp.where(
                    inside, gr[STRIDE_T * s + t].astype(f32), 0.0
                ).astype(bf16)

    split_chunks(slab_ref, gr, STRIDE_T * slab, own_ref, core_ref)
    finish(arrive)
    spreads = (d4_ref, sp3_ref, sp2_ref, sp1_ref)
    volume_back(
        slab, f_ref, level_grad, z1_ref, z2_ref, z3_ref, z4_ref, w1_ref, w2_ref, w3_ref, w4_ref,
        (o0_ref, o1_ref, o2_ref, o3_ref), *spreads, bird_scr, acc2, acc1, accg,
    )


LATE_ORDER = (
    ((0, 0, 2, 2), (0, 1, 0, 1)),
    ((1, 1, 3, 3), (0, 1, 0, 1)),
    ((0, 0, 1, 1), (2, 3, 2, 3)),
    ((2, 2, 3, 3), (2, 3, 2, 3)),
)


def region(info, counts, levels, anchors, goals, late, features, kept):
    return call(
        region_kernel,
        20,
        56,
        (
            shape((1, 16, HY // SLABS, HX)),
            shape(CHUNKS, bf16),
            shape(CHUNKS, bf16),
            shape((FC, VOX), bf16),
            shape((FC, VOX), bf16),
            shape((FC, VOX), bf16),
            shape((FC, VOX), bf16),
        )
        + (shape(SPREADS[0], bf16),)
        + tuple(held(d) for d in SPREADS[1:]),
        [smem(), smem()] + [vmem()] * 14 + [anywhere()] * 12,
        (vmem(),) * 11,
        [pltpu.VMEM(d, bf16) for d in BACK_IN]
        + [
            pltpu.VMEM((R3W, LANES), f32),
            pltpu.VMEM((6, R2W, LANES), f32),
            pltpu.VMEM((6, R1W, LANES), f32),
            pltpu.VMEM((9, RGW, LANES), f32),
            pltpu.SemaphoreType.DMA((12,)),
            pltpu.VMEM((SLABS, PAD_T, TILE, LANES), bf16),
            pltpu.VMEM((GRAD_T, TILE, LANES), bf16),
            pltpu.VMEM((512, 128), f32),
            pltpu.VMEM((128, 128), f32),
            pltpu.VMEM((512, 256), f32),
            pltpu.VMEM((4, 128, 256), f32),
            pltpu.VMEM((16, 32, 256), f32),
            pltpu.VMEM((768, LANES), f32),
            pltpu.VMEM((512, LANES), f32),
            pltpu.VMEM((512, LANES), f32),
            pltpu.VMEM((512, LANES), f32),
        ],
    )(info, counts, *levels, anchors, goals, *late, *features, *kept)


def swap(x, axis, bit):
    count = lax.axis_size(axis)
    return lax.ppermute(x, axis, [(i, i ^ bit) for i in range(count)])


def after(x, *earlier):
    return lax.optimization_barrier((x,) + earlier)[0]


def slab_all(x):
    return [x] + [swap(x, "slab", k) for k in range(1, SLABS)]


def plane_all(x):
    return [x] + [swap(x, "batch", 2 * k) for k in range(1, 4)]


def sum_cores(own, other):
    return [(own[k].astype(f32) + other[k].astype(f32)).astype(bf16) for k in range(4)]


def sum_chips(parts):
    total = parts[0].astype(f32)
    for k in range(1, 4):
        total = total + parts[k].astype(f32)
    return total


def send_parts(parts):
    return parts[0:1] + [swap(parts[k], "batch", 2 * k) for k in range(1, 4)]


def send_half(parts):
    return parts[0], parts[1], swap(jnp.stack(parts[2:4]), "batch", 4)


def send_rest(first, second, arrived):
    first = first.astype(f32) + arrived[0].astype(f32)
    second = (second.astype(f32) + arrived[1].astype(f32)).astype(bf16)
    return first, swap(second, "batch", 2)


def to_first(total, low):
    for k in range(1, SLABS):
        total = total + lax.ppermute(low, "slab", [(k, 0)]).astype(f32)
    return total


def from_first(x, slab, *beside):
    far, *beside = lax.optimization_barrier((lax.ppermute(x, "slab", [(0, 2)]),) + beside)
    x = jnp.where(slab == 2, far, x)
    near = lax.ppermute(x, "slab", [(0, 1), (2, 3)])
    return jnp.where(slab % 2 == 1, near, x), *beside


def gathered_shards(own):
    batches = lax.axis_size("batch")
    share = PAD_T // batches
    chunk = lax.dynamic_slice_in_dim(own, lax.axis_index("batch") * share, share, 0)
    shards = lax.all_gather(chunk, ("slab", "batch"), axis=0, tiled=True)
    shards = shards.reshape(SLABS, 4, 2, CHUNK_T, TILE, LANES)
    late = []
    for core in range(2):
        for chips, slots in LATE_ORDER:
            part = jnp.stack([shards[s, c, core] for c, s in zip(chips, slots)])
            late.append(part.reshape((2, 2) + part.shape[1:]))
    return (shards[0, :, 0], shards[0, :, 1]), late


def even_odd(whole):
    both = whole.reshape(4, 2, CHUNK_T, TILE, LANES)
    return both[:, 0], both[:, 1]


def body(
    points, point_counts, voxel_cells, pos_anchors, pos_counts, reg_targets, params, moment1, moment2
):
    batches = lax.axis_size("batch")
    slab, batch = lax.axis_index("slab"), lax.axis_index("batch")
    direct = batches == 8
    zero = jnp.zeros_like(slab)
    info = jnp.stack([slab, batch if direct else zero, slab if direct else zero]).astype(jnp.int32)
    counts = point_counts.reshape(1, VOX)
    goals = jnp.pad(reg_targets.reshape(14, CELLS), ((2, 0), (0, 0)))
    anchors = pos_anchors.reshape(40, 1)

    if direct:
        chunk, first = spread_own(info, params)
        near = jnp.stack([chunk, swap(chunk, "slab", 1)])
        far = swap(near, "slab", 2)
        first, goals, anchors = from_first(first, slab, goals, anchors)
        small, early = first, first[VFE_T:]
        early = plane_all(early)
    else:
        flat_rows = jnp.pad(params, (0, FLAT_R * LANES - SHARD)).reshape(FLAT_R, LANES)
        first = spread_first(flat_rows[0:VFE_R])
        small, goals, anchors = from_first(first, slab, goals, anchors)
        early, late = gathered_shards(spread_shard(info, flat_rows))
    encoded, s3 = encode(points, counts, voxel_cells.reshape(1, VOX), small)
    features = slab_all(encoded)
    if direct:
        early = jnp.stack(lax.optimization_barrier((*early, encoded))[0:4])
        early = (early, swap(early, "batch", 1))
        near, far = lax.optimization_barrier((near, far, early[0]))[0:2]
        later, near, far = lax.optimization_barrier((points, near, far))
        late = [near, swap(near, "batch", 4), far, swap(far, "batch", 2)]
        x, j1, j2, s1, s2, m1, m2 = encode_slopes(later, counts, small)
        near, near_y, far, far_x = lax.optimization_barrier((*late, x))[0:4]
        near, far = jnp.stack([near, near_y]), jnp.stack([far, far_x])
        late = [near, swap(near, "batch", 2), far, swap(far, "batch", 4)]
        features[0] = after(features[0], x, near, far)
        late = late + [swap(near, "batch", 1), swap(far, "batch", 1)]
    else:
        x, j1, j2, s1, s2, m1, m2 = encode_slopes(points, counts, small)
    level, grid, first_pad, second_pad, taps, *kept = volume(info, features, early)
    if direct:
        near, near_x, far, far_y, near_c, far_c = late
        near_c, far_c, level = lax.optimization_barrier((near_c, far_c, level))
        levels = slab_all(level)
        near_x, far_y, *levels = lax.optimization_barrier((near_x, far_y, *levels))
        late = [near, near_x, far, far_y, near_c, swap(near_x, "batch", 1), far_c, swap(far_y, "batch", 1)]
    if not direct:
        levels = slab_all(level)
    maps, quarter_own, quarter_core, *feature_back = region(
        info, pos_counts, levels, anchors, goals, late, features, kept
    )
    feature_back, spreads = feature_back[0:4], feature_back[4:]
    feature_grad = feature_back[0:1] + [swap(feature_back[k], "slab", k) for k in range(1, SLABS)]
    early_own, early_core = volume_weights(info, (grid, first_pad, second_pad, taps), spreads)
    if direct:
        quarter_other = swap(quarter_core, "batch", 1)
        early_own, early_core, *feature_grad = lax.optimization_barrier(
            (early_own, early_core, *feature_grad)
        )
        parts = sum_cores(early_own, swap(early_core, "batch", 1))
        *parts, quarter_own, quarter_other = lax.optimization_barrier(
            (*parts, quarter_own, quarter_other)
        )
        quarter = sum_cores(quarter_own, quarter_other)
        parts = send_parts(parts)
        *quarter, feature_grad[0] = lax.optimization_barrier((*quarter, feature_grad[0]))
        quarter = send_half(quarter)
    back = encode_back(counts, small, feature_grad, j2, s3, m2)
    if direct:
        early_chunk = sum_chips(lax.optimization_barrier((*parts, back[1]))[0:4])
        early_low = early_chunk.astype(bf16)
        shared, early_low = lax.optimization_barrier((back[1], early_low))
        back = [back[0], shared, back[2]]
        early_chunk = to_first(early_chunk, early_low)
    points_grad, vfe_grad = points_back(counts, small, back, (x, j1, s1, s2, m1))
    if direct:
        *quarter, vfe_grad = lax.optimization_barrier((*quarter, vfe_grad))
        chunk, chunk_far = send_rest(*quarter)
        early_chunk, chunk = lax.optimization_barrier((early_chunk, chunk))
        chunk = chunk + chunk_far.astype(f32)
        chunk = (chunk + jnp.where(slab == 0, early_chunk, 0.0)).astype(bf16)
        squares = jnp.sum(jnp.square(chunk.astype(f32)))
        final = plane_all(chunk)
    else:
        whole = jnp.stack([quarter_own, quarter_core], 1).astype(f32)
        whole_early = lax.psum(jnp.stack([early_own, early_core], 1).astype(f32), "slab")
        whole = lax.psum(whole + jnp.where(slab == 0, whole_early, 0.0), "batch").astype(bf16)
        squares = jnp.sum(jnp.square(whole.astype(f32))) / batches
        final = even_odd(whole)

    total = vfe_grad + jnp.pad(jnp.broadcast_to(squares, (8, LANES)), ((VFE_R, 0), (0, 0)))
    for axis, size in (("slab", SLABS), ("batch", batches)):
        bit = 1
        while bit < size:
            total = total + swap(total, axis, bit)
            if direct and axis == "batch" and bit == 1:
                *final, total = lax.optimization_barrier((*final, total))
                final = jnp.stack(final)
                final = (final, swap(final, "batch", 1))
            bit *= 2
    new_params, new_moment1, new_moment2, norm = update_shard(
        info, *final, total, params, moment1, moment2
    )
    return (maps, points_grad, new_moment1, new_moment2, new_params, norm.reshape(()))


def solution(mesh):
    in_specs = (
        P(None, None, ("batch", "slab")),
        P(("batch", "slab")),
        P(("batch", "slab")),
        P("batch", None),
        P("batch"),
        P("batch", None, None, None),
        P("slab"),
        P("slab"),
        P("slab"),
    )
    out_specs = (
        P("batch", None, "slab", None),
        P(None, None, ("batch", "slab")),
        P("slab"),
        P("slab"),
        P("slab"),
        P(),
    )
    return jax.shard_map(body, mesh=mesh, in_specs=in_specs, out_specs=out_specs, check_vma=False)
```

```python
import functools
import math

import jax
import jax.numpy as jnp
from jax import lax
from jax.experimental import pallas as pl
from jax.experimental.pallas import tpu as pltpu
from jax.sharding import PartitionSpec as P

VF1 = 16
VF2 = 64
FC = 128
C3 = 64
STEP = 10
GY = 32
GX = 64
PTS = 35
VOX = 512
SLABS = 4
ROWS = GY // SLABS
LANES = 128
NPARAM = 2537584
SHARD = NPARAM // SLABS

TILE = 16
STRIDE_T = 310
SHARD_T = 312
PAD_T = 320
FLAT_R = 4960
EARLY_T = 288
EARLY_R = EARLY_T * TILE
VFE_T = 10
VFE_R = VFE_T * TILE
PLANE_T0 = 297
PLANE_T = 942
GRAD_T = 3 * STRIDE_T + PAD_T
CHUNK_T = PAD_T // 8
WIDE_T = (369, 1233)

beta_one = 0.9
beta_two = 0.999
adam_eps = 1e-08
learn_rate = 0.02
weight_decay = 0.01
clip_level = 0.002

f32 = jnp.float32
bf16 = jnp.bfloat16


def call(kernel, micros, megabytes, out_shape, in_specs, out_specs, scratch=()):
    return pl.pallas_call(
        kernel,
        out_shape=out_shape,
        in_specs=in_specs,
        out_specs=out_specs,
        scratch_shapes=list(scratch),
        compiler_params=pltpu.CompilerParams(vmem_limit_bytes=megabytes * 1024 * 1024),
        cost_estimate=pl.CostEstimate(
            flops=int(micros * 1e9), transcendentals=0, bytes_accessed=int(micros * 3e6)
        ),
    )


def vmem():
    return pl.BlockSpec(memory_space=pltpu.VMEM)


def smem():
    return pl.BlockSpec(memory_space=pltpu.SMEM)


def anywhere():
    return pl.BlockSpec(memory_space=pl.ANY)


def held(dims, dtype=bf16):
    return pltpu.VMEM(dims, dtype)


def away(dims, dtype=bf16):
    return pltpu.HBM(dims, dtype)


def shape(dims, dtype=f32):
    return jax.ShapeDtypeStruct(dims, dtype)


def mm(a, b):
    return lax.dot_general(a, b, (((1,), (0,)), ((), ())), preferred_element_type=f32)


def mm_nt(a, b):
    return lax.dot_general(a, b, (((1,), (1,)), ((), ())), preferred_element_type=f32)


def mm_tn(a, b):
    return lax.dot_general(a, b, (((0,), (0,)), ((), ())), preferred_element_type=f32)


def sigmoid(z):
    return 0.5 * jnp.tanh(0.5 * z) + 0.5


def silu(z):
    return z * sigmoid(z)


def silu_slope(z):
    s = sigmoid(z)
    return s * (1.0 + z * (1.0 - s))


def lane_of(dims):
    return lax.broadcasted_iota(jnp.int32, dims, len(dims) - 1)


def row_of(dims):
    return lax.broadcasted_iota(jnp.int32, dims, 0)


def lane_roll(x, shift):
    shift = shift % x.shape[-1]
    return x if shift == 0 else pltpu.roll(x, shift, x.ndim - 1)


def shift_in(v, d, width):
    if d == 0:
        return v
    place = row_of(v.shape) % width
    keep = place > 0 if d > 0 else place < width - 1
    return jnp.where(keep, pltpu.roll(v, d % v.shape[0], 0), 0.0)


def shift_out(v, d, width):
    if d == 0:
        return v
    edge = jnp.zeros((width,) + v.shape[1:], v.dtype)
    if d > 0:
        return jnp.concatenate([edge, v[:-width]], 0)
    return jnp.concatenate([v[width:], edge], 0)


def begin(sources, targets, sems, first=0):
    copies = [
        pltpu.make_async_copy(a, b, sems.at[first + n])
        for n, (a, b) in enumerate(zip(sources, targets))
    ]
    for c in copies:
        c.start()
    return copies


def finish(copies):
    for c in copies:
        c.wait()


def batch_place(info_ref):
    return info_ref[1] // 2, info_ref[1] % 2


def chunk_start(chip, core, slot):
    return CHUNK_T * (2 * jnp.bitwise_xor(chip, slot) + core)


def join_chunks(info_ref, out_ref, own_ref, core_ref):
    chip, core = batch_place(info_ref)
    for slot in range(4):
        out_ref[pl.ds(chunk_start(chip, core, slot), CHUNK_T)] = own_ref[slot]
        out_ref[pl.ds(chunk_start(chip, 1 - core, slot), CHUNK_T)] = core_ref[slot]


def split_chunks(info_ref, scr, base, own_ref, core_ref):
    chip, core = batch_place(info_ref)
    for slot in range(4):
        own_ref[slot] = scr[pl.ds(base + chunk_start(chip, core, slot), CHUNK_T)].astype(bf16)
        core_ref[slot] = scr[pl.ds(base + chunk_start(chip, 1 - core, slot), CHUNK_T)].astype(bf16)


CHUNKS = (4, CHUNK_T, TILE, LANES)


def spread_kernel(slab_ref, flat_ref, out_ref, nat):
    nat[...] = jnp.zeros_like(nat)
    span = 480
    for s in range(SLABS):

        @pl.when(slab_ref[0] == s)
        def _(s=s):
            lanes, first = 16 + 28 * s, 15 - 4 * s
            lane = lane_of((span, LANES))
            count = FLAT_R // span + (FLAT_R % span > 0)
            for i in range(count):
                r0 = i * span
                n = min(span, FLAT_R - r0)
                rolled = lane_roll(flat_ref[r0 : r0 + n, :], lanes)
                nat[first + r0 : first + r0 + n, :] += jnp.where(lane[:n] >= lanes, rolled, 0.0)
                nat[first + r0 + 1 : first + r0 + 1 + n, :] += jnp.where(
                    lane[:n] < lanes, rolled, 0.0
                )
            low = max(0, min(SHARD_T // 2, (WIDE_T[0] - STRIDE_T * s + 1) // 2))
            high = max(low, min(SHARD_T // 2, (WIDE_T[1] - STRIDE_T * s + 1) // 2))
            for a, b, wide in ((0, low, False), (low, high, True), (high, SHARD_T // 2, False)):

                def block(i, carry, wide=wide):
                    base = pl.multiple_of(32 * i, 32)
                    if wide:
                        even = nat[pl.ds(base, 16, stride=2), :]
                        odd = nat[pl.ds(base + 1, 16, stride=2), :]
                    else:
                        even = nat[pl.ds(base, 16), :]
                        odd = nat[pl.ds(base + 16, 16), :]
                    out_ref[2 * i] = even.astype(bf16)
                    out_ref[2 * i + 1] = odd.astype(bf16)
                    return carry

                if b > a:
                    lax.fori_loop(a, b, block, 0, unroll=4)

    for t in range(SHARD_T, PAD_T):
        out_ref[t] = jnp.zeros((TILE, LANES), bf16)


def spread_shard(slab, flat_rows):
    return call(
        spread_kernel,
        4,
        56,
        shape((PAD_T, TILE, LANES), bf16),
        [smem(), vmem()],
        vmem(),
        [pltpu.VMEM((5120, LANES), f32)],
    )(slab, flat_rows)


CHUNK_R = CHUNK_T * TILE
CHUNK_N = CHUNK_R * LANES
WHOLE_R = SHARD // LANES // 8 * 8
REST = SHARD - SHARD // LANES * LANES


def flat_tail(flat_ref):
    rest_r = SHARD // LANES - WHOLE_R
    rows = flat_ref[pl.ds(WHOLE_R * LANES, rest_r * LANES)].reshape(rest_r, LANES)
    return rows, flat_ref[pl.ds(SHARD - REST, REST)].reshape(1, REST)


def spread_own_kernel(info_ref, flat_ref, chunk_ref, first_ref, x_scr, nat):
    batch = info_ref[1]

    @pl.when(batch == 0)
    def _():
        x_scr[0:TILE, :] = jnp.zeros((TILE, LANES), f32)
        x_scr[TILE:, :] = flat_ref[pl.ds(0, CHUNK_N)].reshape(CHUNK_R, LANES)

    @pl.when(jnp.logical_and(batch > 0, batch < 7))
    def _():
        start = pl.multiple_of(batch * CHUNK_N - TILE * LANES, 1024)
        rows = CHUNK_R + TILE
        x_scr[...] = flat_ref[pl.ds(start, rows * LANES)].reshape(rows, LANES)

    @pl.when(batch == 7)
    def _():
        first_r = 7 * CHUNK_R - TILE
        whole = WHOLE_R - first_r
        x_scr[0:whole, :] = flat_ref[pl.ds(first_r * LANES, whole * LANES)].reshape(whole, LANES)
        x_scr[whole:, :] = jnp.zeros((CHUNK_R + TILE - whole, LANES), f32)
        rows, last = flat_tail(flat_ref)
        x_scr[whole : whole + rows.shape[0], :] = rows
        x_scr[whole + rows.shape[0] : whole + rows.shape[0] + 1, 0:REST] = last

    def shifted(first, lanes, rows):
        lane = lane_of((rows, LANES))
        here = lane_roll(x_scr[TILE - first : TILE - first + rows, :], lanes)
        above = lane_roll(x_scr[TILE - 1 - first : TILE - 1 - first + rows, :], lanes)
        return jnp.where(lane >= lanes, here, above)

    for s in range(SLABS):

        @pl.when(info_ref[0] == s)
        def _(s=s):
            nat[...] = shifted(15 - 4 * s, 16 + 28 * s, CHUNK_R)
            low = max(0, min(SHARD_T // 2, (WIDE_T[0] - STRIDE_T * s + 1) // 2))
            high = max(low, min(SHARD_T // 2, (WIDE_T[1] - STRIDE_T * s + 1) // 2))
            for i in range(CHUNK_T // 2):
                block = batch * (CHUNK_T // 2) + i
                wide = jnp.logical_and(block >= low, block < high)
                even = nat[pl.ds(32 * i, 16, stride=2), :]
                odd = nat[pl.ds(32 * i + 1, 16, stride=2), :]
                top, bottom = nat[32 * i : 32 * i + 16, :], nat[32 * i + 16 : 32 * i + 32, :]
                chunk_ref[2 * i] = jnp.where(wide, even, top).astype(bf16)
                chunk_ref[2 * i + 1] = jnp.where(wide, odd, bottom).astype(bf16)

    first_ref[VFE_T : VFE_T + CHUNK_T] = chunk_ref[...]
    x_scr[0:TILE, :] = jnp.zeros((TILE, LANES), f32)
    x_scr[TILE : TILE + VFE_R, :] = flat_ref[pl.ds(0, VFE_R * LANES)].reshape(VFE_R, LANES)
    rows = shifted(15, 16, VFE_R).astype(bf16)
    first_ref[0:VFE_T] = rows.reshape(VFE_T, TILE, LANES)


def spread_own(info, params):
    return call(
        spread_own_kernel,
        3,
        56,
        (shape((CHUNK_T, TILE, LANES), bf16), shape((VFE_T + CHUNK_T, TILE, LANES), bf16)),
        [smem(), vmem()],
        (vmem(), vmem()),
        [pltpu.VMEM((CHUNK_R + TILE, LANES), f32), pltpu.VMEM((CHUNK_R, LANES), f32)],
    )(info, params)


def spread_first_kernel(flat_ref, out_ref, nat):
    lanes, first = 16, 15
    lane = lane_of((VFE_R, LANES))
    rolled = lane_roll(flat_ref[...], lanes)
    nat[...] = jnp.zeros_like(nat)
    nat[first : first + VFE_R, :] += jnp.where(lane >= lanes, rolled, 0.0)
    nat[first + 1 : first + 1 + VFE_R, :] += jnp.where(lane < lanes, rolled, 0.0)
    out_ref[...] = nat[0:VFE_R, :].astype(bf16).reshape(VFE_T, TILE, LANES)


def spread_first(flat_rows):
    return call(
        spread_first_kernel,
        1,
        56,
        shape((VFE_T, TILE, LANES), bf16),
        [vmem()],
        vmem(),
        [pltpu.VMEM((VFE_R + 32, LANES), f32)],
    )(flat_rows)


UPDATE_R = 1024
UPDATE_N = UPDATE_R * LANES


def update_kernel(
    slab_ref, own_ref, core_ref, vfe_ref, params_ref, moment1_ref, moment2_ref,
    new_params_ref, new_moment1_ref, new_moment2_ref, norm_ref,
    quarter_ref, nat, grads,
):
    step = pl.program_id(0)

    @pl.when(step == 0)
    def _():
        gather_grads(slab_ref, own_ref, core_ref, vfe_ref, norm_ref, quarter_ref, nat, grads)

    def update(source, target, clipped):
        param = params_ref[source]
        moment1 = beta_one * moment1_ref[source] + (1.0 - beta_one) * clipped
        moment2 = beta_two * moment2_ref[source] + (1.0 - beta_two) * clipped * clipped
        root = jnp.sqrt(moment2) + adam_eps * (1.0 - beta_two**STEP) ** 0.5
        rate = learn_rate * (1.0 - beta_two**STEP) ** 0.5 / (1.0 - beta_one**STEP)
        new_moment1_ref[target] = moment1
        new_moment2_ref[target] = moment2
        new_params_ref[target] = (1.0 - learn_rate * weight_decay) * param - rate * (moment1 / root)

    last = SHARD // UPDATE_N

    @pl.when(step < last)
    def _():
        rows = pl.ds(pl.multiple_of(step * UPDATE_R, UPDATE_R), UPDATE_R)
        at = pl.ds(pl.multiple_of(step * UPDATE_N, UPDATE_N), UPDATE_N)
        update(at, pl.ds(0, UPDATE_N), grads[rows, :].reshape(UPDATE_N))

    @pl.when(step == last)
    def _():
        first = last * UPDATE_R
        whole = WHOLE_R - first
        rest = SHARD // LANES - WHOLE_R
        for r0, n in ((0, whole), (whole, rest)):
            update(
                pl.ds((first + r0) * LANES, n * LANES),
                pl.ds(r0 * LANES, n * LANES),
                grads[first + r0 : first + r0 + n, :].reshape(n * LANES),
            )
        r0 = whole + rest
        update(
            pl.ds(SHARD - REST, REST),
            pl.ds(r0 * LANES, REST),
            grads[first + r0 : first + r0 + 1, 0:REST].reshape(REST),
        )


def gather_grads(slab_ref, own_ref, core_ref, vfe_ref, norm_ref, quarter_ref, nat, grads):
    join_chunks(slab_ref, quarter_ref, own_ref, core_ref)
    vfe = vfe_ref[0:VFE_R, :]
    squares = vfe_ref[VFE_R : VFE_R + 1, :][0, 0] + jnp.sum(vfe * vfe)
    norm = jnp.sqrt(jnp.broadcast_to(squares, (8, LANES)))
    norm_ref[0, 0] = norm[0, 0]
    scale = (clip_level / jnp.maximum(norm, clip_level))[0:1, :]
    grads[FLAT_R:, :] = jnp.zeros((grads.shape[0] - FLAT_R, LANES), f32)
    span = 480
    for s in range(SLABS):

        @pl.when(slab_ref[0] == s)
        def _(s=s):
            lanes, first = 16 + 28 * s, 15 - 4 * s
            low = max(0, min(SHARD_T // 2, (WIDE_T[0] - STRIDE_T * s + 1) // 2))
            high = max(low, min(SHARD_T // 2, (WIDE_T[1] - STRIDE_T * s + 1) // 2))
            for a, b, wide in ((0, low, False), (low, high, True), (high, SHARD_T // 2, False)):

                def block(i, carry, wide=wide):
                    base = pl.multiple_of(32 * i, 32)
                    even, odd = quarter_ref[2 * i].astype(f32), quarter_ref[2 * i + 1].astype(f32)
                    if wide:
                        nat[pl.ds(base, 16, stride=2), :] = even
                        nat[pl.ds(base + 1, 16, stride=2), :] = odd
                    else:
                        nat[pl.ds(base, 16), :] = even
                        nat[pl.ds(base + 16, 16), :] = odd
                    return carry

                if b > a:
                    lax.fori_loop(a, b, block, 0, unroll=4)
            if s == 0:
                nat[0:VFE_R, :] = vfe
            lane = lane_of((span, LANES))
            count = FLAT_R // span + (FLAT_R % span > 0)
            for i in range(count):
                r0 = i * span
                n = min(span, FLAT_R - r0)
                here = lane_roll(nat[first + r0 : first + r0 + n, :], -lanes)
                after = lane_roll(nat[first + r0 + 1 : first + r0 + 1 + n, :], -lanes)
                grads[r0 : r0 + n, :] = jnp.where(lane[:n] < LANES - lanes, here, after) * scale


def update_shard(info, own, core, vfe, params, moment1, moment2):
    block = pl.BlockSpec((UPDATE_N,), lambda i: (i,))
    steps = pl.cdiv(SHARD, UPDATE_N)
    return pl.pallas_call(
        update_kernel,
        grid=(steps,),
        out_shape=(shape((SHARD,)),) * 3 + (shape((1, 1)),),
        in_specs=[smem()] + [vmem()] * 6,
        out_specs=(block,) * 3 + (smem(),),
        scratch_shapes=[
            pltpu.VMEM((PAD_T, TILE, LANES), bf16),
            pltpu.VMEM((5120, LANES), f32),
            pltpu.VMEM((steps * UPDATE_R, LANES), f32),
        ],
        compiler_params=pltpu.CompilerParams(vmem_limit_bytes=24 * 1024 * 1024),
    )(info, own, core, vfe, params, moment1, moment2)


PART = 5
PARTS = PTS // PART
WIDE = PART * VOX
VFE_SCRATCH = [
    pltpu.VMEM((VOX // LANES, PTS * 16, LANES), f32),
    pltpu.VMEM((16, LANES), f32),
    pltpu.VMEM((64, LANES), f32),
]


def spread_points(points_ref, x_scr):
    x_scr[...] = jnp.zeros_like(x_scr)
    for c in range(7):
        plane = points_ref[c].astype(f32)
        for b in range(VOX // LANES):
            x_scr[b, pl.ds(c, PTS, stride=16), :] = plane[:, b * LANES : (b + 1) * LANES]


def vfe_weights(rows_ref, w1_scr, w2_scr):
    line = rows_ref[0].astype(f32)
    lane = lane_of((16, LANES))
    for o in range(VF1):
        w1_scr[o : o + 1, :] = jnp.where(lane < 7, lane_roll(line, -(16 + 7 * o)), 0.0)[15:16]
    two = rows_ref[1].astype(f32)
    for k in range(4):
        w2_scr[pl.ds(k, 16, stride=4), :] = jnp.where(lane < 32, lane_roll(two, -32 * k), 0.0)
    w1 = w1_scr[...].astype(bf16)[:, 0:16]
    w2 = w2_scr[...]
    w2a = w2.astype(bf16)[:, 0:16]
    w2b = lane_roll(w2, -16).astype(bf16)[:, 0:16]
    w3 = rows_ref[2:10].reshape(FC, LANES)
    w3a = w3[:, 0:64]
    w3b = lane_roll(w3.astype(f32), -64).astype(bf16)[:, 0:64]
    return w1, w2a, w2b, w3a, w3b


def points_part(ref, i):
    return jnp.concatenate(
        [
            ref[b, pl.ds(pl.multiple_of((PART * i + k) * 16, 16), 16), :]
            for k in range(PART)
            for b in range(VOX // LANES)
        ],
        1,
    )


def set_points_part(ref, i, value):
    for k in range(PART):
        for b in range(VOX // LANES):
            at = k * VOX + b * LANES
            ref[b, pl.ds(pl.multiple_of((PART * i + k) * 16, 16), 16), :] = value[:, at : at + LANES]


def part_sum(value):
    total = value[:, 0:VOX]
    for k in range(1, PART):
        total = total + value[:, k * VOX : (k + 1) * VOX]
    return total


def valid_part(i, counts):
    return jnp.concatenate([(PART * i + k < counts).astype(f32) for k in range(PART)], 1)


def widen(value):
    return jnp.concatenate([value] * PART, 1)


LOW = (PARTS, 16, WIDE)
MID = (PARTS, 64, WIDE)
HIGH = (PARTS, 128, WIDE)


def vfe_front(weights, counts, inverse, x_scr, j1_ref, j2_ref, kept=None, done=None):
    w1, w2a, w2b, w3a, w3b = weights
    total = jnp.zeros((VF1, VOX), f32)
    for i in range(PARTS):
        x = points_part(x_scr, i).astype(bf16)
        z = mm(w1, x)
        value = silu(z)
        j1_ref[i] = value.astype(bf16)
        if kept is not None:
            kept[0][i] = x
            kept[1][i] = silu_slope(z).astype(bf16)
        total = total + part_sum(value * valid_part(i, counts))
    mean_one = (total * inverse).astype(bf16)
    shared_two = widen(mm(w2b, mean_one))
    total = jnp.zeros((VF2, VOX), f32)
    for i in range(PARTS):
        z = mm(w2a, j1_ref[i]) + shared_two
        value = silu(z)
        j2_ref[i] = value.astype(bf16)
        if kept is not None:
            kept[2][i] = silu_slope(z).astype(bf16)
            done(i)
        total = total + part_sum(value * valid_part(i, counts))
    mean_two = (total * inverse).astype(bf16)
    shared_three = widen(mm(w3b, mean_two))
    return mean_one, mean_two, shared_three


def encode_kernel(
    points_ref, counts_ref, cells_ref, rows_ref, out_ref, s3_ref,
    x_scr, w1_scr, w2_scr, j1_scr, j2_scr, s3_scr, sems,
):
    spread_points(points_ref, x_scr)
    weights = vfe_weights(rows_ref, w1_scr, w2_scr)
    counts = counts_ref[...]
    inverse = 1.0 / counts.astype(f32)
    _, _, shared_three = vfe_front(weights, counts, inverse, x_scr, j1_scr, j2_scr)
    w3a = weights[3]
    wide_inverse = widen(inverse)
    total = jnp.zeros((FC, VOX), f32)
    copies = []
    for i in range(PARTS):
        z = mm(w3a, j2_scr[i]) + shared_three
        gate = sigmoid(z)
        value = z * gate
        share = valid_part(i, counts) * wide_inverse
        s3_scr[i] = ((gate + value - value * gate) * share).astype(bf16)
        copies += begin([s3_scr.at[i]], [s3_ref.at[i]], sems, i)
        total = total + part_sum(value * share)
    features = total.astype(bf16)
    cells = cells_ref[...]
    row = row_of((16, VOX))
    places = jnp.where(row == 0, cells // GX, cells % GX).astype(f32).astype(bf16)
    out_ref[0:FC, :] = features
    out_ref[FC : FC + 16, :] = places
    finish(copies)


def encode(points, counts, cells, rows):
    return call(
        encode_kernel,
        10,
        20,
        (away((FC + 16, VOX)), away(HIGH)),
        [vmem()] * 4,
        (vmem(), anywhere()),
        VFE_SCRATCH
        + [
            pltpu.VMEM((PARTS, 16, WIDE), bf16),
            pltpu.VMEM((PARTS, 64, WIDE), bf16),
            pltpu.VMEM((PARTS, 128, WIDE), bf16),
            pltpu.SemaphoreType.DMA((PARTS,)),
        ],
    )(points, counts, cells, rows)


def encode_slopes_kernel(
    points_ref, counts_ref, rows_ref,
    x_ref, j1_ref, j2_ref, s1_ref, s2_ref, m1_ref, m2_ref,
    x_scr, w1_scr, w2_scr, xs_scr, j1_scr, j2_scr, s1_scr, s2_scr, sems,
):
    spread_points(points_ref, x_scr)
    weights = vfe_weights(rows_ref, w1_scr, w2_scr)
    counts = counts_ref[...]
    inverse = 1.0 / counts.astype(f32)
    copies = []

    def done(i):
        if i == 0:
            copies.extend(begin((xs_scr, j1_scr, s1_scr), (x_ref, j1_ref, s1_ref), sems, 0))
        copies.extend(
            begin((j2_scr.at[i], s2_scr.at[i]), (j2_ref.at[i], s2_ref.at[i]), sems, 3 + 2 * i)
        )

    mean_one, mean_two, _ = vfe_front(
        weights, counts, inverse, x_scr, j1_scr, j2_scr, (xs_scr, s1_scr, s2_scr), done
    )
    m1_ref[...] = mean_one
    m2_ref[...] = mean_two
    finish(copies)


def encode_slopes(points, counts, rows):
    return call(
        encode_slopes_kernel,
        7,
        20,
        tuple(away(d) for d in (LOW, LOW, MID, LOW, MID))
        + (shape((VF1, VOX), bf16), shape((VF2, VOX), bf16)),
        [vmem()] * 3,
        (anywhere(),) * 5 + (vmem(),) * 2,
        VFE_SCRATCH
        + [pltpu.VMEM(d, bf16) for d in (LOW, LOW, MID, LOW, MID)]
        + [pltpu.SemaphoreType.DMA((3 + 2 * PARTS,))],
    )(points, counts, rows)


def encode_back_kernel(
    counts_ref, rows_ref, g0_ref, g1_ref, g2_ref, g3_ref, j2_scr, s3_scr, m2_ref,
    d2_scr, shared_ref, weight_ref,
    w1_scr, w2_scr,
):
    _, _, _, w3a, w3b = vfe_weights(rows_ref, w1_scr, w2_scr)
    inverse = 1.0 / counts_ref[...].astype(f32)
    grad = g0_ref[...].astype(f32)
    for ref in (g1_ref, g2_ref, g3_ref):
        grad = grad + ref[...].astype(f32)
    grad_three = widen(grad)
    total = jnp.zeros((FC, VOX), f32)
    weight = jnp.zeros((FC, VF2), f32)
    for i in range(PARTS):
        dz = grad_three * s3_scr[i].astype(f32)
        low = dz.astype(bf16)
        d2_scr[i] = mm_tn(w3a, low).astype(bf16)
        total = total + part_sum(dz)
        weight = weight + mm_nt(low, j2_scr[i])
    total = total.astype(bf16)
    weight_ref[...] = jnp.concatenate([weight, mm_nt(total, m2_ref[...])], 1)
    shared_ref[...] = mm_tn(w3b, total) * inverse


def encode_back(counts, rows, grad, j2, s3, m2):
    return call(
        encode_back_kernel,
        8,
        16,
        (held(MID), shape((VF2, VOX)), shape((FC, LANES))),
        [vmem()] * 9,
        (vmem(),) * 3,
        VFE_SCRATCH[1:],
    )(counts, rows, *grad, j2, s3, m2)


def points_back_kernel(
    counts_ref, rows_ref, d2_scr, shared_ref, w3_ref, xs_scr, j1_scr, s1_scr, s2_scr, m1_ref,
    out_ref, weight_ref,
    x_scr, w1_scr, w2_scr, d1_scr,
):
    w1, w2a, w2b, _, _ = vfe_weights(rows_ref, w1_scr, w2_scr)
    counts = counts_ref[...]
    inverse = 1.0 / counts.astype(f32)
    grad_two = widen(shared_ref[...])
    total = jnp.zeros((VF2, VOX), f32)
    grad_w2a = jnp.zeros((VF2, VF1), f32)
    for i in range(PARTS):
        dz = d2_scr[i].astype(f32) + valid_part(i, counts) * grad_two
        dz = dz * s2_scr[i].astype(f32)
        low = dz.astype(bf16)
        d1_scr[i] = mm_tn(w2a, low)
        total = total + part_sum(dz)
        grad_w2a = grad_w2a + mm_nt(low, j1_scr[i])
    total = total.astype(bf16)
    grad_w2b = mm_nt(total, m1_ref[...])
    grad_one = widen(mm_tn(w2b, total) * inverse)
    grad_w1 = jnp.zeros((VF1, 16), f32)
    for i in range(PARTS):
        dz = (d1_scr[i] + valid_part(i, counts) * grad_one) * s1_scr[i].astype(f32)
        low = dz.astype(bf16)
        set_points_part(x_scr, i, mm_tn(w1, low))
        grad_w1 = grad_w1 + mm_nt(low, xs_scr[i])
    for c in range(7):
        for b in range(VOX // LANES):
            out_ref[c, :, b * LANES : (b + 1) * LANES] = x_scr[b, pl.ds(c, PTS, stride=16), :]

    lane = lane_of((16, LANES))
    w1_scr[...] = jnp.concatenate([grad_w1, jnp.zeros((16, LANES - 16), f32)], 1)
    spread = jnp.where(lane < 7, w1_scr[...], 0.0)
    line = jnp.zeros((16, LANES), f32)
    row = row_of((16, LANES))
    for o in range(VF1):
        line = line + jnp.where(row == o, lane_roll(spread, 16 + 7 * o), 0.0)
    line = jnp.sum(line, axis=0, keepdims=True)
    weight_ref[0:16, :] = jnp.where(row == 15, line, 0.0)
    w2_scr[...] = jnp.concatenate([grad_w2a, grad_w2b, jnp.zeros((64, LANES - 32), f32)], 1)
    two = jnp.zeros((16, LANES), f32)
    for k in range(4):
        two = two + lane_roll(w2_scr[pl.ds(k, 16, stride=4), :], 32 * k)
    weight_ref[16:32, :] = two
    weight_ref[32:160, :] = w3_ref[...]
    weight_ref[160:168, :] = jnp.zeros((8, LANES), f32)


def points_back(counts, rows, back, kept):
    return call(
        points_back_kernel,
        7,
        14,
        (shape((7, PTS, VOX)), shape((VFE_R + 8, LANES))),
        [vmem()] * 10,
        (vmem(), vmem()),
        VFE_SCRATCH + [pltpu.VMEM(LOW, f32)],
    )(counts, rows, *back, *kept)


R3 = ROWS + 1
R3W = R3 * GX
R2W = (R3 + 2) * GX
R1W = (R3 + 4) * GX
RG = R3 + 6
RGW = RG * GX
HX = GX // 2
L1_R = ROWS // 2 * HX


def cell_marks(places, first_row):
    value = places.astype(f32)
    high, low = value[0:1], value[1:2]
    upper = high >= GY
    row = jnp.where(upper, high - GY, high)
    column = lax.broadcasted_iota(jnp.int32, (GX, VOX), 0).astype(f32)
    column = (column == low).astype(f32).astype(bf16)
    pieces = []
    for w in range(RG):
        target = first_row - 3 + w
        inside = jnp.logical_and(target >= 0, target < GY)
        target = jnp.where(inside, target, -1).astype(f32)
        pieces.append(column * (row == target).astype(f32).astype(bf16))
    upper = upper.astype(f32)
    return jnp.concatenate(pieces, 0), 1.0 - upper, upper


def conv_weights(rows_ref, start, taps, half, place, scr):
    lane = lane_of((half, LANES))
    left = lane < 64
    for t in range(taps):
        r = []
        for kx in range(3):
            base = start + (3 * t + kx) * half
            r.append(rows_ref[base // TILE : (base + half) // TILE].reshape(half, LANES).astype(f32))
        turned = [lane_roll(v, 64) for v in r]
        at = place(t)
        scr[0, pl.ds(at, half, stride=2), :] = jnp.where(left, r[1], turned[0])
        scr[0, pl.ds(at + 1, half, stride=2), :] = jnp.where(left, turned[1], r[0])
        scr[1, pl.ds(at, half, stride=2), :] = jnp.where(left, r[2], 0.0)
        scr[1, pl.ds(at + 1, half, stride=2), :] = jnp.where(left, turned[2], 0.0)


def conv_weight_grads(out_ref, start, taps, half, place, scr):
    lane = lane_of((half, LANES))
    left = lane < 64
    for t in range(taps):
        at = place(t)
        even = [scr[b, pl.ds(at, half, stride=2), :] for b in range(2)]
        odd = [scr[b, pl.ds(at + 1, half, stride=2), :] for b in range(2)]
        values = (
            jnp.where(left, lane_roll(even[0], 64), odd[0]),
            jnp.where(left, even[0], lane_roll(odd[0], 64)),
            jnp.where(left, even[1], lane_roll(odd[1], 64)),
        )
        for kx in range(3):
            base = start + (3 * t + kx) * half
            out_ref[base // TILE : (base + half) // TILE] = (
                values[kx].astype(bf16).reshape(half // TILE, TILE, LANES)
            )


def both_halves(out_ref, scr):
    for b in range(2):
        out_ref[:, b * LANES : (b + 1) * LANES] = scr[b].astype(bf16)


def keep_halves(scr, value):
    for b in range(2):
        scr[b] = value[:, b * LANES : (b + 1) * LANES]


def tap_place(t):
    return 128 * t


def pair_place(t):
    kd, ky = t // 3, t % 3
    return 128 * ky + 64 * kd if kd < 2 else 384 + 128 * ky


def join_columns(p):
    first, last = p[:, 0:128], p[:, 128:256]
    left = lane_of(first.shape) < 64
    half = jnp.where(left, first + shift_in(last, -1, GX), shift_in(first, 1, GX))
    return half + lane_roll(half, 64)


def split_columns(d):
    left = lane_of(d.shape) < 64
    first = jnp.where(left, d, lane_roll(shift_in(d, -1, GX), 64))
    last = jnp.where(left, shift_in(d, 1, GX), 0.0)
    return jnp.concatenate([first, last], 1).astype(bf16)


def inside_rows(rows, first_row):
    place = first_row + row_of((rows, LANES)) // GX
    return jnp.logical_and(place >= 0, place < GY)


def grid_taps(grid_ref, k):
    return jnp.concatenate(
        [grid_ref[2 * k + kd, ky * GX : ky * GX + R1W, :] for kd in range(3) for ky in range(3)], 1
    )


def pair_taps(ref, at, rows):
    return jnp.concatenate(
        [ref[at, ky * GX : ky * GX + rows, :] for ky in range(3)]
        + [ref[at + 2, ky * GX : ky * GX + rows, :] for ky in range(3)],
        1,
    )


def level_taps(ref):
    planes = {}
    for xp in range(2):
        for yp in range(2):
            count = ROWS // 2 + 1 - yp
            planes[yp, xp] = jnp.concatenate(
                [ref[pl.ds((2 * a + yp) * GX + xp, HX, stride=2), :] for a in range(count)], 0
            )
    pieces = []
    for ky in range(3):
        for kx in range(3):
            v = planes[ky % 2, int(kx != 1)]
            v = v[HX:] if ky == 2 else v[0:L1_R]
            pieces.append((shift_in(v, 1, HX) if kx == 0 else v).astype(bf16))
    return jnp.concatenate(pieces, 1)


def level_taps_back(ref, grad):
    planes = {}
    edge = jnp.zeros((HX, LANES), f32)
    for ky in range(3):
        for kx in range(3):
            t = 3 * ky + kx
            v = grad[:, t * LANES : (t + 1) * LANES]
            v = shift_in(v, -1, HX) if kx == 0 else v
            if ky != 1:
                v = jnp.concatenate([edge, v] if ky == 2 else [v, edge], 0)
            at = (ky % 2, int(kx != 1))
            planes[at] = planes[at] + v if at in planes else v
    for (yp, xp), v in planes.items():
        for a in range(ROWS // 2 + 1 - yp):
            ref[pl.ds((2 * a + yp) * GX + xp, HX, stride=2), :] = v[a * HX : (a + 1) * HX]


GRID = (9, RGW, LANES)
FIRST = (6, R1W, LANES)
SECOND = (6, R2W, LANES)


def volume_kernel(
    slab_ref, f0_ref, f1_ref, f2_ref, f3_ref, own_ref, core_ref,
    level_ref, grid_ref, first_ref, second_ref, taps_ref, z1_ref, z2_ref, z3_ref, z4_ref, w1_ref, w2_ref, w3_ref, w4_ref,
    rows_ref, w1_scr, w2_scr, bird_scr,
):
    join_chunks(slab_ref, rows_ref, own_ref, core_ref)
    w4_ref[...] = rows_ref[LEVEL_T : LEVEL_T + 72].reshape(1152, LANES)
    w2_scr[...] = jnp.zeros_like(w2_scr)
    conv_weights(rows_ref, VFE_R, 9, 64, tap_place, w1_scr)
    both_halves(w1_ref, w1_scr)
    conv_weights(rows_ref, VFE_R + 1728, 9, 32, pair_place, w2_scr)
    both_halves(w2_ref, w2_scr)
    conv_weights(rows_ref, VFE_R + 2592, 9, 32, pair_place, w2_scr)
    both_halves(w3_ref, w2_scr)

    first_row = slab_ref[0] * ROWS - 1
    grid_ref[0] = jnp.zeros((RGW, FC), bf16)
    for slot, f_ref in enumerate((f0_ref, f1_ref, f2_ref, f3_ref)):
        t = jnp.bitwise_xor(slab_ref[0], slot)
        features = f_ref[0:FC, :]
        marks, lower, upper = cell_marks(f_ref[FC : FC + 16, :], first_row)
        both = jnp.concatenate([features * lower.astype(bf16), features * upper.astype(bf16)], 0)
        cells = mm_nt(marks, both).astype(bf16)
        grid_ref[1 + 2 * t] = cells[:, 0:FC]
        grid_ref[2 + 2 * t] = cells[:, FC:]

    first_ref[0] = jnp.zeros((R1W, LANES), bf16)
    first_ref[5] = jnp.zeros((R1W, LANES), bf16)
    keep = inside_rows(R1W, first_row - 2)
    for k in range(4):
        z = join_columns(mm(grid_taps(grid_ref, k), w1_ref[...]))
        z1_ref[k] = jnp.where(keep, silu_slope(z), 0.0).astype(bf16)
        value = jnp.where(keep, silu(z), 0.0).astype(bf16)
        first_ref[k + 1, :, 0:64] = value[:, 0:64]
        first_ref[k, :, 64:128] = value[:, 64:128]
    first_ref[4, :, 64:128] = jnp.zeros((R1W, 64), bf16)

    second_ref[0] = jnp.zeros((R2W, LANES), bf16)
    second_ref[5] = jnp.zeros((R2W, LANES), bf16)
    keep = inside_rows(R2W, first_row - 1)
    for k in range(4):
        z = join_columns(mm(pair_taps(first_ref, k, R2W), w2_ref[...]))
        z2_ref[k] = jnp.where(keep, silu_slope(z), 0.0).astype(bf16)
        value = jnp.where(keep, silu(z), 0.0).astype(bf16)
        second_ref[k + 1, :, 0:64] = value[:, 0:64]
        second_ref[k, :, 64:128] = value[:, 64:128]
    second_ref[4, :, 64:128] = jnp.zeros((R2W, 64), bf16)

    z3 = []
    for k in range(2):
        z3.append(join_columns(mm(pair_taps(second_ref, 2 * k, R3W), w3_ref[...])))
    z = jnp.where(lane_of((R3W, LANES)) < 64, z3[0], z3[1])
    keep = inside_rows(R3W, first_row)
    z3_ref[...] = jnp.where(keep, silu_slope(z), 0.0).astype(bf16)
    bird_scr[...] = jnp.where(keep, silu(z), 0.0)
    taps = level_taps(bird_scr)
    taps_ref[...] = taps
    z = mm(taps, w4_ref[...])
    z4_ref[...] = silu_slope(z).astype(bf16)
    level_ref[...] = silu(z).astype(bf16)


LEVEL_T = VFE_T + 216


def volume(info, features, early):
    return call(
        volume_kernel,
        11,
        56,
        (
            shape((L1_R, LANES), bf16),
            away(GRID),
            away(FIRST),
            away(SECOND),
            away((L1_R, 1152)),
            away((4, R1W, LANES)),
            away((4, R2W, LANES)),
            away((R3W, LANES)),
            away((L1_R, LANES)),
            away((1152, 256)),
            away((768, 256)),
            away((768, 256)),
            away((1152, LANES)),
        ),
        [smem()] + [vmem()] * 6,
        (vmem(),) * 13,
        [
            pltpu.VMEM((PAD_T, TILE, LANES), bf16),
            pltpu.VMEM((2, 1152, LANES), f32),
            pltpu.VMEM((2, 768, LANES), f32),
            pltpu.VMEM((R3W, LANES), f32),
        ],
    )(info, *features, *early)


def volume_back(
    slab, f_ref, level_grad, z1_ref, z2_ref, z3_ref, z4_ref, w1_ref, w2_ref, w3_ref, w4_ref,
    out_refs, d4_ref, sp3_ref, sp2_ref, sp1_ref,
    bird_scr, acc2, acc1, accg,
):
    dz = (level_grad * z4_ref[...].astype(f32)).astype(bf16)
    d4_ref[...] = dz
    level_taps_back(bird_scr, mm_nt(dz, w4_ref[...]))
    dz = bird_scr[...] * z3_ref[...].astype(f32)
    acc2[...] = jnp.zeros_like(acc2)
    acc1[...] = jnp.zeros_like(acc1)
    accg[...] = jnp.zeros_like(accg)

    def pair_back(acc, at, rows, spread, weight):
        back = mm_nt(spread, weight)
        for ky in range(3):
            acc[at, ky * GX : ky * GX + rows, :] += back[:, 128 * ky : 128 * ky + 128]
            acc[at + 2, ky * GX : ky * GX + rows, :] += back[:, 384 + 128 * ky : 512 + 128 * ky]

    def layer_grad(acc, m):
        return acc[m] + lane_roll(acc[m - 1], 64)

    for k in range(2):
        spread = split_columns(dz if k == 0 else lane_roll(dz, 64))
        sp3_ref[k] = spread
        pair_back(acc2, 2 * k, R3W, spread, w3_ref[...])
    for k in range(4):
        spread = split_columns(layer_grad(acc2, k + 1) * z2_ref[k].astype(f32))
        sp2_ref[k] = spread
        pair_back(acc1, k, R2W, spread, w2_ref[...])
    for k in range(4):
        spread = split_columns(layer_grad(acc1, k + 1) * z1_ref[k].astype(f32))
        sp1_ref[k] = spread
        back = mm_nt(spread, w1_ref[...])
        for kd in range(3):
            for ky in range(3):
                t = 3 * kd + ky
                accg[2 * k + kd, ky * GX : ky * GX + R1W, :] += back[:, 128 * t : 128 * t + 128]
    for slot in range(SLABS):
        t = jnp.bitwise_xor(slab, slot)
        marks, lower, upper = cell_marks(f_ref[slot, FC : FC + 16, :], slab * ROWS - 1)
        both = jnp.concatenate([accg[1 + 2 * t].astype(bf16), accg[2 + 2 * t].astype(bf16)], 1)
        both = mm_tn(both, marks)
        value = both[0:FC] * lower + both[FC:] * upper
        out_refs[slot][...] = value.astype(bf16)


SPREADS = ((L1_R, LANES), (2, R3W, 256), (4, R2W, 256), (4, R1W, 256))
BACK_IN = (
    (SLABS, FC + 16, VOX),
    (4, R1W, LANES),
    (4, R2W, LANES),
    (R3W, LANES),
    (L1_R, LANES),
    (1152, 256),
    (768, 256),
    (768, 256),
    (1152, LANES),
)


def volume_weights_kernel(
    info_ref, taps_ref, d4_ref, second_ref, sp3_ref, first_ref, sp2_ref, grid_ref, sp1_ref,
    own_ref, core_ref,
    weight_ref, g1_scr, g2_scr,
):
    weight_ref[0:VFE_T] = jnp.zeros((VFE_T, TILE, LANES), bf16)
    weight_ref[VFE_T + EARLY_T : PAD_T] = jnp.zeros((PAD_T - VFE_T - EARLY_T, TILE, LANES), bf16)
    total = mm_tn(taps_ref[...], d4_ref[...])
    weight_ref[LEVEL_T : LEVEL_T + 72] = total.astype(bf16).reshape(72, TILE, LANES)
    total = mm_tn(pair_taps(second_ref, 0, R3W), sp3_ref[0])
    keep_halves(g2_scr, total + mm_tn(pair_taps(second_ref, 2, R3W), sp3_ref[1]))
    conv_weight_grads(weight_ref, VFE_R + 2592, 9, 32, pair_place, g2_scr)
    total = jnp.zeros((768, 256), f32)
    for k in range(4):
        total = total + mm_tn(pair_taps(first_ref, k, R2W), sp2_ref[k])
    keep_halves(g2_scr, total)
    conv_weight_grads(weight_ref, VFE_R + 1728, 9, 32, pair_place, g2_scr)
    total = jnp.zeros((1152, 256), f32)
    for k in range(4):
        total = total + mm_tn(grid_taps(grid_ref, k), sp1_ref[k])
    keep_halves(g1_scr, total)
    conv_weight_grads(weight_ref, VFE_R, 9, 64, tap_place, g1_scr)
    split_chunks(info_ref, weight_ref, 0, own_ref, core_ref)


def volume_weights(info, kept, grads):
    grid, first, second, taps = kept
    d4, sp3, sp2, sp1 = grads
    return call(
        volume_weights_kernel,
        8,
        14,
        (shape(CHUNKS, bf16),) * 2,
        [smem()] + [vmem()] * 8,
        (vmem(),) * 2,
        [
            pltpu.VMEM((PAD_T, TILE, LANES), bf16),
            pltpu.VMEM((2, 1152, LANES), f32),
            pltpu.VMEM((2, 768, LANES), f32),
        ],
    )(info, taps, d4, second, sp3, first, sp2, grid, sp1)


def split_planes(ref, height, width):
    planes = []
    for yp in range(2):
        for xp in range(2):
            planes.append(
                jnp.concatenate(
                    [
                        ref[pl.ds((2 * a + yp) * width + xp, width // 2, stride=2), :]
                        for a in range(height // 2)
                    ],
                    0,
                )
            )
    return planes


def merge_planes(ref, planes, height, width):
    half = width // 2
    for yp in range(2):
        for xp in range(2):
            for a in range(height // 2):
                ref[pl.ds((2 * a + yp) * width + xp, half, stride=2), :] = planes[2 * yp + xp][
                    a * half : a * half + half
                ]


def stride_taps(planes, width):
    pieces = []
    for ky in range(3):
        for kx in range(3):
            v = planes[2 * (ky != 1) + (kx != 1)]
            v = shift_in(v, 1, width) if kx == 0 else v
            pieces.append((shift_out(v, 1, width) if ky == 0 else v).astype(bf16))
    return jnp.concatenate(pieces, 1)


def stride_taps_back(grad, width):
    planes = [None] * 4
    channels = grad.shape[1] // 9
    for ky in range(3):
        for kx in range(3):
            t = 3 * ky + kx
            v = grad[:, t * channels : (t + 1) * channels]
            v = shift_out(v, -1, width) if ky == 0 else v
            v = shift_in(v, -1, width) if kx == 0 else v
            at = 2 * (ky != 1) + (kx != 1)
            planes[at] = v if planes[at] is None else planes[at] + v
    return planes


def full_taps(v, width):
    across = [shift_in(v, 1 - kx, width).astype(bf16) for kx in range(3)]
    return jnp.concatenate(
        [shift_out(across[kx], 1 - ky, width) for ky in range(3) for kx in range(3)], 1
    )


def full_taps_back(grad, width):
    channels = grad.shape[1] // 9
    total = None
    for kx in range(3):
        column = None
        for ky in range(3):
            t = 3 * ky + kx
            v = shift_out(grad[:, t * channels : (t + 1) * channels], ky - 1, width)
            column = v if column is None else column + v
        column = shift_in(column, kx - 1, width)
        total = column if total is None else total + column
    return total


HY = 16
CELLS = HY * HX


def region_kernel(
    slab_ref, counts_ref, l0_ref, l1_ref, l2_ref, l3_ref, anchors_ref, goals_ref,
    s0_ref, s1_ref, s2_ref, s3_ref, s4_ref, s5_ref, s6_ref, s7_ref,
    f0_in, f1_in, f2_in, f3_in, z1_in, z2_in, z3_in, z4_in, w1_in, w2_in, w3_in, w4_in,
    maps_ref, own_ref, core_ref, o0_ref, o1_ref, o2_ref, o3_ref, d4_ref, sp3_ref, sp2_ref, sp1_ref,
    f_ref, z1_ref, z2_ref, z3_ref, z4_ref, w1_ref, w2_ref, w3_ref, w4_ref,
    bird_scr, acc2, acc1, accg, back_sems,
    wv, gr,
    l1_scr, l2_scr, zu1_scr, zu2_scr, zu3_scr, head_scr, maps_scr, two_scr, three_scr,
):
    slab = slab_ref[0]
    chip, core = batch_place(slab_ref)
    late = (s0_ref, s1_ref, s2_ref, s3_ref, s4_ref, s5_ref, s6_ref, s7_ref)
    for n, (ref, (chips, slots)) in enumerate(zip(late, LATE_ORDER * 2)):
        for k in range(4):
            shard = jnp.bitwise_xor(slab_ref[2], slots[k])
            at = chunk_start(chip, core if n < 4 else 1 - core, chips[k])
            wv[shard, pl.ds(at, CHUNK_T)] = ref[k // 2, k % 2]
    gr[0 : PLANE_T0 + 1] = jnp.zeros((PLANE_T0 + 1, TILE, LANES), bf16)
    gr[PLANE_T0 + 1 + PLANE_T : GRAD_T] = jnp.zeros((GRAD_T - PLANE_T0 - 1 - PLANE_T, TILE, LANES), bf16)
    for slot, ref in enumerate((l0_ref, l1_ref, l2_ref, l3_ref)):
        at = pl.multiple_of(jnp.bitwise_xor(slab, slot) * L1_R, L1_R)
        l1_scr[pl.ds(at, L1_R), :] = ref[...].astype(f32)
    level_one = l1_scr[...]
    arrive = begin(
        (f0_in, f1_in, f2_in, f3_in, z1_in, z2_in, z3_in, z4_in, w1_in, w2_in, w3_in, w4_in),
        (f_ref.at[0], f_ref.at[1], f_ref.at[2], f_ref.at[3], z1_ref, z2_ref, z3_ref, z4_ref, w1_ref, w2_ref, w3_ref, w4_ref),
        back_sems,
    )
    for s in range(1, SLABS):
        wv[s, 0:2] = wv[s, 0:2] + wv[s - 1, STRIDE_T : STRIDE_T + 2]

    def tiles_of(tile, tiles):
        pieces = []
        while tiles:
            s = min((tile + 1) // STRIDE_T, SLABS - 1)
            at = tile + 1 - STRIDE_T * s
            size = min(tiles, STRIDE_T - at) if s < SLABS - 1 else tiles
            pieces.append(wv[s, at : at + size])
            tile, tiles = tile + size, tiles - size
        return pieces[0] if len(pieces) == 1 else jnp.concatenate(pieces, 0)

    def narrow(tile, rows):
        return tiles_of(tile, rows // 16).reshape(rows, LANES)

    def wide(tile, rows):
        both = tiles_of(tile, rows // 8).reshape(rows // 16, 2, TILE, LANES)
        return jnp.concatenate(
            [both[:, 0].reshape(rows, LANES), both[:, 1].reshape(rows, LANES)], 1
        )

    def keep_narrow(tile, value):
        at = tile + 1
        tiles = value.shape[0] // 16
        gr[at : at + tiles] = value.astype(bf16).reshape(tiles, TILE, LANES)

    def keep_wide(tile, value):
        at = tile + 1
        tiles = value.shape[0] // 16
        value = value.astype(bf16)
        left = value[:, 0:128].reshape(tiles, 1, TILE, LANES)
        right = value[:, 128:256].reshape(tiles, 1, TILE, LANES)
        gr[at : at + 2 * tiles] = jnp.concatenate([left, right], 1).reshape(2 * tiles, TILE, LANES)

    t_two, t_three, t_up1, t_up2, t_up3, t_head = 297, 369, 513, 657, 721, 1233

    taps_two = stride_taps(split_planes(l1_scr, 16, 32), 16)
    z2 = mm(taps_two, narrow(t_two, 1152))
    level_two = silu(z2).astype(bf16)
    l2_scr[...] = level_two.astype(f32)
    taps_three = stride_taps(split_planes(l2_scr, 8, 16), 8)
    z3 = mm(taps_three, wide(t_three, 1152))
    level_three = silu(z3).astype(bf16)

    taps_up = full_taps(level_one, 32)
    zu1_scr[...] = mm(taps_up, wide(t_up1, 1152))
    for g in range(4):
        zu2_scr[g] = mm(level_two, wide(t_up2 + 16 * g, 128))
    for g in range(16):
        zu3_scr[g] = mm(level_three, wide(t_up3 + 32 * g, 256))

    lane = lane_of((96, LANES))
    rows = narrow(t_head, 96).astype(f32)
    for c in range(8):
        head_scr[pl.ds(c, 96, stride=8), :] = jnp.where(lane < 16, lane_roll(rows, -16 * c), 0.0)
    head = head_scr[...].astype(bf16)
    head_a, head_b, head_c = head[0:256], head[256:512], head[512:768]
    joined_a = silu(zu1_scr[...]).astype(bf16)
    for g in range(4):
        p, q = g // 2, g % 2
        part = mm(silu(zu2_scr[g]).astype(bf16), head_b)
        for a in range(8):
            two_scr[pl.ds((2 * a + p) * HX + q, 16, stride=2), :] = part[16 * a : 16 * a + 16]
    for g in range(16):
        p, q = g // 4, g % 4
        part = mm(silu(zu3_scr[g]).astype(bf16), head_c)
        for a in range(4):
            three_scr[pl.ds((4 * a + p) * HX + q, 8, stride=4), :] = part[8 * a : 8 * a + 8]
    maps = mm(joined_a, head_a) + two_scr[...] + three_scr[...]
    maps = jnp.transpose(maps)[0:16]
    own = jnp.zeros((16, 128), f32)
    for s in range(SLABS):
        own = own + jnp.where(slab == s, maps[:, 128 * s : 128 * s + 128], 0.0)
    for i in range(HY // SLABS):
        maps_ref[0, :, i, :] = own[:, HX * i : HX * i + HX]

    live_count = counts_ref[0]
    anchors = anchors_ref[...]
    slot = row_of((40, CELLS))
    place = lane_of((40, CELLS))
    positive = [
        jnp.sum(
            jnp.logical_and(anchors == place + k * CELLS, slot < live_count).astype(f32),
            axis=0,
            keepdims=True,
        )
        for k in range(2)
    ]
    row = row_of((16, CELLS))
    second = jnp.logical_or(row == 1, row >= 9)
    marked = jnp.where(second, positive[1], positive[0])
    share = 1.0 / jnp.maximum(live_count.astype(f32), 1.0)
    class_grad = (sigmoid(maps) - marked) * (1.0 / (2.0 * CELLS))
    box_grad = jnp.clip(maps - goals_ref[...], -1.0, 1.0) * marked * share
    dmaps = jnp.where(row < 2, class_grad, box_grad)
    dmaps = jnp.transpose(jnp.concatenate([dmaps, jnp.zeros((LANES - 16, CELLS), f32)], 0))
    maps_scr[...] = dmaps
    low = dmaps.astype(bf16)

    dhead_a = mm_tn(joined_a, low)
    dz = mm_nt(low, head_a) * silu_slope(zu1_scr[...])
    dz = dz.astype(bf16)
    keep_wide(t_up1, mm_tn(taps_up, dz))
    dlevel_one = full_taps_back(mm_nt(dz, wide(t_up1, 1152)), 32)

    dhead_b = jnp.zeros((256, LANES), f32)
    dlevel_two = jnp.zeros((128, 128), f32)
    for g in range(4):
        p, q = g // 2, g % 2
        part = jnp.concatenate(
            [maps_scr[pl.ds((2 * a + p) * HX + q, 16, stride=2), :] for a in range(8)], 0
        ).astype(bf16)
        z = zu2_scr[g]
        dhead_b = dhead_b + mm_tn(silu(z).astype(bf16), part)
        dz = (mm_nt(part, head_b) * silu_slope(z)).astype(bf16)
        keep_wide(t_up2 + 16 * g, mm_tn(level_two, dz))
        dlevel_two = dlevel_two + mm_nt(dz, wide(t_up2 + 16 * g, 128))
    dhead_c = jnp.zeros((256, LANES), f32)
    dlevel_three = jnp.zeros((32, 256), f32)
    for g in range(16):
        p, q = g // 4, g % 4
        part = jnp.concatenate(
            [maps_scr[pl.ds((4 * a + p) * HX + q, 8, stride=4), :] for a in range(4)], 0
        ).astype(bf16)
        z = zu3_scr[g]
        dhead_c = dhead_c + mm_tn(silu(z).astype(bf16), part)
        dz = (mm_nt(part, head_c) * silu_slope(z)).astype(bf16)
        keep_wide(t_up3 + 32 * g, mm_tn(level_three, dz))
        dlevel_three = dlevel_three + mm_nt(dz, wide(t_up3 + 32 * g, 256))

    head_scr[...] = jnp.concatenate([dhead_a, dhead_b, dhead_c], 0)
    rows = jnp.zeros((96, LANES), f32)
    for c in range(8):
        piece = jnp.where(lane < 16, head_scr[pl.ds(c, 96, stride=8), :], 0.0)
        rows = rows + lane_roll(piece, 16 * c)
    keep_narrow(t_head, rows)

    dz = (dlevel_three * silu_slope(z3)).astype(bf16)
    keep_wide(t_three, mm_tn(taps_three, dz))
    merge_planes(l2_scr, stride_taps_back(mm_nt(dz, wide(t_three, 1152)), 8), 8, 16)
    dlevel_two = dlevel_two + l2_scr[...]
    dz = (dlevel_two * silu_slope(z2)).astype(bf16)
    keep_narrow(t_two, mm_tn(taps_two, dz))
    merge_planes(l1_scr, stride_taps_back(mm_nt(dz, narrow(t_two, 1152)), 16), 16, 32)
    dlevel_one = dlevel_one + l1_scr[...]
    l1_scr[...] = dlevel_one
    level_grad = l1_scr[pl.ds(pl.multiple_of(slab * L1_R, L1_R), L1_R), :]
    for s in range(SLABS):

        @pl.when(slab == s)
        def _(s=s):
            start = (15 - 4 * s) * LANES + 16 + 28 * s
            for t in (0, 1) + tuple(range(SHARD_T - 4, PAD_T)):
                tile = STRIDE_T * s - 1 + t
                row = row_of((TILE, LANES))
                if t >= SHARD_T:
                    gr[STRIDE_T * s + t] = jnp.zeros((TILE, LANES), bf16)
                    continue
                if WIDE_T[0] <= tile < WIDE_T[1]:
                    row = 32 * (t // 2) + 2 * row + t % 2
                else:
                    row = TILE * t + row
                at = row * LANES + lane_of((TILE, LANES)) - start
                inside = jnp.logical_and(at >= 0, at < SHARD)
                gr[STRIDE_T * s + t] = jnp.where(
                    inside, gr[STRIDE_T * s + t].astype(f32), 0.0
                ).astype(bf16)

    split_chunks(slab_ref, gr, STRIDE_T * slab, own_ref, core_ref)
    finish(arrive)
    spreads = (d4_ref, sp3_ref, sp2_ref, sp1_ref)
    volume_back(
        slab, f_ref, level_grad, z1_ref, z2_ref, z3_ref, z4_ref, w1_ref, w2_ref, w3_ref, w4_ref,
        (o0_ref, o1_ref, o2_ref, o3_ref), *spreads, bird_scr, acc2, acc1, accg,
    )


LATE_ORDER = (
    ((0, 0, 2, 2), (0, 1, 0, 1)),
    ((1, 1, 3, 3), (0, 1, 0, 1)),
    ((0, 0, 1, 1), (2, 3, 2, 3)),
    ((2, 2, 3, 3), (2, 3, 2, 3)),
)


def region(info, counts, levels, anchors, goals, late, features, kept):
    return call(
        region_kernel,
        20,
        56,
        (
            shape((1, 16, HY // SLABS, HX)),
            shape(CHUNKS, bf16),
            shape(CHUNKS, bf16),
            shape((FC, VOX), bf16),
            shape((FC, VOX), bf16),
            shape((FC, VOX), bf16),
            shape((FC, VOX), bf16),
        )
        + (shape(SPREADS[0], bf16),)
        + tuple(held(d) for d in SPREADS[1:]),
        [smem(), smem()] + [vmem()] * 14 + [anywhere()] * 12,
        (vmem(),) * 11,
        [pltpu.VMEM(d, bf16) for d in BACK_IN]
        + [
            pltpu.VMEM((R3W, LANES), f32),
            pltpu.VMEM((6, R2W, LANES), f32),
            pltpu.VMEM((6, R1W, LANES), f32),
            pltpu.VMEM((9, RGW, LANES), f32),
            pltpu.SemaphoreType.DMA((12,)),
            pltpu.VMEM((SLABS, PAD_T, TILE, LANES), bf16),
            pltpu.VMEM((GRAD_T, TILE, LANES), bf16),
            pltpu.VMEM((512, 128), f32),
            pltpu.VMEM((128, 128), f32),
            pltpu.VMEM((512, 256), f32),
            pltpu.VMEM((4, 128, 256), f32),
            pltpu.VMEM((16, 32, 256), f32),
            pltpu.VMEM((768, LANES), f32),
            pltpu.VMEM((512, LANES), f32),
            pltpu.VMEM((512, LANES), f32),
            pltpu.VMEM((512, LANES), f32),
        ],
    )(info, counts, *levels, anchors, goals, *late, *features, *kept)


def swap(x, axis, bit):
    count = lax.axis_size(axis)
    return lax.ppermute(x, axis, [(i, i ^ bit) for i in range(count)])


def after(x, *earlier):
    return lax.optimization_barrier((x,) + earlier)[0]


def slab_all(x):
    return [x] + [swap(x, "slab", k) for k in range(1, SLABS)]


def plane_all(x):
    return [x] + [swap(x, "batch", 2 * k) for k in range(1, 4)]


def sum_cores(own, other):
    return [(own[k].astype(f32) + other[k].astype(f32)).astype(bf16) for k in range(4)]


def sum_chips(parts):
    total = parts[0].astype(f32)
    for k in range(1, 4):
        total = total + parts[k].astype(f32)
    return total


def send_parts(parts):
    return parts[0:1] + [swap(parts[k], "batch", 2 * k) for k in range(1, 4)]


def send_half(parts):
    return parts[0], parts[1], swap(jnp.stack(parts[2:4]), "batch", 4)


def send_rest(first, second, arrived):
    first = first.astype(f32) + arrived[0].astype(f32)
    second = (second.astype(f32) + arrived[1].astype(f32)).astype(bf16)
    return first, swap(second, "batch", 2)


def to_first(total, low):
    for k in range(1, SLABS):
        total = total + lax.ppermute(low, "slab", [(k, 0)]).astype(f32)
    return total


def from_first(x, slab, *beside):
    far = [lax.ppermute(x, "slab", [(0, k)]) for k in range(SLABS - 1, 0, -1)]
    far[0], *beside = lax.optimization_barrier((far[0],) + beside)
    return jnp.where(slab == 0, x, far[0] + far[1] + far[2]), *beside


def gathered_shards(own):
    batches = lax.axis_size("batch")
    share = PAD_T // batches
    chunk = lax.dynamic_slice_in_dim(own, lax.axis_index("batch") * share, share, 0)
    shards = lax.all_gather(chunk, ("slab", "batch"), axis=0, tiled=True)
    shards = shards.reshape(SLABS, 4, 2, CHUNK_T, TILE, LANES)
    late = []
    for core in range(2):
        for chips, slots in LATE_ORDER:
            part = jnp.stack([shards[s, c, core] for c, s in zip(chips, slots)])
            late.append(part.reshape((2, 2) + part.shape[1:]))
    return (shards[0, :, 0], shards[0, :, 1]), late


def even_odd(whole):
    both = whole.reshape(4, 2, CHUNK_T, TILE, LANES)
    return both[:, 0], both[:, 1]


def body(
    points, point_counts, voxel_cells, pos_anchors, pos_counts, reg_targets, params, moment1, moment2
):
    batches = lax.axis_size("batch")
    slab, batch = lax.axis_index("slab"), lax.axis_index("batch")
    direct = batches == 8
    zero = jnp.zeros_like(slab)
    info = jnp.stack([slab, batch if direct else zero, slab if direct else zero]).astype(jnp.int32)
    counts = point_counts.reshape(1, VOX)
    goals = jnp.pad(reg_targets.reshape(14, CELLS), ((2, 0), (0, 0)))
    anchors = pos_anchors.reshape(40, 1)

    if direct:
        chunk, first = spread_own(info, params)
        near = jnp.stack([chunk, swap(chunk, "slab", 1)])
        far = swap(near, "slab", 2)
        first, goals, anchors = from_first(first, slab, goals, anchors)
        small, early = first, first[VFE_T:]
        early = plane_all(early)
    else:
        flat_rows = jnp.pad(params, (0, FLAT_R * LANES - SHARD)).reshape(FLAT_R, LANES)
        first = spread_first(flat_rows[0:VFE_R])
        small, goals, anchors = from_first(first, slab, goals, anchors)
        early, late = gathered_shards(spread_shard(info, flat_rows))
    encoded, s3 = encode(points, counts, voxel_cells.reshape(1, VOX), small)
    features = slab_all(encoded)
    if direct:
        early = jnp.stack(lax.optimization_barrier((*early, encoded))[0:4])
        early = (early, swap(early, "batch", 1))
        near, far = lax.optimization_barrier((near, far, early[0]))[0:2]
        later, near, far = lax.optimization_barrier((points, near, far))
        late = [near, swap(near, "batch", 4), far, swap(far, "batch", 2)]
        x, j1, j2, s1, s2, m1, m2 = encode_slopes(later, counts, small)
        near, near_y, far, far_x = lax.optimization_barrier((*late, x))[0:4]
        near, far = jnp.stack([near, near_y]), jnp.stack([far, far_x])
        late = [near, swap(near, "batch", 2), far, swap(far, "batch", 4)]
        features[0] = after(features[0], x, near, far)
        late = late + [swap(near, "batch", 1), swap(far, "batch", 1)]
    else:
        x, j1, j2, s1, s2, m1, m2 = encode_slopes(points, counts, small)
    level, grid, first_pad, second_pad, taps, *kept = volume(info, features, early)
    if direct:
        near, near_x, far, far_y, near_c, far_c = late
        near_c, far_c, level = lax.optimization_barrier((near_c, far_c, level))
        levels = slab_all(level)
        near_x, far_y, *levels = lax.optimization_barrier((near_x, far_y, *levels))
        late = [near, near_x, far, far_y, near_c, swap(near_x, "batch", 1), far_c, swap(far_y, "batch", 1)]
    if not direct:
        levels = slab_all(level)
    maps, quarter_own, quarter_core, *feature_back = region(
        info, pos_counts, levels, anchors, goals, late, features, kept
    )
    feature_back, spreads = feature_back[0:4], feature_back[4:]
    feature_grad = feature_back[0:1] + [swap(feature_back[k], "slab", k) for k in range(1, SLABS)]
    early_own, early_core = volume_weights(info, (grid, first_pad, second_pad, taps), spreads)
    if direct:
        quarter_other = swap(quarter_core, "batch", 1)
        early_own, early_core, *feature_grad = lax.optimization_barrier(
            (early_own, early_core, *feature_grad)
        )
        parts = sum_cores(early_own, swap(early_core, "batch", 1))
        *parts, quarter_own, quarter_other = lax.optimization_barrier(
            (*parts, quarter_own, quarter_other)
        )
        quarter = sum_cores(quarter_own, quarter_other)
        parts = send_parts(parts)
        *quarter, feature_grad[0] = lax.optimization_barrier((*quarter, feature_grad[0]))
        quarter = send_half(quarter)
    back = encode_back(counts, small, feature_grad, j2, s3, m2)
    if direct:
        early_chunk = sum_chips(lax.optimization_barrier((*parts, back[1]))[0:4])
        early_low = early_chunk.astype(bf16)
        shared, early_low = lax.optimization_barrier((back[1], early_low))
        back = [back[0], shared, back[2]]
        early_chunk = to_first(early_chunk, early_low)
    points_grad, vfe_grad = points_back(counts, small, back, (x, j1, s1, s2, m1))
    if direct:
        *quarter, vfe_grad = lax.optimization_barrier((*quarter, vfe_grad))
        chunk, chunk_far = send_rest(*quarter)
        early_chunk, chunk = lax.optimization_barrier((early_chunk, chunk))
        chunk = chunk + chunk_far.astype(f32)
        chunk = (chunk + jnp.where(slab == 0, early_chunk, 0.0)).astype(bf16)
        squares = jnp.sum(jnp.square(chunk.astype(f32)))
        final = plane_all(chunk)
    else:
        whole = jnp.stack([quarter_own, quarter_core], 1).astype(f32)
        whole_early = lax.psum(jnp.stack([early_own, early_core], 1).astype(f32), "slab")
        whole = lax.psum(whole + jnp.where(slab == 0, whole_early, 0.0), "batch").astype(bf16)
        squares = jnp.sum(jnp.square(whole.astype(f32))) / batches
        final = even_odd(whole)

    total = vfe_grad + jnp.pad(jnp.broadcast_to(squares, (8, LANES)), ((VFE_R, 0), (0, 0)))
    for axis, size in (("slab", SLABS), ("batch", batches)):
        bit = 1
        while bit < size:
            total = total + swap(total, axis, bit)
            if direct and axis == "batch" and bit == 1:
                *final, total = lax.optimization_barrier((*final, total))
                final = jnp.stack(final)
                final = (final, swap(final, "batch", 1))
            bit *= 2
    new_params, new_moment1, new_moment2, norm = update_shard(
        info, *final, total, params, moment1, moment2
    )
    return (maps, points_grad, new_moment1, new_moment2, new_params, norm.reshape(()))


def solution(mesh):
    in_specs = (
        P(None, None, ("batch", "slab")),
        P(("batch", "slab")),
        P(("batch", "slab")),
        P("batch", None),
        P("batch"),
        P("batch", None, None, None),
        P("slab"),
        P("slab"),
        P("slab"),
    )
    out_specs = (
        P("batch", None, "slab", None),
        P(None, None, ("batch", "slab")),
        P("slab"),
        P("slab"),
        P("slab"),
        P(),
    )
    return jax.shard_map(body, mesh=mesh, in_specs=in_specs, out_specs=out_specs, check_vma=False)
```

```python
import functools
import math

import jax
import jax.numpy as jnp
from jax import lax
from jax.experimental import pallas as pl
from jax.experimental.pallas import tpu as pltpu
from jax.sharding import PartitionSpec as P

VF1 = 16
VF2 = 64
FC = 128
C3 = 64
STEP = 10
GY = 32
GX = 64
PTS = 35
VOX = 512
SLABS = 4
ROWS = GY // SLABS
LANES = 128
NPARAM = 2537584
SHARD = NPARAM // SLABS

TILE = 16
STRIDE_T = 310
SHARD_T = 312
PAD_T = 320
FLAT_R = 4960
EARLY_T = 288
EARLY_R = EARLY_T * TILE
VFE_T = 10
VFE_R = VFE_T * TILE
PLANE_T0 = 297
PLANE_T = 942
GRAD_T = 3 * STRIDE_T + PAD_T
CHUNK_T = PAD_T // 8
WIDE_T = (369, 1233)

beta_one = 0.9
beta_two = 0.999
adam_eps = 1e-08
learn_rate = 0.02
weight_decay = 0.01
clip_level = 0.002

f32 = jnp.float32
bf16 = jnp.bfloat16


def call(kernel, micros, megabytes, out_shape, in_specs, out_specs, scratch=()):
    return pl.pallas_call(
        kernel,
        out_shape=out_shape,
        in_specs=in_specs,
        out_specs=out_specs,
        scratch_shapes=list(scratch),
        compiler_params=pltpu.CompilerParams(vmem_limit_bytes=megabytes * 1024 * 1024),
        cost_estimate=pl.CostEstimate(
            flops=int(micros * 1e9), transcendentals=0, bytes_accessed=int(micros * 3e6)
        ),
    )


def vmem():
    return pl.BlockSpec(memory_space=pltpu.VMEM)


def smem():
    return pl.BlockSpec(memory_space=pltpu.SMEM)


def anywhere():
    return pl.BlockSpec(memory_space=pl.ANY)


def held(dims, dtype=bf16):
    return pltpu.VMEM(dims, dtype)


def away(dims, dtype=bf16):
    return pltpu.HBM(dims, dtype)


def shape(dims, dtype=f32):
    return jax.ShapeDtypeStruct(dims, dtype)


def mm(a, b):
    return lax.dot_general(a, b, (((1,), (0,)), ((), ())), preferred_element_type=f32)


def mm_nt(a, b):
    return lax.dot_general(a, b, (((1,), (1,)), ((), ())), preferred_element_type=f32)


def mm_tn(a, b):
    return lax.dot_general(a, b, (((0,), (0,)), ((), ())), preferred_element_type=f32)


def sigmoid(z):
    return 0.5 * jnp.tanh(0.5 * z) + 0.5


def silu(z):
    return z * sigmoid(z)


def silu_slope(z):
    s = sigmoid(z)
    return s * (1.0 + z * (1.0 - s))


def lane_of(dims):
    return lax.broadcasted_iota(jnp.int32, dims, len(dims) - 1)


def row_of(dims):
    return lax.broadcasted_iota(jnp.int32, dims, 0)


def lane_roll(x, shift):
    shift = shift % x.shape[-1]
    return x if shift == 0 else pltpu.roll(x, shift, x.ndim - 1)


def shift_in(v, d, width):
    if d == 0:
        return v
    place = row_of(v.shape) % width
    keep = place > 0 if d > 0 else place < width - 1
    return jnp.where(keep, pltpu.roll(v, d % v.shape[0], 0), 0.0)


def shift_out(v, d, width):
    if d == 0:
        return v
    edge = jnp.zeros((width,) + v.shape[1:], v.dtype)
    if d > 0:
        return jnp.concatenate([edge, v[:-width]], 0)
    return jnp.concatenate([v[width:], edge], 0)


def begin(sources, targets, sems, first=0):
    copies = [
        pltpu.make_async_copy(a, b, sems.at[first + n])
        for n, (a, b) in enumerate(zip(sources, targets))
    ]
    for c in copies:
        c.start()
    return copies


def finish(copies):
    for c in copies:
        c.wait()


def batch_place(info_ref):
    return info_ref[1] // 2, info_ref[1] % 2


def chunk_start(chip, core, slot):
    return CHUNK_T * (2 * jnp.bitwise_xor(chip, slot) + core)


def join_chunks(info_ref, out_ref, own_ref, core_ref):
    chip, core = batch_place(info_ref)
    for slot in range(4):
        out_ref[pl.ds(chunk_start(chip, core, slot), CHUNK_T)] = own_ref[slot]
        out_ref[pl.ds(chunk_start(chip, 1 - core, slot), CHUNK_T)] = core_ref[slot]


def split_chunks(info_ref, scr, base, own_ref, core_ref):
    chip, core = batch_place(info_ref)
    for slot in range(4):
        own_ref[slot] = scr[pl.ds(base + chunk_start(chip, core, slot), CHUNK_T)].astype(bf16)
        core_ref[slot] = scr[pl.ds(base + chunk_start(chip, 1 - core, slot), CHUNK_T)].astype(bf16)


CHUNKS = (4, CHUNK_T, TILE, LANES)


def spread_kernel(slab_ref, flat_ref, out_ref, nat):
    nat[...] = jnp.zeros_like(nat)
    span = 480
    for s in range(SLABS):

        @pl.when(slab_ref[0] == s)
        def _(s=s):
            lanes, first = 16 + 28 * s, 15 - 4 * s
            lane = lane_of((span, LANES))
            count = FLAT_R // span + (FLAT_R % span > 0)
            for i in range(count):
                r0 = i * span
                n = min(span, FLAT_R - r0)
                rolled = lane_roll(flat_ref[r0 : r0 + n, :], lanes)
                nat[first + r0 : first + r0 + n, :] += jnp.where(lane[:n] >= lanes, rolled, 0.0)
                nat[first + r0 + 1 : first + r0 + 1 + n, :] += jnp.where(
                    lane[:n] < lanes, rolled, 0.0
                )
            low = max(0, min(SHARD_T // 2, (WIDE_T[0] - STRIDE_T * s + 1) // 2))
            high = max(low, min(SHARD_T // 2, (WIDE_T[1] - STRIDE_T * s + 1) // 2))
            for a, b, wide in ((0, low, False), (low, high, True), (high, SHARD_T // 2, False)):

                def block(i, carry, wide=wide):
                    base = pl.multiple_of(32 * i, 32)
                    if wide:
                        even = nat[pl.ds(base, 16, stride=2), :]
                        odd = nat[pl.ds(base + 1, 16, stride=2), :]
                    else:
                        even = nat[pl.ds(base, 16), :]
                        odd = nat[pl.ds(base + 16, 16), :]
                    out_ref[2 * i] = even.astype(bf16)
                    out_ref[2 * i + 1] = odd.astype(bf16)
                    return carry

                if b > a:
                    lax.fori_loop(a, b, block, 0, unroll=4)

    for t in range(SHARD_T, PAD_T):
        out_ref[t] = jnp.zeros((TILE, LANES), bf16)


def spread_shard(slab, flat_rows):
    return call(
        spread_kernel,
        4,
        56,
        shape((PAD_T, TILE, LANES), bf16),
        [smem(), vmem()],
        vmem(),
        [pltpu.VMEM((5120, LANES), f32)],
    )(slab, flat_rows)


CHUNK_R = CHUNK_T * TILE
CHUNK_N = CHUNK_R * LANES
WHOLE_R = SHARD // LANES // 8 * 8
REST = SHARD - SHARD // LANES * LANES


def flat_tail(flat_ref):
    rest_r = SHARD // LANES - WHOLE_R
    rows = flat_ref[pl.ds(WHOLE_R * LANES, rest_r * LANES)].reshape(rest_r, LANES)
    return rows, flat_ref[pl.ds(SHARD - REST, REST)].reshape(1, REST)


def spread_own_kernel(info_ref, flat_ref, chunk_ref, first_ref, x_scr, nat):
    batch = info_ref[1]

    @pl.when(batch == 0)
    def _():
        x_scr[0:TILE, :] = jnp.zeros((TILE, LANES), f32)
        x_scr[TILE:, :] = flat_ref[pl.ds(0, CHUNK_N)].reshape(CHUNK_R, LANES)

    @pl.when(jnp.logical_and(batch > 0, batch < 7))
    def _():
        start = pl.multiple_of(batch * CHUNK_N - TILE * LANES, 1024)
        rows = CHUNK_R + TILE
        x_scr[...] = flat_ref[pl.ds(start, rows * LANES)].reshape(rows, LANES)

    @pl.when(batch == 7)
    def _():
        first_r = 7 * CHUNK_R - TILE
        whole = WHOLE_R - first_r
        x_scr[0:whole, :] = flat_ref[pl.ds(first_r * LANES, whole * LANES)].reshape(whole, LANES)
        x_scr[whole:, :] = jnp.zeros((CHUNK_R + TILE - whole, LANES), f32)
        rows, last = flat_tail(flat_ref)
        x_scr[whole : whole + rows.shape[0], :] = rows
        x_scr[whole + rows.shape[0] : whole + rows.shape[0] + 1, 0:REST] = last

    def shifted(first, lanes, rows):
        lane = lane_of((rows, LANES))
        here = lane_roll(x_scr[TILE - first : TILE - first + rows, :], lanes)
        above = lane_roll(x_scr[TILE - 1 - first : TILE - 1 - first + rows, :], lanes)
        return jnp.where(lane >= lanes, here, above)

    for s in range(SLABS):

        @pl.when(info_ref[0] == s)
        def _(s=s):
            nat[...] = shifted(15 - 4 * s, 16 + 28 * s, CHUNK_R)
            low = max(0, min(SHARD_T // 2, (WIDE_T[0] - STRIDE_T * s + 1) // 2))
            high = max(low, min(SHARD_T // 2, (WIDE_T[1] - STRIDE_T * s + 1) // 2))
            for i in range(CHUNK_T // 2):
                block = batch * (CHUNK_T // 2) + i
                wide = jnp.logical_and(block >= low, block < high)
                even = nat[pl.ds(32 * i, 16, stride=2), :]
                odd = nat[pl.ds(32 * i + 1, 16, stride=2), :]
                top, bottom = nat[32 * i : 32 * i + 16, :], nat[32 * i + 16 : 32 * i + 32, :]
                chunk_ref[2 * i] = jnp.where(wide, even, top).astype(bf16)
                chunk_ref[2 * i + 1] = jnp.where(wide, odd, bottom).astype(bf16)

    first_ref[VFE_T : VFE_T + CHUNK_T] = chunk_ref[...]
    x_scr[0:TILE, :] = jnp.zeros((TILE, LANES), f32)
    x_scr[TILE : TILE + VFE_R, :] = flat_ref[pl.ds(0, VFE_R * LANES)].reshape(VFE_R, LANES)
    rows = shifted(15, 16, VFE_R).astype(bf16)
    first_ref[0:VFE_T] = rows.reshape(VFE_T, TILE, LANES)


def spread_own(info, params):
    return call(
        spread_own_kernel,
        3,
        56,
        (shape((CHUNK_T, TILE, LANES), bf16), shape((VFE_T + CHUNK_T, TILE, LANES), bf16)),
        [smem(), vmem()],
        (vmem(), vmem()),
        [pltpu.VMEM((CHUNK_R + TILE, LANES), f32), pltpu.VMEM((CHUNK_R, LANES), f32)],
    )(info, params)


def spread_first_kernel(flat_ref, out_ref, nat):
    lanes, first = 16, 15
    lane = lane_of((VFE_R, LANES))
    rolled = lane_roll(flat_ref[...], lanes)
    nat[...] = jnp.zeros_like(nat)
    nat[first : first + VFE_R, :] += jnp.where(lane >= lanes, rolled, 0.0)
    nat[first + 1 : first + 1 + VFE_R, :] += jnp.where(lane < lanes, rolled, 0.0)
    out_ref[...] = nat[0:VFE_R, :].astype(bf16).reshape(VFE_T, TILE, LANES)


def spread_first(flat_rows):
    return call(
        spread_first_kernel,
        1,
        56,
        shape((VFE_T, TILE, LANES), bf16),
        [vmem()],
        vmem(),
        [pltpu.VMEM((VFE_R + 32, LANES), f32)],
    )(flat_rows)


UPDATE_R = 1024
UPDATE_N = UPDATE_R * LANES


def update_kernel(
    slab_ref, own_ref, core_ref, vfe_ref, params_ref, moment1_ref, moment2_ref,
    new_params_ref, new_moment1_ref, new_moment2_ref, norm_ref,
    quarter_ref, nat, grads,
):
    step = pl.program_id(0)

    @pl.when(step == 0)
    def _():
        gather_grads(slab_ref, own_ref, core_ref, vfe_ref, norm_ref, quarter_ref, nat, grads)

    def update(source, target, clipped):
        param = params_ref[source]
        moment1 = beta_one * moment1_ref[source] + (1.0 - beta_one) * clipped
        moment2 = beta_two * moment2_ref[source] + (1.0 - beta_two) * clipped * clipped
        root = jnp.sqrt(moment2) + adam_eps * (1.0 - beta_two**STEP) ** 0.5
        rate = learn_rate * (1.0 - beta_two**STEP) ** 0.5 / (1.0 - beta_one**STEP)
        new_moment1_ref[target] = moment1
        new_moment2_ref[target] = moment2
        new_params_ref[target] = (1.0 - learn_rate * weight_decay) * param - rate * (moment1 / root)

    last = SHARD // UPDATE_N

    @pl.when(step < last)
    def _():
        rows = pl.ds(pl.multiple_of(step * UPDATE_R, UPDATE_R), UPDATE_R)
        at = pl.ds(pl.multiple_of(step * UPDATE_N, UPDATE_N), UPDATE_N)
        update(at, pl.ds(0, UPDATE_N), grads[rows, :].reshape(UPDATE_N))

    @pl.when(step == last)
    def _():
        first = last * UPDATE_R
        whole = WHOLE_R - first
        rest = SHARD // LANES - WHOLE_R
        for r0, n in ((0, whole), (whole, rest)):
            update(
                pl.ds((first + r0) * LANES, n * LANES),
                pl.ds(r0 * LANES, n * LANES),
                grads[first + r0 : first + r0 + n, :].reshape(n * LANES),
            )
        r0 = whole + rest
        update(
            pl.ds(SHARD - REST, REST),
            pl.ds(r0 * LANES, REST),
            grads[first + r0 : first + r0 + 1, 0:REST].reshape(REST),
        )


def gather_grads(slab_ref, own_ref, core_ref, vfe_ref, norm_ref, quarter_ref, nat, grads):
    join_chunks(slab_ref, quarter_ref, own_ref, core_ref)
    vfe = vfe_ref[0:VFE_R, :]
    squares = vfe_ref[VFE_R : VFE_R + 1, :][0, 0] + jnp.sum(vfe * vfe)
    norm = jnp.sqrt(jnp.broadcast_to(squares, (8, LANES)))
    norm_ref[0, 0] = norm[0, 0]
    scale = (clip_level / jnp.maximum(norm, clip_level))[0:1, :]
    grads[FLAT_R:, :] = jnp.zeros((grads.shape[0] - FLAT_R, LANES), f32)
    span = 480
    for s in range(SLABS):

        @pl.when(slab_ref[0] == s)
        def _(s=s):
            lanes, first = 16 + 28 * s, 15 - 4 * s
            low = max(0, min(SHARD_T // 2, (WIDE_T[0] - STRIDE_T * s + 1) // 2))
            high = max(low, min(SHARD_T // 2, (WIDE_T[1] - STRIDE_T * s + 1) // 2))
            for a, b, wide in ((0, low, False), (low, high, True), (high, SHARD_T // 2, False)):

                def block(i, carry, wide=wide):
                    base = pl.multiple_of(32 * i, 32)
                    even, odd = quarter_ref[2 * i].astype(f32), quarter_ref[2 * i + 1].astype(f32)
                    if wide:
                        nat[pl.ds(base, 16, stride=2), :] = even
                        nat[pl.ds(base + 1, 16, stride=2), :] = odd
                    else:
                        nat[pl.ds(base, 16), :] = even
                        nat[pl.ds(base + 16, 16), :] = odd
                    return carry

                if b > a:
                    lax.fori_loop(a, b, block, 0, unroll=4)
            if s == 0:
                nat[0:VFE_R, :] = vfe
            lane = lane_of((span, LANES))
            count = FLAT_R // span + (FLAT_R % span > 0)
            for i in range(count):
                r0 = i * span
                n = min(span, FLAT_R - r0)
                here = lane_roll(nat[first + r0 : first + r0 + n, :], -lanes)
                after = lane_roll(nat[first + r0 + 1 : first + r0 + 1 + n, :], -lanes)
                grads[r0 : r0 + n, :] = jnp.where(lane[:n] < LANES - lanes, here, after) * scale


def update_shard(info, own, core, vfe, params, moment1, moment2):
    block = pl.BlockSpec((UPDATE_N,), lambda i: (i,))
    steps = pl.cdiv(SHARD, UPDATE_N)
    return pl.pallas_call(
        update_kernel,
        grid=(steps,),
        out_shape=(shape((SHARD,)),) * 3 + (shape((1, 1)),),
        in_specs=[smem()] + [vmem()] * 6,
        out_specs=(block,) * 3 + (smem(),),
        scratch_shapes=[
            pltpu.VMEM((PAD_T, TILE, LANES), bf16),
            pltpu.VMEM((5120, LANES), f32),
            pltpu.VMEM((steps * UPDATE_R, LANES), f32),
        ],
        compiler_params=pltpu.CompilerParams(vmem_limit_bytes=24 * 1024 * 1024),
    )(info, own, core, vfe, params, moment1, moment2)


PART = 5
PARTS = PTS // PART
WIDE = PART * VOX
VFE_SCRATCH = [
    pltpu.VMEM((VOX // LANES, PTS * 16, LANES), f32),
    pltpu.VMEM((16, LANES), f32),
    pltpu.VMEM((64, LANES), f32),
]


def spread_points(points_ref, x_scr):
    x_scr[...] = jnp.zeros_like(x_scr)
    for c in range(7):
        plane = points_ref[c].astype(f32)
        for b in range(VOX // LANES):
            x_scr[b, pl.ds(c, PTS, stride=16), :] = plane[:, b * LANES : (b + 1) * LANES]


def vfe_weights(rows_ref, w1_scr, w2_scr):
    line = rows_ref[0].astype(f32)
    lane = lane_of((16, LANES))
    for o in range(VF1):
        w1_scr[o : o + 1, :] = jnp.where(lane < 7, lane_roll(line, -(16 + 7 * o)), 0.0)[15:16]
    two = rows_ref[1].astype(f32)
    for k in range(4):
        w2_scr[pl.ds(k, 16, stride=4), :] = jnp.where(lane < 32, lane_roll(two, -32 * k), 0.0)
    w1 = w1_scr[...].astype(bf16)[:, 0:16]
    w2 = w2_scr[...]
    w2a = w2.astype(bf16)[:, 0:16]
    w2b = lane_roll(w2, -16).astype(bf16)[:, 0:16]
    w3 = rows_ref[2:10].reshape(FC, LANES)
    w3a = w3[:, 0:64]
    w3b = lane_roll(w3.astype(f32), -64).astype(bf16)[:, 0:64]
    return w1, w2a, w2b, w3a, w3b


def points_part(ref, i):
    return jnp.concatenate(
        [
            ref[b, pl.ds(pl.multiple_of((PART * i + k) * 16, 16), 16), :]
            for k in range(PART)
            for b in range(VOX // LANES)
        ],
        1,
    )


def set_points_part(ref, i, value):
    for k in range(PART):
        for b in range(VOX // LANES):
            at = k * VOX + b * LANES
            ref[b, pl.ds(pl.multiple_of((PART * i + k) * 16, 16), 16), :] = value[:, at : at + LANES]


def part_sum(value):
    total = value[:, 0:VOX]
    for k in range(1, PART):
        total = total + value[:, k * VOX : (k + 1) * VOX]
    return total


def valid_part(i, counts):
    return jnp.concatenate([(PART * i + k < counts).astype(f32) for k in range(PART)], 1)


def widen(value):
    return jnp.concatenate([value] * PART, 1)


LOW = (PARTS, 16, WIDE)
MID = (PARTS, 64, WIDE)
HIGH = (PARTS, 128, WIDE)


def vfe_front(weights, counts, inverse, x_scr, j1_ref, j2_ref, kept=None, done=None):
    w1, w2a, w2b, w3a, w3b = weights
    total = jnp.zeros((VF1, VOX), f32)
    for i in range(PARTS):
        x = points_part(x_scr, i).astype(bf16)
        z = mm(w1, x)
        value = silu(z)
        j1_ref[i] = value.astype(bf16)
        if kept is not None:
            kept[0][i] = x
            kept[1][i] = silu_slope(z).astype(bf16)
        total = total + part_sum(value * valid_part(i, counts))
    mean_one = (total * inverse).astype(bf16)
    shared_two = widen(mm(w2b, mean_one))
    total = jnp.zeros((VF2, VOX), f32)
    for i in range(PARTS):
        z = mm(w2a, j1_ref[i]) + shared_two
        value = silu(z)
        j2_ref[i] = value.astype(bf16)
        if kept is not None:
            kept[2][i] = silu_slope(z).astype(bf16)
            done(i)
        total = total + part_sum(value * valid_part(i, counts))
    mean_two = (total * inverse).astype(bf16)
    shared_three = widen(mm(w3b, mean_two))
    return mean_one, mean_two, shared_three


def encode_kernel(
    points_ref, counts_ref, cells_ref, rows_ref, out_ref, s3_ref,
    x_scr, w1_scr, w2_scr, j1_scr, j2_scr, s3_scr, sems,
):
    spread_points(points_ref, x_scr)
    weights = vfe_weights(rows_ref, w1_scr, w2_scr)
    counts = counts_ref[...]
    inverse = 1.0 / counts.astype(f32)
    _, _, shared_three = vfe_front(weights, counts, inverse, x_scr, j1_scr, j2_scr)
    w3a = weights[3]
    wide_inverse = widen(inverse)
    total = jnp.zeros((FC, VOX), f32)
    copies = []
    for i in range(PARTS):
        z = mm(w3a, j2_scr[i]) + shared_three
        gate = sigmoid(z)
        value = z * gate
        share = valid_part(i, counts) * wide_inverse
        s3_scr[i] = ((gate + value - value * gate) * share).astype(bf16)
        copies += begin([s3_scr.at[i]], [s3_ref.at[i]], sems, i)
        total = total + part_sum(value * share)
    features = total.astype(bf16)
    cells = cells_ref[...]
    row = row_of((16, VOX))
    places = jnp.where(row == 0, cells // GX, cells % GX).astype(f32).astype(bf16)
    out_ref[0:FC, :] = features
    out_ref[FC : FC + 16, :] = places
    finish(copies)


def encode(points, counts, cells, rows):
    return call(
        encode_kernel,
        10,
        20,
        (away((FC + 16, VOX)), away(HIGH)),
        [vmem()] * 4,
        (vmem(), anywhere()),
        VFE_SCRATCH
        + [
            pltpu.VMEM((PARTS, 16, WIDE), bf16),
            pltpu.VMEM((PARTS, 64, WIDE), bf16),
            pltpu.VMEM((PARTS, 128, WIDE), bf16),
            pltpu.SemaphoreType.DMA((PARTS,)),
        ],
    )(points, counts, cells, rows)


def encode_slopes_kernel(
    points_ref, counts_ref, rows_ref,
    x_ref, j1_ref, j2_ref, s1_ref, s2_ref, m1_ref, m2_ref,
    x_scr, w1_scr, w2_scr, xs_scr, j1_scr, j2_scr, s1_scr, s2_scr, sems,
):
    spread_points(points_ref, x_scr)
    weights = vfe_weights(rows_ref, w1_scr, w2_scr)
    counts = counts_ref[...]
    inverse = 1.0 / counts.astype(f32)
    copies = []

    def done(i):
        if i == 0:
            copies.extend(begin((xs_scr, j1_scr, s1_scr), (x_ref, j1_ref, s1_ref), sems, 0))
        copies.extend(
            begin((j2_scr.at[i], s2_scr.at[i]), (j2_ref.at[i], s2_ref.at[i]), sems, 3 + 2 * i)
        )

    mean_one, mean_two, _ = vfe_front(
        weights, counts, inverse, x_scr, j1_scr, j2_scr, (xs_scr, s1_scr, s2_scr), done
    )
    m1_ref[...] = mean_one
    m2_ref[...] = mean_two
    finish(copies)


def encode_slopes(points, counts, rows):
    return call(
        encode_slopes_kernel,
        7,
        20,
        tuple(away(d) for d in (LOW, LOW, MID, LOW, MID))
        + (shape((VF1, VOX), bf16), shape((VF2, VOX), bf16)),
        [vmem()] * 3,
        (anywhere(),) * 5 + (vmem(),) * 2,
        VFE_SCRATCH
        + [pltpu.VMEM(d, bf16) for d in (LOW, LOW, MID, LOW, MID)]
        + [pltpu.SemaphoreType.DMA((3 + 2 * PARTS,))],
    )(points, counts, rows)


def encode_back_kernel(
    counts_ref, rows_ref, g0_ref, g1_ref, g2_ref, g3_ref, j2_scr, s3_scr, m2_ref,
    d2_scr, shared_ref, weight_ref,
    w1_scr, w2_scr,
):
    _, _, _, w3a, w3b = vfe_weights(rows_ref, w1_scr, w2_scr)
    inverse = 1.0 / counts_ref[...].astype(f32)
    grad = g0_ref[...].astype(f32)
    for ref in (g1_ref, g2_ref, g3_ref):
        grad = grad + ref[...].astype(f32)
    grad_three = widen(grad)
    total = jnp.zeros((FC, VOX), f32)
    weight = jnp.zeros((FC, VF2), f32)
    for i in range(PARTS):
        dz = grad_three * s3_scr[i].astype(f32)
        low = dz.astype(bf16)
        d2_scr[i] = mm_tn(w3a, low).astype(bf16)
        total = total + part_sum(dz)
        weight = weight + mm_nt(low, j2_scr[i])
    total = total.astype(bf16)
    weight_ref[...] = jnp.concatenate([weight, mm_nt(total, m2_ref[...])], 1)
    shared_ref[...] = mm_tn(w3b, total) * inverse


def encode_back(counts, rows, grad, j2, s3, m2):
    return call(
        encode_back_kernel,
        8,
        16,
        (held(MID), shape((VF2, VOX)), shape((FC, LANES))),
        [vmem()] * 9,
        (vmem(),) * 3,
        VFE_SCRATCH[1:],
    )(counts, rows, *grad, j2, s3, m2)


def points_back_kernel(
    counts_ref, rows_ref, d2_scr, shared_ref, w3_ref, xs_scr, j1_scr, s1_scr, s2_scr, m1_ref,
    out_ref, weight_ref,
    x_scr, w1_scr, w2_scr, d1_scr,
):
    w1, w2a, w2b, _, _ = vfe_weights(rows_ref, w1_scr, w2_scr)
    counts = counts_ref[...]
    inverse = 1.0 / counts.astype(f32)
    grad_two = widen(shared_ref[...])
    total = jnp.zeros((VF2, VOX), f32)
    grad_w2a = jnp.zeros((VF2, VF1), f32)
    for i in range(PARTS):
        dz = d2_scr[i].astype(f32) + valid_part(i, counts) * grad_two
        dz = dz * s2_scr[i].astype(f32)
        low = dz.astype(bf16)
        d1_scr[i] = mm_tn(w2a, low)
        total = total + part_sum(dz)
        grad_w2a = grad_w2a + mm_nt(low, j1_scr[i])
    total = total.astype(bf16)
    grad_w2b = mm_nt(total, m1_ref[...])
    grad_one = widen(mm_tn(w2b, total) * inverse)
    grad_w1 = jnp.zeros((VF1, 16), f32)
    for i in range(PARTS):
        dz = (d1_scr[i] + valid_part(i, counts) * grad_one) * s1_scr[i].astype(f32)
        low = dz.astype(bf16)
        set_points_part(x_scr, i, mm_tn(w1, low))
        grad_w1 = grad_w1 + mm_nt(low, xs_scr[i])
    for c in range(7):
        for b in range(VOX // LANES):
            out_ref[c, :, b * LANES : (b + 1) * LANES] = x_scr[b, pl.ds(c, PTS, stride=16), :]

    lane = lane_of((16, LANES))
    w1_scr[...] = jnp.concatenate([grad_w1, jnp.zeros((16, LANES - 16), f32)], 1)
    spread = jnp.where(lane < 7, w1_scr[...], 0.0)
    line = jnp.zeros((16, LANES), f32)
    row = row_of((16, LANES))
    for o in range(VF1):
        line = line + jnp.where(row == o, lane_roll(spread, 16 + 7 * o), 0.0)
    line = jnp.sum(line, axis=0, keepdims=True)
    weight_ref[0:16, :] = jnp.where(row == 15, line, 0.0)
    w2_scr[...] = jnp.concatenate([grad_w2a, grad_w2b, jnp.zeros((64, LANES - 32), f32)], 1)
    two = jnp.zeros((16, LANES), f32)
    for k in range(4):
        two = two + lane_roll(w2_scr[pl.ds(k, 16, stride=4), :], 32 * k)
    weight_ref[16:32, :] = two
    weight_ref[32:160, :] = w3_ref[...]
    weight_ref[160:168, :] = jnp.zeros((8, LANES), f32)


def points_back(counts, rows, back, kept):
    return call(
        points_back_kernel,
        7,
        14,
        (shape((7, PTS, VOX)), shape((VFE_R + 8, LANES))),
        [vmem()] * 10,
        (vmem(), vmem()),
        VFE_SCRATCH + [pltpu.VMEM(LOW, f32)],
    )(counts, rows, *back, *kept)


R3 = ROWS + 1
R3W = R3 * GX
R2W = (R3 + 2) * GX
R1W = (R3 + 4) * GX
RG = R3 + 6
RGW = RG * GX
HX = GX // 2
L1_R = ROWS // 2 * HX


def cell_marks(places, first_row):
    value = places.astype(f32)
    high, low = value[0:1], value[1:2]
    upper = high >= GY
    row = jnp.where(upper, high - GY, high)
    column = lax.broadcasted_iota(jnp.int32, (GX, VOX), 0).astype(f32)
    column = (column == low).astype(f32).astype(bf16)
    pieces = []
    for w in range(RG):
        target = first_row - 3 + w
        inside = jnp.logical_and(target >= 0, target < GY)
        target = jnp.where(inside, target, -1).astype(f32)
        pieces.append(column * (row == target).astype(f32).astype(bf16))
    upper = upper.astype(f32)
    return jnp.concatenate(pieces, 0), 1.0 - upper, upper


def conv_weights(rows_ref, start, taps, half, place, scr):
    lane = lane_of((half, LANES))
    left = lane < 64
    for t in range(taps):
        r = []
        for kx in range(3):
            base = start + (3 * t + kx) * half
            r.append(rows_ref[base // TILE : (base + half) // TILE].reshape(half, LANES).astype(f32))
        turned = [lane_roll(v, 64) for v in r]
        at = place(t)
        scr[0, pl.ds(at, half, stride=2), :] = jnp.where(left, r[1], turned[0])
        scr[0, pl.ds(at + 1, half, stride=2), :] = jnp.where(left, turned[1], r[0])
        scr[1, pl.ds(at, half, stride=2), :] = jnp.where(left, r[2], 0.0)
        scr[1, pl.ds(at + 1, half, stride=2), :] = jnp.where(left, turned[2], 0.0)


def conv_weight_grads(out_ref, start, taps, half, place, scr):
    lane = lane_of((half, LANES))
    left = lane < 64
    for t in range(taps):
        at = place(t)
        even = [scr[b, pl.ds(at, half, stride=2), :] for b in range(2)]
        odd = [scr[b, pl.ds(at + 1, half, stride=2), :] for b in range(2)]
        values = (
            jnp.where(left, lane_roll(even[0], 64), odd[0]),
            jnp.where(left, even[0], lane_roll(odd[0], 64)),
            jnp.where(left, even[1], lane_roll(odd[1], 64)),
        )
        for kx in range(3):
            base = start + (3 * t + kx) * half
            out_ref[base // TILE : (base + half) // TILE] = (
                values[kx].astype(bf16).reshape(half // TILE, TILE, LANES)
            )


def both_halves(out_ref, scr):
    for b in range(2):
        out_ref[:, b * LANES : (b + 1) * LANES] = scr[b].astype(bf16)


def keep_halves(scr, value):
    for b in range(2):
        scr[b] = value[:, b * LANES : (b + 1) * LANES]


def tap_place(t):
    return 128 * t


def pair_place(t):
    kd, ky = t // 3, t % 3
    return 128 * ky + 64 * kd if kd < 2 else 384 + 128 * ky


def join_columns(p):
    first, last = p[:, 0:128], p[:, 128:256]
    left = lane_of(first.shape) < 64
    half = jnp.where(left, first + shift_in(last, -1, GX), shift_in(first, 1, GX))
    return half + lane_roll(half, 64)


def split_columns(d):
    left = lane_of(d.shape) < 64
    first = jnp.where(left, d, lane_roll(shift_in(d, -1, GX), 64))
    last = jnp.where(left, shift_in(d, 1, GX), 0.0)
    return jnp.concatenate([first, last], 1).astype(bf16)


def inside_rows(rows, first_row):
    place = first_row + row_of((rows, LANES)) // GX
    return jnp.logical_and(place >= 0, place < GY)


def grid_taps(grid_ref, k):
    return jnp.concatenate(
        [grid_ref[2 * k + kd, ky * GX : ky * GX + R1W, :] for kd in range(3) for ky in range(3)], 1
    )


def pair_taps(ref, at, rows):
    return jnp.concatenate(
        [ref[at, ky * GX : ky * GX + rows, :] for ky in range(3)]
        + [ref[at + 2, ky * GX : ky * GX + rows, :] for ky in range(3)],
        1,
    )


def level_taps(ref):
    planes = {}
    for xp in range(2):
        for yp in range(2):
            count = ROWS // 2 + 1 - yp
            planes[yp, xp] = jnp.concatenate(
                [ref[pl.ds((2 * a + yp) * GX + xp, HX, stride=2), :] for a in range(count)], 0
            )
    pieces = []
    for ky in range(3):
        for kx in range(3):
            v = planes[ky % 2, int(kx != 1)]
            v = v[HX:] if ky == 2 else v[0:L1_R]
            pieces.append((shift_in(v, 1, HX) if kx == 0 else v).astype(bf16))
    return jnp.concatenate(pieces, 1)


def level_taps_back(ref, grad):
    planes = {}
    edge = jnp.zeros((HX, LANES), f32)
    for ky in range(3):
        for kx in range(3):
            t = 3 * ky + kx
            v = grad[:, t * LANES : (t + 1) * LANES]
            v = shift_in(v, -1, HX) if kx == 0 else v
            if ky != 1:
                v = jnp.concatenate([edge, v] if ky == 2 else [v, edge], 0)
            at = (ky % 2, int(kx != 1))
            planes[at] = planes[at] + v if at in planes else v
    for (yp, xp), v in planes.items():
        for a in range(ROWS // 2 + 1 - yp):
            ref[pl.ds((2 * a + yp) * GX + xp, HX, stride=2), :] = v[a * HX : (a + 1) * HX]


GRID = (9, RGW, LANES)
FIRST = (6, R1W, LANES)
SECOND = (6, R2W, LANES)


def volume_kernel(
    slab_ref, f0_ref, f1_ref, f2_ref, f3_ref, own_ref, core_ref,
    level_ref, grid_ref, first_ref, second_ref, taps_ref, z1_ref, z2_ref, z3_ref, z4_ref, w1_ref, w2_ref, w3_ref, w4_ref,
    rows_ref, w1_scr, w2_scr, bird_scr,
):
    join_chunks(slab_ref, rows_ref, own_ref, core_ref)
    w4_ref[...] = rows_ref[LEVEL_T : LEVEL_T + 72].reshape(1152, LANES)
    w2_scr[...] = jnp.zeros_like(w2_scr)
    conv_weights(rows_ref, VFE_R, 9, 64, tap_place, w1_scr)
    both_halves(w1_ref, w1_scr)
    conv_weights(rows_ref, VFE_R + 1728, 9, 32, pair_place, w2_scr)
    both_halves(w2_ref, w2_scr)
    conv_weights(rows_ref, VFE_R + 2592, 9, 32, pair_place, w2_scr)
    both_halves(w3_ref, w2_scr)

    first_row = slab_ref[0] * ROWS - 1
    grid_ref[0] = jnp.zeros((RGW, FC), bf16)
    for slot, f_ref in enumerate((f0_ref, f1_ref, f2_ref, f3_ref)):
        t = jnp.bitwise_xor(slab_ref[0], slot)
        features = f_ref[0:FC, :]
        marks, lower, upper = cell_marks(f_ref[FC : FC + 16, :], first_row)
        both = jnp.concatenate([features * lower.astype(bf16), features * upper.astype(bf16)], 0)
        cells = mm_nt(marks, both).astype(bf16)
        grid_ref[1 + 2 * t] = cells[:, 0:FC]
        grid_ref[2 + 2 * t] = cells[:, FC:]

    first_ref[0] = jnp.zeros((R1W, LANES), bf16)
    first_ref[5] = jnp.zeros((R1W, LANES), bf16)
    keep = inside_rows(R1W, first_row - 2)
    for k in range(4):
        z = join_columns(mm(grid_taps(grid_ref, k), w1_ref[...]))
        z1_ref[k] = jnp.where(keep, silu_slope(z), 0.0).astype(bf16)
        value = jnp.where(keep, silu(z), 0.0).astype(bf16)
        first_ref[k + 1, :, 0:64] = value[:, 0:64]
        first_ref[k, :, 64:128] = value[:, 64:128]
    first_ref[4, :, 64:128] = jnp.zeros((R1W, 64), bf16)

    second_ref[0] = jnp.zeros((R2W, LANES), bf16)
    second_ref[5] = jnp.zeros((R2W, LANES), bf16)
    keep = inside_rows(R2W, first_row - 1)
    for k in range(4):
        z = join_columns(mm(pair_taps(first_ref, k, R2W), w2_ref[...]))
        z2_ref[k] = jnp.where(keep, silu_slope(z), 0.0).astype(bf16)
        value = jnp.where(keep, silu(z), 0.0).astype(bf16)
        second_ref[k + 1, :, 0:64] = value[:, 0:64]
        second_ref[k, :, 64:128] = value[:, 64:128]
    second_ref[4, :, 64:128] = jnp.zeros((R2W, 64), bf16)

    z3 = []
    for k in range(2):
        z3.append(join_columns(mm(pair_taps(second_ref, 2 * k, R3W), w3_ref[...])))
    z = jnp.where(lane_of((R3W, LANES)) < 64, z3[0], z3[1])
    keep = inside_rows(R3W, first_row)
    z3_ref[...] = jnp.where(keep, silu_slope(z), 0.0).astype(bf16)
    bird_scr[...] = jnp.where(keep, silu(z), 0.0)
    taps = level_taps(bird_scr)
    taps_ref[...] = taps
    z = mm(taps, w4_ref[...])
    z4_ref[...] = silu_slope(z).astype(bf16)
    level_ref[...] = silu(z).astype(bf16)


LEVEL_T = VFE_T + 216


def volume(info, features, early):
    return call(
        volume_kernel,
        11,
        24,
        (
            shape((L1_R, LANES), bf16),
            away(GRID),
            away(FIRST),
            away(SECOND),
            away((L1_R, 1152)),
            away((4, R1W, LANES)),
            away((4, R2W, LANES)),
            away((R3W, LANES)),
            away((L1_R, LANES)),
            away((1152, 256)),
            away((768, 256)),
            away((768, 256)),
            away((1152, LANES)),
        ),
        [smem()] + [vmem()] * 6,
        (vmem(),) * 13,
        [
            pltpu.VMEM((PAD_T, TILE, LANES), bf16),
            pltpu.VMEM((2, 1152, LANES), f32),
            pltpu.VMEM((2, 768, LANES), f32),
            pltpu.VMEM((R3W, LANES), f32),
        ],
    )(info, *features, *early)


def volume_back(
    slab, f_ref, level_grad, z1_ref, z2_ref, z3_ref, z4_ref, w1_ref, w2_ref, w3_ref, w4_ref,
    out_refs, d4_ref, sp3_ref, sp2_ref, sp1_ref,
    bird_scr, acc2, acc1, accg,
):
    dz = (level_grad * z4_ref[...].astype(f32)).astype(bf16)
    d4_ref[...] = dz
    level_taps_back(bird_scr, mm_nt(dz, w4_ref[...]))
    dz = bird_scr[...] * z3_ref[...].astype(f32)
    acc2[...] = jnp.zeros_like(acc2)
    acc1[...] = jnp.zeros_like(acc1)
    accg[...] = jnp.zeros_like(accg)

    def pair_back(acc, at, rows, spread, weight):
        back = mm_nt(spread, weight)
        for ky in range(3):
            acc[at, ky * GX : ky * GX + rows, :] += back[:, 128 * ky : 128 * ky + 128]
            acc[at + 2, ky * GX : ky * GX + rows, :] += back[:, 384 + 128 * ky : 512 + 128 * ky]

    def layer_grad(acc, m):
        return acc[m] + lane_roll(acc[m - 1], 64)

    for k in range(2):
        spread = split_columns(dz if k == 0 else lane_roll(dz, 64))
        sp3_ref[k] = spread
        pair_back(acc2, 2 * k, R3W, spread, w3_ref[...])
    for k in range(4):
        spread = split_columns(layer_grad(acc2, k + 1) * z2_ref[k].astype(f32))
        sp2_ref[k] = spread
        pair_back(acc1, k, R2W, spread, w2_ref[...])
    for k in range(4):
        spread = split_columns(layer_grad(acc1, k + 1) * z1_ref[k].astype(f32))
        sp1_ref[k] = spread
        back = mm_nt(spread, w1_ref[...])
        for kd in range(3):
            for ky in range(3):
                t = 3 * kd + ky
                accg[2 * k + kd, ky * GX : ky * GX + R1W, :] += back[:, 128 * t : 128 * t + 128]
    for slot in range(SLABS):
        t = jnp.bitwise_xor(slab, slot)
        marks, lower, upper = cell_marks(f_ref[slot, FC : FC + 16, :], slab * ROWS - 1)
        both = jnp.concatenate([accg[1 + 2 * t].astype(bf16), accg[2 + 2 * t].astype(bf16)], 1)
        both = mm_tn(both, marks)
        value = both[0:FC] * lower + both[FC:] * upper
        out_refs[slot][...] = value.astype(bf16)


SPREADS = ((L1_R, LANES), (2, R3W, 256), (4, R2W, 256), (4, R1W, 256))
BACK_IN = (
    (SLABS, FC + 16, VOX),
    (4, R1W, LANES),
    (4, R2W, LANES),
    (R3W, LANES),
    (L1_R, LANES),
    (1152, 256),
    (768, 256),
    (768, 256),
    (1152, LANES),
)


def volume_weights_kernel(
    info_ref, taps_ref, d4_ref, second_ref, sp3_ref, first_ref, sp2_ref, grid_ref, sp1_ref,
    own_ref, core_ref,
    weight_ref, g1_scr, g2_scr,
):
    weight_ref[0:VFE_T] = jnp.zeros((VFE_T, TILE, LANES), bf16)
    weight_ref[VFE_T + EARLY_T : PAD_T] = jnp.zeros((PAD_T - VFE_T - EARLY_T, TILE, LANES), bf16)
    total = mm_tn(taps_ref[...], d4_ref[...])
    weight_ref[LEVEL_T : LEVEL_T + 72] = total.astype(bf16).reshape(72, TILE, LANES)
    total = mm_tn(pair_taps(second_ref, 0, R3W), sp3_ref[0])
    keep_halves(g2_scr, total + mm_tn(pair_taps(second_ref, 2, R3W), sp3_ref[1]))
    conv_weight_grads(weight_ref, VFE_R + 2592, 9, 32, pair_place, g2_scr)
    total = jnp.zeros((768, 256), f32)
    for k in range(4):
        total = total + mm_tn(pair_taps(first_ref, k, R2W), sp2_ref[k])
    keep_halves(g2_scr, total)
    conv_weight_grads(weight_ref, VFE_R + 1728, 9, 32, pair_place, g2_scr)
    total = jnp.zeros((1152, 256), f32)
    for k in range(4):
        total = total + mm_tn(grid_taps(grid_ref, k), sp1_ref[k])
    keep_halves(g1_scr, total)
    conv_weight_grads(weight_ref, VFE_R, 9, 64, tap_place, g1_scr)
    split_chunks(info_ref, weight_ref, 0, own_ref, core_ref)


def volume_weights(info, kept, grads):
    grid, first, second, taps = kept
    d4, sp3, sp2, sp1 = grads
    return call(
        volume_weights_kernel,
        8,
        14,
        (shape(CHUNKS, bf16),) * 2,
        [smem()] + [vmem()] * 8,
        (vmem(),) * 2,
        [
            pltpu.VMEM((PAD_T, TILE, LANES), bf16),
            pltpu.VMEM((2, 1152, LANES), f32),
            pltpu.VMEM((2, 768, LANES), f32),
        ],
    )(info, taps, d4, second, sp3, first, sp2, grid, sp1)


def split_planes(ref, height, width):
    planes = []
    for yp in range(2):
        for xp in range(2):
            planes.append(
                jnp.concatenate(
                    [
                        ref[pl.ds((2 * a + yp) * width + xp, width // 2, stride=2), :]
                        for a in range(height // 2)
                    ],
                    0,
                )
            )
    return planes


def merge_planes(ref, planes, height, width):
    half = width // 2
    for yp in range(2):
        for xp in range(2):
            for a in range(height // 2):
                ref[pl.ds((2 * a + yp) * width + xp, half, stride=2), :] = planes[2 * yp + xp][
                    a * half : a * half + half
                ]


def stride_taps(planes, width):
    pieces = []
    for ky in range(3):
        for kx in range(3):
            v = planes[2 * (ky != 1) + (kx != 1)]
            v = shift_in(v, 1, width) if kx == 0 else v
            pieces.append((shift_out(v, 1, width) if ky == 0 else v).astype(bf16))
    return jnp.concatenate(pieces, 1)


def stride_taps_back(grad, width):
    planes = [None] * 4
    channels = grad.shape[1] // 9
    for ky in range(3):
        for kx in range(3):
            t = 3 * ky + kx
            v = grad[:, t * channels : (t + 1) * channels]
            v = shift_out(v, -1, width) if ky == 0 else v
            v = shift_in(v, -1, width) if kx == 0 else v
            at = 2 * (ky != 1) + (kx != 1)
            planes[at] = v if planes[at] is None else planes[at] + v
    return planes


def full_taps(v, width):
    across = [shift_in(v, 1 - kx, width).astype(bf16) for kx in range(3)]
    return jnp.concatenate(
        [shift_out(across[kx], 1 - ky, width) for ky in range(3) for kx in range(3)], 1
    )


def full_taps_back(grad, width):
    channels = grad.shape[1] // 9
    total = None
    for kx in range(3):
        column = None
        for ky in range(3):
            t = 3 * ky + kx
            v = shift_out(grad[:, t * channels : (t + 1) * channels], ky - 1, width)
            column = v if column is None else column + v
        column = shift_in(column, kx - 1, width)
        total = column if total is None else total + column
    return total


HY = 16
CELLS = HY * HX


def region_kernel(
    slab_ref, counts_ref, l0_ref, l1_ref, l2_ref, l3_ref, anchors_ref, goals_ref,
    s0_ref, s1_ref, s2_ref, s3_ref, s4_ref, s5_ref, s6_ref, s7_ref,
    f0_in, f1_in, f2_in, f3_in, z1_in, z2_in, z3_in, z4_in, w1_in, w2_in, w3_in, w4_in,
    maps_ref, own_ref, core_ref, o0_ref, o1_ref, o2_ref, o3_ref, d4_ref, sp3_ref, sp2_ref, sp1_ref,
    f_ref, z1_ref, z2_ref, z3_ref, z4_ref, w1_ref, w2_ref, w3_ref, w4_ref,
    bird_scr, acc2, acc1, accg, back_sems,
    wv, gr,
    l1_scr, l2_scr, zu1_scr, zu2_scr, zu3_scr, head_scr, maps_scr, two_scr, three_scr,
):
    slab = slab_ref[0]
    chip, core = batch_place(slab_ref)
    late = (s0_ref, s1_ref, s2_ref, s3_ref, s4_ref, s5_ref, s6_ref, s7_ref)
    for n, (ref, (chips, slots)) in enumerate(zip(late, LATE_ORDER * 2)):
        for k in range(4):
            shard = jnp.bitwise_xor(slab_ref[2], slots[k])
            at = chunk_start(chip, core if n < 4 else 1 - core, chips[k])
            wv[shard, pl.ds(at, CHUNK_T)] = ref[k // 2, k % 2]
    gr[0 : PLANE_T0 + 1] = jnp.zeros((PLANE_T0 + 1, TILE, LANES), bf16)
    gr[PLANE_T0 + 1 + PLANE_T : GRAD_T] = jnp.zeros((GRAD_T - PLANE_T0 - 1 - PLANE_T, TILE, LANES), bf16)
    for slot, ref in enumerate((l0_ref, l1_ref, l2_ref, l3_ref)):
        at = pl.multiple_of(jnp.bitwise_xor(slab, slot) * L1_R, L1_R)
        l1_scr[pl.ds(at, L1_R), :] = ref[...].astype(f32)
    level_one = l1_scr[...]
    arrive = begin(
        (f0_in, f1_in, f2_in, f3_in, z1_in, z2_in, z3_in, z4_in, w1_in, w2_in, w3_in, w4_in),
        (f_ref.at[0], f_ref.at[1], f_ref.at[2], f_ref.at[3], z1_ref, z2_ref, z3_ref, z4_ref, w1_ref, w2_ref, w3_ref, w4_ref),
        back_sems,
    )
    for s in range(1, SLABS):
        wv[s, 0:2] = wv[s, 0:2] + wv[s - 1, STRIDE_T : STRIDE_T + 2]

    def tiles_of(tile, tiles):
        pieces = []
        while tiles:
            s = min((tile + 1) // STRIDE_T, SLABS - 1)
            at = tile + 1 - STRIDE_T * s
            size = min(tiles, STRIDE_T - at) if s < SLABS - 1 else tiles
            pieces.append(wv[s, at : at + size])
            tile, tiles = tile + size, tiles - size
        return pieces[0] if len(pieces) == 1 else jnp.concatenate(pieces, 0)

    def narrow(tile, rows):
        return tiles_of(tile, rows // 16).reshape(rows, LANES)

    def wide(tile, rows):
        both = tiles_of(tile, rows // 8).reshape(rows // 16, 2, TILE, LANES)
        return jnp.concatenate(
            [both[:, 0].reshape(rows, LANES), both[:, 1].reshape(rows, LANES)], 1
        )

    def keep_narrow(tile, value):
        at = tile + 1
        tiles = value.shape[0] // 16
        gr[at : at + tiles] = value.astype(bf16).reshape(tiles, TILE, LANES)

    def keep_wide(tile, value):
        at = tile + 1
        tiles = value.shape[0] // 16
        value = value.astype(bf16)
        left = value[:, 0:128].reshape(tiles, 1, TILE, LANES)
        right = value[:, 128:256].reshape(tiles, 1, TILE, LANES)
        gr[at : at + 2 * tiles] = jnp.concatenate([left, right], 1).reshape(2 * tiles, TILE, LANES)

    t_two, t_three, t_up1, t_up2, t_up3, t_head = 297, 369, 513, 657, 721, 1233

    taps_two = stride_taps(split_planes(l1_scr, 16, 32), 16)
    z2 = mm(taps_two, narrow(t_two, 1152))
    level_two = silu(z2).astype(bf16)
    l2_scr[...] = level_two.astype(f32)
    taps_three = stride_taps(split_planes(l2_scr, 8, 16), 8)
    z3 = mm(taps_three, wide(t_three, 1152))
    level_three = silu(z3).astype(bf16)

    taps_up = full_taps(level_one, 32)
    zu1_scr[...] = mm(taps_up, wide(t_up1, 1152))
    for g in range(4):
        zu2_scr[g] = mm(level_two, wide(t_up2 + 16 * g, 128))
    for g in range(16):
        zu3_scr[g] = mm(level_three, wide(t_up3 + 32 * g, 256))

    lane = lane_of((96, LANES))
    rows = narrow(t_head, 96).astype(f32)
    for c in range(8):
        head_scr[pl.ds(c, 96, stride=8), :] = jnp.where(lane < 16, lane_roll(rows, -16 * c), 0.0)
    head = head_scr[...].astype(bf16)
    head_a, head_b, head_c = head[0:256], head[256:512], head[512:768]
    joined_a = silu(zu1_scr[...]).astype(bf16)
    for g in range(4):
        p, q = g // 2, g % 2
        part = mm(silu(zu2_scr[g]).astype(bf16), head_b)
        for a in range(8):
            two_scr[pl.ds((2 * a + p) * HX + q, 16, stride=2), :] = part[16 * a : 16 * a + 16]
    for g in range(16):
        p, q = g // 4, g % 4
        part = mm(silu(zu3_scr[g]).astype(bf16), head_c)
        for a in range(4):
            three_scr[pl.ds((4 * a + p) * HX + q, 8, stride=4), :] = part[8 * a : 8 * a + 8]
    maps = mm(joined_a, head_a) + two_scr[...] + three_scr[...]
    maps = jnp.transpose(maps)[0:16]
    own = jnp.zeros((16, 128), f32)
    for s in range(SLABS):
        own = own + jnp.where(slab == s, maps[:, 128 * s : 128 * s + 128], 0.0)
    for i in range(HY // SLABS):
        maps_ref[0, :, i, :] = own[:, HX * i : HX * i + HX]

    live_count = counts_ref[0]
    anchors = anchors_ref[...]
    slot = row_of((40, CELLS))
    place = lane_of((40, CELLS))
    positive = [
        jnp.sum(
            jnp.logical_and(anchors == place + k * CELLS, slot < live_count).astype(f32),
            axis=0,
            keepdims=True,
        )
        for k in range(2)
    ]
    row = row_of((16, CELLS))
    second = jnp.logical_or(row == 1, row >= 9)
    marked = jnp.where(second, positive[1], positive[0])
    share = 1.0 / jnp.maximum(live_count.astype(f32), 1.0)
    class_grad = (sigmoid(maps) - marked) * (1.0 / (2.0 * CELLS))
    box_grad = jnp.clip(maps - goals_ref[...], -1.0, 1.0) * marked * share
    dmaps = jnp.where(row < 2, class_grad, box_grad)
    dmaps = jnp.transpose(jnp.concatenate([dmaps, jnp.zeros((LANES - 16, CELLS), f32)], 0))
    maps_scr[...] = dmaps
    low = dmaps.astype(bf16)

    dhead_a = mm_tn(joined_a, low)
    dz = mm_nt(low, head_a) * silu_slope(zu1_scr[...])
    dz = dz.astype(bf16)
    keep_wide(t_up1, mm_tn(taps_up, dz))
    dlevel_one = full_taps_back(mm_nt(dz, wide(t_up1, 1152)), 32)

    dhead_b = jnp.zeros((256, LANES), f32)
    dlevel_two = jnp.zeros((128, 128), f32)
    for g in range(4):
        p, q = g // 2, g % 2
        part = jnp.concatenate(
            [maps_scr[pl.ds((2 * a + p) * HX + q, 16, stride=2), :] for a in range(8)], 0
        ).astype(bf16)
        z = zu2_scr[g]
        dhead_b = dhead_b + mm_tn(silu(z).astype(bf16), part)
        dz = (mm_nt(part, head_b) * silu_slope(z)).astype(bf16)
        keep_wide(t_up2 + 16 * g, mm_tn(level_two, dz))
        dlevel_two = dlevel_two + mm_nt(dz, wide(t_up2 + 16 * g, 128))
    dhead_c = jnp.zeros((256, LANES), f32)
    dlevel_three = jnp.zeros((32, 256), f32)
    for g in range(16):
        p, q = g // 4, g % 4
        part = jnp.concatenate(
            [maps_scr[pl.ds((4 * a + p) * HX + q, 8, stride=4), :] for a in range(4)], 0
        ).astype(bf16)
        z = zu3_scr[g]
        dhead_c = dhead_c + mm_tn(silu(z).astype(bf16), part)
        dz = (mm_nt(part, head_c) * silu_slope(z)).astype(bf16)
        keep_wide(t_up3 + 32 * g, mm_tn(level_three, dz))
        dlevel_three = dlevel_three + mm_nt(dz, wide(t_up3 + 32 * g, 256))

    head_scr[...] = jnp.concatenate([dhead_a, dhead_b, dhead_c], 0)
    rows = jnp.zeros((96, LANES), f32)
    for c in range(8):
        piece = jnp.where(lane < 16, head_scr[pl.ds(c, 96, stride=8), :], 0.0)
        rows = rows + lane_roll(piece, 16 * c)
    keep_narrow(t_head, rows)

    dz = (dlevel_three * silu_slope(z3)).astype(bf16)
    keep_wide(t_three, mm_tn(taps_three, dz))
    merge_planes(l2_scr, stride_taps_back(mm_nt(dz, wide(t_three, 1152)), 8), 8, 16)
    dlevel_two = dlevel_two + l2_scr[...]
    dz = (dlevel_two * silu_slope(z2)).astype(bf16)
    keep_narrow(t_two, mm_tn(taps_two, dz))
    merge_planes(l1_scr, stride_taps_back(mm_nt(dz, narrow(t_two, 1152)), 16), 16, 32)
    dlevel_one = dlevel_one + l1_scr[...]
    l1_scr[...] = dlevel_one
    level_grad = l1_scr[pl.ds(pl.multiple_of(slab * L1_R, L1_R), L1_R), :]
    for s in range(SLABS):

        @pl.when(slab == s)
        def _(s=s):
            start = (15 - 4 * s) * LANES + 16 + 28 * s
            for t in (0, 1) + tuple(range(SHARD_T - 4, PAD_T)):
                tile = STRIDE_T * s - 1 + t
                row = row_of((TILE, LANES))
                if t >= SHARD_T:
                    gr[STRIDE_T * s + t] = jnp.zeros((TILE, LANES), bf16)
                    continue
                if WIDE_T[0] <= tile < WIDE_T[1]:
                    row = 32 * (t // 2) + 2 * row + t % 2
                else:
                    row = TILE * t + row
                at = row * LANES + lane_of((TILE, LANES)) - start
                inside = jnp.logical_and(at >= 0, at < SHARD)
                gr[STRIDE_T * s + t] = jnp.where(
                    inside, gr[STRIDE_T * s + t].astype(f32), 0.0
                ).astype(bf16)

    split_chunks(slab_ref, gr, STRIDE_T * slab, own_ref, core_ref)
    finish(arrive)
    spreads = (d4_ref, sp3_ref, sp2_ref, sp1_ref)
    volume_back(
        slab, f_ref, level_grad, z1_ref, z2_ref, z3_ref, z4_ref, w1_ref, w2_ref, w3_ref, w4_ref,
        (o0_ref, o1_ref, o2_ref, o3_ref), *spreads, bird_scr, acc2, acc1, accg,
    )


LATE_ORDER = (
    ((0, 0, 2, 2), (0, 1, 0, 1)),
    ((1, 1, 3, 3), (0, 1, 0, 1)),
    ((0, 0, 1, 1), (2, 3, 2, 3)),
    ((2, 2, 3, 3), (2, 3, 2, 3)),
)


def region(info, counts, levels, anchors, goals, late, features, kept):
    return call(
        region_kernel,
        20,
        56,
        (
            shape((1, 16, HY // SLABS, HX)),
            shape(CHUNKS, bf16),
            shape(CHUNKS, bf16),
            shape((FC, VOX), bf16),
            shape((FC, VOX), bf16),
            shape((FC, VOX), bf16),
            shape((FC, VOX), bf16),
        )
        + (shape(SPREADS[0], bf16),)
        + tuple(held(d) for d in SPREADS[1:]),
        [smem(), smem()] + [vmem()] * 14 + [anywhere()] * 12,
        (vmem(),) * 11,
        [pltpu.VMEM(d, bf16) for d in BACK_IN]
        + [
            pltpu.VMEM((R3W, LANES), f32),
            pltpu.VMEM((6, R2W, LANES), f32),
            pltpu.VMEM((6, R1W, LANES), f32),
            pltpu.VMEM((9, RGW, LANES), f32),
            pltpu.SemaphoreType.DMA((12,)),
            pltpu.VMEM((SLABS, PAD_T, TILE, LANES), bf16),
            pltpu.VMEM((GRAD_T, TILE, LANES), bf16),
            pltpu.VMEM((512, 128), f32),
            pltpu.VMEM((128, 128), f32),
            pltpu.VMEM((512, 256), f32),
            pltpu.VMEM((4, 128, 256), f32),
            pltpu.VMEM((16, 32, 256), f32),
            pltpu.VMEM((768, LANES), f32),
            pltpu.VMEM((512, LANES), f32),
            pltpu.VMEM((512, LANES), f32),
            pltpu.VMEM((512, LANES), f32),
        ],
    )(info, counts, *levels, anchors, goals, *late, *features, *kept)


def swap(x, axis, bit):
    count = lax.axis_size(axis)
    return lax.ppermute(x, axis, [(i, i ^ bit) for i in range(count)])


def after(x, *earlier):
    return lax.optimization_barrier((x,) + earlier)[0]


def slab_all(x):
    return [x] + [swap(x, "slab", k) for k in range(1, SLABS)]


def plane_all(x):
    return [x] + [swap(x, "batch", 2 * k) for k in range(1, 4)]


def sum_cores(own, other):
    return [(own[k].astype(f32) + other[k].astype(f32)).astype(bf16) for k in range(4)]


def sum_chips(parts):
    total = parts[0].astype(f32)
    for k in range(1, 4):
        total = total + parts[k].astype(f32)
    return total


def send_parts(parts):
    return parts[0:1] + [swap(parts[k], "batch", 2 * k) for k in range(1, 4)]


def send_half(parts):
    return parts[0], parts[1], swap(jnp.stack(parts[2:4]), "batch", 4)


def send_rest(first, second, arrived):
    first = first.astype(f32) + arrived[0].astype(f32)
    second = (second.astype(f32) + arrived[1].astype(f32)).astype(bf16)
    return first, swap(second, "batch", 2)


def to_first(total, low):
    for k in range(1, SLABS):
        total = total + lax.ppermute(low, "slab", [(k, 0)]).astype(f32)
    return total


def from_first(x, slab, *beside):
    far = [lax.ppermute(x, "slab", [(0, k)]) for k in range(SLABS - 1, 0, -1)]
    far[0], *beside = lax.optimization_barrier((far[0],) + beside)
    return jnp.where(slab == 0, x, far[0] + far[1] + far[2]), *beside


def gathered_shards(own):
    batches = lax.axis_size("batch")
    share = PAD_T // batches
    chunk = lax.dynamic_slice_in_dim(own, lax.axis_index("batch") * share, share, 0)
    shards = lax.all_gather(chunk, ("slab", "batch"), axis=0, tiled=True)
    shards = shards.reshape(SLABS, 4, 2, CHUNK_T, TILE, LANES)
    late = []
    for core in range(2):
        for chips, slots in LATE_ORDER:
            part = jnp.stack([shards[s, c, core] for c, s in zip(chips, slots)])
            late.append(part.reshape((2, 2) + part.shape[1:]))
    return (shards[0, :, 0], shards[0, :, 1]), late


def even_odd(whole):
    both = whole.reshape(4, 2, CHUNK_T, TILE, LANES)
    return both[:, 0], both[:, 1]


def body(
    points, point_counts, voxel_cells, pos_anchors, pos_counts, reg_targets, params, moment1, moment2
):
    batches = lax.axis_size("batch")
    slab, batch = lax.axis_index("slab"), lax.axis_index("batch")
    direct = batches == 8
    zero = jnp.zeros_like(slab)
    info = jnp.stack([slab, batch if direct else zero, slab if direct else zero]).astype(jnp.int32)
    counts = point_counts.reshape(1, VOX)
    goals = jnp.pad(reg_targets.reshape(14, CELLS), ((2, 0), (0, 0)))
    anchors = pos_anchors.reshape(40, 1)

    if direct:
        chunk, first = spread_own(info, params)
        near = jnp.stack([chunk, swap(chunk, "slab", 1)])
        far = swap(near, "slab", 2)
        first, goals, anchors = from_first(first, slab, goals, anchors)
        small, early = first, first[VFE_T:]
        early = plane_all(early)
    else:
        flat_rows = jnp.pad(params, (0, FLAT_R * LANES - SHARD)).reshape(FLAT_R, LANES)
        first = spread_first(flat_rows[0:VFE_R])
        small, goals, anchors = from_first(first, slab, goals, anchors)
        early, late = gathered_shards(spread_shard(info, flat_rows))
    encoded, s3 = encode(points, counts, voxel_cells.reshape(1, VOX), small)
    features = slab_all(encoded)
    if direct:
        early = jnp.stack(lax.optimization_barrier((*early, encoded))[0:4])
        early = (early, swap(early, "batch", 1))
        near, far = lax.optimization_barrier((near, far, early[0]))[0:2]
        later, near, far = lax.optimization_barrier((points, near, far))
        late = [near, swap(near, "batch", 4), far, swap(far, "batch", 2)]
        x, j1, j2, s1, s2, m1, m2 = encode_slopes(later, counts, small)
        near, near_y, far, far_x = lax.optimization_barrier((*late, x))[0:4]
        near, far = jnp.stack([near, near_y]), jnp.stack([far, far_x])
        late = [near, swap(near, "batch", 2), far, swap(far, "batch", 4)]
        features[0] = after(features[0], x, near, far)
        late = late + [swap(near, "batch", 1), swap(far, "batch", 1)]
    else:
        x, j1, j2, s1, s2, m1, m2 = encode_slopes(points, counts, small)
    level, grid, first_pad, second_pad, taps, *kept = volume(info, features, early)
    if direct:
        near, near_x, far, far_y, near_c, far_c = late
        near_c, far_c, level = lax.optimization_barrier((near_c, far_c, level))
        levels = slab_all(level)
        near_x, far_y, *levels = lax.optimization_barrier((near_x, far_y, *levels))
        late = [near, near_x, far, far_y, near_c, swap(near_x, "batch", 1), far_c, swap(far_y, "batch", 1)]
    if not direct:
        levels = slab_all(level)
    maps, quarter_own, quarter_core, *feature_back = region(
        info, pos_counts, levels, anchors, goals, late, features, kept
    )
    feature_back, spreads = feature_back[0:4], feature_back[4:]
    feature_grad = feature_back[0:1] + [swap(feature_back[k], "slab", k) for k in range(1, SLABS)]
    early_own, early_core = volume_weights(info, (grid, first_pad, second_pad, taps), spreads)
    if direct:
        quarter_other = swap(quarter_core, "batch", 1)
        early_own, early_core, *feature_grad = lax.optimization_barrier(
            (early_own, early_core, *feature_grad)
        )
        parts = sum_cores(early_own, swap(early_core, "batch", 1))
        *parts, quarter_own, quarter_other = lax.optimization_barrier(
            (*parts, quarter_own, quarter_other)
        )
        quarter = sum_cores(quarter_own, quarter_other)
        parts = send_parts(parts)
        *quarter, feature_grad[0] = lax.optimization_barrier((*quarter, feature_grad[0]))
        quarter = send_half(quarter)
    back = encode_back(counts, small, feature_grad, j2, s3, m2)
    if direct:
        early_chunk = sum_chips(lax.optimization_barrier((*parts, back[1]))[0:4])
        early_low = early_chunk.astype(bf16)
        shared, early_low = lax.optimization_barrier((back[1], early_low))
        back = [back[0], shared, back[2]]
        early_chunk = to_first(early_chunk, early_low)
    points_grad, vfe_grad = points_back(counts, small, back, (x, j1, s1, s2, m1))
    if direct:
        *quarter, vfe_grad = lax.optimization_barrier((*quarter, vfe_grad))
        chunk, chunk_far = send_rest(*quarter)
        early_chunk, chunk = lax.optimization_barrier((early_chunk, chunk))
        chunk = chunk + chunk_far.astype(f32)
        chunk = (chunk + jnp.where(slab == 0, early_chunk, 0.0)).astype(bf16)
        squares = jnp.sum(jnp.square(chunk.astype(f32)))
        final = plane_all(chunk)
    else:
        whole = jnp.stack([quarter_own, quarter_core], 1).astype(f32)
        whole_early = lax.psum(jnp.stack([early_own, early_core], 1).astype(f32), "slab")
        whole = lax.psum(whole + jnp.where(slab == 0, whole_early, 0.0), "batch").astype(bf16)
        squares = jnp.sum(jnp.square(whole.astype(f32))) / batches
        final = even_odd(whole)

    total = vfe_grad + jnp.pad(jnp.broadcast_to(squares, (8, LANES)), ((VFE_R, 0), (0, 0)))
    for axis, size in (("slab", SLABS), ("batch", batches)):
        bit = 1
        while bit < size:
            total = total + swap(total, axis, bit)
            if direct and axis == "batch" and bit == 1:
                *final, total = lax.optimization_barrier((*final, total))
                final = jnp.stack(final)
                final = (final, swap(final, "batch", 1))
            bit *= 2
    new_params, new_moment1, new_moment2, norm = update_shard(
        info, *final, total, params, moment1, moment2
    )
    return (maps, points_grad, new_moment1, new_moment2, new_params, norm.reshape(()))


def solution(mesh):
    in_specs = (
        P(None, None, ("batch", "slab")),
        P(("batch", "slab")),
        P(("batch", "slab")),
        P("batch", None),
        P("batch"),
        P("batch", None, None, None),
        P("slab"),
        P("slab"),
        P("slab"),
    )
    out_specs = (
        P("batch", None, "slab", None),
        P(None, None, ("batch", "slab")),
        P("slab"),
        P("slab"),
        P("slab"),
        P(),
    )
    return jax.shard_map(body, mesh=mesh, in_specs=in_specs, out_specs=out_specs, check_vma=False)
```
